32 devices in a mesh: section: 4 (over y, x), dp: 8 (over z, core).
Axes of the slice: x: 2, y: 2, z: 4, core: 2. Of those that a mesh axis runs over, the one named last changes fastest.
Arguments:
- images_global: bfloat16 [4, 16, 14, 14, 1024], P(None, 'dp'), may hold values from -7 to 7
- images_local: bfloat16 [4, 32, 6, 6, 1024], P(None, 'dp'), may hold values from -7 to 7
- weights: bfloat16 [13631488], P('section'), may hold values from -0.09375 to 0.09375
- norm_gains: float32 [16384], P('section'), may hold values from 0.5 to 1.5
- norm_shifts: float32 [16384], P('section'), may hold values from -0.5 to 0.5
- cotangent_global: bfloat16 [4, 16, 7, 7, 2048], P(None, 'dp'), may hold values from -6 to 6
- cotangent_local: bfloat16 [4, 32, 3, 3, 2048], P(None, 'dp'), may hold values from -6 to 6
Outputs:
- output_global: bfloat16 [4, 16, 7, 7, 2048], P('section', 'dp')
- output_local: bfloat16 [4, 32, 3, 3, 2048], P('section', 'dp')
- gradient_global: bfloat16 [4, 16, 14, 14, 1024], P('section', 'dp')
- gradient_local: bfloat16 [4, 32, 6, 6, 1024], P('section', 'dp')
- weight_gradient: float32 [13631488], P(('section', 'dp'))
- gain_gradient: float32 [16384], P(('section', 'dp'))
- shift_gradient: float32 [16384], P(('section', 'dp'))
The draws below stay inside these ranges and needn't reach their ends.
All inputs are finite; a program needn't handle non-finite values.
Results may differ from the reference program's by a relative error of at most 0.02.
Values may be sent and summed in bfloat16 or wider, within the bound.
A program may use at most 256 MiB of HBM per device.

```python
import jax
import jax.numpy as jnp
from jax import lax

C_IN = 1024
C_MID = 512
C_OUT = 2048
CROPS_G = 2
CROPS_L = 4
GRID_G = 14
GRID_L = 6
MICRO = 4
IMAGES = 8
WSEGMENT = 3407872
GSEGMENT = 4096
N_SECTION = 4


def ramp_scale(base, count):
    levels = jnp.exp(jnp.linspace(jnp.log(0.5), jnp.log(1.5), count)).astype(jnp.float32)
    return base * levels.reshape((1, count) + (1,) * (base.ndim - 2))


def draw_images_global(key, part):
    key = jax.random.fold_in(key, 11)
    shape = (MICRO, IMAGES * CROPS_G, GRID_G, GRID_G, C_IN)
    base = jnp.clip(jax.random.normal(key, shape, jnp.float32), -4.5, 4.5)
    return ramp_scale(base, IMAGES * CROPS_G).astype(jnp.bfloat16)


def draw_images_local(key, part):
    key = jax.random.fold_in(key, 23)
    shape = (MICRO, IMAGES * CROPS_L, GRID_L, GRID_L, C_IN)
    base = jnp.clip(jax.random.normal(key, shape, jnp.float32), -4.5, 4.5)
    return ramp_scale(base, IMAGES * CROPS_L).astype(jnp.bfloat16)


def block_levels(own_key, extent, split, smallest, top_value):
    gain = 1.0
    for axis_at, parts in split:
        heights = jax.random.uniform(jax.random.fold_in(jax.random.fold_in(own_key, 6), axis_at), (parts,), jnp.float32, smallest / len(split), top_value / len(split))
        gain = gain * jnp.repeat(jnp.exp(heights), extent[axis_at] // parts).reshape((-1,) + (1,) * (len(extent) - 1 - axis_at))
    return gain


def noise(own_key, dims, width, reach, pieces=(), dtype=jnp.bfloat16):
    level = block_levels(own_key, dims, pieces, -0.22, 0.18) if pieces else 1.0
    drawn = jax.random.normal(own_key, dims, jnp.float32) * width * level
    return jnp.minimum(jnp.maximum(drawn, -reach), reach).astype(dtype)


def setup_inputs(seed: int = 0) -> dict:
    seeds = jax.random.split(jax.random.key(seed), 8)
    return {
        "images_global": draw_images_global(jax.random.fold_in(seeds[7], 71), 0),
        "images_local": draw_images_local(jax.random.fold_in(seeds[7], 71), 0),
        "weights": noise(seeds[2], (N_SECTION * WSEGMENT,), (9 * C_MID) ** -0.5, 0.09375, ((0, 4),)),
        "norm_gains": jnp.clip(1.0 + 0.1 * jax.random.normal(seeds[3], (N_SECTION * GSEGMENT,), jnp.float32), 0.5, 1.5),
        "norm_shifts": jnp.clip(jax.random.uniform(seeds[4], (N_SECTION * GSEGMENT,), jnp.float32, -0.5, 0.5) * block_levels(seeds[4], (N_SECTION * GSEGMENT,), ((0, 4),), -0.4, 0.0), -0.5, 0.5),
        "cotangent_global": noise(seeds[5], (MICRO, IMAGES * CROPS_G, GRID_G // 2, GRID_G // 2, C_OUT), 1.0, 6.0, ((1, 8),)),
        "cotangent_local": noise(seeds[6], (MICRO, IMAGES * CROPS_L, GRID_L // 2, GRID_L // 2, C_OUT), 1.0, 6.0, ((1, 8),)),
    }


EPSILON = 1e-05

@jax.custom_vjp
def low(v):
    return lax.optimization_barrier(v.astype(jnp.bfloat16)).astype(jnp.float32)

@jax.custom_vjp
def low_back(v):
    return v

def low_keep(v):
    return (low(v), None)

def low_pass(kept, grad):
    return (grad,)

def back_keep(v):
    return (v, None)

def back_low(kept, grad):
    return (low(grad),)
low.defvjp(low_keep, low_pass)
low_back.defvjp(back_keep, back_low)

def normalize_full(before, gain_slice, shift_slice):
    average = lax.optimization_barrier(jnp.mean(before, axis=(0, 1, 2)))
    variance = lax.optimization_barrier(jnp.mean(before * before, axis=(0, 1, 2))) - average * average
    return (before - average) * lax.rsqrt(variance + EPSILON) * gain_slice + shift_slice

def pointwise(pictures, matrix):
    return jnp.einsum('bhwc,cd->bhwd', pictures, matrix, precision=lax.Precision.HIGHEST)

def spatial_conv(pictures, matrix, stride):
    channels = pictures.shape[-1]
    kernel = matrix.reshape(3, 3, channels, matrix.shape[1])
    return lax.conv_general_dilated(pictures, kernel, (stride, stride), ((1, 1), (1, 1)), dimension_numbers=('NHWC', 'HWIO', 'NHWC'), precision=lax.Precision.HIGHEST)

def layer_chain(weight_values, gain_values, shift_values, pictures):

    def weight_matrix(segment_number, start, height, width_cols):
        anchor = segment_number * WSEGMENT + start
        return weight_values[anchor:anchor + height * width_cols].reshape(height, width_cols)

    def norm_at(before, segment_number, start):
        channels = before.shape[-1]
        anchor = segment_number * GSEGMENT + start
        return normalize_full(before, gain_values[anchor:anchor + channels], shift_values[anchor:anchor + channels])
    reduced = low_back(pointwise(pictures, weight_matrix(0, 0, C_IN, C_MID)))
    hidden = low(jax.nn.silu(norm_at(reduced, 0, 0)))
    spatial = low_back(spatial_conv(hidden, weight_matrix(0, C_IN * C_MID, 9 * C_MID, C_MID), 2))
    handed_over = low_back(low(jax.nn.silu(norm_at(spatial, 0, C_MID))))
    sampled_values = low_back(pictures[:, ::2, ::2, :])
    main_term = low_back(pointwise(handed_over, weight_matrix(1, 0, C_MID, C_OUT)))
    short_term = low_back(pointwise(sampled_values, weight_matrix(1, C_MID * C_OUT, C_IN, C_OUT)))
    carried_over = low_back(low(jax.nn.silu(norm_at(main_term, 1, 0) + norm_at(short_term, 1, C_OUT))))
    reduced_two = low_back(pointwise(carried_over, weight_matrix(2, 0, C_OUT, C_MID)))
    hidden_two = low(jax.nn.silu(norm_at(reduced_two, 2, 0)))
    spatial_two = low_back(spatial_conv(hidden_two, weight_matrix(2, C_OUT * C_MID, 9 * C_MID, C_MID), 1))
    handed_two = low_back(low(jax.nn.silu(norm_at(spatial_two, 2, C_MID))))
    expanded = low_back(pointwise(handed_two, weight_matrix(3, 0, C_MID, C_OUT)))
    return jax.nn.silu(norm_at(expanded, 3, 0) + low_back(carried_over))

def reference(images_global, images_local, weights, norm_gains, norm_shifts, cotangent_global, cotangent_local):

    def forward(weight_values, gain_values, shift_values, global_all, local_all):

        def one_micro(pictures_pair):
            return (layer_chain(weight_values, gain_values, shift_values, pictures_pair[0]), layer_chain(weight_values, gain_values, shift_values, pictures_pair[1]))
        return lax.map(jax.checkpoint(one_micro), (global_all, local_all))
    output_values, pullback = jax.vjp(forward, weights.astype(jnp.float32), norm_gains, norm_shifts, images_global.astype(jnp.float32), images_local.astype(jnp.float32))
    gradients = pullback((cotangent_global.astype(jnp.float32), cotangent_local.astype(jnp.float32)))
    return (output_values[0].astype(jnp.bfloat16), output_values[1].astype(jnp.bfloat16), gradients[3].astype(jnp.bfloat16), gradients[4].astype(jnp.bfloat16), gradients[0], gradients[1], gradients[2])
```

```python
import functools

import jax
import jax.numpy as jnp
import numpy as np
from jax import lax
from jax.sharding import PartitionSpec as P

C_IN = 1024
C_MID = 512
C_OUT = 2048
WSEGMENT = 3407872
GSEGMENT = 4096
EPSILON = 1e-05
F32 = jnp.float32
BF16 = jnp.bfloat16


def round_up(value, unit):
    return -(-value // unit) * unit


class Layout:
    def __init__(self, shape_global, shape_local, dp_count):
        self.micro = shape_global[0]
        self.crops = (shape_global[1], shape_local[1])
        self.sides = (shape_global[2] // 2, shape_local[2] // 2)
        used = [crops * side * side for crops, side in zip(self.crops, self.sides)]
        self.used = used
        first = round_up(used[0], 8)
        self.rows = round_up(first + round_up(used[1], 8), 16)
        self.spans = ((0, first), (first, self.rows))
        self.totals = [count * dp_count for count in used]

    def valid(self, down, right):
        flags = np.zeros((self.rows,), bool)
        for (start, _), crops, side in zip(self.spans, self.crops, self.sides):
            for crop in range(crops):
                for i in range(side):
                    for j in range(side):
                        inside = 0 <= i + down < side and 0 <= j + right < side
                        flags[start + (crop * side + i) * side + j] = inside
        return flags

    def shift(self, values, down, right):
        pieces = []
        for (start, stop), side in zip(self.spans, self.sides):
            steps = down * side + right
            pieces.append(jnp.roll(values[..., start:stop, :], -steps, axis=-2))
        flags = jnp.asarray(self.valid(down, right))[:, None]
        return jnp.where(flags, jnp.concatenate(pieces, axis=-2), 0)

    def pack(self, in_global, in_local):
        parts = []
        for part, (start, stop) in zip((in_global, in_local), self.spans):
            pads = [(0, 0)] * (part.ndim - 2) + [(0, stop - start - part.shape[-2]), (0, 0)]
            parts.append(jnp.pad(part, pads))
        return jnp.concatenate(parts, axis=-2)

    def unpack(self, values):
        return [
            values[..., start : start + used, :]
            for (start, _), used in zip(self.spans, self.used)
        ]


def first_taps():
    return [
        (2 * (p != 1) + (q != 1), -(p == 0), -(q == 0)) for p in range(3) for q in range(3)
    ]


def second_taps():
    return [(p - 1, q - 1) for p in range(3) for q in range(3)]


def phases_of(pictures):
    micro, crops, side, _, channels = pictures.shape
    half = side // 2
    split = pictures.reshape(micro, crops, half, 2, half, 2, channels)
    return split.transpose(3, 5, 0, 1, 2, 4, 6).reshape(4, micro, crops * half * half, channels)


def whole_grid(rows, crops, half):
    channels = rows.shape[-1]
    split = rows.reshape(2, 2, crops, half, half, channels)
    return split.transpose(2, 3, 0, 4, 1, 5).reshape(1, crops, 2 * half, 2 * half, channels)


def sending_weights(weights, section, ranks):
    part = C_MID // ranks
    rows = WSEGMENT // (C_MID * ranks)

    def padded(pieces):
        joined = jnp.concatenate(pieces, axis=1)
        return jnp.pad(joined, ((0, 0), (0, rows - joined.shape[1]), (0, 0)))

    def cut(start, height, width):
        return weights[start : start + height * width].reshape(height, width)

    def across(matrix):
        height, width = matrix.shape
        return matrix.reshape(height, ranks, width // ranks).transpose(1, 0, 2)

    def spatial(start):
        return (
            cut(start, 9 * C_MID, C_MID)
            .reshape(9, ranks, part, C_MID)
            .transpose(1, 0, 2, 3)
            .reshape(ranks, 9 * part, C_MID)
        )

    empty = jnp.zeros((ranks, C_IN, part), BF16)

    def first():
        return padded([spatial(C_IN * C_MID)]), across(cut(0, C_IN, C_MID))

    def second():
        return (
            padded([across(cut(0, C_MID, C_OUT)), across(cut(C_MID * C_OUT, C_IN, C_OUT))]),
            empty,
        )

    def third():
        reduce = cut(0, C_OUT, C_MID).reshape(ranks, C_OUT // ranks, C_MID)
        return padded([reduce, spatial(C_OUT * C_MID)]), empty

    def fourth():
        return padded([across(cut(0, C_MID, C_OUT))]), empty

    return lax.switch(section, [first, second, third, fourth])


def segment_gradient(pieces, small, section, ranks):
    part = C_MID // ranks
    total_rows = WSEGMENT // C_MID

    def finished(rows):
        return jnp.pad(rows, ((0, total_rows - rows.shape[0]), (0, 0)))

    def across(block):
        return block.transpose(1, 0, 2).reshape(-1, C_MID)

    def spatial(block):
        return block.reshape(ranks, 9, part, C_MID).transpose(1, 0, 2, 3).reshape(-1, C_MID)

    def first():
        return finished(
            jnp.concatenate(
                [small.transpose(1, 0, 2).reshape(-1, C_MID), spatial(pieces[:, : 9 * part])]
            )
        )

    def second():
        return finished(across(pieces[:, : C_MID + C_IN]))

    def third():
        tall = C_OUT // ranks
        return finished(
            jnp.concatenate(
                [pieces[:, :tall].reshape(-1, C_MID), spatial(pieces[:, tall : tall + 9 * part])]
            )
        )

    def fourth():
        return finished(across(pieces[:, :C_MID]))

    return lax.switch(section, [first, second, third, fourth])


def mat(left, right):
    return jnp.einsum("...rc,cd->...rd", left, right, preferred_element_type=F32)


def mat_back(left, right):
    return jnp.einsum("...rd,cd->...rc", left, right, preferred_element_type=F32)


def inner(left, right):
    return jnp.einsum("rc,rd->cd", left, right, preferred_element_type=F32)


def silu_slope(before):
    sigmoid = jax.nn.sigmoid(before)
    return sigmoid * (1.0 + before * (1.0 - sigmoid))


def per_device(
    images_global, images_local, weights, norm_gains, norm_shifts, cotangent_global, cotangent_local
):
    section = lax.axis_index("section")
    ranks = lax.axis_size("section")
    dp_count = lax.axis_size("dp")
    lay = Layout(images_global.shape, images_local.shape, dp_count)
    micro, rows = lay.micro, lay.rows
    part = C_MID // ranks
    wide = C_OUT // ranks

    pictures = lay.pack(phases_of(images_global), phases_of(images_local))
    cotangent = lay.pack(
        cotangent_global.reshape(micro, -1, C_OUT), cotangent_local.reshape(micro, -1, C_OUT)
    )
    cotangent = lax.dynamic_slice_in_dim(cotangent, section * wide, wide, 2)
    sent, sent_small = sending_weights(weights, section, ranks)
    held = lax.all_to_all(sent, "section", 0, 0, tiled=True)
    a0 = lax.all_to_all(sent_small, "section", 0, 0, tiled=True)[0]
    b0 = held[0, : 9 * part]
    c0 = held[1, :C_MID]
    p0 = held[1, C_MID : C_MID + C_IN]
    a1 = held[2, :wide]
    b1 = held[2, wide : wide + 9 * part]
    c1 = held[3, :C_MID]
    a0_whole = lax.all_gather(a0, "section", axis=1, tiled=True)
    scales = lax.all_gather(jnp.stack([norm_gains, norm_shifts]), "section")

    def norm_slice(segment, start, width):
        block = lax.dynamic_slice_in_dim(
            scales[segment], start + section * (width // ranks), width // ranks, 1
        )
        return block[0], block[1]

    n01 = norm_slice(0, 0, C_MID)
    n02 = norm_slice(0, C_MID, C_MID)
    n11 = norm_slice(1, 0, C_OUT)
    n12 = norm_slice(1, C_OUT, C_OUT)
    n21 = norm_slice(2, 0, C_MID)
    n22 = norm_slice(2, C_MID, C_MID)
    n31 = norm_slice(3, 0, C_OUT)

    mask = jnp.asarray(lay.valid(0, 0))[:, None]

    def group_sums(values):
        if values.ndim == 4:
            values = jnp.sum(values, 0)
        return jnp.stack([jnp.sum(values[:, a:b], 1) for a, b in lay.spans], axis=1)

    def spread(per_group):
        return jnp.concatenate(
            [
                jnp.broadcast_to(per_group[:, k, None], (micro, b - a, per_group.shape[-1]))
                for k, (a, b) in enumerate(lay.spans)
            ],
            axis=1,
        )

    def statistics(values, fold):
        totals = jnp.asarray(lay.totals, F32)[None, :, None] * fold
        sums = jnp.stack([group_sums(values), group_sums(values * values)])
        sums = lax.psum(sums, "dp") / totals
        average = sums[0]
        return spread(average), spread(lax.rsqrt(sums[1] - average * average + EPSILON))

    def normalized(values, stats):
        return (values - stats[0]) * stats[1]

    def change(upstream, normeds, stats, norms, fold):
        totals = jnp.asarray(lay.totals, F32)[None, :, None] * fold
        sums = lax.psum(
            jnp.stack([group_sums(upstream)] + [group_sums(upstream * n) for n in normeds]), "dp"
        )
        result, gains = [], []
        for number, (normed, stat, norm) in enumerate(zip(normeds, stats, norms)):
            gain = norm[0]
            dz = stat[1] * (
                upstream * gain
                - spread(sums[0] * gain / totals)
                - normed * spread(sums[1 + number] * gain / totals)
            )
            result.append(jnp.where(mask, dz, 0).astype(BF16))
            gains.append(
                jnp.stack([jnp.sum(sums[1 + number], (0, 1)), jnp.sum(sums[0], (0, 1))])
            )
        return result, gains

    def scatter(values):
        blocks = values.astype(BF16).reshape(values.shape[:-1] + (ranks, -1))
        blocks = jnp.moveaxis(blocks, -2, 0)
        got = lax.all_to_all(blocks, "section", 0, 0, tiled=True)
        return jnp.sum(got.astype(F32), 0)

    def gather(values):
        return lax.all_gather(values, "section", axis=values.ndim - 1, tiled=True)

    def to_owner(values):
        blocks = jnp.moveaxis(values, -3, 0)
        return lax.all_to_all(blocks, "section", 0, 0, tiled=True)

    z1 = mat(pictures, a0)
    s01 = statistics(z1, 4)
    h1 = normalized(z1, s01) * n01[0] + n01[1]
    hidden = jax.nn.silu(h1).astype(BF16)
    patches0 = jnp.concatenate(
        [lay.shift(hidden[phase], down, right) for phase, down, right in first_taps()], axis=-1
    )
    z2 = scatter(mat(patches0, b0))
    s02 = statistics(z2, 1)
    h0_slice = jax.nn.silu(normalized(z2, s02) * n02[0] + n02[1])
    h0 = gather(jnp.where(mask, h0_slice, 0).astype(BF16))
    sampled = pictures[0]
    zc = mat(h0, c0)
    zs = mat(sampled, p0)
    s11, s12 = statistics(zc, 1), statistics(zs, 1)
    before1 = (
        normalized(zc, s11) * n11[0] + n11[1] + normalized(zs, s12) * n12[0] + n12[1]
    )
    y1 = jnp.where(mask, jax.nn.silu(before1), 0).astype(BF16)
    za = scatter(mat(y1, a1))
    s21 = statistics(za, 1)
    before2 = normalized(za, s21) * n21[0] + n21[1]
    hidden2 = jax.nn.silu(before2).astype(BF16)
    patches1 = jnp.concatenate(
        [lay.shift(hidden2, down, right) for down, right in second_taps()], axis=-1
    )
    zb = scatter(mat(patches1, b1))
    s22 = statistics(zb, 1)
    before3 = normalized(zb, s22) * n22[0] + n22[1]
    h2 = gather(jnp.where(mask, jax.nn.silu(before3), 0).astype(BF16))
    zd = mat(h2, c1)
    s31 = statistics(zd, 1)
    normed31 = normalized(zd, s31)
    before4 = normed31 * n31[0] + n31[1] + y1.astype(F32)
    output = jax.nn.silu(before4).astype(BF16)

    upstream4 = cotangent.astype(F32) * silu_slope(before4)
    skip = upstream4.astype(BF16)
    (ddzd,), (g31,) = change(upstream4, [normed31], [s31], [n31], 1)
    dh2 = scatter(mat_back(ddzd, c1)).astype(BF16).astype(F32)
    (ddzb,), (g22,) = change(
        dh2 * silu_slope(before3), [normalized(zb, s22)], [s22], [n22], 1
    )
    ddzb = gather(ddzb)
    spread1 = mat_back(ddzb, b1)
    da2 = sum(
        lay.shift(spread1[..., k * part : (k + 1) * part], -down, -right)
        for k, (down, right) in enumerate(second_taps())
    )
    (ddza,), (g21,) = change(
        da2 * silu_slope(before2), [normalized(za, s21)], [s21], [n21], 1
    )
    ddza = gather(ddza)
    dy1 = (mat_back(ddza, a1) + skip.astype(F32)).astype(BF16).astype(F32)
    (ddzc, ddzs), (g11, g12) = change(
        dy1 * silu_slope(before1),
        [normalized(zc, s11), normalized(zs, s12)],
        [s11, s12],
        [n11, n12],
        1,
    )
    dh0 = scatter(mat_back(ddzc, c0)).astype(BF16).astype(F32)
    dxs = jnp.sum(to_owner(mat_back(ddzs, p0).astype(BF16)).astype(F32), 0).astype(BF16)
    (ddz2,), (g02,) = change(
        dh0 * silu_slope(normalized(z2, s02) * n02[0] + n02[1]),
        [normalized(z2, s02)],
        [s02],
        [n02],
        1,
    )
    ddz2 = gather(ddz2)
    spread0 = mat_back(ddz2, b0)
    da1 = [0, 0, 0, 0]
    for k, (phase, down, right) in enumerate(first_taps()):
        da1[phase] = da1[phase] + lay.shift(
            spread0[..., k * part : (k + 1) * part], -down, -right
        )
    (ddz1,), (g01,) = change(
        jnp.stack(da1) * silu_slope(h1), [normalized(z1, s01)], [s01], [n01], 4
    )
    own = to_owner(ddz1)
    own = jnp.moveaxis(own, 0, -2).reshape(own.shape[1:-1] + (C_MID,))
    gradient = mat_back(own, a0_whole)
    gradient = jnp.concatenate([gradient[:1] + dxs.astype(F32), gradient[1:]]).astype(BF16)

    def flat(values):
        return values.reshape(-1, values.shape[-1])

    def stacked(pieces):
        joined = jnp.concatenate(pieces)
        return jnp.pad(joined, ((0, WSEGMENT // (C_MID * ranks) - joined.shape[0]), (0, 0)))

    slices = jnp.stack(
        [
            stacked([inner(flat(patches0), flat(ddz2))]),
            stacked([inner(flat(h0), flat(ddzc)), inner(flat(sampled), flat(ddzs))]),
            stacked([inner(flat(y1), flat(ddza)), inner(flat(patches1), flat(ddzb))]),
            stacked([inner(flat(h2), flat(ddzd))]),
        ]
    ).astype(BF16)
    small = inner(flat(pictures), flat(ddz1)).astype(BF16)
    small = jnp.stack([small] + [jnp.zeros_like(small)] * (ranks - 1))
    arrived = lax.all_to_all(slices, "section", 0, 0, tiled=True).astype(F32)
    arrived_small = lax.all_to_all(small, "section", 0, 0, tiled=True).astype(F32)
    segment = segment_gradient(arrived, arrived_small, section, ranks)
    weight_gradient = lax.psum_scatter(segment.reshape(-1), "dp", scatter_dimension=0, tiled=True)

    everything = lax.all_gather(
        jnp.concatenate([g01, g02, g11, g12, g21, g22, g31], axis=1), "section"
    )

    def joined(start, width):
        block = everything[:, :, start : start + width // ranks]
        return jnp.moveaxis(block, 0, 1).reshape(2, width)

    offsets = np.cumsum([0, part, part, wide, wide, part, part])
    f01, f02, f11, f12, f21, f22, f31 = [
        joined(int(start), width)
        for start, width in zip(offsets, [C_MID, C_MID, C_OUT, C_OUT, C_MID, C_MID, C_OUT])
    ]
    blank = jnp.zeros((2, GSEGMENT - 2 * C_MID), F32)
    segments = jnp.stack(
        [
            jnp.concatenate([f01, f02, blank], 1),
            jnp.concatenate([f11, f12], 1),
            jnp.concatenate([f21, f22, blank], 1),
            jnp.concatenate([f31, jnp.zeros((2, GSEGMENT - C_OUT), F32)], 1),
        ]
    )
    share = GSEGMENT // dp_count
    own_norms = lax.dynamic_index_in_dim(segments, section, 0, keepdims=False)
    own_norms = lax.dynamic_slice_in_dim(own_norms, lax.axis_index("dp") * share, share, 1)

    arrived = to_owner(output)
    arrived = jnp.moveaxis(arrived, 0, -2).reshape(rows, C_OUT)
    out_global, out_local = lay.unpack(arrived)
    grad_global, grad_local = lay.unpack(gradient)
    return (
        out_global.reshape(1, lay.crops[0], lay.sides[0], lay.sides[0], C_OUT),
        out_local.reshape(1, lay.crops[1], lay.sides[1], lay.sides[1], C_OUT),
        whole_grid(grad_global, lay.crops[0], lay.sides[0]),
        whole_grid(grad_local, lay.crops[1], lay.sides[1]),
        weight_gradient,
        own_norms[0],
        own_norms[1],
    )


def solution(mesh):
    images = P(None, "dp", None, None, None)
    made = P("section", "dp", None, None, None)
    return jax.shard_map(
        per_device,
        mesh=mesh,
        in_specs=(images, images, P("section"), P("section"), P("section"), images, images),
        out_specs=(made, made, made, made) + (P(("section", "dp")),) * 3,
        check_vma=False,
    )
```

```python
import functools

import jax
import jax.numpy as jnp
import numpy as np
from jax import lax
from jax.experimental import pallas as pl
from jax.experimental.pallas import tpu as pltpu
from jax.sharding import PartitionSpec as P

C_IN = 1024
C_MID = 512
C_OUT = 2048
WSEGMENT = 3407872
GSEGMENT = 4096
EPSILON = 1e-05
F32 = jnp.float32
BF16 = jnp.bfloat16


def round_up(value, unit):
    return -(-value // unit) * unit


class Layout:
    def __init__(self, shape_global, shape_local, dp_count):
        self.micro = shape_global[0]
        self.crops = (shape_global[1], shape_local[1])
        self.sides = (shape_global[2] // 2, shape_local[2] // 2)
        used = [crops * side * side for crops, side in zip(self.crops, self.sides)]
        self.used = used
        first = round_up(used[0], 8)
        self.rows = round_up(first + round_up(used[1], 8), 16)
        self.spans = ((0, first), (first, self.rows))
        self.totals = [count * dp_count for count in used]

    def valid(self, down, right):
        flags = np.zeros((self.rows,), bool)
        for (start, _), crops, side in zip(self.spans, self.crops, self.sides):
            for crop in range(crops):
                for i in range(side):
                    for j in range(side):
                        inside = 0 <= i + down < side and 0 <= j + right < side
                        flags[start + (crop * side + i) * side + j] = inside
        return flags

    def shift(self, values, down, right):
        pieces = []
        for (start, stop), side in zip(self.spans, self.sides):
            steps = down * side + right
            pieces.append(jnp.roll(values[..., start:stop, :], -steps, axis=-2))
        flags = jnp.asarray(self.valid(down, right))[:, None]
        return jnp.where(flags, jnp.concatenate(pieces, axis=-2), 0)

    def pack(self, in_global, in_local):
        parts = []
        for part, (start, stop) in zip((in_global, in_local), self.spans):
            pads = [(0, 0)] * (part.ndim - 2) + [(0, stop - start - part.shape[-2]), (0, 0)]
            parts.append(jnp.pad(part, pads))
        return jnp.concatenate(parts, axis=-2)

    def unpack(self, values):
        return [
            values[..., start : start + used, :]
            for (start, _), used in zip(self.spans, self.used)
        ]


def first_taps():
    return [
        (2 * (p != 1) + (q != 1), -(p == 0), -(q == 0)) for p in range(3) for q in range(3)
    ]


def second_taps():
    return [(p - 1, q - 1) for p in range(3) for q in range(3)]


def phases_of(pictures):
    micro, crops, side, _, channels = pictures.shape
    half = side // 2
    split = pictures.reshape(micro, crops, half, 2, half, 2, channels)
    return split.transpose(3, 5, 0, 1, 2, 4, 6).reshape(4, micro, crops * half * half, channels)


def whole_grid(rows, crops, half):
    channels = rows.shape[-1]
    split = rows.reshape(2, 2, crops, half, half, channels)
    return split.transpose(2, 3, 0, 4, 1, 5).reshape(1, crops, 2 * half, 2 * half, channels)


def segment_gradient(pieces, small, section, ranks):
    part = C_MID // ranks
    total_rows = WSEGMENT // C_MID

    def finished(rows):
        return jnp.pad(rows, ((0, total_rows - rows.shape[0]), (0, 0)))

    def across(block):
        return block.transpose(1, 0, 2).reshape(-1, C_MID)

    def spatial(block):
        return block.reshape(ranks, 9, part, C_MID).transpose(1, 0, 2, 3).reshape(-1, C_MID)

    def first():
        return finished(
            jnp.concatenate(
                [small.transpose(1, 0, 2).reshape(-1, C_MID), spatial(pieces[:, : 9 * part])]
            )
        )

    def second():
        return finished(across(pieces[:, : C_MID + C_IN]))

    def third():
        tall = C_OUT // ranks
        return finished(
            jnp.concatenate(
                [pieces[:, :tall].reshape(-1, C_MID), spatial(pieces[:, tall : tall + 9 * part])]
            )
        )

    def fourth():
        return finished(across(pieces[:, :C_MID]))

    return lax.switch(section, [first, second, third, fourth])


MESH = pl.DeviceIdType.MESH
ROWS, WIDE = WSEGMENT // C_MID, WSEGMENT // C_OUT
SUM_Z2, SUM_ZA, SUM_ZB, SUM_DH2, SUM_DH0 = range(5)
GET_H0, GET_H2, GET_DDZB, GET_DDZA, GET_DDZ2 = range(5)
F01, F02, F21, F22, B22, B21, B02, B01 = range(8)
F31, B31 = range(2)
F11, B11 = range(2)
N01, N02, N21, N22 = range(4)
N11, N12, N31 = range(3)
PIECES = ("a0", "b0", "c0", "p0", "a1", "b1", "c1")
SOURCE = (0, 0, 1, 1, 2, 2, 3)
PAD = 16


def dot(left, right):
    return lax.dot_general(left, right, (((1,), (0,)), ((), ())), preferred_element_type=F32)


def dot_back(left, right):
    return lax.dot_general(left, right, (((1,), (1,)), ((), ())), preferred_element_type=F32)


def dot_rows(left, right):
    return lax.dot_general(left, right, (((0,), (0,)), ((), ())), preferred_element_type=F32)


def silu(value):
    return value * jax.nn.sigmoid(value)


def silu_slope(before):
    sigmoid = jax.nn.sigmoid(before)
    return sigmoid * (1.0 + before * (1.0 - sigmoid))


def scratch_table(lay, ranks, dp_count):
    micro, rows = lay.micro, lay.rows
    part, wide = C_MID // ranks, C_OUT // ranks
    others = ranks - 1
    vmem, dma = pltpu.VMEM, pltpu.SemaphoreType.DMA
    return dict(
        x=vmem((4, micro, rows, C_IN), BF16),
        cot=vmem((micro, rows, wide), BF16),
        a0=vmem((C_IN, part), BF16),
        b0=vmem((9 * part, C_MID), BF16),
        c0=vmem((C_MID, wide), BF16),
        p0=vmem((C_IN, wide), BF16),
        a1=vmem((wide, C_MID), BF16),
        b1=vmem((9 * part, C_MID), BF16),
        c1=vmem((C_MID, wide), BF16),
        a0_all=vmem((C_IN, C_MID), BF16),
        scales=vmem((ranks, 2, GSEGMENT), F32),
        z1=vmem((4, micro, rows, part), F32),
        u1=vmem((4, micro, rows, part), F32),
        zn=vmem((3, micro, rows, part), F32),
        un=vmem((3, micro, rows, part), F32),
        zw=vmem((3, micro, rows, wide), F32),
        uw=vmem((micro, rows, wide), F32),
        y1=vmem((micro, rows, wide), BF16),
        skip=vmem((micro, rows, wide), BF16),
        ddzd=vmem((micro, rows, wide), BF16),
        ddzc=vmem((micro, rows, wide), BF16),
        ddzs=vmem((micro, rows, wide), BF16),
        patches=vmem((2, micro, rows, 9 * part), BF16),
        slide=vmem((PAD + rows + PAD, part), F32),
        fan=vmem((PAD + rows + PAD, 9 * part), F32),
        stat_n=vmem((4, micro, 8, part), F32),
        stat_w=vmem((3, micro, 8, wide), F32),
        sum_send=vmem((5, micro, rows, C_MID), BF16),
        sum_recv=vmem((5, micro, others, rows, part), BF16),
        get=vmem((5, micro, rows, C_MID), BF16),
        norm_n=vmem((8, micro, dp_count, 4, part), F32),
        norm_w=vmem((2, micro, dp_count, 4, wide), F32),
        norm_v=vmem((2, micro, dp_count, 8, wide), F32),
        out_send=vmem((micro, rows, wide), BF16),
        out_own=vmem((rows, C_OUT), BF16),
        dxs_send=vmem((micro, rows, C_IN), BF16),
        dxs_recv=vmem((ranks, rows, C_IN), BF16),
        ddz1=vmem((4, micro, rows, part), BF16),
        ddz1_own=vmem((4, rows, C_MID), BF16),
        gains=vmem((ranks, 2, C_MID + 3 * wide), F32),
        stage=vmem((256, C_MID), BF16),
        stage_sem=dma,
        load_sem=dma((2,)),
        piece_own=dma((7,)),
        piece_send=dma((7,)),
        piece_recv=dma((7,)),
        pass_send=dma((7,)),
        pass_recv=dma((7,)),
        scale_send=dma,
        scale_recv=dma,
        all_send=dma,
        all_recv=dma,
        sum_send_sem=dma((5, micro)),
        sum_recv_sem=dma((5, micro)),
        get_send_sem=dma((5, micro)),
        get_recv_sem=dma((5, micro)),
        norm_n_send=dma((8, micro)),
        norm_n_recv=dma((8, micro)),
        norm_w_send=dma((2, micro)),
        norm_w_recv=dma((2, micro)),
        norm_v_send=dma((2, micro)),
        norm_v_recv=dma((2, micro)),
        own_send=dma((3,)),
        own_recv=dma((3,)),
        own_copy=dma((3,)),
        gain_send=dma,
        gain_recv=dma,
    )


def chain_kernel(lay, ranks, dp_count, names, *refs):
    inputs = ("x_in", "cot_in", "narrow_in", "wide_in", "scales_in", "masks")
    outputs = ("out", "grad", "gains_out", "dw", "da0")
    r = dict(zip(inputs + outputs + names, refs))
    micro, rows = lay.micro, lay.rows
    first = lay.spans[0][1]
    part, wide = C_MID // ranks, C_OUT // ranks
    section, dp = lax.axis_index("section"), lax.axis_index("dp")
    core = lax.rem(dp, 2)
    sibling = (section, dp + 1 - 2 * core)
    masks = r["masks"]
    mine = pl.ds(pl.multiple_of(section * part, part), part)
    mine_wide = pl.ds(pl.multiple_of(section * wide, wide), wide)

    def other(k):
        return lax.rem(section + k, ranks)

    def across_dp(act):
        if dp_count <= 8:
            for k in range(1, dp_count):
                act((section, lax.rem(dp + k, dp_count)))
        else:

            def step(k, carry):
                act((section, lax.rem(dp + k, dp_count)))
                return carry

            lax.fori_loop(1, dp_count, step, 0)

    def remote(src, dst, send, recv, device):
        return pltpu.make_async_remote_copy(
            src_ref=src,
            dst_ref=dst,
            send_sem=send,
            recv_sem=recv,
            device_id=device,
            device_id_type=MESH,
        )

    def wait_bytes(ref, sem):
        pltpu.make_async_copy(ref, ref, sem).wait()

    def each_micro(body):
        def step(m, carry):
            body(m)
            return carry

        lax.fori_loop(0, micro, step, 0)

    barrier = pltpu.get_barrier_semaphore()

    def greet(device):
        pl.semaphore_signal(barrier, inc=1, device_id=device, device_id_type=MESH)

    across_dp(greet)
    for k in range(1, ranks):
        greet((other(k), dp))
    pltpu.make_async_copy(r["x_in"], r["x"], r["load_sem"].at[0]).start()
    pltpu.make_async_copy(r["cot_in"], r["cot"], r["load_sem"].at[1]).start()
    r["slide"][...] = jnp.zeros(r["slide"].shape, F32)
    r["fan"][...] = jnp.zeros(r["fan"].shape, F32)
    pl.semaphore_wait(barrier, dp_count - 1 + ranks - 1)

    def blocks(number, target, half):
        name = PIECES[number]
        dst = r[name]
        height = dst.shape[0]
        start = 0 if half is None else half * (height // 2)
        count = height if half is None else height // 2
        start = start if half is None else pl.multiple_of(start, 64)
        if name == "a0":
            cols = pl.ds(pl.multiple_of(target * part, part), part)
            return [(r["narrow_in"].at[pl.ds(start, count), cols], dst.at[pl.ds(start, count)])]
        if name in ("c0", "p0", "c1"):
            base = C_MID if name == "p0" else 0
            cols = pl.ds(pl.multiple_of(target * wide, wide), wide)
            return [
                (
                    r["wide_in"].at[pl.ds(pl.multiple_of(base + start, 64), count), cols],
                    dst.at[pl.ds(start, count)],
                )
            ]
        if name == "a1":
            return [
                (
                    r["narrow_in"].at[pl.ds(pl.multiple_of(target * wide + start, 64), count)],
                    dst.at[pl.ds(start, count)],
                )
            ]
        base = C_IN if name == "b0" else C_OUT
        pairs = []
        for i in range(count // 64):
            unit = i if half is None else half * (count // 64) + i
            row = base + C_MID * (unit // 2) + part * target + 64 * lax.rem(unit, 2)
            pairs.append(
                (
                    r["narrow_in"].at[pl.ds(pl.multiple_of(row, 64), 64)],
                    dst.at[pl.ds(pl.multiple_of(64 * unit, 64), 64)],
                )
            )
        return pairs

    def send_piece(number):
        for k in range(1, ranks):
            for src, dst in blocks(number, other(k), core):
                remote(
                    src, dst, r["piece_send"].at[number], r["piece_recv"].at[number], (other(k), dp)
                ).start()
        for src, dst in blocks(number, section, None):
            pltpu.make_async_copy(src, dst, r["piece_own"].at[number]).start()

    def half_of(number, which):
        ref = r[PIECES[number]]
        count = ref.shape[0] // 2
        return ref.at[pl.ds(pl.multiple_of(which * count, 64), count)]

    def pass_on(number):
        @pl.when(section != SOURCE[number])
        def _():
            half = half_of(number, core)
            wait_bytes(half, r["piece_recv"].at[number])
            remote(
                half, half, r["pass_send"].at[number], r["pass_recv"].at[number], sibling
            ).start()

    def need(number):
        @pl.when(section != SOURCE[number])
        def _():
            wait_bytes(half_of(number, core), r["pass_recv"].at[number])

        @pl.when(section == SOURCE[number])
        def _():
            wait_bytes(r[PIECES[number]], r["piece_own"].at[number])

    scales = r["scales"]
    for k in range(1, ranks):
        remote(
            r["scales_in"], scales.at[section], r["scale_send"], r["scale_recv"], (other(k), dp)
        ).start()
    for source in range(ranks):

        @pl.when(section == source)
        def _():
            for number in range(7):
                if SOURCE[number] == source:
                    send_piece(number)

    scales[section] = r["scales_in"][...]
    wait_bytes(r["x"], r["load_sem"].at[0])
    wait_bytes(r["cot"], r["load_sem"].at[1])

    def affine(segment, start, width):
        at = pl.ds(pl.multiple_of(start + section * width, width), width)
        return scales[segment, 0:1, at], scales[segment, 1:2, at]

    def affine_n(norm):
        return affine(2 * (norm // 2), C_MID * (norm % 2), part)

    def affine_w(norm):
        return affine((1, 1, 3)[norm], (0, C_OUT, 0)[norm], wide)

    def per_group(function, *values):
        top = function(0, *[v[:first] for v in values])
        low = function(1, *[v[first:] for v in values])
        return jnp.concatenate([top, low], axis=0)

    def widened(flags, width):
        return flags if width == part else jnp.concatenate([flags] * (width // part), axis=1)

    def keep(values):
        flags = widened(masks[4], values.shape[1])
        return jnp.where(flags > 0, values, 0.0)

    def moments(values):
        return [
            jnp.sum(v, axis=0, keepdims=True)
            for v in (
                values[:first],
                values[first:],
                values[:first] * values[:first],
                values[first:] * values[first:],
            )
        ]

    def norm_refs(kind):
        return r["norm_" + kind], r["norm_" + kind + "_send"], r["norm_" + kind + "_recv"]

    def norm_start(kind, event, m, sums):
        buffer, send, recv = norm_refs(kind)
        slot = buffer.at[event, m, dp]
        for i, value in enumerate(sums):
            slot[pl.ds(i, 1), :] = value
        for i in range(len(sums), buffer.shape[3]):
            slot[pl.ds(i, 1), :] = jnp.zeros((1, slot.shape[1]), F32)
        across_dp(
            lambda device: remote(
                slot, slot, send.at[event, m], recv.at[event, m], device
            ).start()
        )

    def norm_finish(kind, event, m):
        buffer, _, recv = norm_refs(kind)
        wait_bytes(buffer.at[event, m, pl.ds(0, dp_count - 1)], recv.at[event, m])
        return jnp.sum(buffer[event, m], axis=0)

    def finish_moments(kind, event, m, store, fold):
        totals = norm_finish(kind, event, m)
        return [
            keep_moments(totals[4 * i : 4 * i + 4], s, m, fold) for i, s in enumerate(store)
        ]

    def keep_moments(sums, store, m, fold):
        ref, norm = store
        found = []
        for group in range(2):
            count = float(lay.totals[group] * fold)
            mean = sums[group : group + 1] / count
            square = sums[2 + group : 3 + group] / count
            found += [mean, lax.rsqrt(square - mean * mean + EPSILON)]
        for i, value in enumerate(found):
            ref[norm, m, pl.ds(i, 1), :] = value
        return found

    def moments_of(ref, norm, m):
        return [ref[norm, m, pl.ds(i, 1), :] for i in range(4)]

    def normalized(values, found):
        return per_group(lambda g, v: (v - found[2 * g]) * found[2 * g + 1], values)

    def norm_change(upstream, normed, found, gain, sums, fold):
        def one(group, u, n):
            count = float(lay.totals[group] * fold)
            plain = sums[0][group] * gain / count
            along = sums[1][group] * gain / count
            return found[2 * group + 1] * (u * gain - plain - n * along)

        return keep(per_group(one, upstream, normed)).astype(BF16)

    def add_gains(place, sums):
        at = pl.ds(place, sums[0][0].shape[1])
        own = r["gains"].at[section]
        own[pl.ds(0, 1), at] += sums[1][0] + sums[1][1]
        own[pl.ds(1, 1), at] += sums[0][0] + sums[0][1]

    def rows_of(totals, at):
        return [totals[at : at + 1], totals[at + 1 : at + 2]]

    def upstream_sums(upstream, normeds):
        sums = []
        for v in [upstream] + [upstream * n for n in normeds]:
            sums += [
                jnp.sum(v[:first], axis=0, keepdims=True),
                jnp.sum(v[first:], axis=0, keepdims=True),
            ]
        return sums

    def slid(ref, cols, down, right):
        pieces = []
        for (start, stop), side in zip(lay.spans, lay.sides):
            at = PAD + start + down * side + right
            pieces.append(ref[pl.ds(at, stop - start), cols])
        values = jnp.concatenate(pieces, axis=0)
        flags = masks[(down + 1) * 3 + right + 1]
        return jnp.where(flags > 0, values, 0.0)

    def sum_start(event, m, values):
        send = r["sum_send"]
        send[event, m] = values.astype(BF16)
        for k in range(1, ranks):
            cols = pl.ds(pl.multiple_of(other(k) * part, part), part)
            remote(
                send.at[event, m, :, cols],
                r["sum_recv"].at[event, m, k - 1],
                r["sum_send_sem"].at[event, m],
                r["sum_recv_sem"].at[event, m],
                (other(k), dp),
            ).start()

    def sum_finish(event, m):
        wait_bytes(r["sum_recv"].at[event, m], r["sum_recv_sem"].at[event, m])
        total = r["sum_send"][event, m, :, mine].astype(F32)
        for k in range(ranks - 1):
            total = total + r["sum_recv"][event, m, k].astype(F32)
        return total

    def get_start(event, m, values):
        get = r["get"]
        get[event, m, :, mine] = values
        for k in range(1, ranks):
            remote(
                get.at[event, m, :, mine],
                get.at[event, m, :, mine],
                r["get_send_sem"].at[event, m],
                r["get_recv_sem"].at[event, m],
                (other(k), dp),
            ).start()

    def get_finish(event, m):
        wait_bytes(
            r["get"].at[event, m, :, pl.ds(0, C_MID - part)], r["get_recv_sem"].at[event, m]
        )
        return r["get"][event, m]

    def own_start(number, m, src, dst):
        @pl.when(section != m)
        def _():
            remote(
                src, dst, r["own_send"].at[number], r["own_recv"].at[number], (m, dp)
            ).start()

        @pl.when(section == m)
        def _():
            pltpu.make_async_copy(src, dst, r["own_copy"].at[number]).start()

    z1, zn, zw, y1 = r["z1"], r["zn"], r["zw"], r["y1"]
    r["gains"][section] = jnp.zeros(r["gains"].shape[1:], F32)
    pass_on(0)
    need(0)

    def do_z1(m):
        sums = None
        for phase in range(4):
            value = dot(r["x"][phase, m], r["a0"][...])
            z1[phase, m] = value
            found = moments(value)
            sums = found if sums is None else [a + b for a, b in zip(sums, found)]
        norm_start("n", F01, m, sums)

    each_micro(do_z1)
    wait_bytes(r["scales"].at[pl.ds(0, ranks - 1)], r["scale_recv"])
    pass_on(1)
    need(1)

    def do_a1(m):
        (found,) = finish_moments("n", F01, m, [(r["stat_n"], N01)], 4)
        gain, shift = affine_n(N01)
        taps = first_taps()
        for phase in range(4):
            value = silu(normalized(z1[phase, m], found) * gain + shift)
            r["slide"][pl.ds(PAD, rows), :] = value
            for k, (at, down, right) in enumerate(taps):
                if at == phase:
                    r["patches"][0, m, :, pl.ds(k * part, part)] = slid(
                        r["slide"], slice(None), down, right
                    ).astype(BF16)
        sum_start(SUM_Z2, m, dot(r["patches"][0, m], r["b0"][...]))

    each_micro(do_a1)
    for number in (2, 3):
        pass_on(number)

    def do_z2(m):
        value = sum_finish(SUM_Z2, m)
        zn[0, m] = value
        norm_start("n", F02, m, moments(value))

    each_micro(do_z2)
    need(3)

    def do_zs(m):
        zw[N12, m] = dot(r["x"][0, m], r["p0"][...])

    each_micro(do_zs)

    def do_h0(m):
        (found,) = finish_moments("n", F02, m, [(r["stat_n"], N02)], 1)
        gain, shift = affine_n(N02)
        get_start(GET_H0, m, keep(silu(normalized(zn[0, m], found) * gain + shift)).astype(BF16))

    each_micro(do_h0)
    need(2)

    def do_zc(m):
        value = dot(get_finish(GET_H0, m), r["c0"][...])
        zw[N11, m] = value
        norm_start("v", F11, m, moments(value) + moments(zw[N12, m]))

    each_micro(do_zc)
    for number in (4, 5, 6):
        pass_on(number)
    need(4)

    def before1(m):
        main = normalized(zw[N11, m], moments_of(r["stat_w"], N11, m))
        short = normalized(zw[N12, m], moments_of(r["stat_w"], N12, m))
        gain_main, shift_main = affine_w(N11)
        gain_short, shift_short = affine_w(N12)
        return main * gain_main + shift_main + short * gain_short + shift_short, main, short

    def do_y1(m):
        finish_moments("v", F11, m, [(r["stat_w"], N11), (r["stat_w"], N12)], 1)
        value = keep(silu(before1(m)[0])).astype(BF16)
        y1[m] = value
        sum_start(SUM_ZA, m, dot(value, r["a1"][...]))

    each_micro(do_y1)

    def do_za(m):
        value = sum_finish(SUM_ZA, m)
        zn[1, m] = value
        norm_start("n", F21, m, moments(value))

    each_micro(do_za)
    need(5)

    def do_a2(m):
        (found,) = finish_moments("n", F21, m, [(r["stat_n"], N21)], 1)
        gain, shift = affine_n(N21)
        r["slide"][pl.ds(PAD, rows), :] = silu(normalized(zn[1, m], found) * gain + shift)
        for k, (down, right) in enumerate(second_taps()):
            r["patches"][1, m, :, pl.ds(k * part, part)] = slid(
                r["slide"], slice(None), down, right
            ).astype(BF16)
        sum_start(SUM_ZB, m, dot(r["patches"][1, m], r["b1"][...]))

    each_micro(do_a2)

    def do_zb(m):
        value = sum_finish(SUM_ZB, m)
        zn[2, m] = value
        norm_start("n", F22, m, moments(value))

    each_micro(do_zb)

    def do_h2(m):
        (found,) = finish_moments("n", F22, m, [(r["stat_n"], N22)], 1)
        gain, shift = affine_n(N22)
        get_start(GET_H2, m, keep(silu(normalized(zn[2, m], found) * gain + shift)).astype(BF16))

    each_micro(do_h2)
    need(6)

    def do_zd(m):
        value = dot(get_finish(GET_H2, m), r["c1"][...])
        zw[N31, m] = value
        norm_start("w", F31, m, moments(value))

    each_micro(do_zd)

    def do_output(m):
        (found,) = finish_moments("w", F31, m, [(r["stat_w"], N31)], 1)
        gain, shift = affine_w(N31)
        normed = normalized(zw[N31, m], found)
        before = normed * gain + shift + y1[m].astype(F32)
        sigmoid = jax.nn.sigmoid(before)
        r["out_send"][m] = (before * sigmoid).astype(BF16)
        upstream = r["cot"][m].astype(F32) * (sigmoid * (1.0 + before * (1.0 - sigmoid)))
        r["skip"][m] = upstream.astype(BF16)
        r["uw"][m] = upstream
        norm_start("w", B31, m, upstream_sums(upstream, [normed]))

    each_micro(do_output)

    def do_ddzd(m):
        totals = norm_finish("w", B31, m)
        sums = [rows_of(totals, 0), rows_of(totals, 2)]
        add_gains(C_MID + 2 * wide, sums)
        found = moments_of(r["stat_w"], N31, m)
        normed = normalized(zw[N31, m], found)
        value = norm_change(r["uw"][m], normed, found, affine_w(N31)[0], sums, 1)
        r["ddzd"][m] = value
        sum_start(SUM_DH2, m, dot_back(value, r["c1"][...]))

    each_micro(do_ddzd)

    def send_output(m):
        own_start(0, m, r["out_send"].at[m], r["out_own"].at[:, mine_wide])

    each_micro(send_output)

    def narrow_upstream(norm, place, event, m, value):
        found = moments_of(r["stat_n"], norm, m)
        gain, shift = affine_n(norm)
        normed = normalized(zn[place, m], found)
        upstream = value * silu_slope(normed * gain + shift)
        r["un"][place, m] = upstream
        norm_start("n", event, m, upstream_sums(upstream, [normed]))

    def narrow_change(norm, place, event, m):
        totals = norm_finish("n", event, m)
        sums = [rows_of(totals, 0), rows_of(totals, 2)]
        add_gains(part * norm, sums)
        found = moments_of(r["stat_n"], norm, m)
        normed = normalized(zn[place, m], found)
        return norm_change(r["un"][place, m], normed, found, affine_n(norm)[0], sums, 1)

    def tall(ref, count):
        return ref.reshape(micro * rows, count)

    def weight_gradient(base, left, right, height, unit):
        def step(i, carry):
            at = pl.multiple_of(i * unit, unit)
            columns = left(pl.ds(at, unit))
            value = dot_rows(columns.reshape(micro * rows, unit), right)
            r["stage"][pl.ds(0, unit), :] = value.astype(BF16)
            copy = pltpu.make_async_copy(
                r["stage"].at[pl.ds(0, unit)],
                r["dw"].at[pl.ds(pl.multiple_of(base + at, 128), unit)],
                r["stage_sem"],
            )
            copy.start()
            copy.wait()
            return carry

        lax.fori_loop(0, height // unit, step, 0)

    share = WSEGMENT // (C_MID * ranks)

    def do_dh2(m):
        value = sum_finish(SUM_DH2, m).astype(BF16).astype(F32)
        narrow_upstream(N22, 2, B22, m, value)

    each_micro(do_dh2)
    weight_gradient(
        3 * share,
        lambda at: r["get"][GET_H2, :, :, at],
        r["ddzd"][...].reshape(micro * rows, wide),
        C_MID,
        256,
    )

    def do_ddzb(m):
        get_start(GET_DDZB, m, narrow_change(N22, 2, B22, m))

    each_micro(do_ddzb)

    def fan_out(m, event, weight):
        r["fan"][pl.ds(PAD, rows), :] = dot_back(get_finish(event, m), weight[...])

    def do_da2(m):
        fan_out(m, GET_DDZB, r["b1"])
        total = None
        for k, (down, right) in enumerate(second_taps()):
            term = slid(r["fan"], pl.ds(k * part, part), -down, -right)
            total = term if total is None else total + term
        narrow_upstream(N21, 1, B21, m, total)

    each_micro(do_da2)
    weight_gradient(
        2 * share + wide,
        lambda at: r["patches"][1, :, :, at],
        r["get"][GET_DDZB].reshape(micro * rows, C_MID),
        9 * part,
        128,
    )

    def do_ddza(m):
        get_start(GET_DDZA, m, narrow_change(N21, 1, B21, m))

    each_micro(do_ddza)

    def do_dy1(m):
        value = dot_back(get_finish(GET_DDZA, m), r["a1"][...]) + r["skip"][m].astype(F32)
        value = value.astype(BF16).astype(F32)
        before, main, short = before1(m)
        upstream = value * silu_slope(before)
        r["uw"][m] = upstream
        norm_start("v", B11, m, upstream_sums(upstream, [main, short]))

    each_micro(do_dy1)
    weight_gradient(
        2 * share,
        lambda at: y1[:, :, at],
        r["get"][GET_DDZA].reshape(micro * rows, C_MID),
        wide,
        256,
    )

    def do_ddzc(m):
        totals = norm_finish("v", B11, m)
        plain = rows_of(totals, 0)
        for norm, at, name in ((N11, 2, "ddzc"), (N12, 4, "ddzs")):
            sums = [plain, rows_of(totals, at)]
            add_gains(C_MID + norm * wide, sums)
            found = moments_of(r["stat_w"], norm, m)
            normed = normalized(zw[norm, m], found)
            r[name][m] = norm_change(r["uw"][m], normed, found, affine_w(norm)[0], sums, 1)
        sum_start(SUM_DH0, m, dot_back(r["ddzc"][m], r["c0"][...]))

    each_micro(do_ddzc)

    def do_dxs(m):
        r["dxs_send"][m] = dot_back(r["ddzs"][m], r["p0"][...]).astype(BF16)
        own_start(1, m, r["dxs_send"].at[m], r["dxs_recv"].at[section])

    each_micro(do_dxs)

    def do_dh0(m):
        value = sum_finish(SUM_DH0, m).astype(BF16).astype(F32)
        narrow_upstream(N02, 0, B02, m, value)

    each_micro(do_dh0)
    weight_gradient(
        share,
        lambda at: r["get"][GET_H0, :, :, at],
        r["ddzc"][...].reshape(micro * rows, wide),
        C_MID,
        256,
    )

    def do_ddz2(m):
        get_start(GET_DDZ2, m, narrow_change(N02, 0, B02, m))

    each_micro(do_ddz2)
    for k in range(1, ranks):
        remote(
            r["a0"], r["a0_all"].at[:, mine], r["all_send"], r["all_recv"], (other(k), dp)
        ).start()
    r["a0_all"][:, mine] = r["a0"][...]
    weight_gradient(
        share + C_MID,
        lambda at: r["x"][0, :, :, at],
        r["ddzs"][...].reshape(micro * rows, wide),
        C_IN,
        256,
    )

    def do_da1(m):
        fan_out(m, GET_DDZ2, r["b0"])
        gain, shift = affine_n(N01)
        found = moments_of(r["stat_n"], N01, m)
        sums = None
        for phase in range(4):
            total = None
            for k, (at, down, right) in enumerate(first_taps()):
                if at == phase:
                    term = slid(r["fan"], pl.ds(k * part, part), -down, -right)
                    total = term if total is None else total + term
            normed = normalized(z1[phase, m], found)
            upstream = total * silu_slope(normed * gain + shift)
            r["u1"][phase, m] = upstream
            terms = upstream_sums(upstream, [normed])
            sums = terms if sums is None else [a + b for a, b in zip(sums, terms)]
        norm_start("n", B01, m, sums)

    each_micro(do_da1)
    weight_gradient(
        0,
        lambda at: r["patches"][0, :, :, at],
        r["get"][GET_DDZ2].reshape(micro * rows, C_MID),
        9 * part,
        128,
    )

    def do_ddz1(m):
        totals = norm_finish("n", B01, m)
        sums = [rows_of(totals, 0), rows_of(totals, 2)]
        add_gains(0, sums)
        found = moments_of(r["stat_n"], N01, m)
        gain = affine_n(N01)[0]
        for phase in range(4):
            normed = normalized(z1[phase, m], found)
            r["ddz1"][phase, m] = norm_change(r["u1"][phase, m], normed, found, gain, sums, 4)
        own_start(2, m, r["ddz1"].at[:, m], r["ddz1_own"].at[:, :, mine])

    each_micro(do_ddz1)
    for k in range(1, ranks):
        remote(
            r["gains"].at[section],
            r["gains"].at[section],
            r["gain_send"],
            r["gain_recv"],
            (other(k), dp),
        ).start()

    def da0_step(i, carry):
        at = pl.ds(pl.multiple_of(i * 128, 128), 128)
        total = None
        for phase in range(4):
            value = dot_rows(
                r["x"][phase, :, :, at].reshape(micro * rows, 128),
                r["ddz1"][phase].reshape(micro * rows, part),
            )
            total = value if total is None else total + value
        r["da0"][pl.ds(pl.multiple_of(i * 128, 128), 128), :] = total.astype(BF16)
        return carry

    lax.fori_loop(0, C_IN // 128, da0_step, 0)

    out_own, dxs, ddz1_own = r["out_own"], r["dxs_recv"], r["ddz1_own"]
    wait_bytes(out_own.at[:, mine_wide], r["own_copy"].at[0])
    wait_bytes(out_own.at[:, pl.ds(0, C_OUT - wide)], r["own_recv"].at[0])
    r["out"][...] = out_own[...]
    wait_bytes(r["a0_all"].at[:, pl.ds(0, C_MID - part)], r["all_recv"])
    wait_bytes(dxs.at[0], r["own_copy"].at[1])
    wait_bytes(dxs.at[pl.ds(0, ranks - 1)], r["own_recv"].at[1])
    wait_bytes(ddz1_own.at[:, :, mine], r["own_copy"].at[2])
    wait_bytes(ddz1_own.at[:, :, pl.ds(0, C_MID - part)], r["own_recv"].at[2])
    for phase in range(4):
        value = dot_back(ddz1_own[phase], r["a0_all"][...])
        if phase == 0:
            extra = dxs[0].astype(F32)
            for k in range(1, ranks):
                extra = extra + dxs[k].astype(F32)
            value = value + extra.astype(BF16).astype(F32)
        r["grad"][phase] = value.astype(BF16)
    wait_bytes(r["gains"].at[pl.ds(0, ranks - 1)], r["gain_recv"])
    r["gains_out"][...] = r["gains"][...]

    def sent(m):
        for event in range(5):
            wait_bytes(r["sum_recv"].at[event, m], r["sum_send_sem"].at[event, m])
            wait_bytes(
                r["get"].at[event, m, :, pl.ds(0, C_MID - part)], r["get_send_sem"].at[event, m]
            )
        for kind, events in (("n", 8), ("w", 2), ("v", 2)):
            buffer, send, _ = norm_refs(kind)
            for event in range(events):
                wait_bytes(buffer.at[event, m, pl.ds(0, dp_count - 1)], send.at[event, m])

    each_micro(sent)
    wait_bytes(out_own.at[:, pl.ds(0, C_OUT - wide)], r["own_send"].at[0])
    wait_bytes(dxs.at[pl.ds(0, ranks - 1)], r["own_send"].at[1])
    wait_bytes(ddz1_own.at[:, :, pl.ds(0, C_MID - part)], r["own_send"].at[2])
    wait_bytes(r["a0_all"].at[:, pl.ds(0, C_MID - part)], r["all_send"])
    wait_bytes(r["gains"].at[pl.ds(0, ranks - 1)], r["gain_send"])
    wait_bytes(scales.at[pl.ds(0, ranks - 1)], r["scale_send"])
    for number in range(7):

        @pl.when(section != SOURCE[number])
        def _():
            wait_bytes(half_of(number, core), r["pass_send"].at[number])

        @pl.when(section == SOURCE[number])
        def _():
            for _ in range(ranks - 1):
                wait_bytes(half_of(number, core), r["piece_send"].at[number])


def chain(lay, ranks, dp_count, pictures, cotangent, narrow, wide_view, scales, masks):
    micro, rows = lay.micro, lay.rows
    part, wide = C_MID // ranks, C_OUT // ranks
    table = scratch_table(lay, ranks, dp_count)
    shapes = (
        jax.ShapeDtypeStruct((rows, C_OUT), BF16),
        jax.ShapeDtypeStruct((4, rows, C_IN), BF16),
        jax.ShapeDtypeStruct((ranks, 2, C_MID + 3 * wide), F32),
        jax.ShapeDtypeStruct((ROWS, C_MID), BF16),
        jax.ShapeDtypeStruct((C_IN, part), BF16),
    )
    anywhere = pl.BlockSpec(memory_space=pl.ANY)
    inside = pl.BlockSpec(memory_space=pltpu.VMEM)
    return pl.pallas_call(
        functools.partial(chain_kernel, lay, ranks, dp_count, tuple(table)),
        out_shape=shapes,
        in_specs=[anywhere] * 4 + [inside] * 2,
        out_specs=[inside] * 3 + [anywhere, inside],
        scratch_shapes=list(table.values()),
        compiler_params=pltpu.CompilerParams(
            collective_id=0, has_side_effects=True, vmem_limit_bytes=63 * 2**20
        ),
        name="chain",
    )(pictures, cotangent, narrow, wide_view, scales, masks)


def per_device(
    images_global, images_local, weights, norm_gains, norm_shifts, cotangent_global, cotangent_local
):
    section = lax.axis_index("section")
    ranks = lax.axis_size("section")
    dp_count = lax.axis_size("dp")
    lay = Layout(images_global.shape, images_local.shape, dp_count)
    micro, rows = lay.micro, lay.rows
    part = C_MID // ranks
    wide = C_OUT // ranks

    pictures = lay.pack(phases_of(images_global), phases_of(images_local))
    at = section * wide
    cotangent = lay.pack(
        lax.dynamic_slice_in_dim(cotangent_global, at, wide, 4).reshape(micro, -1, wide),
        lax.dynamic_slice_in_dim(cotangent_local, at, wide, 4).reshape(micro, -1, wide),
    )
    masks = np.stack(
        [lay.valid(down, right) for down in (-1, 0, 1) for right in (-1, 0, 1)]
    ).astype(np.float32)
    masks = jnp.broadcast_to(jnp.asarray(masks)[:, :, None], (9, rows, part))
    out, gradient, gains, slices, small = chain(
        lay,
        ranks,
        dp_count,
        pictures,
        cotangent,
        weights.reshape(ROWS, C_MID),
        weights.reshape(WIDE, C_OUT),
        jnp.stack([norm_gains, norm_shifts]),
        masks,
    )

    small = jnp.stack([small] + [jnp.zeros_like(small)] * (ranks - 1))
    slices = slices.reshape(ranks, ROWS // ranks, C_MID)
    arrived = lax.all_to_all(slices, "section", 0, 0, tiled=True).astype(F32)
    arrived_small = lax.all_to_all(small, "section", 0, 0, tiled=True).astype(F32)
    segment = segment_gradient(arrived, arrived_small, section, ranks)
    weight_gradient = lax.psum_scatter(segment.reshape(-1), "dp", scatter_dimension=0, tiled=True)

    def joined(start, width):
        block = gains[:, :, start : start + width // ranks]
        return jnp.moveaxis(block, 0, 1).reshape(2, width)

    f01, f02, f21, f22 = [joined(part * i, C_MID) for i in range(4)]
    f11, f12, f31 = [joined(C_MID + wide * i, C_OUT) for i in range(3)]
    blank = jnp.zeros((2, GSEGMENT - 2 * C_MID), F32)
    segments = jnp.stack(
        [
            jnp.concatenate([f01, f02, blank], 1),
            jnp.concatenate([f11, f12], 1),
            jnp.concatenate([f21, f22, blank], 1),
            jnp.concatenate([f31, jnp.zeros((2, GSEGMENT - C_OUT), F32)], 1),
        ]
    )
    share = GSEGMENT // dp_count
    own_norms = lax.dynamic_index_in_dim(segments, section, 0, keepdims=False)
    own_norms = lax.dynamic_slice_in_dim(own_norms, lax.axis_index("dp") * share, share, 1)

    out_global, out_local = lay.unpack(out)
    grad_global, grad_local = lay.unpack(gradient)
    return (
        out_global.reshape(1, lay.crops[0], lay.sides[0], lay.sides[0], C_OUT),
        out_local.reshape(1, lay.crops[1], lay.sides[1], lay.sides[1], C_OUT),
        whole_grid(grad_global, lay.crops[0], lay.sides[0]),
        whole_grid(grad_local, lay.crops[1], lay.sides[1]),
        weight_gradient,
        own_norms[0],
        own_norms[1],
    )


def solution(mesh):
    images = P(None, "dp", None, None, None)
    made = P("section", "dp", None, None, None)
    return jax.shard_map(
        per_device,
        mesh=mesh,
        in_specs=(images, images, P("section"), P("section"), P("section"), images, images),
        out_specs=(made, made, made, made) + (P(("section", "dp")),) * 3,
        check_vma=False,
    )
```

```python
import functools
from types import SimpleNamespace

import jax
import jax.numpy as jnp
import numpy as np
from jax import lax
from jax.experimental import pallas as pl
from jax.experimental.pallas import tpu as pltpu
from jax.sharding import PartitionSpec as P

C_IN = 1024
C_MID = 512
C_OUT = 2048
WSEGMENT = 3407872
GSEGMENT = 4096
EPSILON = 1e-05
F32 = jnp.float32
BF16 = jnp.bfloat16


def round_up(value, unit):
    return -(-value // unit) * unit


class Layout:
    def __init__(self, shape_global, shape_local, dp_count):
        self.micro = shape_global[0]
        self.crops = (shape_global[1], shape_local[1])
        self.sides = (shape_global[2] // 2, shape_local[2] // 2)
        used = [crops * side * side for crops, side in zip(self.crops, self.sides)]
        self.used = used
        first = round_up(used[0], 8)
        self.rows = round_up(first + round_up(used[1], 8), 16)
        self.spans = ((0, first), (first, self.rows))
        self.totals = [count * dp_count for count in used]
        self.fast = dp_count in (2, 4, 8) and WSEGMENT // C_MID // dp_count % 64 == 0

    def valid(self, down, right):
        flags = np.zeros((self.rows,), bool)
        for (start, _), crops, side in zip(self.spans, self.crops, self.sides):
            for crop in range(crops):
                for i in range(side):
                    for j in range(side):
                        inside = 0 <= i + down < side and 0 <= j + right < side
                        flags[start + (crop * side + i) * side + j] = inside
        return flags

    def shift(self, values, down, right):
        pieces = []
        for (start, stop), side in zip(self.spans, self.sides):
            steps = down * side + right
            pieces.append(jnp.roll(values[..., start:stop, :], -steps, axis=-2))
        flags = jnp.asarray(self.valid(down, right))[:, None]
        return jnp.where(flags, jnp.concatenate(pieces, axis=-2), 0)

    def pack(self, in_global, in_local):
        parts = []
        for part, (start, stop) in zip((in_global, in_local), self.spans):
            pads = [(0, 0)] * (part.ndim - 2) + [(0, stop - start - part.shape[-2]), (0, 0)]
            parts.append(jnp.pad(part, pads))
        return jnp.concatenate(parts, axis=-2)

    def unpack(self, values):
        return [
            values[..., start : start + used, :]
            for (start, _), used in zip(self.spans, self.used)
        ]


def first_taps():
    return [
        (2 * (p != 1) + (q != 1), -(p == 0), -(q == 0)) for p in range(3) for q in range(3)
    ]


def second_taps():
    return [(p - 1, q - 1) for p in range(3) for q in range(3)]


def phases_of(pictures):
    micro, crops, side, _, channels = pictures.shape
    half = side // 2
    split = pictures.reshape(micro, crops, half, 2, half, 2, channels)
    return split.transpose(3, 5, 0, 1, 2, 4, 6).reshape(4, micro, crops * half * half, channels)


def whole_grid(rows, crops, half):
    channels = rows.shape[-1]
    split = rows.reshape(2, 2, crops, half, half, channels)
    return split.transpose(2, 3, 0, 4, 1, 5).reshape(1, crops, 2 * half, 2 * half, channels)


def segment_gradient(pieces, small, section, ranks):
    part = C_MID // ranks
    total_rows = WSEGMENT // C_MID

    def finished(rows):
        return jnp.pad(rows, ((0, total_rows - rows.shape[0]), (0, 0)))

    def across(block):
        return block.transpose(1, 0, 2).reshape(-1, C_MID)

    def spatial(block):
        return block.reshape(ranks, 9, part, C_MID).transpose(1, 0, 2, 3).reshape(-1, C_MID)

    def first():
        return finished(
            jnp.concatenate(
                [small.transpose(1, 0, 2).reshape(-1, C_MID), spatial(pieces[:, : 9 * part])]
            )
        )

    def second():
        return finished(across(pieces[:, : C_MID + C_IN]))

    def third():
        tall = C_OUT // ranks
        return finished(
            jnp.concatenate(
                [pieces[:, :tall].reshape(-1, C_MID), spatial(pieces[:, tall : tall + 9 * part])]
            )
        )

    def fourth():
        return finished(across(pieces[:, :C_MID]))

    return lax.switch(section, [first, second, third, fourth])


MESH = pl.DeviceIdType.MESH
ROWS, WIDE = WSEGMENT // C_MID, WSEGMENT // C_OUT
SUM_Z2, SUM_ZA, SUM_ZB, SUM_DH2, SUM_DH0 = range(5)
GET_H0, GET_H2, GET_DDZB, GET_DDZA, GET_DDZ2 = range(5)
F01, F02, F21, F22, B22, B21, B02, B01 = range(8)
F31, B31 = range(2)
F11, B11 = range(2)
N01, N02, N21, N22 = range(4)
N11, N12, N31 = range(3)
A0, B0, C0, P0, A1, B1, C1 = range(7)
SOURCE = (0, 0, 1, 1, 2, 2, 3)
PAD = 16
HEIGHTS = (0, 9 * C_MID // 4, C_MID, C_IN, C_OUT // 4, 9 * C_MID // 4, C_MID)


def dot(left, right):
    return lax.dot_general(left, right, (((1,), (0,)), ((), ())), preferred_element_type=F32)


def dot_back(left, right):
    return lax.dot_general(left, right, (((1,), (1,)), ((), ())), preferred_element_type=F32)


def dot_rows(left, right):
    return lax.dot_general(left, right, (((0,), (0,)), ((), ())), preferred_element_type=F32)


def silu(value):
    return value * jax.nn.sigmoid(value)


def silu_slope(before):
    sigmoid = jax.nn.sigmoid(before)
    return sigmoid * (1.0 + before * (1.0 - sigmoid))


def scratch_table(lay, ranks, dp_count):
    micro, rows = lay.micro, lay.rows
    part, wide = C_MID // ranks, C_OUT // ranks
    others = ranks - 1
    vmem, dma = pltpu.VMEM, pltpu.SemaphoreType.DMA
    return dict(
        x=vmem((4, micro, rows, C_IN), BF16),
        cot=vmem((micro, rows, wide), BF16),
        a0=vmem((C_IN, part), BF16),
        b0=vmem((9 * part, C_MID), BF16),
        c0=vmem((C_MID, wide), BF16),
        p0=vmem((C_IN, wide), BF16),
        a1=vmem((wide, C_MID), BF16),
        b1=vmem((9 * part, C_MID), BF16),
        c1=vmem((C_MID, wide), BF16),
        a0_all=vmem((C_IN, C_MID), BF16),
        scales=vmem((ranks, 2, GSEGMENT), F32),
        z1=vmem((4, micro, rows, part), F32),
        u1=vmem((4, micro, rows, part), F32),
        zn=vmem((3, micro, rows, part), F32),
        un=vmem((3, micro, rows, part), F32),
        zw=vmem((3, micro, rows, wide), F32),
        uw=vmem((micro, rows, wide), F32),
        y1=vmem((micro, rows, wide), BF16),
        skip=vmem((micro, rows, wide), BF16),
        ddzd=vmem((micro, rows, wide), BF16),
        ddzc=vmem((micro, rows, wide), BF16),
        ddzs=vmem((micro, rows, wide), BF16),
        patches=vmem((2, micro, rows, 9 * part), BF16),
        slide=vmem((PAD + rows + PAD, part), F32),
        fan=vmem((PAD + rows + PAD, 9 * part), F32),
        stat_n=vmem((4, micro, 8, part), F32),
        stat_w=vmem((3, micro, 8, wide), F32),
        sum_send=vmem((5, micro, rows, C_MID), BF16),
        sum_recv=vmem((5, micro, others, rows, part), BF16),
        get=vmem((5, micro, rows, C_MID), BF16),
        norm_n=vmem((8, micro, dp_count, 4, part), F32),
        norm_w=vmem((2, micro, dp_count, 4, wide), F32),
        norm_v=vmem((2, micro, dp_count, 8, wide), F32),
        out_send=vmem((micro, rows, wide), BF16),
        out_own=vmem((rows, C_OUT), BF16),
        dxs_send=vmem((micro, rows, C_IN), BF16),
        dxs_recv=vmem((ranks, rows, C_IN), BF16),
        ddz1=vmem((4, micro, rows, part), BF16),
        ddz1_own=vmem((4, rows, C_MID), BF16),
        gains=vmem((ranks, 2, C_MID + 3 * wide), F32),
        load_sem=dma((2,)),
        piece_own=dma((7,)),
        piece_send=dma((7,)),
        piece_recv=dma((7,)),
        pass_send=dma((7,)),
        pass_recv=dma((7,)),
        scale_send=dma,
        scale_recv=dma,
        all_send=dma,
        all_recv=dma,
        sum_send_sem=dma((5, micro)),
        sum_recv_sem=dma((5, micro)),
        get_send_sem=dma((5, micro)),
        get_recv_sem=dma((5, micro)),
        norm_n_send=dma((8, micro)),
        norm_n_recv=dma((8, micro)),
        norm_w_send=dma((2, micro)),
        norm_w_recv=dma((2, micro)),
        norm_v_send=dma((2, micro)),
        norm_v_recv=dma((2, micro)),
        own_send=dma((3,)),
        own_recv=dma((3,)),
        own_copy=dma((3,)),
        gain_send=dma,
        gain_recv=dma,
        **gradient_scratch(lay, ranks, dp_count),
    )


def gradient_scratch(lay, ranks, dp_count):
    vmem, dma = pltpu.VMEM, pltpu.SemaphoreType.DMA
    if not lay.fast:
        return dict(stage=vmem((256, C_MID), BF16), stage_sem=dma)
    part = C_MID // ranks
    height, chips = sum(HEIGHTS), dp_count // 2
    return dict(
        dw=vmem((height, C_MID), BF16),
        dw_pair=vmem((height // 2, C_MID), BF16),
        dw_near=vmem((chips - 1, height // dp_count, C_MID), BF16),
        dw_sum=vmem((height // dp_count, C_MID), F32),
        da=vmem((C_IN, part), BF16),
        da_pair=vmem((C_IN // 2, part), BF16),
        da_near=vmem((chips - 1, C_IN // dp_count, part), BF16),
        da_sum=vmem((C_IN // dp_count, part), F32),
        share=vmem((ROWS // dp_count, C_MID), F32),
        pair_send=dma((7,)),
        pair_recv=dma((7,)),
        near_send=dma((7,)),
        near_recv=dma((7,)),
        share_send=dma((7, 16)),
        share_recv=dma,
    )


def chain_kernel(lay, ranks, dp_count, names, *refs):
    inputs = ("x_in", "cot_in", "narrow_in", "wide_in", "scales_in", "masks")
    outputs = ("out", "grad", "gains_out") + (("dw_out",) if lay.fast else ("dw", "da0"))
    r = SimpleNamespace(**dict(zip(inputs + outputs + names, refs)))
    pieces = (r.a0, r.b0, r.c0, r.p0, r.a1, r.b1, r.c1)
    micro, rows = lay.micro, lay.rows
    first = lay.spans[0][1]
    part, wide = C_MID // ranks, C_OUT // ranks
    section, dp = lax.axis_index("section"), lax.axis_index("dp")
    core = lax.rem(dp, 2)
    sibling = (section, dp + 1 - 2 * core)
    masks = r.masks
    mine = pl.ds(pl.multiple_of(section * part, part), part)
    mine_wide = pl.ds(pl.multiple_of(section * wide, wide), wide)

    def other(k):
        return lax.rem(section + k, ranks)

    def across_dp(act):
        if dp_count <= 8:
            for k in range(1, dp_count):
                act((section, lax.rem(dp + k, dp_count)))
        else:

            def step(k, carry):
                act((section, lax.rem(dp + k, dp_count)))
                return carry

            lax.fori_loop(1, dp_count, step, 0)

    def remote(src, dst, send, recv, device):
        return pltpu.make_async_remote_copy(
            src_ref=src,
            dst_ref=dst,
            send_sem=send,
            recv_sem=recv,
            device_id=device,
            device_id_type=MESH,
        )

    def wait_bytes(ref, sem):
        pltpu.make_async_copy(ref, ref, sem).wait()

    def each_micro(body):
        def step(m, carry):
            body(m)
            return carry

        lax.fori_loop(0, micro, step, 0)

    barrier = pltpu.get_barrier_semaphore()

    def greet(device):
        pl.semaphore_signal(barrier, inc=1, device_id=device, device_id_type=MESH)

    if lay.fast:
        r.share[...] = jnp.zeros(r.share.shape, F32)
        for k in range(ranks):
            for j in range(dp_count):
                if k or j:
                    greet((other(k), lax.rem(dp + j, dp_count)))
        greetings = ranks * dp_count - 1
    else:
        across_dp(greet)
        for k in range(1, ranks):
            greet((other(k), dp))
        greetings = dp_count - 1 + ranks - 1
    pltpu.make_async_copy(r.x_in, r.x, r.load_sem.at[0]).start()
    pltpu.make_async_copy(r.cot_in, r.cot, r.load_sem.at[1]).start()
    r.slide[...] = jnp.zeros(r.slide.shape, F32)
    r.fan[...] = jnp.zeros(r.fan.shape, F32)
    pl.semaphore_wait(barrier, greetings)

    def blocks(number, target, half):
        dst = pieces[number]
        height = dst.shape[0]
        start = 0 if half is None else half * (height // 2)
        count = height if half is None else height // 2
        start = start if half is None else pl.multiple_of(start, 64)
        if number == A0:
            cols = pl.ds(pl.multiple_of(target * part, part), part)
            return [(r.narrow_in.at[pl.ds(start, count), cols], dst.at[pl.ds(start, count)])]
        if number in (C0, P0, C1):
            base = C_MID if number == P0 else 0
            cols = pl.ds(pl.multiple_of(target * wide, wide), wide)
            return [
                (
                    r.wide_in.at[pl.ds(pl.multiple_of(base + start, 64), count), cols],
                    dst.at[pl.ds(start, count)],
                )
            ]
        if number == A1:
            return [
                (
                    r.narrow_in.at[pl.ds(pl.multiple_of(target * wide + start, 64), count)],
                    dst.at[pl.ds(start, count)],
                )
            ]
        base = C_IN if number == B0 else C_OUT
        pairs = []
        for i in range(count // 64):
            unit = i if half is None else half * (count // 64) + i
            row = base + C_MID * (unit // 2) + part * target + 64 * lax.rem(unit, 2)
            pairs.append(
                (
                    r.narrow_in.at[pl.ds(pl.multiple_of(row, 64), 64)],
                    dst.at[pl.ds(pl.multiple_of(64 * unit, 64), 64)],
                )
            )
        return pairs

    def send_piece(number):
        for k in range(1, ranks):
            for src, dst in blocks(number, other(k), core):
                remote(
                    src, dst, r.piece_send.at[number], r.piece_recv.at[number], (other(k), dp)
                ).start()
        for src, dst in blocks(number, section, None):
            pltpu.make_async_copy(src, dst, r.piece_own.at[number]).start()

    def half_of(number, which):
        ref = pieces[number]
        count = ref.shape[0] // 2
        return ref.at[pl.ds(pl.multiple_of(which * count, 64), count)]

    def pass_on(number):
        @pl.when(section != SOURCE[number])
        def _():
            half = half_of(number, core)
            wait_bytes(half, r.piece_recv.at[number])
            remote(
                half, half, r.pass_send.at[number], r.pass_recv.at[number], sibling
            ).start()

    def need(number):
        @pl.when(section != SOURCE[number])
        def _():
            wait_bytes(half_of(number, core), r.pass_recv.at[number])

        @pl.when(section == SOURCE[number])
        def _():
            wait_bytes(pieces[number], r.piece_own.at[number])

    scales = r.scales
    for k in range(1, ranks):
        remote(
            r.scales_in, scales.at[section], r.scale_send, r.scale_recv, (other(k), dp)
        ).start()
    for source in range(ranks):

        @pl.when(section == source)
        def _():
            for number in range(7):
                if SOURCE[number] == source:
                    send_piece(number)

    scales[section] = r.scales_in[...]
    wait_bytes(r.x, r.load_sem.at[0])
    wait_bytes(r.cot, r.load_sem.at[1])

    def affine(segment, start, width):
        at = pl.ds(pl.multiple_of(start + section * width, width), width)
        return scales[segment, 0:1, at], scales[segment, 1:2, at]

    def affine_n(norm):
        return affine(2 * (norm // 2), C_MID * (norm % 2), part)

    def affine_w(norm):
        return affine((1, 1, 3)[norm], (0, C_OUT, 0)[norm], wide)

    def per_group(function, *values):
        top = function(0, *[v[:first] for v in values])
        low = function(1, *[v[first:] for v in values])
        return jnp.concatenate([top, low], axis=0)

    def widened(flags, width):
        return flags if width == part else jnp.concatenate([flags] * (width // part), axis=1)

    def keep(values):
        flags = widened(masks[4], values.shape[1])
        return jnp.where(flags > 0, values, 0.0)

    def moments(values):
        return [
            jnp.sum(v, axis=0, keepdims=True)
            for v in (
                values[:first],
                values[first:],
                values[:first] * values[:first],
                values[first:] * values[first:],
            )
        ]

    narrow = (r.norm_n, r.norm_n_send, r.norm_n_recv)
    broad = (r.norm_w, r.norm_w_send, r.norm_w_recv)
    double = (r.norm_v, r.norm_v_send, r.norm_v_recv)

    def norm_start(kind, event, m, sums):
        buffer, send, recv = kind
        slot = buffer.at[event, m, dp]
        for i, value in enumerate(sums):
            slot[pl.ds(i, 1), :] = value
        for i in range(len(sums), buffer.shape[3]):
            slot[pl.ds(i, 1), :] = jnp.zeros((1, slot.shape[1]), F32)
        across_dp(
            lambda device: remote(
                slot, slot, send.at[event, m], recv.at[event, m], device
            ).start()
        )

    def norm_finish(kind, event, m):
        buffer, _, recv = kind
        wait_bytes(buffer.at[event, m, pl.ds(0, dp_count - 1)], recv.at[event, m])
        return jnp.sum(buffer[event, m], axis=0)

    def finish_moments(kind, event, m, store, fold):
        totals = norm_finish(kind, event, m)
        return [
            keep_moments(totals[4 * i : 4 * i + 4], s, m, fold) for i, s in enumerate(store)
        ]

    def keep_moments(sums, store, m, fold):
        ref, norm = store
        found = []
        for group in range(2):
            count = float(lay.totals[group] * fold)
            mean = sums[group : group + 1] / count
            square = sums[2 + group : 3 + group] / count
            found += [mean, lax.rsqrt(square - mean * mean + EPSILON)]
        for i, value in enumerate(found):
            ref[norm, m, pl.ds(i, 1), :] = value
        return found

    def moments_of(ref, norm, m):
        return [ref[norm, m, pl.ds(i, 1), :] for i in range(4)]

    def normalized(values, found):
        return per_group(lambda g, v: (v - found[2 * g]) * found[2 * g + 1], values)

    def norm_change(upstream, normed, found, gain, sums, fold):
        def one(group, u, n):
            count = float(lay.totals[group] * fold)
            plain = sums[0][group] * gain / count
            along = sums[1][group] * gain / count
            return found[2 * group + 1] * (u * gain - plain - n * along)

        return keep(per_group(one, upstream, normed)).astype(BF16)

    def add_gains(place, sums):
        at = pl.ds(place, sums[0][0].shape[1])
        own = r.gains.at[section]
        own[pl.ds(0, 1), at] += sums[1][0] + sums[1][1]
        own[pl.ds(1, 1), at] += sums[0][0] + sums[0][1]

    def rows_of(totals, at):
        return [totals[at : at + 1], totals[at + 1 : at + 2]]

    def upstream_sums(upstream, normeds):
        sums = []
        for v in [upstream] + [upstream * n for n in normeds]:
            sums += [
                jnp.sum(v[:first], axis=0, keepdims=True),
                jnp.sum(v[first:], axis=0, keepdims=True),
            ]
        return sums

    def slid(ref, cols, down, right):
        pieces = []
        for (start, stop), side in zip(lay.spans, lay.sides):
            at = PAD + start + down * side + right
            pieces.append(ref[pl.ds(at, stop - start), cols])
        values = jnp.concatenate(pieces, axis=0)
        flags = masks[(down + 1) * 3 + right + 1]
        return jnp.where(flags > 0, values, 0.0)

    def sum_start(event, m, values):
        send = r.sum_send
        send[event, m] = values.astype(BF16)
        for k in range(1, ranks):
            cols = pl.ds(pl.multiple_of(other(k) * part, part), part)
            remote(
                send.at[event, m, :, cols],
                r.sum_recv.at[event, m, k - 1],
                r.sum_send_sem.at[event, m],
                r.sum_recv_sem.at[event, m],
                (other(k), dp),
            ).start()

    def sum_finish(event, m):
        wait_bytes(r.sum_recv.at[event, m], r.sum_recv_sem.at[event, m])
        total = r.sum_send[event, m, :, mine].astype(F32)
        for k in range(ranks - 1):
            total = total + r.sum_recv[event, m, k].astype(F32)
        return total

    def get_start(event, m, values):
        get = r.get
        get[event, m, :, mine] = values
        for k in range(1, ranks):
            remote(
                get.at[event, m, :, mine],
                get.at[event, m, :, mine],
                r.get_send_sem.at[event, m],
                r.get_recv_sem.at[event, m],
                (other(k), dp),
            ).start()

    def get_finish(event, m):
        wait_bytes(
            r.get.at[event, m, :, pl.ds(0, C_MID - part)], r.get_recv_sem.at[event, m]
        )
        return r.get[event, m]

    def own_start(number, m, src, dst):
        @pl.when(section != m)
        def _():
            remote(
                src, dst, r.own_send.at[number], r.own_recv.at[number], (m, dp)
            ).start()

        @pl.when(section == m)
        def _():
            pltpu.make_async_copy(src, dst, r.own_copy.at[number]).start()

    z1, zn, zw, y1 = r.z1, r.zn, r.zw, r.y1
    r.gains[section] = jnp.zeros(r.gains.shape[1:], F32)
    pass_on(0)
    need(0)

    def do_z1(m):
        sums = None
        for phase in range(4):
            value = dot(r.x[phase, m], r.a0[...])
            z1[phase, m] = value
            found = moments(value)
            sums = found if sums is None else [a + b for a, b in zip(sums, found)]
        norm_start(narrow, F01, m, sums)

    each_micro(do_z1)
    wait_bytes(r.scales.at[pl.ds(0, ranks - 1)], r.scale_recv)
    pass_on(1)
    need(1)

    def do_a1(m):
        (found,) = finish_moments(narrow, F01, m, [(r.stat_n, N01)], 4)
        gain, shift = affine_n(N01)
        taps = first_taps()
        for phase in range(4):
            value = silu(normalized(z1[phase, m], found) * gain + shift)
            r.slide[pl.ds(PAD, rows), :] = value
            for k, (at, down, right) in enumerate(taps):
                if at == phase:
                    r.patches[0, m, :, pl.ds(k * part, part)] = slid(
                        r.slide, slice(None), down, right
                    ).astype(BF16)
        sum_start(SUM_Z2, m, dot(r.patches[0, m], r.b0[...]))

    each_micro(do_a1)
    for number in (2, 3):
        pass_on(number)

    def do_z2(m):
        value = sum_finish(SUM_Z2, m)
        zn[0, m] = value
        norm_start(narrow, F02, m, moments(value))

    each_micro(do_z2)
    need(3)

    def do_zs(m):
        zw[N12, m] = dot(r.x[0, m], r.p0[...])

    each_micro(do_zs)

    def do_h0(m):
        (found,) = finish_moments(narrow, F02, m, [(r.stat_n, N02)], 1)
        gain, shift = affine_n(N02)
        get_start(GET_H0, m, keep(silu(normalized(zn[0, m], found) * gain + shift)).astype(BF16))

    each_micro(do_h0)
    need(2)

    def do_zc(m):
        value = dot(get_finish(GET_H0, m), r.c0[...])
        zw[N11, m] = value
        norm_start(double, F11, m, moments(value) + moments(zw[N12, m]))

    each_micro(do_zc)
    for number in (4, 5, 6):
        pass_on(number)
    need(4)

    def before1(m):
        main = normalized(zw[N11, m], moments_of(r.stat_w, N11, m))
        short = normalized(zw[N12, m], moments_of(r.stat_w, N12, m))
        gain_main, shift_main = affine_w(N11)
        gain_short, shift_short = affine_w(N12)
        return main * gain_main + shift_main + short * gain_short + shift_short, main, short

    def do_y1(m):
        finish_moments(double, F11, m, [(r.stat_w, N11), (r.stat_w, N12)], 1)
        value = keep(silu(before1(m)[0])).astype(BF16)
        y1[m] = value
        sum_start(SUM_ZA, m, dot(value, r.a1[...]))

    each_micro(do_y1)

    def do_za(m):
        value = sum_finish(SUM_ZA, m)
        zn[1, m] = value
        norm_start(narrow, F21, m, moments(value))

    each_micro(do_za)
    need(5)

    def do_a2(m):
        (found,) = finish_moments(narrow, F21, m, [(r.stat_n, N21)], 1)
        gain, shift = affine_n(N21)
        r.slide[pl.ds(PAD, rows), :] = silu(normalized(zn[1, m], found) * gain + shift)
        for k, (down, right) in enumerate(second_taps()):
            r.patches[1, m, :, pl.ds(k * part, part)] = slid(
                r.slide, slice(None), down, right
            ).astype(BF16)
        sum_start(SUM_ZB, m, dot(r.patches[1, m], r.b1[...]))

    each_micro(do_a2)

    def do_zb(m):
        value = sum_finish(SUM_ZB, m)
        zn[2, m] = value
        norm_start(narrow, F22, m, moments(value))

    each_micro(do_zb)

    def do_h2(m):
        (found,) = finish_moments(narrow, F22, m, [(r.stat_n, N22)], 1)
        gain, shift = affine_n(N22)
        get_start(GET_H2, m, keep(silu(normalized(zn[2, m], found) * gain + shift)).astype(BF16))

    each_micro(do_h2)
    need(6)

    def do_zd(m):
        value = dot(get_finish(GET_H2, m), r.c1[...])
        zw[N31, m] = value
        norm_start(broad, F31, m, moments(value))

    each_micro(do_zd)

    def do_output(m):
        (found,) = finish_moments(broad, F31, m, [(r.stat_w, N31)], 1)
        gain, shift = affine_w(N31)
        normed = normalized(zw[N31, m], found)
        before = normed * gain + shift + y1[m].astype(F32)
        sigmoid = jax.nn.sigmoid(before)
        r.out_send[m] = (before * sigmoid).astype(BF16)
        upstream = r.cot[m].astype(F32) * (sigmoid * (1.0 + before * (1.0 - sigmoid)))
        r.skip[m] = upstream.astype(BF16)
        r.uw[m] = upstream
        norm_start(broad, B31, m, upstream_sums(upstream, [normed]))

    each_micro(do_output)

    def do_ddzd(m):
        totals = norm_finish(broad, B31, m)
        sums = [rows_of(totals, 0), rows_of(totals, 2)]
        add_gains(C_MID + 2 * wide, sums)
        found = moments_of(r.stat_w, N31, m)
        normed = normalized(zw[N31, m], found)
        value = norm_change(r.uw[m], normed, found, affine_w(N31)[0], sums, 1)
        r.ddzd[m] = value
        sum_start(SUM_DH2, m, dot_back(value, r.c1[...]))

    each_micro(do_ddzd)

    def send_output(m):
        own_start(0, m, r.out_send.at[m], r.out_own.at[:, mine_wide])

    each_micro(send_output)

    def narrow_upstream(norm, place, event, m, value):
        found = moments_of(r.stat_n, norm, m)
        gain, shift = affine_n(norm)
        normed = normalized(zn[place, m], found)
        upstream = value * silu_slope(normed * gain + shift)
        r.un[place, m] = upstream
        norm_start(narrow, event, m, upstream_sums(upstream, [normed]))

    def narrow_change(norm, place, event, m):
        totals = norm_finish(narrow, event, m)
        sums = [rows_of(totals, 0), rows_of(totals, 2)]
        add_gains(part * norm, sums)
        found = moments_of(r.stat_n, norm, m)
        normed = normalized(zn[place, m], found)
        return norm_change(r.un[place, m], normed, found, affine_n(norm)[0], sums, 1)

    def tall(ref, count):
        return ref.reshape(micro * rows, count)

    share_rows = ROWS // ranks
    slice_base = (0, 0, share_rows, share_rows + C_MID, 2 * share_rows, 2 * share_rows + wide, 3 * share_rows)
    chips = dp_count // 2
    chip = dp // 2
    rank = core * chips + chip
    base_rows = [sum(HEIGHTS[:number]) for number in range(7)]

    def own_piece(number, refs):
        whole, pair, near, total = refs
        base, height = base_rows[number], whole.shape[0] if number == A0 else HEIGHTS[number]
        each = height // dp_count
        return (
            whole.at[pl.ds(base, height)],
            pair.at[pl.ds(base // 2, height // 2)],
            near.at[:, pl.ds(base // dp_count, each)],
            total.at[pl.ds(base // dp_count, each)],
            height,
        )

    def gradient_refs(number):
        if number == A0:
            return own_piece(number, (r.da, r.da_pair, r.da_near, r.da_sum))
        return own_piece(number, (r.dw, r.dw_pair, r.dw_near, r.dw_sum))

    def make(number, left, right, unit):
        height = HEIGHTS[number]
        right = right.reshape(micro * rows, C_MID)

        def step(i, carry):
            at = pl.multiple_of(i * unit, unit)
            value = dot_rows(left(pl.ds(at, unit)).reshape(micro * rows, unit), right)
            if lay.fast:
                r.dw[pl.ds(pl.multiple_of(base_rows[number] + at, 128), unit), :] = value.astype(BF16)
            else:
                r.stage[pl.ds(0, unit), :] = value.astype(BF16)
                copy = pltpu.make_async_copy(
                    r.stage.at[pl.ds(0, unit)],
                    r.dw.at[pl.ds(pl.multiple_of(slice_base[number] + at, 128), unit)],
                    r.stage_sem,
                )
                copy.start()
                copy.wait()
            return carry

        lax.fori_loop(0, height // unit, step, 0)
        to_sibling(number)

    def to_sibling(number):
        if not lay.fast:
            return
        whole, pair, _, _, height = gradient_refs(number)
        half = height // 2
        remote(
            whole.at[pl.ds(pl.multiple_of((1 - core) * half, 64), half)],
            pair,
            r.pair_send.at[number],
            r.pair_recv.at[number],
            sibling,
        ).start()

    def fold(number):
        if not lay.fast:
            return
        whole, pair, near, _, height = gradient_refs(number)
        half, each = height // 2, height // dp_count
        wait_bytes(pair, r.pair_recv.at[number])
        mine_rows = whole.at[pl.ds(pl.multiple_of(core * half, 64), half)]

        def step(i, carry):
            at = pl.ds(pl.multiple_of(i * 64, 64), 64)
            mine_rows[at, :] = (mine_rows[at, :].astype(F32) + pair[at, :].astype(F32)).astype(BF16)
            return carry

        lax.fori_loop(0, half // 64, step, 0)
        for k in range(1, chips):
            target = lax.rem(chip + k, chips)
            remote(
                mine_rows.at[pl.ds(pl.multiple_of(target * each, 16), each)],
                near.at[k - 1],
                r.near_send.at[number],
                r.near_recv.at[number],
                (section, 2 * target + core),
            ).start()

    def units(number):
        height = C_IN if number == A0 else HEIGHTS[number]
        each = height // dp_count
        whole = ROWS // dp_count
        unit = 64 if number in (A0, A1) else 16
        found = []
        for i in range(each // unit):
            row = rank * each + i * unit
            if number == A0:
                owner, at, cols = row // whole, lax.rem(row, whole), mine
            elif number in (C0, P0, C1):
                row = row + (C_MID if number == P0 else 0)
                owner, cols = row // (whole // ranks), slice(None)
                at = section * (whole // ranks) + lax.rem(row, whole // ranks)
            else:
                if number == A1:
                    row = row + section * wide
                else:
                    base = C_IN if number == B0 else C_OUT
                    row = base + C_MID * (row // part) + part * section + lax.rem(row, part)
                owner, at, cols = row // whole, lax.rem(row, whole), slice(None)
            place = r.share.at[pl.ds(pl.multiple_of(at, unit), unit), cols]
            found.append((owner, place))
        return unit, found

    def finish(number):
        if not lay.fast:
            return
        whole, _, near, total, height = gradient_refs(number)
        each = height // dp_count
        wait_bytes(near, r.near_recv.at[number])
        value = whole[pl.ds(pl.multiple_of(rank * each, 16), each), :].astype(F32)
        for k in range(chips - 1):
            value = value + near[k].astype(F32)
        total[...] = value
        unit, found = units(number)
        for i, (owner, place) in enumerate(found):
            src = total.at[pl.ds(i * unit, unit)]
            here = (owner == dp) & (section == SOURCE[number])

            @pl.when(here)
            def _():
                pltpu.make_async_copy(src, place, r.share_recv).start()

            @pl.when(jnp.logical_not(here))
            def _():
                remote(
                    src,
                    place,
                    r.share_send.at[number, i],
                    r.share_recv,
                    (SOURCE[number], owner),
                ).start()

    def finish_shares():
        whole = ROWS // dp_count
        sizes = (C_IN + 9 * C_MID, ranks * (C_MID + C_IN), C_OUT + 9 * C_MID, ranks * C_MID)
        count = jnp.int32(0)
        for source, size in enumerate(sizes):
            count = jnp.where(section == source, size, count)
        count = jnp.clip(count - whole * dp, 0, whole)
        lengths = {min(max(size - whole * d, 0), whole) for size in sizes for d in range(dp_count)}
        for length in sorted(lengths):
            if length:

                @pl.when(count == length)
                def _():
                    wait_bytes(r.share.at[pl.ds(0, length)], r.share_recv)

        lanes = [pl.ds(part * q, part) for q in range(ranks)]

        @pl.when(lax.rem(section, 2) == 0)
        def _():
            for q in range(ranks):
                r.dw_out[pl.ds(q, whole, stride=ranks), :] = r.share[:, lanes[q]]

        @pl.when(lax.rem(section, 2) == 1)
        def _():
            short = whole // ranks
            for t in range(ranks):
                for q in range(ranks):
                    r.dw_out[pl.ds(ranks * t + q, short, stride=ranks * ranks), :] = r.share[
                        pl.ds(t * short, short), lanes[q]
                    ]

    def gradients_sent():
        for number in range(7):
            _, pair, near, total, _ = gradient_refs(number)
            wait_bytes(pair, r.pair_send.at[number])
            wait_bytes(near, r.near_send.at[number])
            unit, found = units(number)
            for i, (owner, _) in enumerate(found):

                @pl.when((owner != dp) | (section != SOURCE[number]))
                def _():
                    wait_bytes(total.at[pl.ds(i * unit, unit)], r.share_send.at[number, i])


    def do_dh2(m):
        value = sum_finish(SUM_DH2, m).astype(BF16).astype(F32)
        narrow_upstream(N22, 2, B22, m, value)

    each_micro(do_dh2)
    make(C1, lambda at: r.get[GET_H2, :, :, at], r.ddzd[...], 256)

    def do_ddzb(m):
        get_start(GET_DDZB, m, narrow_change(N22, 2, B22, m))

    each_micro(do_ddzb)
    fold(C1)

    def fan_out(m, event, weight):
        r.fan[pl.ds(PAD, rows), :] = dot_back(get_finish(event, m), weight[...])

    def do_da2(m):
        fan_out(m, GET_DDZB, r.b1)
        total = None
        for k, (down, right) in enumerate(second_taps()):
            term = slid(r.fan, pl.ds(k * part, part), -down, -right)
            total = term if total is None else total + term
        narrow_upstream(N21, 1, B21, m, total)

    each_micro(do_da2)
    make(B1, lambda at: r.patches[1, :, :, at], r.get[GET_DDZB], 128)

    def do_ddza(m):
        get_start(GET_DDZA, m, narrow_change(N21, 1, B21, m))

    each_micro(do_ddza)
    fold(B1)

    def do_dy1(m):
        value = dot_back(get_finish(GET_DDZA, m), r.a1[...]) + r.skip[m].astype(F32)
        value = value.astype(BF16).astype(F32)
        before, main, short = before1(m)
        upstream = value * silu_slope(before)
        r.uw[m] = upstream
        norm_start(double, B11, m, upstream_sums(upstream, [main, short]))

    each_micro(do_dy1)
    make(A1, lambda at: y1[:, :, at], r.get[GET_DDZA], 256)
    finish(C1)

    def do_ddzc(m):
        totals = norm_finish(double, B11, m)
        plain = rows_of(totals, 0)
        for norm, at, target in ((N11, 2, r.ddzc), (N12, 4, r.ddzs)):
            sums = [plain, rows_of(totals, at)]
            add_gains(C_MID + norm * wide, sums)
            found = moments_of(r.stat_w, norm, m)
            normed = normalized(zw[norm, m], found)
            target[m] = norm_change(r.uw[m], normed, found, affine_w(norm)[0], sums, 1)
        sum_start(SUM_DH0, m, dot_back(r.ddzc[m], r.c0[...]))

    each_micro(do_ddzc)

    def do_dxs(m):
        r.dxs_send[m] = dot_back(r.ddzs[m], r.p0[...]).astype(BF16)
        own_start(1, m, r.dxs_send.at[m], r.dxs_recv.at[section])

    each_micro(do_dxs)

    def do_dh0(m):
        value = sum_finish(SUM_DH0, m).astype(BF16).astype(F32)
        narrow_upstream(N02, 0, B02, m, value)

    each_micro(do_dh0)
    make(C0, lambda at: r.get[GET_H0, :, :, at], r.ddzc[...], 256)
    fold(A1)

    def do_ddz2(m):
        get_start(GET_DDZ2, m, narrow_change(N02, 0, B02, m))

    each_micro(do_ddz2)
    for k in range(1, ranks):
        remote(
            r.a0, r.a0_all.at[:, mine], r.all_send, r.all_recv, (other(k), dp)
        ).start()
    r.a0_all[:, mine] = r.a0[...]
    make(P0, lambda at: r.x[0, :, :, at], r.ddzs[...], 256)
    fold(C0)
    finish(B1)

    def do_da1(m):
        fan_out(m, GET_DDZ2, r.b0)
        gain, shift = affine_n(N01)
        found = moments_of(r.stat_n, N01, m)
        sums = None
        for phase in range(4):
            total = None
            for k, (at, down, right) in enumerate(first_taps()):
                if at == phase:
                    term = slid(r.fan, pl.ds(k * part, part), -down, -right)
                    total = term if total is None else total + term
            normed = normalized(z1[phase, m], found)
            upstream = total * silu_slope(normed * gain + shift)
            r.u1[phase, m] = upstream
            terms = upstream_sums(upstream, [normed])
            sums = terms if sums is None else [a + b for a, b in zip(sums, terms)]
        norm_start(narrow, B01, m, sums)

    each_micro(do_da1)
    make(B0, lambda at: r.patches[0, :, :, at], r.get[GET_DDZ2], 128)
    fold(P0)
    finish(A1)

    def do_ddz1(m):
        totals = norm_finish(narrow, B01, m)
        sums = [rows_of(totals, 0), rows_of(totals, 2)]
        add_gains(0, sums)
        found = moments_of(r.stat_n, N01, m)
        gain = affine_n(N01)[0]
        for phase in range(4):
            normed = normalized(z1[phase, m], found)
            r.ddz1[phase, m] = norm_change(r.u1[phase, m], normed, found, gain, sums, 4)
        own_start(2, m, r.ddz1.at[:, m], r.ddz1_own.at[:, :, mine])

    each_micro(do_ddz1)
    for k in range(1, ranks):
        remote(
            r.gains.at[section],
            r.gains.at[section],
            r.gain_send,
            r.gain_recv,
            (other(k), dp),
        ).start()

    def da0_step(i, carry):
        at = pl.ds(pl.multiple_of(i * 128, 128), 128)
        total = None
        for phase in range(4):
            value = dot_rows(
                r.x[phase, :, :, at].reshape(micro * rows, 128),
                r.ddz1[phase].reshape(micro * rows, part),
            )
            total = value if total is None else total + value
        da0 = r.da if lay.fast else r.da0
        da0[pl.ds(pl.multiple_of(i * 128, 128), 128), :] = total.astype(BF16)
        return carry

    lax.fori_loop(0, C_IN // 128, da0_step, 0)
    to_sibling(A0)
    fold(B0)
    finish(C0)
    finish(P0)
    fold(A0)
    finish(B0)

    out_own, dxs, ddz1_own = r.out_own, r.dxs_recv, r.ddz1_own
    wait_bytes(out_own.at[:, mine_wide], r.own_copy.at[0])
    wait_bytes(out_own.at[:, pl.ds(0, C_OUT - wide)], r.own_recv.at[0])
    r.out[...] = out_own[...]
    wait_bytes(r.a0_all.at[:, pl.ds(0, C_MID - part)], r.all_recv)
    wait_bytes(dxs.at[0], r.own_copy.at[1])
    wait_bytes(dxs.at[pl.ds(0, ranks - 1)], r.own_recv.at[1])
    wait_bytes(ddz1_own.at[:, :, mine], r.own_copy.at[2])
    wait_bytes(ddz1_own.at[:, :, pl.ds(0, C_MID - part)], r.own_recv.at[2])
    for phase in range(4):
        value = dot_back(ddz1_own[phase], r.a0_all[...])
        if phase == 0:
            extra = dxs[0].astype(F32)
            for k in range(1, ranks):
                extra = extra + dxs[k].astype(F32)
            value = value + extra.astype(BF16).astype(F32)
        r.grad[phase] = value.astype(BF16)
    finish(A0)
    wait_bytes(r.gains.at[pl.ds(0, ranks - 1)], r.gain_recv)
    r.gains_out[...] = r.gains[...]

    if lay.fast:
        finish_shares()
        gradients_sent()

    def sent(m):
        for event in range(5):
            wait_bytes(r.sum_recv.at[event, m], r.sum_send_sem.at[event, m])
            wait_bytes(
                r.get.at[event, m, :, pl.ds(0, C_MID - part)], r.get_send_sem.at[event, m]
            )
        for kind, events in ((narrow, 8), (broad, 2), (double, 2)):
            buffer, send, _ = kind
            for event in range(events):
                wait_bytes(buffer.at[event, m, pl.ds(0, dp_count - 1)], send.at[event, m])

    each_micro(sent)
    wait_bytes(out_own.at[:, pl.ds(0, C_OUT - wide)], r.own_send.at[0])
    wait_bytes(dxs.at[pl.ds(0, ranks - 1)], r.own_send.at[1])
    wait_bytes(ddz1_own.at[:, :, pl.ds(0, C_MID - part)], r.own_send.at[2])
    wait_bytes(r.a0_all.at[:, pl.ds(0, C_MID - part)], r.all_send)
    wait_bytes(r.gains.at[pl.ds(0, ranks - 1)], r.gain_send)
    wait_bytes(scales.at[pl.ds(0, ranks - 1)], r.scale_send)
    for number in range(7):

        @pl.when(section != SOURCE[number])
        def _():
            wait_bytes(half_of(number, core), r.pass_send.at[number])

        @pl.when(section == SOURCE[number])
        def _():
            for _ in range(ranks - 1):
                wait_bytes(half_of(number, core), r.piece_send.at[number])


def chain(lay, ranks, dp_count, pictures, cotangent, narrow, wide_view, scales, masks):
    micro, rows = lay.micro, lay.rows
    part, wide = C_MID // ranks, C_OUT // ranks
    table = scratch_table(lay, ranks, dp_count)
    shapes = (
        jax.ShapeDtypeStruct((rows, C_OUT), BF16),
        jax.ShapeDtypeStruct((4, rows, C_IN), BF16),
        jax.ShapeDtypeStruct((ranks, 2, C_MID + 3 * wide), F32),
    )
    if lay.fast:
        shapes += (jax.ShapeDtypeStruct((WSEGMENT // dp_count // 128, 128), F32),)
    else:
        shapes += (
            jax.ShapeDtypeStruct((ROWS, C_MID), BF16),
            jax.ShapeDtypeStruct((C_IN, part), BF16),
        )
    anywhere = pl.BlockSpec(memory_space=pl.ANY)
    inside = pl.BlockSpec(memory_space=pltpu.VMEM)
    return pl.pallas_call(
        functools.partial(chain_kernel, lay, ranks, dp_count, tuple(table)),
        out_shape=shapes,
        in_specs=[anywhere] * 4 + [inside] * 2,
        out_specs=[inside] * 4 if lay.fast else [inside] * 3 + [anywhere, inside],
        scratch_shapes=list(table.values()),
        compiler_params=pltpu.CompilerParams(
            collective_id=0, has_side_effects=True, vmem_limit_bytes=63 * 2**20
        ),
        name="chain",
    )(pictures, cotangent, narrow, wide_view, scales, masks)


def summed_gradient(slices, small, section, ranks):
    small = jnp.stack([small] + [jnp.zeros_like(small)] * (ranks - 1))
    slices = slices.reshape(ranks, ROWS // ranks, C_MID)
    arrived = lax.all_to_all(slices, "section", 0, 0, tiled=True).astype(F32)
    arrived_small = lax.all_to_all(small, "section", 0, 0, tiled=True).astype(F32)
    segment = segment_gradient(arrived, arrived_small, section, ranks)
    return lax.psum_scatter(segment.reshape(-1), "dp", scatter_dimension=0, tiled=True)


def per_device(
    images_global, images_local, weights, norm_gains, norm_shifts, cotangent_global, cotangent_local
):
    section = lax.axis_index("section")
    ranks = lax.axis_size("section")
    dp_count = lax.axis_size("dp")
    lay = Layout(images_global.shape, images_local.shape, dp_count)
    micro, rows = lay.micro, lay.rows
    part = C_MID // ranks
    wide = C_OUT // ranks

    pictures = lay.pack(phases_of(images_global), phases_of(images_local))
    at = section * wide
    cotangent = lay.pack(
        lax.dynamic_slice_in_dim(cotangent_global, at, wide, 4).reshape(micro, -1, wide),
        lax.dynamic_slice_in_dim(cotangent_local, at, wide, 4).reshape(micro, -1, wide),
    )
    masks = np.stack(
        [lay.valid(down, right) for down in (-1, 0, 1) for right in (-1, 0, 1)]
    ).astype(np.float32)
    masks = jnp.broadcast_to(jnp.asarray(masks)[:, :, None], (9, rows, part))
    out, gradient, gains, *slices = chain(
        lay,
        ranks,
        dp_count,
        pictures,
        cotangent,
        weights.reshape(ROWS, C_MID),
        weights.reshape(WIDE, C_OUT),
        jnp.stack([norm_gains, norm_shifts]),
        masks,
    )

    if lay.fast:
        weight_gradient = slices[0].reshape(-1)
    else:
        weight_gradient = summed_gradient(*slices, section, ranks)

    def joined(start, width):
        block = gains[:, :, start : start + width // ranks]
        return jnp.moveaxis(block, 0, 1).reshape(2, width)

    f01, f02, f21, f22 = [joined(part * i, C_MID) for i in range(4)]
    f11, f12, f31 = [joined(C_MID + wide * i, C_OUT) for i in range(3)]
    blank = jnp.zeros((2, GSEGMENT - 2 * C_MID), F32)
    segments = jnp.stack(
        [
            jnp.concatenate([f01, f02, blank], 1),
            jnp.concatenate([f11, f12], 1),
            jnp.concatenate([f21, f22, blank], 1),
            jnp.concatenate([f31, jnp.zeros((2, GSEGMENT - C_OUT), F32)], 1),
        ]
    )
    share = GSEGMENT // dp_count
    own_norms = lax.dynamic_index_in_dim(segments, section, 0, keepdims=False)
    own_norms = lax.dynamic_slice_in_dim(own_norms, lax.axis_index("dp") * share, share, 1)

    out_global, out_local = lay.unpack(out)
    grad_global, grad_local = lay.unpack(gradient)
    return (
        out_global.reshape(1, lay.crops[0], lay.sides[0], lay.sides[0], C_OUT),
        out_local.reshape(1, lay.crops[1], lay.sides[1], lay.sides[1], C_OUT),
        whole_grid(grad_global, lay.crops[0], lay.sides[0]),
        whole_grid(grad_local, lay.crops[1], lay.sides[1]),
        weight_gradient,
        own_norms[0],
        own_norms[1],
    )


def solution(mesh):
    images = P(None, "dp", None, None, None)
    made = P("section", "dp", None, None, None)
    return jax.shard_map(
        per_device,
        mesh=mesh,
        in_specs=(images, images, P("section"), P("section"), P("section"), images, images),
        out_specs=(made, made, made, made) + (P(("section", "dp")),) * 3,
        check_vma=False,
    )
```

```python
import functools
from types import SimpleNamespace

import jax
import jax.numpy as jnp
import numpy as np
from jax import lax
from jax.experimental import pallas as pl
from jax.experimental.pallas import tpu as pltpu
from jax.sharding import PartitionSpec as P

C_IN = 1024
C_MID = 512
C_OUT = 2048
WSEGMENT = 3407872
GSEGMENT = 4096
EPSILON = 1e-05
F32 = jnp.float32
BF16 = jnp.bfloat16


def round_up(value, unit):
    return -(-value // unit) * unit


class Layout:
    def __init__(self, shape_global, shape_local, dp_count):
        self.micro = shape_global[0]
        self.crops = (shape_global[1], shape_local[1])
        self.sides = (shape_global[2] // 2, shape_local[2] // 2)
        used = [crops * side * side for crops, side in zip(self.crops, self.sides)]
        self.used = used
        first = round_up(used[0], 8)
        self.rows = round_up(first + round_up(used[1], 8), 16)
        self.spans = ((0, first), (first, self.rows))
        self.totals = [count * dp_count for count in used]
        self.fast = dp_count in (2, 4, 8) and WSEGMENT // C_MID // dp_count % 64 == 0

    def valid(self, down, right):
        flags = np.zeros((self.rows,), bool)
        for (start, _), crops, side in zip(self.spans, self.crops, self.sides):
            for crop in range(crops):
                for i in range(side):
                    for j in range(side):
                        inside = 0 <= i + down < side and 0 <= j + right < side
                        flags[start + (i * side + j) * crops + crop] = inside
        return flags

    def pack(self, in_global, in_local):
        parts = []
        for part, (start, stop) in zip((in_global, in_local), self.spans):
            pads = [(0, 0)] * (part.ndim - 2) + [(0, stop - start - part.shape[-2]), (0, 0)]
            parts.append(jnp.pad(part, pads))
        return jnp.concatenate(parts, axis=-2)

    def unpack(self, values):
        return [
            values[..., start : start + used, :]
            for (start, _), used in zip(self.spans, self.used)
        ]


def first_taps():
    return [
        (2 * (p != 1) + (q != 1), -(p == 0), -(q == 0)) for p in range(3) for q in range(3)
    ]


def second_taps():
    return [(p - 1, q - 1) for p in range(3) for q in range(3)]


def phases_of(pictures):
    micro, crops, side, _, channels = pictures.shape
    half = side // 2
    split = pictures.reshape(micro, crops, half, 2, half, 2, channels)
    return split.transpose(3, 5, 0, 2, 4, 1, 6).reshape(4, micro, half * half * crops, channels)


def half_grid(rows, crops, side):
    return rows.reshape(1, side, side, crops, -1).transpose(0, 3, 1, 2, 4)


def whole_grid(rows, crops, half):
    channels = rows.shape[-1]
    split = rows.reshape(2, 2, half, half, crops, channels)
    return split.transpose(4, 2, 0, 3, 1, 5).reshape(1, crops, 2 * half, 2 * half, channels)


def segment_gradient(pieces, small, section, ranks):
    part = C_MID // ranks
    total_rows = WSEGMENT // C_MID

    def finished(rows):
        return jnp.pad(rows, ((0, total_rows - rows.shape[0]), (0, 0)))

    def across(block):
        return block.transpose(1, 0, 2).reshape(-1, C_MID)

    def spatial(block):
        return block.reshape(ranks, 9, part, C_MID).transpose(1, 0, 2, 3).reshape(-1, C_MID)

    def first():
        return finished(
            jnp.concatenate(
                [small.transpose(1, 0, 2).reshape(-1, C_MID), spatial(pieces[:, : 9 * part])]
            )
        )

    def second():
        return finished(across(pieces[:, : C_MID + C_IN]))

    def third():
        tall = C_OUT // ranks
        return finished(
            jnp.concatenate(
                [pieces[:, :tall].reshape(-1, C_MID), spatial(pieces[:, tall : tall + 9 * part])]
            )
        )

    def fourth():
        return finished(across(pieces[:, :C_MID]))

    return lax.switch(section, [first, second, third, fourth])


MESH = pl.DeviceIdType.MESH
ROWS = WSEGMENT // C_MID
SUM_Z2, SUM_ZA, SUM_ZB, SUM_DH2, SUM_DH0 = range(5)
GET_H0, GET_H2, GET_DDZB, GET_DDZA, GET_DDZ2 = range(5)
F01, F02, F21, F22, B22, B21, B02, B01 = range(8)
F31, B31, F11, F12 = range(4)
B11 = 0
N01, N02, N21, N22 = range(4)
N11, N12, N31 = range(3)
A0, B0, C0, P0, A1, B1, C1 = range(7)
SOURCE = (0, 0, 1, 1, 2, 2, 3)
PAD = 16
SLOTS = 3
HEIGHTS = (0, 9 * C_MID // 4, C_MID, C_IN, C_OUT // 4, 9 * C_MID // 4, C_MID)


def dot(left, right):
    return lax.dot_general(left, right, (((1,), (0,)), ((), ())), preferred_element_type=F32)


def dot_back(left, right):
    return lax.dot_general(left, right, (((1,), (1,)), ((), ())), preferred_element_type=F32)


def dot_rows(left, right):
    return lax.dot_general(left, right, (((0,), (0,)), ((), ())), preferred_element_type=F32)


def silu(value):
    return value * jax.nn.sigmoid(value)


def silu_slope(before):
    sigmoid = jax.nn.sigmoid(before)
    return sigmoid * (1.0 + before * (1.0 - sigmoid))


def scratch_table(lay, ranks, dp_count):
    micro, rows = lay.micro, lay.rows
    part, wide = C_MID // ranks, C_OUT // ranks
    others = ranks - 1
    vmem, dma = pltpu.VMEM, pltpu.SemaphoreType.DMA
    return dict(
        x=vmem((4, micro, rows, C_IN), BF16),
        cot=vmem((micro, rows, wide), BF16),
        a0=vmem((C_IN, part), BF16),
        b0=vmem((9 * part, C_MID), BF16),
        c0=vmem((C_MID, wide), BF16),
        p0=vmem((C_IN, wide), BF16),
        a1=vmem((wide, C_MID), BF16),
        b1=vmem((9 * part, C_MID), BF16),
        c1=vmem((C_MID, wide), BF16),
        a0_all=vmem((C_IN, C_MID), BF16),
        raw=vmem((SLOTS, 2048, 128), BF16),
        ready=vmem((ranks, C_MID, C_MID), BF16),
        raw_sem=dma((SLOTS,)),
        scales=vmem((ranks, 2, GSEGMENT), F32),
        z1=vmem((4, micro, rows, part), F32),
        u1=vmem((4, micro, rows, part), F32),
        zn=vmem((3, micro, rows, part), F32),
        un=vmem((3, micro, rows, part), F32),
        zw=vmem((3, micro, rows, wide), F32),
        uw=vmem((micro, rows, wide), F32),
        y1=vmem((micro, rows, wide), BF16),
        skip=vmem((micro, rows, wide), BF16),
        ddzd=vmem((micro, rows, wide), BF16),
        ddzc=vmem((micro, rows, wide), BF16),
        ddzs=vmem((micro, rows, wide), BF16),
        patches=vmem((2, micro, rows, 9 * part), BF16),
        slide=vmem((PAD + rows + PAD, part), F32),
        fan=vmem((PAD + rows + PAD, 9 * part), F32),
        stat_n=vmem((4, micro, 8, part), F32),
        stat_w=vmem((3, micro, 8, wide), F32),
        sum_send=vmem((5, micro, rows, C_MID), BF16),
        sum_recv=vmem((5, micro, others, rows, part), BF16),
        get=vmem((5, micro, rows, C_MID), BF16),
        norm_n=vmem((8, micro, dp_count, 4, part), F32),
        norm_w=vmem((4, micro, dp_count, 4, wide), F32),
        **joint_scratch(lay, dp_count, wide),
        out_send=vmem((micro, rows, wide), BF16),
        out_own=vmem((rows, C_OUT), BF16),
        dxs_send=vmem((micro, rows, C_IN), BF16),
        dxs_recv=vmem((ranks, rows, C_IN), BF16),
        ddz1=vmem((4, micro, rows, part), BF16),
        ddz1_own=vmem((4, rows, C_MID), BF16),
        gains=vmem((ranks, 2, C_MID + 3 * wide), F32),
        load_sem=dma((2,)),
        piece_send=dma((7,)),
        piece_recv=dma((7,)),
        pass_send=dma((7, 3)),
        pass_recv=dma((7, 3)),
        scale_send=dma,
        scale_recv=dma,
        all_send=dma((2,)),
        all_recv=dma((2,)),
        sum_send_sem=dma((5, micro)),
        sum_recv_sem=dma((5, micro)),
        get_send_sem=dma((5, micro)),
        get_recv_sem=dma((5, micro)),
        norm_n_send=dma((8, micro)),
        norm_n_recv=dma((8, micro)),
        norm_w_send=dma((4, micro)),
        norm_w_recv=dma((4, micro)),
        own_send=dma((3,)),
        own_recv=dma((3,)),
        own_copy=dma((3,)),
        gain_send=dma,
        gain_recv=dma,
        **gradient_scratch(lay, ranks, dp_count),
    )


def joint_scratch(lay, dp_count, wide):
    vmem, dma, micro = pltpu.VMEM, pltpu.SemaphoreType.DMA, lay.micro
    if not lay.fast:
        return dict(
            norm_v=vmem((1, micro, dp_count, 8, wide), F32),
            norm_v_send=dma((1, micro)),
            norm_v_recv=dma((1, micro)),
        )
    return dict(
        joint=vmem((micro, 8, wide), F32),
        joint_all=vmem((micro, 8, wide), F32),
        joint_pair=vmem((micro, 8, wide // 2), F32),
        joint_line=vmem((micro, dp_count // 2, 8, wide // 2), F32),
        joint_send=dma((3, micro)),
        joint_recv=dma((3, micro)),
    )


def gradient_scratch(lay, ranks, dp_count):
    vmem, dma = pltpu.VMEM, pltpu.SemaphoreType.DMA
    if not lay.fast:
        return dict(stage=vmem((256, C_MID), BF16), stage_sem=dma)
    part = C_MID // ranks
    height, chips = sum(HEIGHTS), dp_count // 2
    return dict(
        dw=vmem((height, C_MID), BF16),
        dw_pair=vmem((height // 2, C_MID), BF16),
        dw_near=vmem((chips - 1, height // dp_count, C_MID), BF16),
        dw_sum=vmem((height // dp_count, C_MID), BF16),
        da=vmem((C_IN, part), BF16),
        da_pair=vmem((C_IN // 2, part), BF16),
        da_near=vmem((chips - 1, C_IN // dp_count, part), BF16),
        dw_relay=vmem((height // dp_count, C_MID), BF16),
        da_relay=vmem((C_IN // dp_count, part), BF16),
        relay_send=dma((7,)),
        relay_recv=dma((7,)),
        da_sum=vmem((C_IN // dp_count, part), BF16),
        share=vmem((ROWS // dp_count, C_MID), BF16),
        pair_send=dma((7,)),
        pair_recv=dma((7,)),
        near_send=dma((7,)),
        near_recv=dma((7,)),
        share_send=dma((7, 16)),
        share_recv=dma,
    )


def chain_kernel(lay, ranks, dp_count, names, *refs):
    inputs = ("x_in", "cot_in", "w_in", "scales_in", "masks")
    outputs = ("out", "grad", "gains_out") + (("dw_out",) if lay.fast else ("dw", "da0"))
    r = SimpleNamespace(**dict(zip(inputs + outputs + names, refs)))
    pieces = (r.a0, r.b0, r.c0, r.p0, r.a1, r.b1, r.c1)
    micro, rows = lay.micro, lay.rows
    first = lay.spans[0][1]
    part, wide = C_MID // ranks, C_OUT // ranks
    section, dp = lax.axis_index("section"), lax.axis_index("dp")
    core = lax.rem(dp, 2)
    sibling = (section, dp + 1 - 2 * core)
    masks = r.masks
    mine = pl.ds(pl.multiple_of(section * part, part), part)
    mine_wide = pl.ds(pl.multiple_of(section * wide, wide), wide)

    def other(k):
        return lax.rem(section + k, ranks)

    def across_dp(act):
        if dp_count <= 8:
            for k in range(1, dp_count):
                act((section, lax.rem(dp + k, dp_count)))
        else:

            def step(k, carry):
                act((section, lax.rem(dp + k, dp_count)))
                return carry

            lax.fori_loop(1, dp_count, step, 0)

    def remote(src, dst, send, recv, device):
        return pltpu.make_async_remote_copy(
            src_ref=src,
            dst_ref=dst,
            send_sem=send,
            recv_sem=recv,
            device_id=device,
            device_id_type=MESH,
        )

    def wait_bytes(ref, sem):
        pltpu.make_async_copy(ref, ref, sem).wait()

    def some_micros(body, first_micro, last_micro):
        def step(m, carry):
            body(m)
            return carry

        lax.fori_loop(first_micro, last_micro, step, 0)

    def each_micro(body):
        some_micros(body, 0, micro)

    barrier = pltpu.get_barrier_semaphore()

    def greet(device):
        pl.semaphore_signal(barrier, inc=1, device_id=device, device_id_type=MESH)

    if lay.fast:
        r.share[...] = jnp.zeros(r.share.shape, BF16)
        for k in range(ranks):
            for j in range(dp_count):
                if k or j:
                    greet((other(k), lax.rem(dp + j, dp_count)))
        greetings = ranks * dp_count - 1
    else:
        across_dp(greet)
        for k in range(1, ranks):
            greet((other(k), dp))
        greetings = dp_count - 1 + ranks - 1
    pltpu.make_async_copy(r.x_in, r.x, r.load_sem.at[0]).start()
    r.slide[...] = jnp.zeros(r.slide.shape, F32)
    r.fan[...] = jnp.zeros(r.fan.shape, F32)

    place = lax.rem(dp, 4)
    group = dp - place
    pair_place = lax.rem(place + 2, 4)
    pair = (section, group + pair_place)

    def run_jobs(jobs):
        def load(number):
            start, count, _ = jobs[number]
            start = start if isinstance(start, int) else pl.multiple_of(start, 512)
            slot = number % SLOTS
            return pltpu.make_async_copy(
                r.w_in.at[pl.ds(start, count)], r.raw.at[slot, pl.ds(0, count)], r.raw_sem.at[slot]
            )

        for number in range(min(SLOTS, len(jobs))):
            load(number).start()
        for number, (_, count, use) in enumerate(jobs):
            load(number).wait()
            use(r.raw[number % SLOTS, pl.ds(0, count), :])
            if number + SLOTS < len(jobs):
                load(number + SLOTS).start()

    def by_rows(value):
        return value.reshape(value.shape[0] // 4, C_MID)

    def by_columns(value):
        return value.reshape(value.shape[0] // 16, C_OUT)

    def first_jobs(source):
        jobs = []

        def keep_a0(i):
            def use(value):
                r.a0_all[pl.ds(C_MID * i, C_MID), :] = by_rows(value)

            return (2048 * i, 2048, use)

        def keep_taps(base, j, row):
            def use(value):
                matrix = by_rows(value)
                for t in range(ranks):
                    if t != source:
                        r.ready[t, pl.ds(row + part * j, part), :] = matrix[part * t : part * (t + 1)]

            return (2048 * (base + 2 * place + j), 2048, use)

        def keep_wide(chunk, row):
            def use(value):
                matrix = by_columns(value)
                for t in range(ranks):
                    if t != source:
                        r.ready[t, pl.ds(row, 128), :] = matrix[:, wide * t : wide * (t + 1)]

            return (2048 * chunk, 2048, use)

        def keep_tall(t):
            def use(value):
                r.ready[t, pl.ds(0, 128), :] = by_rows(value)

            return (2048 * t + 512 * place, 512, use)

        if source == 0:
            jobs = [keep_a0(0), keep_a0(1)] + [keep_taps(2, j, 0) for j in range(3)]
        elif source == 1:
            jobs = [keep_wide(place, 0)] + [keep_wide(4 + 2 * place + j, 128 + 128 * j) for j in range(2)]
        elif source == 2:
            jobs = [keep_tall(t) for t in range(ranks) if t != source]
            jobs += [keep_taps(4, j, 128) for j in range(3)]
        else:
            jobs = [keep_wide(place, 0)]
        return jobs

    def own_jobs(source):
        def put(ref, row, count):
            def use(value):
                ref[pl.ds(row, count), :] = by_rows(value)

            return use

        def put_wide(ref, row):
            def use(value):
                ref[pl.ds(row, 128), :] = by_columns(value)[:, wide * source : wide * (source + 1)]

            return use

        if source == 0:
            return [(2048 * (2 + tap), 512, put(r.b0, part * tap, part)) for tap in range(9)]
        if source == 1:
            jobs = [(2048 * i, 2048, put_wide(r.c0, 128 * i)) for i in range(4)]
            return jobs + [(2048 * (4 + i), 2048, put_wide(r.p0, 128 * i)) for i in range(8)]
        if source == 2:
            jobs = [(2048 * source, 2048, put(r.a1, 0, wide))]
            start = 512 * source
            return jobs + [
                (2048 * (4 + tap) + start, 512, put(r.b1, part * tap, part)) for tap in range(9)
            ]
        return [(2048 * i, 2048, put_wide(r.c1, 128 * i)) for i in range(4)]

    def send_piece(number):
        count = pieces[number].shape[0] // 4
        at = pl.ds(pl.multiple_of(place * count, 32), count)
        for k in range(1, ranks):
            t = other(k)
            if number == A0:
                src = r.a0_all.at[at, pl.ds(pl.multiple_of(t * part, part), part)]
            else:
                row = {B0: 32 * place, B1: 128 + 32 * place, P0: 128}.get(number, 0)
                src = r.ready.at[t, pl.ds(pl.multiple_of(row, 32) if number in (B0, B1) else row, count)]
            remote(
                src,
                pieces[number].at[at],
                r.piece_send.at[number],
                r.piece_recv.at[number],
                (t, dp),
            ).start()

    def quarter_of(number, which):
        ref = pieces[number]
        count = ref.shape[0] // 4
        return ref.at[pl.ds(pl.multiple_of(which * count, 32), count)]

    def pass_quarter(number, way, which, device):
        quarter = quarter_of(number, which)
        remote(
            quarter, quarter, r.pass_send.at[number, way], r.pass_recv.at[number, way], device
        ).start()

    def pass_on(number):
        @pl.when(section != SOURCE[number])
        def _():
            wait_bytes(quarter_of(number, place), r.piece_recv.at[number])
            pass_quarter(number, 1, place, pair)
            pass_quarter(number, 0, place, sibling)

    def pass_back(number):
        @pl.when(section != SOURCE[number])
        def _():
            wait_bytes(quarter_of(number, pair_place), r.pass_recv.at[number, 1])
            pass_quarter(number, 2, pair_place, sibling)

    def need(number):
        @pl.when(section != SOURCE[number])
        def _():
            wait_bytes(quarter_of(number, 0), r.pass_recv.at[number, 0])
            wait_bytes(quarter_of(number, 0), r.pass_recv.at[number, 2])

    def at_source(source, action):
        @pl.when(section == source)
        def _():
            action()

    for source in range(ranks):
        at_source(source, lambda: run_jobs(first_jobs(source)))
    pl.semaphore_wait(barrier, greetings)
    scales = r.scales
    for k in range(1, ranks):
        remote(
            r.scales_in, scales.at[section], r.scale_send, r.scale_recv, (other(k), dp)
        ).start()
    at_source(0, lambda: (send_piece(A0), send_piece(B0)))
    at_source(2, lambda: (send_piece(A1), send_piece(B1)))
    at_source(3, lambda: send_piece(C1))
    scales[section] = r.scales_in[...]

    @pl.when(section == 0)
    def _():
        r.a0[...] = r.a0_all[:, :part]

    pltpu.make_async_copy(r.cot_in, r.cot, r.load_sem.at[1]).start()
    wait_bytes(r.x, r.load_sem.at[0])

    def affine(segment, start, width):
        at = pl.ds(pl.multiple_of(start + section * width, width), width)
        return scales[segment, 0:1, at], scales[segment, 1:2, at]

    def affine_n(norm):
        return affine(2 * (norm // 2), C_MID * (norm % 2), part)

    def affine_w(norm):
        return affine((1, 1, 3)[norm], (0, C_OUT, 0)[norm], wide)

    def per_group(function, *values):
        top = function(0, *[v[:first] for v in values])
        low = function(1, *[v[first:] for v in values])
        return jnp.concatenate([top, low], axis=0)

    def widened(flags, width):
        return flags if width == part else jnp.concatenate([flags] * (width // part), axis=1)

    def keep(values):
        flags = widened(masks[4], values.shape[1])
        return jnp.where(flags > 0, values, 0.0)

    def moments(values):
        return [
            jnp.sum(v, axis=0, keepdims=True)
            for v in (
                values[:first],
                values[first:],
                values[:first] * values[:first],
                values[first:] * values[first:],
            )
        ]

    narrow = (r.norm_n, r.norm_n_send, r.norm_n_recv)
    broad = (r.norm_w, r.norm_w_send, r.norm_w_recv)
    double = None if lay.fast else (r.norm_v, r.norm_v_send, r.norm_v_recv)

    def norm_start(kind, event, m, sums):
        buffer, send, recv = kind
        slot = buffer.at[event, m, dp]
        for i, value in enumerate(sums):
            slot[pl.ds(i, 1), :] = value
        for i in range(len(sums), buffer.shape[3]):
            slot[pl.ds(i, 1), :] = jnp.zeros((1, slot.shape[1]), F32)
        across_dp(
            lambda device: remote(
                slot, slot, send.at[event, m], recv.at[event, m], device
            ).start()
        )

    def norm_finish(kind, event, m):
        buffer, _, recv = kind
        wait_bytes(buffer.at[event, m, pl.ds(0, dp_count - 1)], recv.at[event, m])
        return jnp.sum(buffer[event, m], axis=0)

    half_lanes = wide // 2
    my_half = pl.ds(pl.multiple_of(core * half_lanes, half_lanes), half_lanes)
    sibling_half = pl.ds(pl.multiple_of((1 - core) * half_lanes, half_lanes), half_lanes)

    def joint_copy(way, m, src, dst, device):
        remote(src, dst, r.joint_send.at[way, m], r.joint_recv.at[way, m], device).start()

    def joint_start(m, sums):
        if not lay.fast:
            return norm_start(double, B11, m, sums)
        for i, value in enumerate(sums):
            r.joint[m, pl.ds(i, 1), :] = value
        for i in range(len(sums), 8):
            r.joint[m, pl.ds(i, 1), :] = jnp.zeros((1, wide), F32)
        joint_copy(0, m, r.joint.at[m, :, sibling_half], r.joint_pair.at[m], sibling)

    def joint_line(m):
        wait_bytes(r.joint_pair.at[m], r.joint_recv.at[0, m])
        r.joint_line[m, dp // 2] = r.joint[m, :, my_half] + r.joint_pair[m]
        slot = r.joint_line.at[m, dp // 2]
        for k in range(1, dp_count // 2):
            target = lax.rem(dp // 2 + k, dp_count // 2)
            joint_copy(1, m, slot, slot, (section, 2 * target + core))

    def joint_back(m):
        wait_bytes(r.joint_line.at[m, pl.ds(0, dp_count // 2 - 1)], r.joint_recv.at[1, m])
        r.joint_all[m, :, my_half] = jnp.sum(r.joint_line[m], axis=0)
        slot = r.joint_all.at[m, :, my_half]
        joint_copy(2, m, slot, slot, sibling)

    def joint_finish(m):
        if not lay.fast:
            return norm_finish(double, B11, m)
        wait_bytes(r.joint_pair.at[m], r.joint_recv.at[2, m])
        return r.joint_all[m]

    def finish_moments(kind, event, m, store, fold):
        sums = norm_finish(kind, event, m)
        ref, norm = store
        found = []
        for group in range(2):
            count = float(lay.totals[group] * fold)
            mean = sums[group : group + 1] / count
            square = sums[2 + group : 3 + group] / count
            found += [mean, lax.rsqrt(square - mean * mean + EPSILON)]
        for i, value in enumerate(found):
            ref[norm, m, pl.ds(i, 1), :] = value
        return found

    def moments_of(ref, norm, m):
        return [ref[norm, m, pl.ds(i, 1), :] for i in range(4)]

    def normalized(values, found):
        return per_group(lambda g, v: (v - found[2 * g]) * found[2 * g + 1], values)

    def norm_change(upstream, normed, found, gain, sums, fold):
        def one(group, u, n):
            count = float(lay.totals[group] * fold)
            plain = sums[0][group] * gain / count
            along = sums[1][group] * gain / count
            return found[2 * group + 1] * (u * gain - plain - n * along)

        return keep(per_group(one, upstream, normed)).astype(BF16)

    def add_gains(place, sums):
        at = pl.ds(place, sums[0][0].shape[1])
        own = r.gains.at[section]
        own[pl.ds(0, 1), at] += sums[1][0] + sums[1][1]
        own[pl.ds(1, 1), at] += sums[0][0] + sums[0][1]

    def rows_of(totals, at):
        return [totals[at : at + 1], totals[at + 1 : at + 2]]

    def upstream_sums(upstream, normeds):
        sums = []
        for v in [upstream] + [upstream * n for n in normeds]:
            sums += [
                jnp.sum(v[:first], axis=0, keepdims=True),
                jnp.sum(v[first:], axis=0, keepdims=True),
            ]
        return sums

    def slid(ref, cols, down, right):
        pieces = []
        for (start, stop), side, crops in zip(lay.spans, lay.sides, lay.crops):
            at = PAD + start + (down * side + right) * crops
            pieces.append(ref[pl.ds(at, stop - start), cols])
        values = jnp.concatenate(pieces, axis=0)
        flags = masks[(down + 1) * 3 + right + 1]
        return jnp.where(flags > 0, values, 0.0)

    def sum_start(event, m, values):
        send = r.sum_send
        send[event, m] = values.astype(BF16)
        for k in range(1, ranks):
            cols = pl.ds(pl.multiple_of(other(k) * part, part), part)
            remote(
                send.at[event, m, :, cols],
                r.sum_recv.at[event, m, k - 1],
                r.sum_send_sem.at[event, m],
                r.sum_recv_sem.at[event, m],
                (other(k), dp),
            ).start()

    def sum_finish(event, m):
        wait_bytes(r.sum_recv.at[event, m], r.sum_recv_sem.at[event, m])
        total = r.sum_send[event, m, :, mine].astype(F32)
        for k in range(ranks - 1):
            total = total + r.sum_recv[event, m, k].astype(F32)
        return total

    def get_start(event, m, values):
        get = r.get
        get[event, m, :, mine] = values
        for k in range(1, ranks):
            remote(
                get.at[event, m, :, mine],
                get.at[event, m, :, mine],
                r.get_send_sem.at[event, m],
                r.get_recv_sem.at[event, m],
                (other(k), dp),
            ).start()

    def get_wait(event, m):
        wait_bytes(
            r.get.at[event, m, :, pl.ds(0, C_MID - part)], r.get_recv_sem.at[event, m]
        )

    def get_finish(event, m):
        get_wait(event, m)
        return r.get[event, m]

    def own_start(number, m, src, dst):
        @pl.when(section != m)
        def _():
            remote(
                src, dst, r.own_send.at[number], r.own_recv.at[number], (m, dp)
            ).start()

        @pl.when(section == m)
        def _():
            pltpu.make_async_copy(src, dst, r.own_copy.at[number]).start()

    z1, zn, zw, y1 = r.z1, r.zn, r.zw, r.y1
    r.gains[section] = jnp.zeros(r.gains.shape[1:], F32)
    pass_on(A0)
    at_source(1, lambda: (send_piece(C0), send_piece(P0)))
    pass_back(A0)
    need(A0)

    def do_z1(m):
        sums = None
        for phase in range(4):
            value = dot(r.x[phase, m], r.a0[...])
            z1[phase, m] = value
            found = moments(value)
            sums = found if sums is None else [a + b for a, b in zip(sums, found)]
        norm_start(narrow, F01, m, sums)

    each_micro(do_z1)
    for source in range(ranks):
        at_source(source, lambda: run_jobs(own_jobs(source)))
    wait_bytes(r.cot, r.load_sem.at[1])
    wait_bytes(r.scales.at[pl.ds(0, ranks - 1)], r.scale_recv)
    pass_on(B0)

    def do_a1(m):
        found = finish_moments(narrow, F01, m, (r.stat_n, N01), 4)
        gain, shift = affine_n(N01)
        taps = first_taps()
        for phase in range(4):
            value = silu(normalized(z1[phase, m], found) * gain + shift)
            r.slide[pl.ds(PAD, rows), :] = value
            for k, (at, down, right) in enumerate(taps):
                if at == phase:
                    r.patches[0, m, :, pl.ds(k * part, part)] = slid(
                        r.slide, slice(None), down, right
                    ).astype(BF16)

    each_micro(do_a1)
    pass_back(B0)
    need(B0)

    def do_s2(m):
        sum_start(SUM_Z2, m, dot(r.patches[0, m], r.b0[...]))

    each_micro(do_s2)
    pass_on(C0)
    pass_on(P0)

    def do_z2(m):
        value = sum_finish(SUM_Z2, m)
        zn[0, m] = value
        norm_start(narrow, F02, m, moments(value))

    each_micro(do_z2)
    pass_back(C0)
    pass_back(P0)
    need(P0)

    def do_zs(m):
        value = dot(r.x[0, m], r.p0[...])
        zw[N12, m] = value
        norm_start(broad, F12, m, moments(value))

    each_micro(do_zs)

    def do_h0(m):
        found = finish_moments(narrow, F02, m, (r.stat_n, N02), 1)
        gain, shift = affine_n(N02)
        get_start(GET_H0, m, keep(silu(normalized(zn[0, m], found) * gain + shift)).astype(BF16))

    each_micro(do_h0)
    pass_on(A1)
    pass_on(B1)
    need(C0)

    def do_zc(m):
        value = dot(get_finish(GET_H0, m), r.c0[...])
        zw[N11, m] = value
        norm_start(broad, F11, m, moments(value))

    each_micro(do_zc)
    pass_back(A1)
    pass_on(C1)
    need(A1)

    def before1(m):
        main = normalized(zw[N11, m], moments_of(r.stat_w, N11, m))
        short = normalized(zw[N12, m], moments_of(r.stat_w, N12, m))
        gain_main, shift_main = affine_w(N11)
        gain_short, shift_short = affine_w(N12)
        return main * gain_main + shift_main + short * gain_short + shift_short, main, short

    def do_y1(m):
        finish_moments(broad, F12, m, (r.stat_w, N12), 1)
        finish_moments(broad, F11, m, (r.stat_w, N11), 1)
        value = keep(silu(before1(m)[0])).astype(BF16)
        y1[m] = value
        sum_start(SUM_ZA, m, dot(value, r.a1[...]))

    each_micro(do_y1)
    pass_back(B1)

    def do_za(m):
        value = sum_finish(SUM_ZA, m)
        zn[1, m] = value
        norm_start(narrow, F21, m, moments(value))

    each_micro(do_za)
    pass_back(C1)
    need(B1)

    def do_a2(m):
        found = finish_moments(narrow, F21, m, (r.stat_n, N21), 1)
        gain, shift = affine_n(N21)
        r.slide[pl.ds(PAD, rows), :] = silu(normalized(zn[1, m], found) * gain + shift)
        for k, (down, right) in enumerate(second_taps()):
            r.patches[1, m, :, pl.ds(k * part, part)] = slid(
                r.slide, slice(None), down, right
            ).astype(BF16)
        sum_start(SUM_ZB, m, dot(r.patches[1, m], r.b1[...]))

    each_micro(do_a2)

    def do_zb(m):
        value = sum_finish(SUM_ZB, m)
        zn[2, m] = value
        norm_start(narrow, F22, m, moments(value))

    each_micro(do_zb)

    def do_h2(m):
        found = finish_moments(narrow, F22, m, (r.stat_n, N22), 1)
        gain, shift = affine_n(N22)
        get_start(GET_H2, m, keep(silu(normalized(zn[2, m], found) * gain + shift)).astype(BF16))

    each_micro(do_h2)
    need(C1)

    def do_zd(m):
        value = dot(get_finish(GET_H2, m), r.c1[...])
        zw[N31, m] = value
        norm_start(broad, F31, m, moments(value))

    each_micro(do_zd)
    half_rows = pl.ds(pl.multiple_of(core * (C_IN // 2), 64), C_IN // 2)

    def lanes_of(which):
        return pl.ds(pl.multiple_of(which * part, part), part)

    for k in range(1, ranks):

        @pl.when(other(k) != 0)
        def _():
            remote(
                r.a0.at[half_rows],
                r.a0_all.at[half_rows, mine],
                r.all_send.at[0],
                r.all_recv.at[0],
                (other(k), dp),
            ).start()

    @pl.when(section != 0)
    def _():
        r.a0_all[:, mine] = r.a0[...]

    a0_others = r.a0_all.at[pl.ds(0, C_IN // 2), pl.ds(0, C_MID - part)]
    def do_output(m):
        found = finish_moments(broad, F31, m, (r.stat_w, N31), 1)
        gain, shift = affine_w(N31)
        normed = normalized(zw[N31, m], found)
        before = normed * gain + shift + y1[m].astype(F32)
        sigmoid = jax.nn.sigmoid(before)
        r.out_send[m] = (before * sigmoid).astype(BF16)
        upstream = r.cot[m].astype(F32) * (sigmoid * (1.0 + before * (1.0 - sigmoid)))
        r.skip[m] = upstream.astype(BF16)
        r.uw[m] = upstream
        norm_start(broad, B31, m, upstream_sums(upstream, [normed]))

    each_micro(do_output)

    def do_ddzd(m):
        totals = norm_finish(broad, B31, m)
        sums = [rows_of(totals, 0), rows_of(totals, 2)]
        add_gains(C_MID + 2 * wide, sums)
        found = moments_of(r.stat_w, N31, m)
        normed = normalized(zw[N31, m], found)
        value = norm_change(r.uw[m], normed, found, affine_w(N31)[0], sums, 1)
        r.ddzd[m] = value
        sum_start(SUM_DH2, m, dot_back(value, r.c1[...]))

    each_micro(do_ddzd)

    def send_output(m):
        own_start(0, m, r.out_send.at[m], r.out_own.at[:, mine_wide])

    def narrow_upstream(norm, place, event, m, value):
        found = moments_of(r.stat_n, norm, m)
        gain, shift = affine_n(norm)
        normed = normalized(zn[place, m], found)
        upstream = value * silu_slope(normed * gain + shift)
        r.un[place, m] = upstream
        norm_start(narrow, event, m, upstream_sums(upstream, [normed]))

    def narrow_change(norm, place, event, m):
        totals = norm_finish(narrow, event, m)
        sums = [rows_of(totals, 0), rows_of(totals, 2)]
        add_gains(part * norm, sums)
        found = moments_of(r.stat_n, norm, m)
        normed = normalized(zn[place, m], found)
        return norm_change(r.un[place, m], normed, found, affine_n(norm)[0], sums, 1)

    def tall(ref, count):
        return ref.reshape(micro * rows, count)

    share_rows = ROWS // ranks
    slice_base = (0, 0, share_rows, share_rows + C_MID, 2 * share_rows, 2 * share_rows + wide, 3 * share_rows)
    chips = dp_count // 2
    chip = dp // 2
    base_rows = [sum(HEIGHTS[:number]) for number in range(7)]

    def own_piece(number, refs):
        whole, pair, near, total, relayed = refs
        base, height = base_rows[number], whole.shape[0] if number == A0 else HEIGHTS[number]
        each = height // dp_count
        return (
            whole.at[pl.ds(base, height)],
            pair.at[pl.ds(base // 2, height // 2)],
            near.at[:, pl.ds(base // dp_count, each)],
            total.at[pl.ds(base // dp_count, each)],
            relayed.at[pl.ds(base // dp_count, each)],
            height,
        )

    def gradient_refs(number):
        if number == A0:
            return own_piece(number, (r.da, r.da_pair, r.da_near, r.da_sum, r.da_relay))
        return own_piece(number, (r.dw, r.dw_pair, r.dw_near, r.dw_sum, r.dw_relay))

    def make(number, left, right, unit):
        height = HEIGHTS[number]
        right = right.reshape(micro * rows, C_MID)

        def step(i, carry):
            at = pl.multiple_of(i * unit, unit)
            value = dot_rows(left(pl.ds(at, unit)).reshape(micro * rows, unit), right)
            if lay.fast:
                r.dw[pl.ds(pl.multiple_of(base_rows[number] + at, 128), unit), :] = value.astype(BF16)
            else:
                r.stage[pl.ds(0, unit), :] = value.astype(BF16)
                copy = pltpu.make_async_copy(
                    r.stage.at[pl.ds(0, unit)],
                    r.dw.at[pl.ds(pl.multiple_of(slice_base[number] + at, 128), unit)],
                    r.stage_sem,
                )
                copy.start()
                copy.wait()
            return carry

        lax.fori_loop(0, height // unit, step, 0)
        to_sibling(number)

    def to_sibling(number):
        if not lay.fast:
            return
        whole, pair, _, _, _, height = gradient_refs(number)
        each = height // dp_count
        for i in range(chips):
            remote(
                whole.at[pl.ds(pl.multiple_of((2 * i + 1 - core) * each, 16), each)],
                pair.at[pl.ds(i * each, each)],
                r.pair_send.at[number],
                r.pair_recv.at[number],
                sibling,
            ).start()

    lined = chips == 4
    at_end = (chip == 0) | (chip == chips - 1)
    inner = jnp.where(chip < 2, 1, 2) if lined else chip
    across = 3 - inner

    def rows_for(number, target):
        each = gradient_refs(number)[-1] // dp_count
        return pl.ds(pl.multiple_of((2 * target + core) * each, 16), each)

    def send_near(number, target, k):
        whole, _, near, _, _, _ = gradient_refs(number)
        remote(
            whole.at[rows_for(number, target)],
            near.at[k - 1],
            r.near_send.at[number],
            r.near_recv.at[number],
            (section, 2 * target + core),
        ).start()

    def fold(number):
        if not lay.fast:
            return
        whole, pair, near, _, relayed, height = gradient_refs(number)
        each = height // dp_count
        wait_bytes(pair, r.pair_recv.at[number])
        for k in range(1, chips + 1):
            target = lax.rem(chip + k, chips)
            at = rows_for(number, target)
            theirs = pair[pl.ds(pl.multiple_of(target * each, 16), each), :]
            whole[at, :] = (whole[at, :].astype(F32) + theirs.astype(F32)).astype(BF16)
            if k == chips:
                continue
            if not lined:
                send_near(number, target, k)
                continue

            @pl.when(jnp.logical_not(at_end) & (target != across))
            def _():
                send_near(number, target, k)

            @pl.when(at_end & (target != across))
            def _():
                send_near(number, target, k)

            @pl.when(at_end & (target == across))
            def _():
                remote(
                    whole.at[at],
                    relayed,
                    r.relay_send.at[number],
                    r.relay_recv.at[number],
                    (section, 2 * inner + core),
                ).start()

    def relay(number):
        if not (lay.fast and lined):
            return
        whole, _, _, _, relayed, height = gradient_refs(number)

        @pl.when(jnp.logical_not(at_end))
        def _():
            wait_bytes(relayed, r.relay_recv.at[number])
            at = rows_for(number, across)
            whole[at, :] = (whole[at, :].astype(F32) + relayed[...].astype(F32)).astype(BF16)

            @pl.when(chip == 1)
            def _():
                send_near(number, across, 1)

            @pl.when(chip == 2)
            def _():
                send_near(number, across, 3)

    def units(number):
        height = C_IN if number == A0 else HEIGHTS[number]
        each = height // dp_count
        whole = ROWS // dp_count
        unit = 64 if number in (A0, A1) else 16
        found = []
        for i in range(each // unit):
            row = dp * each + i * unit
            if number == A0:
                owner, at, cols = row // whole, lax.rem(row, whole), mine
            elif number in (C0, P0, C1):
                row = row + (C_MID if number == P0 else 0)
                owner, cols = row // (whole // ranks), slice(None)
                at = section * (whole // ranks) + lax.rem(row, whole // ranks)
            else:
                if number == A1:
                    row = row + section * wide
                else:
                    base = C_IN if number == B0 else C_OUT
                    row = base + C_MID * (row // part) + part * section + lax.rem(row, part)
                owner, at, cols = row // whole, lax.rem(row, whole), slice(None)
            place = r.share.at[pl.ds(pl.multiple_of(at, unit), unit), cols]
            found.append((owner, place))
        return unit, found

    def finish(number):
        if not lay.fast:
            return
        whole, _, near, total, _, height = gradient_refs(number)
        each = height // dp_count
        value = whole[pl.ds(pl.multiple_of(dp * each, 16), each), :].astype(F32)
        if lined:

            @pl.when(at_end)
            def _():
                wait_bytes(near, r.near_recv.at[number])

            @pl.when(jnp.logical_not(at_end))
            def _():
                wait_bytes(near.at[pl.ds(0, 2)], r.near_recv.at[number])

            second = jnp.where(at_end, near[1].astype(F32), 0.0)
            value = value + near[0].astype(F32) + second + near[2].astype(F32)
        else:
            wait_bytes(near, r.near_recv.at[number])
            for k in range(chips - 1):
                value = value + near[k].astype(F32)
        total[...] = value.astype(BF16)
        unit, found = units(number)
        for i, (owner, place) in enumerate(found):
            src = total.at[pl.ds(i * unit, unit)]
            here = (owner == dp) & (section == SOURCE[number])

            @pl.when(here)
            def _():
                pltpu.make_async_copy(src, place, r.share_recv).start()

            @pl.when(jnp.logical_not(here))
            def _():
                remote(
                    src,
                    place,
                    r.share_send.at[number, i],
                    r.share_recv,
                    (SOURCE[number], owner),
                ).start()

    def finish_shares():
        whole = ROWS // dp_count
        sizes = (C_IN + 9 * C_MID, ranks * (C_MID + C_IN), C_OUT + 9 * C_MID, ranks * C_MID)
        count = jnp.int32(0)
        for source, size in enumerate(sizes):
            count = jnp.where(section == source, size, count)
        count = jnp.clip(count - whole * dp, 0, whole)
        lengths = {min(max(size - whole * d, 0), whole) for size in sizes for d in range(dp_count)}
        for length in sorted(lengths):
            if length:

                @pl.when(count == length)
                def _():
                    wait_bytes(r.share.at[pl.ds(0, length)], r.share_recv)

        lanes = [pl.ds(part * q, part) for q in range(ranks)]

        @pl.when(lax.rem(section, 2) == 0)
        def _():
            for q in range(ranks):
                r.dw_out[pl.ds(q, whole, stride=ranks), :] = r.share[:, lanes[q]].astype(F32)

        @pl.when(lax.rem(section, 2) == 1)
        def _():
            short = whole // ranks
            for t in range(ranks):
                for q in range(ranks):
                    r.dw_out[pl.ds(ranks * t + q, short, stride=ranks * ranks), :] = r.share[
                        pl.ds(t * short, short), lanes[q]
                    ].astype(F32)

    def gradients_sent():
        for number in range(7):
            _, pair, near, total, relayed, _ = gradient_refs(number)
            wait_bytes(pair, r.pair_send.at[number])
            if lined:

                @pl.when(at_end)
                def _():
                    wait_bytes(near.at[pl.ds(0, 2)], r.near_send.at[number])
                    wait_bytes(relayed, r.relay_send.at[number])

                @pl.when(jnp.logical_not(at_end))
                def _():
                    wait_bytes(near, r.near_send.at[number])

            else:
                wait_bytes(near, r.near_send.at[number])
            unit, found = units(number)
            for i, (owner, _) in enumerate(found):

                @pl.when((owner != dp) | (section != SOURCE[number]))
                def _():
                    wait_bytes(total.at[pl.ds(i * unit, unit)], r.share_send.at[number, i])


    def do_dh2(m):
        value = sum_finish(SUM_DH2, m).astype(BF16).astype(F32)
        narrow_upstream(N22, 2, B22, m, value)

    each_micro(do_dh2)
    make(C1, lambda at: r.get[GET_H2, :, :, at], r.ddzd[...], 256)

    def do_ddzb(m):
        get_start(GET_DDZB, m, narrow_change(N22, 2, B22, m))

    each_micro(do_ddzb)
    fold(C1)

    def fan_out(m, event, weight):
        r.fan[pl.ds(PAD, rows), :] = dot_back(r.get[event, m], weight[...])

    def do_da2(m):
        get_finish(GET_DDZB, m)
        fan_out(m, GET_DDZB, r.b1)
        total = None
        for k, (down, right) in enumerate(second_taps()):
            term = slid(r.fan, pl.ds(k * part, part), -down, -right)
            total = term if total is None else total + term
        narrow_upstream(N21, 1, B21, m, total)

    each_micro(do_da2)

    @pl.when(section != 0)
    def _():
        wait_bytes(a0_others, r.all_recv.at[0])
        for k in range(1, ranks):
            block = r.a0_all.at[half_rows, lanes_of(other(k))]
            remote(block, block, r.all_send.at[1], r.all_recv.at[1], sibling).start()

    relay(C1)
    make(B1, lambda at: r.patches[1, :, :, at], r.get[GET_DDZB], 128)

    def do_ddza(m):
        get_start(GET_DDZA, m, narrow_change(N21, 1, B21, m))

    each_micro(do_ddza)
    fold(B1)

    def do_dy1(m):
        value = dot_back(get_finish(GET_DDZA, m), r.a1[...]) + r.skip[m].astype(F32)
        value = value.astype(BF16).astype(F32)
        before, main, short = before1(m)
        upstream = value * silu_slope(before)
        r.uw[m] = upstream
        joint_start(m, upstream_sums(upstream, [main, short]))

    each_micro(do_dy1)
    if lay.fast:
        each_micro(joint_line)
    each_micro(send_output)
    make(A1, lambda at: y1[:, :, at], r.get[GET_DDZA], 256)
    relay(B1)
    if lay.fast:
        each_micro(joint_back)

    def do_ddzc(m):
        totals = joint_finish(m)
        plain = rows_of(totals, 0)
        for norm, at, target in ((N11, 2, r.ddzc), (N12, 4, r.ddzs)):
            sums = [plain, rows_of(totals, at)]
            add_gains(C_MID + norm * wide, sums)
            found = moments_of(r.stat_w, norm, m)
            normed = normalized(zw[norm, m], found)
            target[m] = norm_change(r.uw[m], normed, found, affine_w(norm)[0], sums, 1)
        sum_start(SUM_DH0, m, dot_back(r.ddzc[m], r.c0[...]))

    each_micro(do_ddzc)
    fold(A1)

    def do_dxs(m):
        r.dxs_send[m] = dot_back(r.ddzs[m], r.p0[...]).astype(BF16)

    each_micro(do_dxs)
    make(C0, lambda at: r.get[GET_H0, :, :, at], r.ddzc[...], 256)
    make(P0, lambda at: r.x[0, :, :, at], r.ddzs[...], 256)

    def do_dh0(m):
        value = sum_finish(SUM_DH0, m).astype(BF16).astype(F32)
        narrow_upstream(N02, 0, B02, m, value)

    each_micro(do_dh0)
    fold(C0)
    fold(P0)
    relay(A1)

    def do_ddz2(m):
        get_start(GET_DDZ2, m, narrow_change(N02, 0, B02, m))

    each_micro(do_ddz2)
    relay(C0)
    each_micro(lambda m: get_wait(GET_DDZ2, m))
    make(B0, lambda at: r.patches[0, :, :, at], r.get[GET_DDZ2], 128)
    relay(P0)

    def send_dxs(m):
        own_start(1, m, r.dxs_send.at[m], r.dxs_recv.at[section])

    send_dxs(0)

    def do_da1(m):
        fan_out(m, GET_DDZ2, r.b0)

        @pl.when(m > 0)
        def _():
            send_dxs(m)

        gain, shift = affine_n(N01)
        found = moments_of(r.stat_n, N01, m)
        sums = None
        for phase in range(4):
            total = None
            for k, (at, down, right) in enumerate(first_taps()):
                if at == phase:
                    term = slid(r.fan, pl.ds(k * part, part), -down, -right)
                    total = term if total is None else total + term
            normed = normalized(z1[phase, m], found)
            upstream = total * silu_slope(normed * gain + shift)
            r.u1[phase, m] = upstream
            terms = upstream_sums(upstream, [normed])
            sums = terms if sums is None else [a + b for a, b in zip(sums, terms)]
        norm_start(narrow, B01, m, sums)

    each_micro(do_da1)
    fold(B0)
    finish(C1)
    finish(B1)
    finish(A1)

    def do_ddz1(m):
        totals = norm_finish(narrow, B01, m)
        sums = [rows_of(totals, 0), rows_of(totals, 2)]
        add_gains(0, sums)
        found = moments_of(r.stat_n, N01, m)
        gain = affine_n(N01)[0]
        for phase in range(4):
            normed = normalized(z1[phase, m], found)
            r.ddz1[phase, m] = norm_change(r.u1[phase, m], normed, found, gain, sums, 4)
        own_start(2, m, r.ddz1.at[:, m], r.ddz1_own.at[:, :, mine])

    each_micro(do_ddz1)
    relay(B0)
    for k in range(1, ranks):
        remote(
            r.gains.at[section],
            r.gains.at[section],
            r.gain_send,
            r.gain_recv,
            (other(k), dp),
        ).start()

    def da0_step(i, carry):
        at = pl.ds(pl.multiple_of(i * 128, 128), 128)
        total = None
        for phase in range(4):
            value = dot_rows(
                r.x[phase, :, :, at].reshape(micro * rows, 128),
                r.ddz1[phase].reshape(micro * rows, part),
            )
            total = value if total is None else total + value
        da0 = r.da if lay.fast else r.da0
        da0[pl.ds(pl.multiple_of(i * 128, 128), 128), :] = total.astype(BF16)
        return carry

    lax.fori_loop(0, C_IN // 128, da0_step, 0)
    to_sibling(A0)
    finish(C0)
    fold(A0)
    finish(P0)
    relay(A0)
    finish(B0)
    finish(A0)

    out_own, dxs, ddz1_own = r.out_own, r.dxs_recv, r.ddz1_own
    wait_bytes(out_own.at[:, mine_wide], r.own_copy.at[0])
    wait_bytes(out_own.at[:, pl.ds(0, C_OUT - wide)], r.own_recv.at[0])
    r.out[...] = out_own[...]

    @pl.when(section != 0)
    def _():
        wait_bytes(a0_others, r.all_recv.at[1])

    wait_bytes(dxs.at[0], r.own_copy.at[1])
    wait_bytes(dxs.at[pl.ds(0, ranks - 1)], r.own_recv.at[1])
    wait_bytes(ddz1_own.at[:, :, mine], r.own_copy.at[2])
    wait_bytes(ddz1_own.at[:, :, pl.ds(0, C_MID - part)], r.own_recv.at[2])
    for phase in range(4):
        value = dot_back(ddz1_own[phase], r.a0_all[...])
        if phase == 0:
            extra = dxs[0].astype(F32)
            for k in range(1, ranks):
                extra = extra + dxs[k].astype(F32)
            value = value + extra.astype(BF16).astype(F32)
        r.grad[phase] = value.astype(BF16)
    wait_bytes(r.gains.at[pl.ds(0, ranks - 1)], r.gain_recv)
    r.gains_out[...] = r.gains[...]

    if lay.fast:
        finish_shares()
        gradients_sent()

    def sent(m):
        for event in range(5):
            wait_bytes(r.sum_recv.at[event, m], r.sum_send_sem.at[event, m])
            wait_bytes(
                r.get.at[event, m, :, pl.ds(0, C_MID - part)], r.get_send_sem.at[event, m]
            )
        for kind, events in ((narrow, 8), (broad, 4)) + (() if lay.fast else ((double, 1),)):
            buffer, send, _ = kind
            for event in range(events):
                wait_bytes(buffer.at[event, m, pl.ds(0, dp_count - 1)], send.at[event, m])
        if lay.fast:
            wait_bytes(r.joint_pair.at[m], r.joint_send.at[0, m])
            wait_bytes(
                r.joint_line.at[m, pl.ds(0, dp_count // 2 - 1)], r.joint_send.at[1, m]
            )
            wait_bytes(r.joint_pair.at[m], r.joint_send.at[2, m])

    each_micro(sent)
    wait_bytes(out_own.at[:, pl.ds(0, C_OUT - wide)], r.own_send.at[0])
    wait_bytes(dxs.at[pl.ds(0, ranks - 1)], r.own_send.at[1])
    wait_bytes(ddz1_own.at[:, :, pl.ds(0, C_MID - part)], r.own_send.at[2])

    @pl.when(section == 0)
    def _():
        wait_bytes(a0_others, r.all_send.at[0])

    @pl.when(section != 0)
    def _():
        wait_bytes(a0_others.at[:, pl.ds(0, (ranks - 2) * part)], r.all_send.at[0])
        wait_bytes(a0_others, r.all_send.at[1])

    wait_bytes(r.gains.at[pl.ds(0, ranks - 1)], r.gain_send)
    wait_bytes(scales.at[pl.ds(0, ranks - 1)], r.scale_send)
    for number in range(7):

        @pl.when(section != SOURCE[number])
        def _():
            for way in range(3):
                wait_bytes(quarter_of(number, 0), r.pass_send.at[number, way])

        @pl.when(section == SOURCE[number])
        def _():
            count = pieces[number].shape[0] // 4
            wait_bytes(pieces[number].at[pl.ds(0, (ranks - 1) * count)], r.piece_send.at[number])


def chain(lay, ranks, dp_count, pictures, cotangent, weights, scales, masks):
    micro, rows = lay.micro, lay.rows
    part, wide = C_MID // ranks, C_OUT // ranks
    table = scratch_table(lay, ranks, dp_count)
    shapes = (
        jax.ShapeDtypeStruct((rows, C_OUT), BF16),
        jax.ShapeDtypeStruct((4, rows, C_IN), BF16),
        jax.ShapeDtypeStruct((ranks, 2, C_MID + 3 * wide), F32),
    )
    if lay.fast:
        shapes += (jax.ShapeDtypeStruct((WSEGMENT // dp_count // 128, 128), F32),)
    else:
        shapes += (
            jax.ShapeDtypeStruct((ROWS, C_MID), BF16),
            jax.ShapeDtypeStruct((C_IN, part), BF16),
        )
    anywhere = pl.BlockSpec(memory_space=pl.ANY)
    inside = pl.BlockSpec(memory_space=pltpu.VMEM)
    return pl.pallas_call(
        functools.partial(chain_kernel, lay, ranks, dp_count, tuple(table)),
        out_shape=shapes,
        in_specs=[anywhere] * 3 + [inside] * 2,
        out_specs=[inside] * 4 if lay.fast else [inside] * 3 + [anywhere, inside],
        scratch_shapes=list(table.values()),
        compiler_params=pltpu.CompilerParams(
            collective_id=0, has_side_effects=True, vmem_limit_bytes=63 * 2**20
        ),
        name="chain",
    )(pictures, cotangent, weights, scales, masks)


def summed_gradient(slices, small, section, ranks):
    small = jnp.stack([small] + [jnp.zeros_like(small)] * (ranks - 1))
    slices = slices.reshape(ranks, ROWS // ranks, C_MID)
    arrived = lax.all_to_all(slices, "section", 0, 0, tiled=True).astype(F32)
    arrived_small = lax.all_to_all(small, "section", 0, 0, tiled=True).astype(F32)
    segment = segment_gradient(arrived, arrived_small, section, ranks)
    return lax.psum_scatter(segment.reshape(-1), "dp", scatter_dimension=0, tiled=True)


def per_device(
    images_global, images_local, weights, norm_gains, norm_shifts, cotangent_global, cotangent_local
):
    section = lax.axis_index("section")
    ranks = lax.axis_size("section")
    dp_count = lax.axis_size("dp")
    lay = Layout(images_global.shape, images_local.shape, dp_count)
    micro, rows = lay.micro, lay.rows
    part = C_MID // ranks
    wide = C_OUT // ranks

    pictures = lay.pack(phases_of(images_global), phases_of(images_local))
    at = section * wide
    cotangent = lay.pack(
        *[
            jnp.moveaxis(lax.dynamic_slice_in_dim(part_of, at, wide, 4), 1, 3).reshape(micro, -1, wide)
            for part_of in (cotangent_global, cotangent_local)
        ]
    )
    masks = np.stack(
        [lay.valid(down, right) for down in (-1, 0, 1) for right in (-1, 0, 1)]
    ).astype(np.float32)
    masks = jnp.asarray(np.ascontiguousarray(np.broadcast_to(masks[:, :, None], (9, rows, part))))
    out, gradient, gains, *slices = chain(
        lay,
        ranks,
        dp_count,
        pictures,
        cotangent,
        weights.reshape(-1, 128),
        jnp.stack([norm_gains, norm_shifts]),
        masks,
    )

    if lay.fast:
        weight_gradient = slices[0].reshape(-1)
    else:
        weight_gradient = summed_gradient(*slices, section, ranks)

    def joined(start, width):
        block = gains[:, :, start : start + width // ranks]
        return jnp.moveaxis(block, 0, 1).reshape(2, width)

    f01, f02, f21, f22 = [joined(part * i, C_MID) for i in range(4)]
    f11, f12, f31 = [joined(C_MID + wide * i, C_OUT) for i in range(3)]
    blank = jnp.zeros((2, GSEGMENT - 2 * C_MID), F32)
    segments = jnp.stack(
        [
            jnp.concatenate([f01, f02, blank], 1),
            jnp.concatenate([f11, f12], 1),
            jnp.concatenate([f21, f22, blank], 1),
            jnp.concatenate([f31, jnp.zeros((2, GSEGMENT - C_OUT), F32)], 1),
        ]
    )
    share = GSEGMENT // dp_count
    own_norms = lax.dynamic_index_in_dim(segments, section, 0, keepdims=False)
    own_norms = lax.dynamic_slice_in_dim(own_norms, lax.axis_index("dp") * share, share, 1)

    out_global, out_local = lay.unpack(out)
    grad_global, grad_local = lay.unpack(gradient)
    return (
        half_grid(out_global, lay.crops[0], lay.sides[0]),
        half_grid(out_local, lay.crops[1], lay.sides[1]),
        whole_grid(grad_global, lay.crops[0], lay.sides[0]),
        whole_grid(grad_local, lay.crops[1], lay.sides[1]),
        weight_gradient,
        own_norms[0],
        own_norms[1],
    )


def solution(mesh):
    images = P(None, "dp", None, None, None)
    made = P("section", "dp", None, None, None)
    return jax.shard_map(
        per_device,
        mesh=mesh,
        in_specs=(images, images, P("section"), P("section"), P("section"), images, images),
        out_specs=(made, made, made, made) + (P(("section", "dp")),) * 3,
        check_vma=False,
    )
```

```python
import functools
from types import SimpleNamespace

import jax
import jax.numpy as jnp
import numpy as np
from jax import lax
from jax.experimental import pallas as pl
from jax.experimental.pallas import tpu as pltpu
from jax.sharding import PartitionSpec as P

C_IN = 1024
C_MID = 512
C_OUT = 2048
WSEGMENT = 3407872
GSEGMENT = 4096
EPSILON = 1e-05
F32 = jnp.float32
BF16 = jnp.bfloat16


def round_up(value, unit):
    return -(-value // unit) * unit


class Layout:
    def __init__(self, shape_global, shape_local, dp_count):
        self.micro = shape_global[0]
        self.crops = (shape_global[1], shape_local[1])
        self.sides = (shape_global[2] // 2, shape_local[2] // 2)
        used = [crops * side * side for crops, side in zip(self.crops, self.sides)]
        self.used = used
        first = round_up(used[0], 8)
        self.rows = round_up(first + round_up(used[1], 8), 16)
        self.spans = ((0, first), (first, self.rows))
        self.totals = [count * dp_count for count in used]
        self.fast = dp_count == 8 and WSEGMENT // C_MID // dp_count % 64 == 0

    def valid(self, down, right):
        flags = np.zeros((self.rows,), bool)
        for (start, _), crops, side in zip(self.spans, self.crops, self.sides):
            for crop in range(crops):
                for i in range(side):
                    for j in range(side):
                        inside = 0 <= i + down < side and 0 <= j + right < side
                        flags[start + (i * side + j) * crops + crop] = inside
        return flags


def first_taps():
    return [
        (2 * (p != 1) + (q != 1), -(p == 0), -(q == 0)) for p in range(3) for q in range(3)
    ]


def second_taps():
    return [(p - 1, q - 1) for p in range(3) for q in range(3)]


def segment_gradient(pieces, small, section, ranks):
    part = C_MID // ranks
    total_rows = WSEGMENT // C_MID

    def finished(rows):
        return jnp.pad(rows, ((0, total_rows - rows.shape[0]), (0, 0)))

    def across(block):
        return block.transpose(1, 0, 2).reshape(-1, C_MID)

    def spatial(block):
        return block.reshape(ranks, 9, part, C_MID).transpose(1, 0, 2, 3).reshape(-1, C_MID)

    def first():
        return finished(
            jnp.concatenate(
                [small.transpose(1, 0, 2).reshape(-1, C_MID), spatial(pieces[:, : 9 * part])]
            )
        )

    def second():
        return finished(across(pieces[:, : C_MID + C_IN]))

    def third():
        tall = C_OUT // ranks
        return finished(
            jnp.concatenate(
                [pieces[:, :tall].reshape(-1, C_MID), spatial(pieces[:, tall : tall + 9 * part])]
            )
        )

    def fourth():
        return finished(across(pieces[:, :C_MID]))

    return lax.switch(section, [first, second, third, fourth])


MESH = pl.DeviceIdType.MESH
ROWS = WSEGMENT // C_MID
SUM_Z2, SUM_ZA, SUM_ZB, SUM_DH2, SUM_DH0 = range(5)
GET_H0, GET_H2, GET_DDZB, GET_DDZA, GET_DDZ2 = range(5)
F01, F02, F21, F22, B22, B21, B02, B01 = range(8)
F31, B31 = range(2)
F12, F11, F31_LATE, B31_LATE = range(4)
B11, J12, J11 = range(3)
N01, N02, N21, N22 = range(4)
N11, N12, N31 = range(3)
A0, B0, C0, P0, A1, B1, C1 = range(7)
SOURCE = (0, 0, 1, 1, 2, 2, 3)
PAD = 16
SLOTS = 3
READY = 640
HEIGHTS = (0, 9 * C_MID // 4, C_MID, C_IN, C_OUT // 4, 9 * C_MID // 4, C_MID)


def dot(left, right):
    return lax.dot_general(left, right, (((1,), (0,)), ((), ())), preferred_element_type=F32)


def dot_back(left, right):
    return lax.dot_general(left, right, (((1,), (1,)), ((), ())), preferred_element_type=F32)


def dot_rows(left, right):
    return lax.dot_general(left, right, (((0,), (0,)), ((), ())), preferred_element_type=F32)


def silu(value):
    return value * jax.nn.sigmoid(value)


def silu_slope(before):
    sigmoid = jax.nn.sigmoid(before)
    return sigmoid * (1.0 + before * (1.0 - sigmoid))


def grid_shape(lay, group, fold, channels):
    side = fold * lay.sides[group]
    return (side, side, lay.crops[group], channels)


def phase_shape(lay, group):
    side = lay.sides[group]
    return (side, 2, side, 2, lay.crops[group], C_IN)


def scratch_table(lay, ranks, dp_count):
    micro, rows = lay.micro, lay.rows
    part, wide = C_MID // ranks, C_OUT // ranks
    others = ranks - 1
    vmem, dma = pltpu.VMEM, pltpu.SemaphoreType.DMA
    return dict(
        x=vmem((4, micro, rows, C_IN), BF16),
        cot=vmem((micro, rows, wide), BF16),
        x_grid=vmem((2,) + grid_shape(lay, 0, 2, C_IN), BF16),
        x_grid_2=vmem((2,) + grid_shape(lay, 1, 2, C_IN), BF16),
        cot_grid=vmem((micro,) + grid_shape(lay, 0, 1, wide), BF16),
        cot_grid_2=vmem((micro,) + grid_shape(lay, 1, 1, wide), BF16),
        a0=vmem((C_IN, part), BF16),
        b0=vmem((9 * part, C_MID), BF16),
        c0=vmem((C_MID, wide), BF16),
        p0=vmem((C_IN, wide), BF16),
        a1=vmem((wide, C_MID), BF16),
        b1=vmem((9 * part, C_MID), BF16),
        c1=vmem((C_MID, wide), BF16),
        a0_all=vmem((C_IN, C_MID), BF16),
        raw=vmem((SLOTS, 2048, 128), BF16),
        raw_sem=dma((SLOTS,)),
        scales=vmem((2, ranks, 1, GSEGMENT), F32),
        z1=vmem((4, micro, rows, part), F32),
        u1=vmem((4, micro, rows, part), F32),
        zn=vmem((3, micro, rows, part), F32),
        un=vmem((3, micro, rows, part), F32),
        zw=vmem((3, micro, rows, wide), F32),
        uw=vmem((micro, rows, wide), F32),
        y1=vmem((micro, rows, wide), BF16),
        skip=vmem((micro, rows, wide), BF16),
        ddzd=vmem((micro, rows, wide), BF16),
        ddzs=vmem((micro, rows, wide), BF16),
        patches=vmem((2, micro, rows, 9 * part), BF16),
        slide=vmem((PAD + rows + PAD, part), F32),
        fan=vmem((PAD + rows + PAD, 9 * part), F32),
        stat_n=vmem((4, micro, 8, part), F32),
        stat_w=vmem((3, micro, 8, wide), F32),
        sum_send=vmem((5, micro, rows, C_MID), BF16),
        sum_recv=vmem((5, micro, others, rows, part), BF16),
        get=vmem((5, micro, rows, C_MID), BF16),
        norm_n=vmem((4, micro, dp_count, 4, part), F32),
        norm_w=vmem((2 if lay.fast else 3, micro, dp_count, 4, wide), F32),
        **joint_scratch(lay, dp_count, wide),
        out_send=vmem((micro, rows, wide), BF16),
        out_own=vmem((rows, C_OUT), BF16),
        out_grid=vmem(grid_shape(lay, 0, 1, C_OUT), BF16),
        out_grid_2=vmem(grid_shape(lay, 1, 1, C_OUT), BF16),
        grad_grid=vmem(phase_shape(lay, 0), BF16),
        grad_grid_2=vmem(phase_shape(lay, 1), BF16),
        result_sem=dma((5,)),
        dxs_send=vmem((micro, rows, C_IN), BF16),
        dxs_recv=vmem((ranks, rows, C_IN), BF16),
        ddz1=vmem((4, micro, rows, part), BF16),
        ddz1_own=vmem((4, rows, C_MID), BF16),
        gains=vmem((ranks, 2, C_MID + 3 * wide), F32),
        x_sem=dma((2, 2)),
        cot_sem=dma((2,)),
        piece_send=dma((7,)),
        piece_recv=dma((7,)),
        pass_send=dma((7, 3)),
        pass_recv=dma((7, 3)),
        eight_send=dma((4, 3)),
        eight_recv=dma((4, 3)),
        scale_send=dma((2,)),
        scale_recv=dma((2,)),
        all_send=dma((2,)),
        all_recv=dma((2,)),
        sum_send_sem=dma((5, micro)),
        sum_recv_sem=dma((5, micro)),
        get_send_sem=dma((5, micro)),
        get_recv_sem=dma((5, micro)),
        norm_n_send=dma((8, micro)),
        norm_n_recv=dma((8, micro)),
        norm_w_send=dma((4, micro)),
        norm_w_recv=dma((4, micro)),
        own_send=dma((3,)),
        own_recv=dma((3,)),
        own_copy=dma((3,)),
        gain_send=dma,
        gain_recv=dma,
        **gradient_scratch(lay, ranks, dp_count),
    )


def joint_scratch(lay, dp_count, wide):
    vmem, dma, micro = pltpu.VMEM, pltpu.SemaphoreType.DMA, lay.micro
    if not lay.fast:
        return dict(
            norm_v=vmem((1, micro, dp_count, 8, wide), F32),
            norm_v_send=dma((1, micro)),
            norm_v_recv=dma((1, micro)),
        )
    return dict(
        joint=vmem((3, micro, 8, wide), F32),
        joint_all=vmem((3, micro, 8, wide), F32),
        joint_pair=vmem((3, micro, 8, wide // 2), F32),
        joint_line=vmem((3, micro, dp_count // 2, 8, wide // 2), F32),
        joint_send=dma((3, 3, micro)),
        joint_recv=dma((3, 3, micro)),
    )


def gradient_scratch(lay, ranks, dp_count):
    vmem, dma = pltpu.VMEM, pltpu.SemaphoreType.DMA
    if not lay.fast:
        return dict(
            stage=vmem((256, C_MID), BF16),
            stage_sem=dma,
            ready=vmem((ranks * READY, C_MID), BF16),
        )
    part = C_MID // ranks
    height, chips = sum(HEIGHTS), dp_count // 2
    return dict(
        dw=vmem((height, C_MID), BF16),
        dw_pair=vmem((height // 2, C_MID), BF16),
        dw_near=vmem((chips - 1, height // dp_count, C_MID), BF16),
        dw_sum=vmem((height // dp_count, C_MID), BF16),
        da=vmem((C_IN, part), BF16),
        da_pair=vmem((C_IN // 2, part), BF16),
        da_near=vmem((chips - 1, C_IN // dp_count, part), BF16),
        dw_relay=vmem((height // dp_count, C_MID), BF16),
        da_relay=vmem((C_IN // dp_count, part), BF16),
        relay_send=dma((7,)),
        relay_recv=dma((7,)),
        da_sum=vmem((C_IN // dp_count, part), BF16),
        share=vmem((ROWS // dp_count, C_MID), BF16),
        pair_send=dma((7,)),
        pair_recv=dma((7,)),
        near_send=dma((7,)),
        near_recv=dma((7,)),
        share_send=dma((7, 16)),
        share_recv=dma,
    )


def chain_kernel(lay, ranks, dp_count, names, *refs):
    inputs = ("x_in", "x_in_2", "cot_in", "cot_in_2", "w_in", "gains_in", "shifts_in", "masks")
    outputs = ("out", "out_2", "grad", "grad_2")
    outputs += ("gain_share", "shift_share", "share_out") if lay.fast else ("gains_out", "dw", "da0")
    r = SimpleNamespace(**dict(zip(inputs + outputs + names, refs)))
    pieces = (r.a0, r.b0, r.c0, r.p0, r.a1, r.b1, r.c1)
    micro, rows = lay.micro, lay.rows
    first = lay.spans[0][1]
    part, wide = C_MID // ranks, C_OUT // ranks
    section, dp = lax.axis_index("section"), lax.axis_index("dp")
    core = lax.rem(dp, 2)
    sibling = (section, dp + 1 - 2 * core)
    masks = r.masks
    mine = pl.ds(pl.multiple_of(section * part, part), part)
    mine_wide = pl.ds(pl.multiple_of(section * wide, wide), wide)

    def other(k):
        return lax.rem(section + k, ranks)

    def across_dp(act):
        if dp_count <= 8:
            for k in range(1, dp_count):
                act((section, lax.rem(dp + k, dp_count)))
        else:

            def step(k, carry):
                act((section, lax.rem(dp + k, dp_count)))
                return carry

            lax.fori_loop(1, dp_count, step, 0)

    def remote(src, dst, send, recv, device):
        return pltpu.make_async_remote_copy(
            src_ref=src,
            dst_ref=dst,
            send_sem=send,
            recv_sem=recv,
            device_id=device,
            device_id_type=MESH,
        )

    def wait_bytes(ref, sem):
        pltpu.make_async_copy(ref, ref, sem).wait()

    def some_micros(body, first_micro, last_micro):
        def step(m, carry):
            body(m)
            return carry

        lax.fori_loop(first_micro, last_micro, step, 0)

    def each_micro(body):
        some_micros(body, 0, micro)

    barrier = pltpu.get_barrier_semaphore()

    def greet(device):
        pl.semaphore_signal(barrier, inc=1, device_id=device, device_id_type=MESH)

    if lay.fast:
        r.share[...] = jnp.zeros(r.share.shape, BF16)
        for k in range(ranks):
            for j in range(dp_count):
                if k or j:
                    greet((other(k), lax.rem(dp + j, dp_count)))
        greetings = ranks * dp_count - 1
    else:
        across_dp(greet)
        for k in range(1, ranks):
            greet((other(k), dp))
        greetings = dp_count - 1 + ranks - 1

    def load_grids(m):
        slot = m % 2
        return (
            pltpu.make_async_copy(r.x_in.at[m], r.x_grid.at[slot], r.x_sem.at[0, slot]),
            pltpu.make_async_copy(r.x_in_2.at[m], r.x_grid_2.at[slot], r.x_sem.at[1, slot]),
        )

    for m in range(2):
        for copy in load_grids(m):
            copy.start()
    r.slide[...] = jnp.zeros(r.slide.shape, F32)
    r.fan[...] = jnp.zeros(r.fan.shape, F32)

    place = lax.rem(dp, 4)
    group = dp - place
    pair_place = lax.rem(place + 2, 4)
    pair = (section, group + pair_place)

    place_8 = lax.rem(dp, 8)
    group_8 = dp - place_8
    chip_8 = place_8 // 2
    EIGHTH, STEP = 9 * part // 8, 3 * part // 8

    def eighth(which, step):
        return r.b0.at[pl.ds(pl.multiple_of(EIGHTH * which + STEP * step, 16), STEP)]

    def eight_copy(way, step, src, dst, device):
        remote(src, dst, r.eight_send.at[way, step], r.eight_recv.at[way, step], device).start()

    def send_b0():
        for step in range(3):
            for k in range(1, ranks):
                row = READY * other(k) + 16 * place_8 + STEP * step
                src = ready.at[pl.ds(pl.multiple_of(row, 16), STEP)]
                eight_copy(0, step, src, eighth(place_8, step), (other(k), dp))

    def pass_on_b0(step):
        @pl.when(section != 0)
        def _():
            own = eighth(place_8, step)
            wait_bytes(own, r.eight_recv.at[0, step])
            for k in range(1, 4):
                target = lax.rem(chip_8 + k, 4)
                eight_copy(1, step, own, own, (section, group_8 + 2 * target + core))
            eight_copy(2, step, own, own, sibling)

    def pass_back_b0(step):
        @pl.when(section != 0)
        def _():
            wait_bytes(r.b0.at[pl.ds(0, 3 * STEP)], r.eight_recv.at[1, step])
            for k in range(1, 4):
                theirs = eighth(2 * lax.rem(chip_8 + k, 4) + core, step)
                eight_copy(3, step, theirs, theirs, sibling)

    def need_b0():
        @pl.when(section != 0)
        def _():
            for step in range(3):
                wait_bytes(r.b0.at[pl.ds(0, STEP)], r.eight_recv.at[2, step])
                wait_bytes(r.b0.at[pl.ds(0, 3 * STEP)], r.eight_recv.at[3, step])

    def b0_sent():
        three = r.b0.at[pl.ds(0, 3 * STEP)]
        for step in range(3):

            @pl.when(section == 0)
            def _():
                wait_bytes(three, r.eight_send.at[0, step])

            @pl.when(section != 0)
            def _():
                wait_bytes(three, r.eight_send.at[1, step])
                wait_bytes(r.b0.at[pl.ds(0, STEP)], r.eight_send.at[2, step])
                wait_bytes(three, r.eight_send.at[3, step])

    ready = r.dw if lay.fast else r.ready

    def parts(number):
        return 2 if number in (A1, C1) else 4

    def place_in(number):
        return core if parts(number) == 2 else place

    def run_jobs(jobs):
        def load(number):
            start, count, _ = jobs[number]
            start = start if isinstance(start, int) else pl.multiple_of(start, 512)
            slot = number % SLOTS
            return pltpu.make_async_copy(
                r.w_in.at[pl.ds(start, count)], r.raw.at[slot, pl.ds(0, count)], r.raw_sem.at[slot]
            )

        for number in range(min(SLOTS, len(jobs))):
            load(number).start()
        for number, (_, count, use) in enumerate(jobs):
            load(number).wait()
            use(r.raw[number % SLOTS, pl.ds(0, count), :])
            if number + SLOTS < len(jobs):
                load(number + SLOTS).start()

    def by_rows(value):
        return value.reshape(value.shape[0] // 4, C_MID)

    def by_columns(value):
        return value.reshape(value.shape[0] // 16, C_OUT)

    def first_jobs(source):
        jobs = []

        def keep_a0(i):
            def use(value):
                r.a0_all[pl.ds(C_MID * i, C_MID), :] = by_rows(value)

            return (2048 * i, 2048, use)

        def keep_taps(base, row):
            def use(value):
                matrix = by_rows(value)
                for t in range(ranks):
                    if t != source:
                        ready[pl.ds(READY * t + row, part), :] = matrix[part * t : part * (t + 1)]

            return (2048 * base, 2048, use)

        def keep_wide(chunk, row):
            def use(value):
                matrix = by_columns(value)
                for t in range(ranks):
                    if t != source:
                        ready[pl.ds(READY * t + row, 128), :] = matrix[:, wide * t : wide * (t + 1)]

            return (2048 * chunk, 2048, use)

        def keep_tall(t):
            def use(value):
                ready[pl.ds(READY * t, 256), :] = by_rows(value)

            return (2048 * t + 1024 * core, 1024, use)

        if source == 0:
            jobs = [keep_a0(0), keep_a0(1)] + [keep_taps(2 + place_8 + j, part * j) for j in range(2)]
        elif source == 1:
            jobs = [keep_wide(place, 0)] + [keep_wide(4 + 2 * place + j, 128 + 128 * j) for j in range(2)]
        elif source == 2:
            jobs = [keep_tall(t) for t in range(ranks) if t != source]
            jobs += [keep_taps(4 + 2 * place + j, 256 + part * j) for j in range(3)]
        else:
            jobs = [keep_wide(2 * core + j, 128 * j) for j in range(2)]
        return jobs

    def own_jobs(source):
        def put(ref, row, count):
            def use(value):
                ref[pl.ds(row, count), :] = by_rows(value)

            return use

        def put_wide(ref, row):
            def use(value):
                ref[pl.ds(row, 128), :] = by_columns(value)[:, wide * source : wide * (source + 1)]

            return use

        if source == 0:
            return [(2048 * (2 + tap), 512, put(r.b0, part * tap, part)) for tap in range(9)]
        if source == 1:
            jobs = [(2048 * i, 2048, put_wide(r.c0, 128 * i)) for i in range(4)]
            return jobs + [(2048 * (4 + i), 2048, put_wide(r.p0, 128 * i)) for i in range(8)]
        if source == 2:
            jobs = [(2048 * source, 2048, put(r.a1, 0, wide))]
            start = 512 * source
            return jobs + [
                (2048 * (4 + tap) + start, 512, put(r.b1, part * tap, part)) for tap in range(9)
            ]
        return [(2048 * i, 2048, put_wide(r.c1, 128 * i)) for i in range(4)]

    def send_piece(number):
        count = pieces[number].shape[0] // parts(number)
        at = pl.ds(pl.multiple_of(place_in(number) * count, 32), count)
        for k in range(1, ranks):
            t = other(k)
            if number == A0:
                src = r.a0_all.at[at, pl.ds(pl.multiple_of(t * part, part), part)]
            else:
                row = {B1: 256 + 32 * place, P0: 128}.get(number, 0)
                src = ready.at[pl.ds(pl.multiple_of(READY * t + row, 32), count)]
            remote(
                src,
                pieces[number].at[at],
                r.piece_send.at[number],
                r.piece_recv.at[number],
                (t, dp),
            ).start()

    def quarter_of(number, which):
        ref = pieces[number]
        count = ref.shape[0] // parts(number)
        return ref.at[pl.ds(pl.multiple_of(which * count, 32), count)]

    def pass_quarter(number, way, which, device):
        quarter = quarter_of(number, which)
        remote(
            quarter, quarter, r.pass_send.at[number, way], r.pass_recv.at[number, way], device
        ).start()

    def pass_on(number):
        @pl.when(section != SOURCE[number])
        def _():
            own = place_in(number)
            wait_bytes(quarter_of(number, own), r.piece_recv.at[number])
            if parts(number) == 4:
                pass_quarter(number, 1, own, pair)
            pass_quarter(number, 0, own, sibling)

    def pass_back(number):
        @pl.when(section != SOURCE[number])
        def _():
            wait_bytes(quarter_of(number, pair_place), r.pass_recv.at[number, 1])
            pass_quarter(number, 2, pair_place, sibling)

    def need(number):
        @pl.when(section != SOURCE[number])
        def _():
            wait_bytes(quarter_of(number, 0), r.pass_recv.at[number, 0])
            if parts(number) == 4:
                wait_bytes(quarter_of(number, 0), r.pass_recv.at[number, 2])

    def at_source(source, action):
        @pl.when(section == source)
        def _():
            action()

    for source in range(ranks):
        at_source(source, lambda: run_jobs(first_jobs(source)))
    pl.semaphore_wait(barrier, greetings)
    scales = r.scales
    for k in range(1, ranks):
        for i, row in enumerate((r.gains_in, r.shifts_in)):
            remote(
                row, scales.at[i, section], r.scale_send.at[i], r.scale_recv.at[i], (other(k), dp)
            ).start()
    at_source(0, lambda: (send_piece(A0), send_b0()))
    at_source(2, lambda: (send_piece(A1), send_piece(B1)))
    at_source(3, lambda: send_piece(C1))
    scales[0, section] = r.gains_in[...]
    scales[1, section] = r.shifts_in[...]

    @pl.when(section == 0)
    def _():
        r.a0[...] = r.a0_all[:, :part]

    mine_columns = pl.ds(pl.multiple_of(section * wide, wide), wide)
    cot_copies = (
        pltpu.make_async_copy(r.cot_in.at[:, :, :, :, mine_columns], r.cot_grid, r.cot_sem.at[0]),
        pltpu.make_async_copy(
            r.cot_in_2.at[:, :, :, :, mine_columns], r.cot_grid_2, r.cot_sem.at[1]
        ),
    )
    for copy in cot_copies:
        copy.start()

    def clear_padding(ref):
        for used, (start, stop) in zip(lay.used, lay.spans):
            low = (start + used) // 16 * 16
            high = -(-stop // 16) * 16
            if start + used < stop:
                ref[pl.ds(low, high - low), :] = jnp.zeros((high - low, ref.shape[1]), BF16)

    def by_phase(grid, group, down, right):
        side, crops = lay.sides[group], lay.crops[group]
        split = grid.reshape(side, 2, side, 2, crops, C_IN)
        return split[:, down, :, right].reshape(side * side * crops, C_IN)

    for m in range(micro):
        for copy in load_grids(m):
            copy.wait()
        for phase in range(4):
            clear_padding(r.x.at[phase, m])
            for group, grid in enumerate((r.x_grid, r.x_grid_2)):
                at = pl.ds(lay.spans[group][0], lay.used[group])
                r.x[phase, m, at, :] = by_phase(grid[m % 2], group, phase // 2, phase % 2)
        if m + 2 < micro:
            for copy in load_grids(m + 2):
                copy.start()

    def affine(segment, start, width):
        at = pl.ds(pl.multiple_of(start + section * width, width), width)
        return scales[0, segment, :, at], scales[1, segment, :, at]

    def affine_n(norm):
        return affine(2 * (norm // 2), C_MID * (norm % 2), part)

    def affine_w(norm):
        return affine((1, 1, 3)[norm], (0, C_OUT, 0)[norm], wide)

    def per_group(function, *values):
        top = function(0, *[v[:first] for v in values])
        low = function(1, *[v[first:] for v in values])
        return jnp.concatenate([top, low], axis=0)

    def widened(flags, width):
        return flags if width == part else jnp.concatenate([flags] * (width // part), axis=1)

    def keep(values):
        flags = widened(masks[4], values.shape[1])
        return jnp.where(flags > 0, values, 0.0)

    def moments(values):
        return [
            jnp.sum(v, axis=0, keepdims=True)
            for v in (
                values[:first],
                values[first:],
                values[:first] * values[:first],
                values[first:] * values[first:],
            )
        ]

    f31, b31 = (F31, B31) if lay.fast else (F31_LATE, B31_LATE)
    narrow = (r.norm_n, r.norm_n_send, r.norm_n_recv)
    broad = (r.norm_w, r.norm_w_send, r.norm_w_recv)
    double = None if lay.fast else (r.norm_v, r.norm_v_send, r.norm_v_recv)

    def norm_sent(kind, event, m):
        buffer, send, _ = kind
        wait_bytes(buffer.at[0, m, pl.ds(0, dp_count - 1)], send.at[event, m])

    def norm_start(kind, event, m, sums):
        buffer, send, recv = kind
        turns = buffer.shape[0]
        if event >= turns:
            norm_sent(kind, event - turns, m)
        slot = buffer.at[event % turns, m, dp]
        for i, value in enumerate(sums):
            slot[pl.ds(i, 1), :] = value
        for i in range(len(sums), buffer.shape[3]):
            slot[pl.ds(i, 1), :] = jnp.zeros((1, slot.shape[1]), F32)
        across_dp(
            lambda device: remote(
                slot, slot, send.at[event, m], recv.at[event, m], device
            ).start()
        )

    def norm_finish(kind, event, m):
        buffer, _, recv = kind
        wait_bytes(buffer.at[0, m, pl.ds(0, dp_count - 1)], recv.at[event, m])
        return jnp.sum(buffer[event % buffer.shape[0], m], axis=0)

    half_lanes = wide // 2
    my_half = pl.ds(pl.multiple_of(core * half_lanes, half_lanes), half_lanes)
    sibling_half = pl.ds(pl.multiple_of((1 - core) * half_lanes, half_lanes), half_lanes)

    def joint_copy(event, way, m, src, dst, device):
        remote(
            src, dst, r.joint_send.at[event, way, m], r.joint_recv.at[event, way, m], device
        ).start()

    def joint_start(event, m, sums):
        for i, value in enumerate(sums):
            r.joint[event, m, pl.ds(i, 1), :] = value
        for i in range(len(sums), 8):
            r.joint[event, m, pl.ds(i, 1), :] = jnp.zeros((1, wide), F32)
        joint_copy(
            event, 0, m, r.joint.at[event, m, :, sibling_half], r.joint_pair.at[event, m], sibling
        )

    def joint_line(event, m):
        wait_bytes(r.joint_pair.at[event, m], r.joint_recv.at[event, 0, m])
        r.joint_line[event, m, dp // 2] = r.joint[event, m, :, my_half] + r.joint_pair[event, m]
        slot = r.joint_line.at[event, m, dp // 2]
        for k in range(1, dp_count // 2):
            target = lax.rem(dp // 2 + k, dp_count // 2)
            joint_copy(event, 1, m, slot, slot, (section, 2 * target + core))

    def joint_back(event, m):
        wait_bytes(
            r.joint_line.at[event, m, pl.ds(0, dp_count // 2 - 1)], r.joint_recv.at[event, 1, m]
        )
        r.joint_all[event, m, :, my_half] = jnp.sum(r.joint_line[event, m], axis=0)
        slot = r.joint_all.at[event, m, :, my_half]
        joint_copy(event, 2, m, slot, slot, sibling)

    def joint_finish(event, m):
        wait_bytes(r.joint_pair.at[event, m], r.joint_recv.at[event, 2, m])
        return r.joint_all[event, m]

    def each_joint(step, event):
        if lay.fast:
            each_micro(lambda m: step(event, m))

    def finish_moments(kind, event, m, store, fold):
        if kind is None:
            sums = joint_finish(event, m)
        else:
            sums = norm_finish(kind, event, m)
        ref, norm = store
        found = []
        for group in range(2):
            count = float(lay.totals[group] * fold)
            mean = sums[group : group + 1] / count
            square = sums[2 + group : 3 + group] / count
            found += [mean, lax.rsqrt(square - mean * mean + EPSILON)]
        for i, value in enumerate(found):
            ref[norm, m, pl.ds(i, 1), :] = value
        return found

    def moments_of(ref, norm, m):
        return [ref[norm, m, pl.ds(i, 1), :] for i in range(4)]

    def normalized(values, found):
        return per_group(lambda g, v: (v - found[2 * g]) * found[2 * g + 1], values)

    def norm_change(upstream, normed, found, gain, sums, fold):
        def one(group, u, n):
            count = float(lay.totals[group] * fold)
            plain = sums[0][group] * gain / count
            along = sums[1][group] * gain / count
            return found[2 * group + 1] * (u * gain - plain - n * along)

        return keep(per_group(one, upstream, normed)).astype(BF16)

    def add_gains(place, sums):
        at = pl.ds(place, sums[0][0].shape[1])
        own = r.gains.at[section]
        own[pl.ds(0, 1), at] += sums[1][0] + sums[1][1]
        own[pl.ds(1, 1), at] += sums[0][0] + sums[0][1]

    def rows_of(totals, at):
        return [totals[at : at + 1], totals[at + 1 : at + 2]]

    def upstream_sums(upstream, normeds):
        sums = []
        for v in [upstream] + [upstream * n for n in normeds]:
            sums += [
                jnp.sum(v[:first], axis=0, keepdims=True),
                jnp.sum(v[first:], axis=0, keepdims=True),
            ]
        return sums

    def slid(ref, cols, down, right):
        pieces = []
        for (start, stop), side, crops in zip(lay.spans, lay.sides, lay.crops):
            at = PAD + start + (down * side + right) * crops
            pieces.append(ref[pl.ds(at, stop - start), cols])
        values = jnp.concatenate(pieces, axis=0)
        flags = masks[(down + 1) * 3 + right + 1]
        return jnp.where(flags > 0, values, 0.0)

    def sum_start(event, m, values):
        send = r.sum_send
        send[event, m] = values.astype(BF16)
        for k in range(1, ranks):
            cols = pl.ds(pl.multiple_of(other(k) * part, part), part)
            remote(
                send.at[event, m, :, cols],
                r.sum_recv.at[event, m, k - 1],
                r.sum_send_sem.at[event, m],
                r.sum_recv_sem.at[event, m],
                (other(k), dp),
            ).start()

    def sum_finish(event, m):
        wait_bytes(r.sum_recv.at[event, m], r.sum_recv_sem.at[event, m])
        total = r.sum_send[event, m, :, mine].astype(F32)
        for k in range(ranks - 1):
            total = total + r.sum_recv[event, m, k].astype(F32)
        return total

    def get_start(event, m, values):
        get = r.get
        get[event, m, :, mine] = values
        for k in range(1, ranks):
            remote(
                get.at[event, m, :, mine],
                get.at[event, m, :, mine],
                r.get_send_sem.at[event, m],
                r.get_recv_sem.at[event, m],
                (other(k), dp),
            ).start()

    def get_wait(event, m):
        wait_bytes(
            r.get.at[event, m, :, pl.ds(0, C_MID - part)], r.get_recv_sem.at[event, m]
        )

    def get_finish(event, m):
        get_wait(event, m)
        return r.get[event, m]

    def own_start(number, m, src, dst):
        @pl.when(section != m)
        def _():
            remote(
                src, dst, r.own_send.at[number], r.own_recv.at[number], (m, dp)
            ).start()

        @pl.when(section == m)
        def _():
            pltpu.make_async_copy(src, dst, r.own_copy.at[number]).start()

    z1, zn, zw, y1 = r.z1, r.zn, r.zw, r.y1
    r.gains[section] = jnp.zeros(r.gains.shape[1:], F32)
    pass_on(A0)
    at_source(1, lambda: (send_piece(C0), send_piece(P0)))
    pass_on_b0(0)
    pass_back(A0)
    need(A0)
    pass_on_b0(1)

    def do_z1(m):
        sums = None
        for phase in range(4):
            value = dot(r.x[phase, m], r.a0[...])
            z1[phase, m] = value
            found = moments(value)
            sums = found if sums is None else [a + b for a, b in zip(sums, found)]
        norm_start(narrow, F01, m, sums)

    each_micro(do_z1)
    pass_on_b0(2)
    for source in range(ranks):
        at_source(source, lambda: run_jobs(own_jobs(source)))
    for group, grid in enumerate((r.cot_grid, r.cot_grid_2)):
        cot_copies[group].wait()
        for m in range(micro):
            if group == 0:
                clear_padding(r.cot.at[m])
            r.cot[m, pl.ds(lay.spans[group][0], lay.used[group]), :] = grid[m].reshape(
                lay.used[group], wide
            )
    for i in range(2):
        wait_bytes(scales.at[i, pl.ds(0, ranks - 1)], r.scale_recv.at[i])

    def do_a1(m):
        found = finish_moments(narrow, F01, m, (r.stat_n, N01), 4)
        gain, shift = affine_n(N01)
        taps = first_taps()
        for phase in range(4):
            value = silu(normalized(z1[phase, m], found) * gain + shift)
            r.slide[pl.ds(PAD, rows), :] = value
            for k, (at, down, right) in enumerate(taps):
                if at == phase:
                    r.patches[0, m, :, pl.ds(k * part, part)] = slid(
                        r.slide, slice(None), down, right
                    ).astype(BF16)

    each_micro(do_a1)
    for step in range(3):
        pass_back_b0(step)
    need_b0()

    def do_s2(m):
        sum_start(SUM_Z2, m, dot(r.patches[0, m], r.b0[...]))

    each_micro(do_s2)
    pass_on(A1)
    pass_on(C1)
    pass_on(C0)

    def do_z2(m):
        value = sum_finish(SUM_Z2, m)
        zn[0, m] = value
        norm_start(narrow, F02, m, moments(value))

    each_micro(do_z2)
    pass_on(P0)

    def do_zs(m):
        value = dot(r.x[0, m], r.p0[...])
        zw[N12, m] = value
        if lay.fast:
            joint_start(J12, m, moments(value))
        else:
            norm_start(broad, F12, m, moments(value))


    def do_h0(m):
        found = finish_moments(narrow, F02, m, (r.stat_n, N02), 1)
        gain, shift = affine_n(N02)
        get_start(GET_H0, m, keep(silu(normalized(zn[0, m], found) * gain + shift)).astype(BF16))

    each_micro(do_h0)
    pass_back(C0)
    pass_back(P0)
    need(P0)
    each_micro(do_zs)
    each_joint(joint_line, J12)
    need(C0)

    def do_zc(m):
        value = dot(get_finish(GET_H0, m), r.c0[...])
        zw[N11, m] = value
        if lay.fast:
            joint_start(J11, m, moments(value))
        else:
            norm_start(broad, F11, m, moments(value))

    each_micro(do_zc)
    each_joint(joint_line, J11)
    each_joint(joint_back, J12)
    each_joint(joint_back, J11)
    need(A1)

    def before1(m):
        main = normalized(zw[N11, m], moments_of(r.stat_w, N11, m))
        short = normalized(zw[N12, m], moments_of(r.stat_w, N12, m))
        gain_main, shift_main = affine_w(N11)
        gain_short, shift_short = affine_w(N12)
        return main * gain_main + shift_main + short * gain_short + shift_short, main, short

    def do_y1(m):
        if lay.fast:
            finish_moments(None, J12, m, (r.stat_w, N12), 1)
            finish_moments(None, J11, m, (r.stat_w, N11), 1)
        else:
            finish_moments(broad, F12, m, (r.stat_w, N12), 1)
            finish_moments(broad, F11, m, (r.stat_w, N11), 1)
        value = keep(silu(before1(m)[0])).astype(BF16)
        y1[m] = value
        sum_start(SUM_ZA, m, dot(value, r.a1[...]))

    each_micro(do_y1)
    pass_on(B1)

    def do_za(m):
        value = sum_finish(SUM_ZA, m)
        zn[1, m] = value
        norm_start(narrow, F21, m, moments(value))

    each_micro(do_za)
    pass_back(B1)
    need(B1)

    def do_a2(m):
        found = finish_moments(narrow, F21, m, (r.stat_n, N21), 1)
        gain, shift = affine_n(N21)
        r.slide[pl.ds(PAD, rows), :] = silu(normalized(zn[1, m], found) * gain + shift)
        for k, (down, right) in enumerate(second_taps()):
            r.patches[1, m, :, pl.ds(k * part, part)] = slid(
                r.slide, slice(None), down, right
            ).astype(BF16)
        sum_start(SUM_ZB, m, dot(r.patches[1, m], r.b1[...]))

    each_micro(do_a2)

    def do_zb(m):
        value = sum_finish(SUM_ZB, m)
        zn[2, m] = value
        norm_start(narrow, F22, m, moments(value))

    each_micro(do_zb)

    def do_h2(m):
        found = finish_moments(narrow, F22, m, (r.stat_n, N22), 1)
        gain, shift = affine_n(N22)
        get_start(GET_H2, m, keep(silu(normalized(zn[2, m], found) * gain + shift)).astype(BF16))

    each_micro(do_h2)
    need(C1)

    def do_zd(m):
        value = dot(get_finish(GET_H2, m), r.c1[...])
        zw[N31, m] = value
        norm_start(broad, f31, m, moments(value))

    each_micro(do_zd)
    half_rows = pl.ds(pl.multiple_of(core * (C_IN // 2), 64), C_IN // 2)

    def lanes_of(which):
        return pl.ds(pl.multiple_of(which * part, part), part)

    for k in range(1, ranks):

        @pl.when(other(k) != 0)
        def _():
            remote(
                r.a0.at[half_rows],
                r.a0_all.at[half_rows, mine],
                r.all_send.at[0],
                r.all_recv.at[0],
                (other(k), dp),
            ).start()

    @pl.when(section != 0)
    def _():
        r.a0_all[:, mine] = r.a0[...]

    a0_others = r.a0_all.at[pl.ds(0, C_IN // 2), pl.ds(0, C_MID - part)]
    def do_output(m):
        found = finish_moments(broad, f31, m, (r.stat_w, N31), 1)
        gain, shift = affine_w(N31)
        normed = normalized(zw[N31, m], found)
        before = normed * gain + shift + y1[m].astype(F32)
        sigmoid = jax.nn.sigmoid(before)
        r.out_send[m] = (before * sigmoid).astype(BF16)
        upstream = r.cot[m].astype(F32) * (sigmoid * (1.0 + before * (1.0 - sigmoid)))
        r.skip[m] = upstream.astype(BF16)
        r.uw[m] = upstream
        norm_start(broad, b31, m, upstream_sums(upstream, [normed]))

    each_micro(do_output)

    def do_ddzd(m):
        totals = norm_finish(broad, b31, m)
        sums = [rows_of(totals, 0), rows_of(totals, 2)]
        add_gains(C_MID + 2 * wide, sums)
        found = moments_of(r.stat_w, N31, m)
        normed = normalized(zw[N31, m], found)
        value = norm_change(r.uw[m], normed, found, affine_w(N31)[0], sums, 1)
        r.ddzd[m] = value
        sum_start(SUM_DH2, m, dot_back(value, r.c1[...]))

    each_micro(do_ddzd)

    def send_output(m):
        own_start(0, m, r.out_send.at[m], r.out_own.at[:, mine_wide])

    def narrow_upstream(norm, place, event, m, value):
        found = moments_of(r.stat_n, norm, m)
        gain, shift = affine_n(norm)
        normed = normalized(zn[place, m], found)
        upstream = value * silu_slope(normed * gain + shift)
        r.un[place, m] = upstream
        norm_start(narrow, event, m, upstream_sums(upstream, [normed]))

    def narrow_change(norm, place, event, m):
        totals = norm_finish(narrow, event, m)
        sums = [rows_of(totals, 0), rows_of(totals, 2)]
        add_gains(part * norm, sums)
        found = moments_of(r.stat_n, norm, m)
        normed = normalized(zn[place, m], found)
        return norm_change(r.un[place, m], normed, found, affine_n(norm)[0], sums, 1)

    def tall(ref, count):
        return ref.reshape(micro * rows, count)

    share_rows = ROWS // ranks
    slice_base = (0, 0, share_rows, share_rows + C_MID, 2 * share_rows, 2 * share_rows + wide, 3 * share_rows)
    chips = dp_count // 2
    chip = dp // 2
    base_rows = [sum(HEIGHTS[:number]) for number in range(7)]

    def own_piece(number, refs):
        whole, pair, near, total, relayed = refs
        base, height = base_rows[number], whole.shape[0] if number == A0 else HEIGHTS[number]
        each = height // dp_count
        return (
            whole.at[pl.ds(base, height)],
            pair.at[pl.ds(base // 2, height // 2)],
            near.at[:, pl.ds(base // dp_count, each)],
            total.at[pl.ds(base // dp_count, each)],
            relayed.at[pl.ds(base // dp_count, each)],
            height,
        )

    def gradient_refs(number):
        if number == A0:
            return own_piece(number, (r.da, r.da_pair, r.da_near, r.da_sum, r.da_relay))
        return own_piece(number, (r.dw, r.dw_pair, r.dw_near, r.dw_sum, r.dw_relay))

    def make(number, left, right, unit):
        height = HEIGHTS[number]
        right = right.reshape(micro * rows, C_MID)

        def step(i, carry):
            at = pl.multiple_of(i * unit, unit)
            value = dot_rows(left(pl.ds(at, unit)).reshape(micro * rows, unit), right)
            if lay.fast:
                r.dw[pl.ds(pl.multiple_of(base_rows[number] + at, 128), unit), :] = value.astype(BF16)
            else:
                r.stage[pl.ds(0, unit), :] = value.astype(BF16)
                copy = pltpu.make_async_copy(
                    r.stage.at[pl.ds(0, unit)],
                    r.dw.at[pl.ds(pl.multiple_of(slice_base[number] + at, 128), unit)],
                    r.stage_sem,
                )
                copy.start()
                copy.wait()
            return carry

        lax.fori_loop(0, height // unit, step, 0)
        to_sibling(number)

    def to_sibling(number):
        if not lay.fast:
            return
        whole, pair, _, _, _, height = gradient_refs(number)
        each = height // dp_count
        for i in range(chips):
            remote(
                whole.at[pl.ds(pl.multiple_of((2 * i + 1 - core) * each, 16), each)],
                pair.at[pl.ds(i * each, each)],
                r.pair_send.at[number],
                r.pair_recv.at[number],
                sibling,
            ).start()

    lined = chips == 4
    at_end = (chip == 0) | (chip == chips - 1)
    inner = jnp.where(chip < 2, 1, 2) if lined else chip
    across = 3 - inner

    def rows_for(number, target):
        each = gradient_refs(number)[-1] // dp_count
        return pl.ds(pl.multiple_of((2 * target + core) * each, 16), each)

    def send_near(number, target, k):
        whole, _, near, _, _, _ = gradient_refs(number)
        remote(
            whole.at[rows_for(number, target)],
            near.at[k - 1],
            r.near_send.at[number],
            r.near_recv.at[number],
            (section, 2 * target + core),
        ).start()

    def fold(number):
        if not lay.fast:
            return
        whole, pair, near, _, relayed, height = gradient_refs(number)
        each = height // dp_count
        wait_bytes(pair, r.pair_recv.at[number])
        for k in sorted(range(1, chips + 1), key=lambda k: k != 2):
            target = lax.rem(chip + k, chips)
            at = rows_for(number, target)
            theirs = pair[pl.ds(pl.multiple_of(target * each, 16), each), :]
            whole[at, :] = (whole[at, :].astype(F32) + theirs.astype(F32)).astype(BF16)
            if k == chips:
                continue
            if not lined or number == A0:
                send_near(number, target, k)
                continue

            @pl.when(jnp.logical_not(at_end) & (target != across))
            def _():
                send_near(number, target, k)

            @pl.when(at_end & (target != across))
            def _():
                send_near(number, target, k)

            @pl.when(at_end & (target == across))
            def _():
                remote(
                    whole.at[at],
                    relayed,
                    r.relay_send.at[number],
                    r.relay_recv.at[number],
                    (section, 2 * inner + core),
                ).start()

    def relay(number):
        if not (lay.fast and lined and number != A0):
            return
        whole, _, _, _, relayed, height = gradient_refs(number)

        @pl.when(jnp.logical_not(at_end))
        def _():
            wait_bytes(relayed, r.relay_recv.at[number])
            at = rows_for(number, across)
            whole[at, :] = (whole[at, :].astype(F32) + relayed[...].astype(F32)).astype(BF16)

            @pl.when(chip == 1)
            def _():
                send_near(number, across, 1)

            @pl.when(chip == 2)
            def _():
                send_near(number, across, 3)

    def units(number):
        height = C_IN if number == A0 else HEIGHTS[number]
        each = height // dp_count
        whole = ROWS // dp_count
        unit = 64 if number in (A0, A1) else 16
        found = []
        for i in range(each // unit):
            row = dp * each + i * unit
            if number == A0:
                owner, at, cols = row // whole, lax.rem(row, whole), mine
            elif number in (C0, P0, C1):
                row = row + (C_MID if number == P0 else 0)
                owner, cols = row // (whole // ranks), slice(None)
                at = section * (whole // ranks) + lax.rem(row, whole // ranks)
            else:
                if number == A1:
                    row = row + section * wide
                else:
                    base = C_IN if number == B0 else C_OUT
                    row = base + C_MID * (row // part) + part * section + lax.rem(row, part)
                owner, at, cols = row // whole, lax.rem(row, whole), slice(None)
            place = r.share.at[pl.ds(pl.multiple_of(at, unit), unit), cols]
            found.append((owner, place))
        return unit, found

    def finish(number):
        if not lay.fast:
            return
        whole, _, near, total, _, height = gradient_refs(number)
        each = height // dp_count
        value = whole[pl.ds(pl.multiple_of(dp * each, 16), each), :].astype(F32)
        if lined and number != A0:

            @pl.when(at_end)
            def _():
                wait_bytes(near, r.near_recv.at[number])

            @pl.when(jnp.logical_not(at_end))
            def _():
                wait_bytes(near.at[pl.ds(0, 2)], r.near_recv.at[number])

            second = jnp.where(at_end, near[1].astype(F32), 0.0)
            value = value + near[0].astype(F32) + second + near[2].astype(F32)
        else:
            wait_bytes(near, r.near_recv.at[number])
            for k in range(chips - 1):
                value = value + near[k].astype(F32)
        total[...] = value.astype(BF16)
        unit, found = units(number)
        for i, (owner, place) in enumerate(found):
            src = total.at[pl.ds(i * unit, unit)]
            here = (owner == dp) & (section == SOURCE[number])

            @pl.when(here)
            def _():
                pltpu.make_async_copy(src, place, r.share_recv).start()

            @pl.when(jnp.logical_not(here))
            def _():
                remote(
                    src,
                    place,
                    r.share_send.at[number, i],
                    r.share_recv,
                    (SOURCE[number], owner),
                ).start()

    def finish_shares():
        whole = ROWS // dp_count
        sizes = (C_IN + 9 * C_MID, ranks * (C_MID + C_IN), C_OUT + 9 * C_MID, ranks * C_MID)
        count = jnp.int32(0)
        for source, size in enumerate(sizes):
            count = jnp.where(section == source, size, count)
        count = jnp.clip(count - whole * dp, 0, whole)
        lengths = {min(max(size - whole * d, 0), whole) for size in sizes for d in range(dp_count)}
        for length in sorted(lengths):
            if length:

                @pl.when(count == length)
                def _():
                    wait_bytes(r.share.at[pl.ds(0, length)], r.share_recv)

    def store_norm_shares():
        shares = (r.gain_share, r.shift_share)
        count = GSEGMENT // dp_count
        for share in shares:
            share[...] = jnp.zeros(share.shape, F32)
        for source in range(ranks):
            for device in range(dp_count):
                start = device * count
                wide_norm = source % 2 == 1
                used = {1: 2 * C_OUT, 3: C_OUT}.get(source, 2 * C_MID)
                if start >= used:
                    continue

                @pl.when((section == source) & (dp == device))
                def _():
                    for i, share in enumerate(shares):
                        if wide_norm:
                            norm = start // C_OUT + (2 if source == 3 else 0)
                            place_in = start % C_OUT
                            at = C_MID + norm * wide + place_in % wide
                            share[...] = r.gains[place_in // wide, pl.ds(i, 1), pl.ds(at, count)]
                        else:
                            at = part * (source + start // C_MID)
                            for t in range(ranks):
                                share[:, pl.ds(part * t, part)] = r.gains[t, pl.ds(i, 1), pl.ds(at, part)]

    def gradients_sent():
        for number in range(7):
            _, pair, near, total, relayed, _ = gradient_refs(number)
            wait_bytes(pair, r.pair_send.at[number])
            if lined and number != A0:

                @pl.when(at_end)
                def _():
                    wait_bytes(near.at[pl.ds(0, 2)], r.near_send.at[number])
                    wait_bytes(relayed, r.relay_send.at[number])

                @pl.when(jnp.logical_not(at_end))
                def _():
                    wait_bytes(near, r.near_send.at[number])

            else:
                wait_bytes(near, r.near_send.at[number])
            unit, found = units(number)
            for i, (owner, _) in enumerate(found):

                @pl.when((owner != dp) | (section != SOURCE[number]))
                def _():
                    wait_bytes(total.at[pl.ds(i * unit, unit)], r.share_send.at[number, i])


    def do_dh2(m):
        value = sum_finish(SUM_DH2, m).astype(BF16).astype(F32)
        narrow_upstream(N22, 2, B22, m, value)

    each_micro(do_dh2)
    b0_sent()
    for number in (A0, C0, P0, A1, B1, C1):

        @pl.when(section != SOURCE[number])
        def _():
            for way in range(3 if parts(number) == 4 else 1):
                wait_bytes(quarter_of(number, 0), r.pass_send.at[number, way])

        @pl.when(section == SOURCE[number])
        def _():
            for _ in range(ranks - 1):
                wait_bytes(quarter_of(number, 0), r.piece_send.at[number])
    make(C1, lambda at: r.get[GET_H2, :, :, at], r.ddzd[...], 256)

    def do_ddzb(m):
        get_start(GET_DDZB, m, narrow_change(N22, 2, B22, m))

    each_micro(do_ddzb)
    fold(C1)

    def fan_out(m, event, weight):
        r.fan[pl.ds(PAD, rows), :] = dot_back(r.get[event, m], weight[...])

    def do_da2(m):
        get_finish(GET_DDZB, m)
        fan_out(m, GET_DDZB, r.b1)
        total = None
        for k, (down, right) in enumerate(second_taps()):
            term = slid(r.fan, pl.ds(k * part, part), -down, -right)
            total = term if total is None else total + term
        narrow_upstream(N21, 1, B21, m, total)

    each_micro(do_da2)

    @pl.when(section != 0)
    def _():
        wait_bytes(a0_others, r.all_recv.at[0])
        for k in range(1, ranks):
            block = r.a0_all.at[half_rows, lanes_of(other(k))]
            remote(block, block, r.all_send.at[1], r.all_recv.at[1], sibling).start()

    relay(C1)
    make(B1, lambda at: r.patches[1, :, :, at], r.get[GET_DDZB], 128)

    def do_ddza(m):
        get_start(GET_DDZA, m, narrow_change(N21, 1, B21, m))

    each_micro(do_ddza)
    fold(B1)

    def do_dy1(m):
        value = dot_back(get_finish(GET_DDZA, m), r.a1[...]) + r.skip[m].astype(F32)
        value = value.astype(BF16).astype(F32)
        before, main, short = before1(m)
        upstream = value * silu_slope(before)
        r.uw[m] = upstream
        sums = upstream_sums(upstream, [main, short])
        if lay.fast:
            joint_start(B11, m, sums)
        else:
            norm_start(double, B11, m, sums)

    each_micro(do_dy1)
    each_joint(joint_line, B11)
    each_micro(send_output)
    make(A1, lambda at: y1[:, :, at], r.get[GET_DDZA], 256)
    relay(B1)
    each_joint(joint_back, B11)

    def do_ddzc(m):
        totals = joint_finish(B11, m) if lay.fast else norm_finish(double, B11, m)
        plain = rows_of(totals, 0)
        for norm, at, target in ((N11, 2, r.ddzd), (N12, 4, r.ddzs)):
            sums = [plain, rows_of(totals, at)]
            add_gains(C_MID + norm * wide, sums)
            found = moments_of(r.stat_w, norm, m)
            normed = normalized(zw[norm, m], found)
            target[m] = norm_change(r.uw[m], normed, found, affine_w(norm)[0], sums, 1)
        sum_start(SUM_DH0, m, dot_back(r.ddzd[m], r.c0[...]))

    each_micro(do_ddzc)
    fold(A1)

    def do_dxs(m):
        r.dxs_send[m] = dot_back(r.ddzs[m], r.p0[...]).astype(BF16)

    each_micro(do_dxs)
    make(C0, lambda at: r.get[GET_H0, :, :, at], r.ddzd[...], 256)
    make(P0, lambda at: r.x[0, :, :, at], r.ddzs[...], 256)

    def do_dh0(m):
        value = sum_finish(SUM_DH0, m).astype(BF16).astype(F32)
        narrow_upstream(N02, 0, B02, m, value)

    def send_dxs(m):
        own_start(1, m, r.dxs_send.at[m], r.dxs_recv.at[section])

    each_micro(do_dh0)
    fold(C0)
    fold(P0)
    relay(A1)

    def do_ddz2(m):
        get_start(GET_DDZ2, m, narrow_change(N02, 0, B02, m))

    each_micro(do_ddz2)
    relay(C0)
    send_dxs(0)

    def do_da1(m):
        get_wait(GET_DDZ2, m)
        fan_out(m, GET_DDZ2, r.b0)

        @pl.when(m > 0)
        def _():
            send_dxs(m)

        gain, shift = affine_n(N01)
        found = moments_of(r.stat_n, N01, m)
        sums = None
        for phase in range(4):
            total = None
            for k, (at, down, right) in enumerate(first_taps()):
                if at == phase:
                    term = slid(r.fan, pl.ds(k * part, part), -down, -right)
                    total = term if total is None else total + term
            normed = normalized(z1[phase, m], found)
            upstream = total * silu_slope(normed * gain + shift)
            r.u1[phase, m] = upstream
            terms = upstream_sums(upstream, [normed])
            sums = terms if sums is None else [a + b for a, b in zip(sums, terms)]
        norm_start(narrow, B01, m, sums)

    each_micro(do_da1)
    relay(P0)
    make(B0, lambda at: r.patches[0, :, :, at], r.get[GET_DDZ2], 128)

    out_own = r.out_own
    wait_bytes(out_own.at[:, mine_wide], r.own_copy.at[0])
    wait_bytes(out_own.at[:, pl.ds(0, C_OUT - wide)], r.own_recv.at[0])
    def store_grid(refs, values, pick):
        for group, ref in enumerate(refs):
            start, used = lay.spans[group][0], lay.used[group]
            side, crops = lay.sides[group], lay.crops[group]
            grid = values[start : start + used].astype(BF16).reshape(side, side, crops, values.shape[1])
            pick(ref, grid)

    def store_output(ref, grid):
        ref[...] = grid

    store_grid((r.out_grid, r.out_grid_2), out_own[...].astype(F32), store_output)
    results = [
        pltpu.make_async_copy(src, dst, r.result_sem.at[i])
        for i, (src, dst) in enumerate(
            (
                (r.out_grid, r.out),
                (r.out_grid_2, r.out_2),
                (r.grad_grid, r.grad),
                (r.grad_grid_2, r.grad_2),
            )
        )
    ]
    results[0].start()
    results[1].start()

    def do_ddz1(m):
        totals = norm_finish(narrow, B01, m)
        sums = [rows_of(totals, 0), rows_of(totals, 2)]
        add_gains(0, sums)
        found = moments_of(r.stat_n, N01, m)
        gain = affine_n(N01)[0]
        for phase in range(4):
            normed = normalized(z1[phase, m], found)
            r.ddz1[phase, m] = norm_change(r.u1[phase, m], normed, found, gain, sums, 4)
        own_start(2, m, r.ddz1.at[:, m], r.ddz1_own.at[:, :, mine])

    each_micro(do_ddz1)
    fold(B0)
    finish(C1)
    finish(B1)
    finish(A1)
    for k in range(1, ranks):
        remote(
            r.gains.at[section],
            r.gains.at[section],
            r.gain_send,
            r.gain_recv,
            (other(k), dp),
        ).start()

    def da0_step(i, carry):
        at = pl.ds(pl.multiple_of(i * 128, 128), 128)
        total = None
        for phase in range(4):
            value = dot_rows(
                r.x[phase, :, :, at].reshape(micro * rows, 128),
                r.ddz1[phase].reshape(micro * rows, part),
            )
            total = value if total is None else total + value
        da0 = r.da if lay.fast else r.da0
        da0[pl.ds(pl.multiple_of(i * 128, 128), 128), :] = total.astype(BF16)
        return carry

    lax.fori_loop(0, C_IN // 128, da0_step, 0)
    to_sibling(A0)
    finish(C0)
    relay(B0)
    fold(A0)
    finish(P0)
    relay(A0)
    finish(B0)
    finish(A0)

    dxs, ddz1_own = r.dxs_recv, r.ddz1_own

    @pl.when(section != 0)
    def _():
        wait_bytes(a0_others, r.all_recv.at[1])

    wait_bytes(dxs.at[0], r.own_copy.at[1])
    wait_bytes(dxs.at[pl.ds(0, ranks - 1)], r.own_recv.at[1])
    wait_bytes(ddz1_own.at[:, :, mine], r.own_copy.at[2])
    wait_bytes(ddz1_own.at[:, :, pl.ds(0, C_MID - part)], r.own_recv.at[2])
    for phase in range(4):
        value = dot_back(ddz1_own[phase], r.a0_all[...])
        if phase == 0:
            extra = dxs[0].astype(F32)
            for k in range(1, ranks):
                extra = extra + dxs[k].astype(F32)
            value = value + extra.astype(BF16).astype(F32)

        def store_phase(ref, grid):
            ref[:, phase // 2, :, phase % 2] = grid

        store_grid((r.grad_grid, r.grad_grid_2), value, store_phase)
    wait_bytes(r.gains.at[pl.ds(0, ranks - 1)], r.gain_recv)
    if lay.fast:
        store_norm_shares()
    else:
        r.gains_out[...] = r.gains[...]

    results[2].start()
    results[3].start()
    if lay.fast:
        finish_shares()
        results.append(pltpu.make_async_copy(r.share, r.share_out, r.result_sem.at[4]))
        results[4].start()
        gradients_sent()

    def sent(m):
        for event in range(5):
            wait_bytes(r.sum_recv.at[event, m], r.sum_send_sem.at[event, m])
            wait_bytes(
                r.get.at[event, m, :, pl.ds(0, C_MID - part)], r.get_send_sem.at[event, m]
            )
        for kind, events in ((narrow, 8), (broad, 2)) if lay.fast else ((narrow, 8), (broad, 4), (double, 1)):
            for event in range(events - kind[0].shape[0], events):
                norm_sent(kind, event, m)
        if lay.fast:
            for event in (B11, J12, J11):
                wait_bytes(r.joint_pair.at[event, m], r.joint_send.at[event, 0, m])
                wait_bytes(
                    r.joint_line.at[event, m, pl.ds(0, dp_count // 2 - 1)],
                    r.joint_send.at[event, 1, m],
                )
                wait_bytes(r.joint_pair.at[event, m], r.joint_send.at[event, 2, m])

    each_micro(sent)
    for copy in results:
        copy.wait()
    wait_bytes(out_own.at[:, pl.ds(0, C_OUT - wide)], r.own_send.at[0])
    wait_bytes(dxs.at[pl.ds(0, ranks - 1)], r.own_send.at[1])
    wait_bytes(ddz1_own.at[:, :, pl.ds(0, C_MID - part)], r.own_send.at[2])

    @pl.when(section == 0)
    def _():
        wait_bytes(a0_others, r.all_send.at[0])

    @pl.when(section != 0)
    def _():
        wait_bytes(a0_others.at[:, pl.ds(0, (ranks - 2) * part)], r.all_send.at[0])
        wait_bytes(a0_others, r.all_send.at[1])

    wait_bytes(r.gains.at[pl.ds(0, ranks - 1)], r.gain_send)
    for i in range(2):
        wait_bytes(scales.at[i, pl.ds(0, ranks - 1)], r.scale_send.at[i])


def chain(lay, ranks, dp_count, operands):
    micro, rows = lay.micro, lay.rows
    part, wide = C_MID // ranks, C_OUT // ranks
    table = scratch_table(lay, ranks, dp_count)
    shapes = (
        *[jax.ShapeDtypeStruct(grid_shape(lay, group, 1, C_OUT), BF16) for group in range(2)],
        *[jax.ShapeDtypeStruct(phase_shape(lay, group), BF16) for group in range(2)],
    )
    if lay.fast:
        shapes += (jax.ShapeDtypeStruct((1, GSEGMENT // dp_count), F32),) * 2
        shapes += (jax.ShapeDtypeStruct((ROWS // dp_count, C_MID), BF16),)
    else:
        shapes += (
            jax.ShapeDtypeStruct((ranks, 2, C_MID + 3 * wide), F32),
            jax.ShapeDtypeStruct((ROWS, C_MID), BF16),
            jax.ShapeDtypeStruct((C_IN, part), BF16),
        )
    anywhere = pl.BlockSpec(memory_space=pl.ANY)
    inside = pl.BlockSpec(memory_space=pltpu.VMEM)
    return pl.pallas_call(
        functools.partial(chain_kernel, lay, ranks, dp_count, tuple(table)),
        out_shape=shapes,
        in_specs=[anywhere] * 5 + [inside] * 3,
        out_specs=[anywhere] * 4 + ([inside] * 2 + [anywhere] if lay.fast else [inside, anywhere, inside]),
        scratch_shapes=list(table.values()),
        compiler_params=pltpu.CompilerParams(
            collective_id=0, has_side_effects=True, vmem_limit_bytes=63 * 2**20
        ),
        name="chain",
    )(*operands)


def summed_gradient(slices, small, section, ranks):
    small = jnp.stack([small] + [jnp.zeros_like(small)] * (ranks - 1))
    slices = slices.reshape(ranks, ROWS // ranks, C_MID)
    arrived = lax.all_to_all(slices, "section", 0, 0, tiled=True).astype(F32)
    arrived_small = lax.all_to_all(small, "section", 0, 0, tiled=True).astype(F32)
    segment = segment_gradient(arrived, arrived_small, section, ranks)
    return lax.psum_scatter(segment.reshape(-1), "dp", scatter_dimension=0, tiled=True)


def norm_shares(gains, ranks, dp_count):
    part, wide = C_MID // ranks, C_OUT // ranks

    def joined(start, width):
        block = gains[:, :, start : start + width // ranks]
        return jnp.moveaxis(block, 0, 1).reshape(2, width)

    f01, f02, f21, f22 = [joined(part * i, C_MID) for i in range(4)]
    f11, f12, f31 = [joined(C_MID + wide * i, C_OUT) for i in range(3)]
    blank = jnp.zeros((2, GSEGMENT - 2 * C_MID), F32)
    segments = jnp.stack(
        [
            jnp.concatenate([f01, f02, blank], 1),
            jnp.concatenate([f11, f12], 1),
            jnp.concatenate([f21, f22, blank], 1),
            jnp.concatenate([f31, jnp.zeros((2, GSEGMENT - C_OUT), F32)], 1),
        ]
    )
    share = GSEGMENT // dp_count
    own_norms = lax.dynamic_index_in_dim(segments, lax.axis_index("section"), 0, keepdims=False)
    return lax.dynamic_slice_in_dim(own_norms, lax.axis_index("dp") * share, share, 1)


def deliver_kernel(ranks, *refs):
    plain, share_in, norms_in, refs = refs[:4], refs[4], refs[5:7], refs[7:]
    plain_out, share_out, norms_out, refs = refs[:4], refs[4], refs[5:7], refs[7:]
    held, share, order, load_sem, store_sem = refs[:4], refs[4], refs[5], refs[6], refs[7]
    loads = [
        pltpu.make_async_copy(src, dst, load_sem.at[i])
        for i, (src, dst) in enumerate(zip(plain + (share_in,), held + (share,)))
    ]
    stores = [
        pltpu.make_async_copy(src, dst, store_sem.at[i])
        for i, (src, dst) in enumerate(zip(held + (order,), plain_out + (share_out,)))
    ]
    turn = (4, 2, 0, 3, 1)
    for i in turn:
        loads[i].start()
    for src, dst in zip(norms_in, norms_out):
        dst[...] = src[...]
    whole, lanes = share.shape[0], 128
    for i in turn:
        loads[i].wait()
        if i == 4:
            odd = lax.rem(lax.axis_index("section"), 2)

            @pl.when(odd == 0)
            def _():
                for q in range(ranks):
                    order[pl.ds(q, whole, stride=ranks), :] = share[:, lanes * q : lanes * (q + 1)].astype(F32)

            @pl.when(odd == 1)
            def _():
                short = whole // ranks
                for t in range(ranks):
                    for q in range(ranks):
                        order[pl.ds(ranks * t + q, short, stride=ranks * ranks), :] = share[
                            t * short : (t + 1) * short, lanes * q : lanes * (q + 1)
                        ].astype(F32)

        stores[i].start()
    for i in turn:
        stores[i].wait()


def deliver(results, ranks):
    plain, norms, share = results[:4], results[4:6], results[6]
    order = jax.ShapeDtypeStruct((share.size // 128, 128), F32)
    anywhere = pl.BlockSpec(memory_space=pl.ANY)
    inside = pl.BlockSpec(memory_space=pltpu.VMEM)
    specs = [anywhere] * 5 + [inside] * 2
    like = [jax.ShapeDtypeStruct(v.shape, v.dtype) for v in plain]
    return pl.pallas_call(
        functools.partial(deliver_kernel, ranks),
        out_shape=like + [order] + [jax.ShapeDtypeStruct(v.shape, v.dtype) for v in norms],
        in_specs=specs,
        out_specs=specs,
        scratch_shapes=[pltpu.VMEM(v.shape, v.dtype) for v in list(plain) + [share, order]]
        + [pltpu.SemaphoreType.DMA((5,))] * 2,
        name="deliver",
    )(*plain, share, *norms)


def per_device(
    images_global, images_local, weights, norm_gains, norm_shifts, cotangent_global, cotangent_local
):
    section = lax.axis_index("section")
    ranks = lax.axis_size("section")
    dp_count = lax.axis_size("dp")
    lay = Layout(images_global.shape, images_local.shape, dp_count)
    micro, rows = lay.micro, lay.rows
    part = C_MID // ranks
    wide = C_OUT // ranks

    def cells_first(pictures):
        return jnp.moveaxis(pictures, 1, 3)

    masks = np.stack(
        [lay.valid(down, right) for down in (-1, 0, 1) for right in (-1, 0, 1)]
    ).astype(np.float32)
    masks = jnp.asarray(np.ascontiguousarray(np.broadcast_to(masks[:, :, None], (9, rows, part))))
    results = chain(
        lay,
        ranks,
        dp_count,
        (
            cells_first(images_global),
            cells_first(images_local),
            cells_first(cotangent_global),
            cells_first(cotangent_local),
            weights.reshape(-1, 128),
            norm_gains[None],
            norm_shifts[None],
            masks,
        ),
    )

    if lay.fast:
        results = deliver(results, ranks)
    out_global, out_local, grad_global, grad_local, *rest = results
    if lay.fast:
        share, gain_share, shift_share = rest
        own_norms, weight_gradient = (gain_share[0], shift_share[0]), share.reshape(-1)
    else:
        own_norms = norm_shares(rest[0], ranks, dp_count)
        weight_gradient = summed_gradient(*rest[1:], section, ranks)

    def crops_first(grid, side, crops):
        return jnp.moveaxis(grid.reshape(1, side, side, crops, -1), 3, 1)

    return (
        crops_first(out_global, lay.sides[0], lay.crops[0]),
        crops_first(out_local, lay.sides[1], lay.crops[1]),
        crops_first(grad_global, 2 * lay.sides[0], lay.crops[0]),
        crops_first(grad_local, 2 * lay.sides[1], lay.crops[1]),
        weight_gradient,
        own_norms[0],
        own_norms[1],
    )


def solution(mesh):
    images = P(None, "dp", None, None, None)
    made = P("section", "dp", None, None, None)
    return jax.shard_map(
        per_device,
        mesh=mesh,
        in_specs=(images, images, P("section"), P("section"), P("section"), images, images),
        out_specs=(made, made, made, made) + (P(("section", "dp")),) * 3,
        check_vma=False,
    )
```

```python
import functools
from types import SimpleNamespace

import jax
import jax.numpy as jnp
import numpy as np
from jax import lax
from jax.experimental import pallas as pl
from jax.experimental.pallas import tpu as pltpu
from jax.sharding import PartitionSpec as P

C_IN = 1024
C_MID = 512
C_OUT = 2048
WSEGMENT = 3407872
GSEGMENT = 4096
EPSILON = 1e-05
F32 = jnp.float32
BF16 = jnp.bfloat16


def round_up(value, unit):
    return -(-value // unit) * unit


class Layout:
    def __init__(self, shape_global, shape_local, dp_count):
        self.micro = shape_global[0]
        self.crops = (shape_global[1], shape_local[1])
        self.sides = (shape_global[2] // 2, shape_local[2] // 2)
        used = [crops * side * side for crops, side in zip(self.crops, self.sides)]
        self.used = used
        first = round_up(used[0], 8)
        self.rows = round_up(first + round_up(used[1], 8), 16)
        self.spans = ((0, first), (first, self.rows))
        self.totals = [count * dp_count for count in used]
        self.fast = dp_count == 8 and WSEGMENT // C_MID // dp_count % 64 == 0

    def valid(self, down, right):
        flags = np.zeros((self.rows,), bool)
        for (start, _), crops, side in zip(self.spans, self.crops, self.sides):
            for crop in range(crops):
                for i in range(side):
                    for j in range(side):
                        inside = 0 <= i + down < side and 0 <= j + right < side
                        flags[start + (i * side + j) * crops + crop] = inside
        return flags


def first_taps():
    return [
        (2 * (p != 1) + (q != 1), -(p == 0), -(q == 0)) for p in range(3) for q in range(3)
    ]


def second_taps():
    return [(p - 1, q - 1) for p in range(3) for q in range(3)]


def segment_gradient(pieces, small, section, ranks):
    part = C_MID // ranks
    total_rows = WSEGMENT // C_MID

    def finished(rows):
        return jnp.pad(rows, ((0, total_rows - rows.shape[0]), (0, 0)))

    def across(block):
        return block.transpose(1, 0, 2).reshape(-1, C_MID)

    def spatial(block):
        return block.reshape(ranks, 9, part, C_MID).transpose(1, 0, 2, 3).reshape(-1, C_MID)

    def first():
        return finished(
            jnp.concatenate(
                [small.transpose(1, 0, 2).reshape(-1, C_MID), spatial(pieces[:, : 9 * part])]
            )
        )

    def second():
        return finished(across(pieces[:, : C_MID + C_IN]))

    def third():
        tall = C_OUT // ranks
        return finished(
            jnp.concatenate(
                [pieces[:, :tall].reshape(-1, C_MID), spatial(pieces[:, tall : tall + 9 * part])]
            )
        )

    def fourth():
        return finished(across(pieces[:, :C_MID]))

    return lax.switch(section, [first, second, third, fourth])


MESH = pl.DeviceIdType.MESH
ROWS = WSEGMENT // C_MID
SUM_Z2, SUM_ZA, SUM_ZB, SUM_DH2, SUM_DH0 = range(5)
GET_H0, GET_H2, GET_DDZB, GET_DDZA, GET_DDZ2 = range(5)
F01, F02, F21, F22, B22, B21, B02, B01 = range(8)
F31, B31 = range(2)
F12, F11, F31_LATE, B31_LATE = range(4)
B11, J12, J11 = range(3)
N01, N02, N21, N22 = range(4)
N11, N12, N31 = range(3)
A0, B0, C0, P0, A1, B1, C1 = range(7)
SOURCE = (0, 0, 1, 1, 2, 2, 3)
PAD = 16
SLOTS = 3
HELD = (4, 5, 6)
READY = 640
HEIGHTS = (0, 9 * C_MID // 4, C_MID, C_IN, C_OUT // 4, 9 * C_MID // 4, C_MID)


def dot(left, right):
    return lax.dot_general(left, right, (((1,), (0,)), ((), ())), preferred_element_type=F32)


def dot_back(left, right):
    return lax.dot_general(left, right, (((1,), (1,)), ((), ())), preferred_element_type=F32)


def dot_rows(left, right):
    return lax.dot_general(left, right, (((0,), (0,)), ((), ())), preferred_element_type=F32)


def silu(value):
    return value * jax.nn.sigmoid(value)


def silu_slope(before):
    sigmoid = jax.nn.sigmoid(before)
    return sigmoid * (1.0 + before * (1.0 - sigmoid))


def grid_shape(lay, group, fold, channels):
    side = fold * lay.sides[group]
    return (side, side, lay.crops[group], channels)


def phase_shape(lay, group):
    side = lay.sides[group]
    return (side, 2, side, 2, lay.crops[group], C_IN)


def scratch_table(lay, ranks, dp_count):
    micro, rows = lay.micro, lay.rows
    part, wide = C_MID // ranks, C_OUT // ranks
    others = ranks - 1
    vmem, dma = pltpu.VMEM, pltpu.SemaphoreType.DMA
    return dict(
        x=vmem((4, micro, rows, C_IN), BF16),
        cot=vmem((micro, rows, wide), BF16),
        x_grid=vmem((2,) + grid_shape(lay, 0, 2, C_IN), BF16),
        x_grid_2=vmem((2,) + grid_shape(lay, 1, 2, C_IN), BF16),
        cot_grid=vmem((micro,) + grid_shape(lay, 0, 1, wide), BF16),
        cot_grid_2=vmem((micro,) + grid_shape(lay, 1, 1, wide), BF16),
        a0=vmem((C_IN, part), BF16),
        b0=vmem((9 * part, C_MID), BF16),
        c0=vmem((C_MID, wide), BF16),
        p0=vmem((C_IN, wide), BF16),
        a1=vmem((wide, C_MID), BF16),
        b1=vmem((9 * part, C_MID), BF16),
        c1=vmem((C_MID, wide), BF16),
        a0_all=vmem((C_IN, C_MID), BF16),
        raw=vmem((SLOTS, 2048, 128), BF16),
        raw_sem=dma((SLOTS,)),
        scales=vmem((2, ranks, 1, GSEGMENT), F32),
        z1=vmem((4, micro, rows, part), F32),
        u1=vmem((4, micro, rows, part), F32),
        zn=vmem((3, micro, rows, part), F32),
        un=vmem((3, micro, rows, part), F32),
        zw=vmem((3, micro, rows, wide), F32),
        uw=vmem((micro, rows, wide), F32),
        y1=vmem((micro, rows, wide), BF16),
        skip=vmem((micro, rows, wide), BF16),
        ddzd=vmem((micro, rows, wide), BF16),
        ddzs=vmem((micro, rows, wide), BF16),
        patches=vmem((2, micro, rows, 9 * part), BF16),
        slide=vmem((PAD + rows + PAD, part), F32),
        fan=vmem((PAD + rows + PAD, 9 * part), F32),
        stat_n=vmem((4, micro, 8, part), F32),
        stat_w=vmem((3, micro, 8, wide), F32),
        sum_send=vmem((5, micro, rows, C_MID), BF16),
        sum_recv=vmem((5, micro, others, rows, part), BF16),
        get=vmem((5, micro, rows, C_MID), BF16),
        norm_n=vmem((4, micro, dp_count, 4, part), F32),
        norm_w=vmem((2 if lay.fast else 3, micro, dp_count, 4, wide), F32),
        **joint_scratch(lay, dp_count, wide),
        out_send=vmem((micro, rows, wide), BF16),
        out_own=vmem((rows, C_OUT), BF16),
        out_grid=vmem(grid_shape(lay, 0, 1, C_OUT), BF16),
        out_grid_2=vmem(grid_shape(lay, 1, 1, C_OUT), BF16),
        grad_grid=vmem(phase_shape(lay, 0), BF16),
        grad_grid_2=vmem(phase_shape(lay, 1), BF16),
        result_sem=dma((5,)),
        dxs_send=vmem((micro, rows, C_IN), BF16),
        dxs_recv=vmem((ranks, rows, C_IN), BF16),
        ddz1=vmem((4, micro, rows, part), BF16),
        ddz1_own=vmem((4, rows, C_MID), BF16),
        gains=vmem((ranks, 2, C_MID + 3 * wide), F32),
        x_sem=dma((2, 2)),
        cot_sem=dma((2,)),
        piece_send=dma((7,)),
        piece_recv=dma((7,)),
        pass_send=dma((7,)),
        pass_recv=dma((7, 3)),
        eight_send=dma,
        eight_recv=dma((4, 3)),
        scale_send=dma((2,)),
        scale_recv=dma((2,)),
        all_send=dma((2,)),
        all_recv=dma((2,)),
        sum_send_sem=dma,
        sum_recv_sem=dma((5, micro)),
        get_send_sem=dma,
        get_recv_sem=dma((5, micro)),
        norm_n_send=dma((2,)),
        norm_n_recv=dma((4, micro)),
        norm_w_send=dma((2,)),
        norm_w_recv=dma((2 if lay.fast else 3, micro)),
        own_send=dma((3,)),
        own_recv=dma((3,)),
        own_copy=dma((3,)),
        gain_send=dma,
        gain_recv=dma,
        **gradient_scratch(lay, ranks, dp_count),
    )


def joint_scratch(lay, dp_count, wide):
    vmem, dma, micro = pltpu.VMEM, pltpu.SemaphoreType.DMA, lay.micro
    if not lay.fast:
        return dict(
            norm_v=vmem((1, micro, dp_count, 8, wide), F32),
            norm_v_send=dma((1,)),
            norm_v_recv=dma((1, micro)),
        )
    return dict(
        joint=vmem((3, micro, 8, wide), F32),
        joint_all=vmem((3, micro, 8, wide), F32),
        joint_pair=vmem((3, micro, 8, wide // 2), F32),
        joint_line=vmem((3, micro, dp_count // 2, 8, wide // 2), F32),
        joint_send=dma((3,)),
        joint_recv=dma((2, 3, micro)),
    )


def gradient_scratch(lay, ranks, dp_count):
    vmem, dma = pltpu.VMEM, pltpu.SemaphoreType.DMA
    if not lay.fast:
        return dict(
            stage=vmem((256, C_MID), BF16),
            stage_sem=dma,
            ready=vmem((ranks * READY, C_MID), BF16),
        )
    part = C_MID // ranks
    height, chips = sum(HEIGHTS), dp_count // 2
    return dict(
        dw=vmem((height, C_MID), BF16),
        dw_pair=vmem((height // 2, C_MID), BF16),
        dw_near=vmem((chips - 1, height // dp_count, C_MID), BF16),
        dw_sum=vmem((height // dp_count, C_MID), BF16),
        da=vmem((C_IN, part), BF16),
        da_pair=vmem((C_IN // 2, part), BF16),
        da_near=vmem((chips - 1, C_IN // dp_count, part), BF16),
        dw_relay=vmem((height // dp_count, C_MID), BF16),
        da_relay=vmem((C_IN // dp_count, part), BF16),
        relay_send=dma,
        relay_recv=dma((7,)),
        da_sum=vmem((C_IN // dp_count, part), BF16),
        share=vmem((ROWS // dp_count, C_MID), BF16),
        pair_send=dma((2,)),
        pair_recv=dma((7,)),
        near_send=dma((2,)),
        near_recv=dma((7,)),
        share_send=dma((2,)),
        share_recv=dma,
        hold=vmem((ROWS // dp_count, C_MID), BF16),
        hold_2=vmem((ROWS // dp_count // ranks, C_MID), BF16),
        hold_recv=dma((3,)),
        ship_send=dma((3,)),
    )


def chain_kernel(lay, ranks, dp_count, names, *refs):
    inputs = ("x_in", "x_in_2", "cot_in", "cot_in_2", "w_in", "gains_in", "shifts_in", "masks")
    outputs = ("out", "out_2", "grad", "grad_2")
    outputs += ("gain_share", "shift_share", "share_out") if lay.fast else ("gains_out", "dw", "da0")
    r = SimpleNamespace(**dict(zip(inputs + outputs + names, refs)))
    pieces = (r.a0, r.b0, r.c0, r.p0, r.a1, r.b1, r.c1)
    micro, rows = lay.micro, lay.rows
    first = lay.spans[0][1]
    part, wide = C_MID // ranks, C_OUT // ranks
    section, dp = lax.axis_index("section"), lax.axis_index("dp")
    core = lax.rem(dp, 2)
    sibling = (section, dp + 1 - 2 * core)
    masks = r.masks
    mine = pl.ds(pl.multiple_of(section * part, part), part)
    mine_wide = pl.ds(pl.multiple_of(section * wide, wide), wide)

    def other(k):
        return lax.rem(section + k, ranks)

    def across_dp(act):
        if dp_count <= 8:
            for k in range(1, dp_count):
                act((section, lax.rem(dp + k, dp_count)))
        else:

            def step(k, carry):
                act((section, lax.rem(dp + k, dp_count)))
                return carry

            lax.fori_loop(1, dp_count, step, 0)

    def remote(src, dst, send, recv, device):
        return pltpu.make_async_remote_copy(
            src_ref=src,
            dst_ref=dst,
            send_sem=send,
            recv_sem=recv,
            device_id=device,
            device_id_type=MESH,
        )

    def wait_bytes(ref, sem):
        pltpu.make_async_copy(ref, ref, sem).wait()

    def some_micros(body, first_micro, last_micro):
        def step(m, carry):
            body(m)
            return carry

        lax.fori_loop(first_micro, last_micro, step, 0)

    def each_micro(body):
        some_micros(body, 0, micro)

    waiting = []

    def flush():
        while waiting:
            waiting.pop()(micro - 1)

    def stage(body):
        if not waiting:
            some_micros(body, 0, micro - 1)
        else:
            before = waiting.pop()

            def step(i, carry):
                @pl.when(i == 1)
                def _():
                    before(micro - 1)

                @pl.when(i != 1)
                def _():
                    body(jnp.maximum(i - 1, 0))

                return carry

            lax.fori_loop(0, micro, step, 0)
        waiting.append(body)

    barrier = pltpu.get_barrier_semaphore()

    def greet(device):
        pl.semaphore_signal(barrier, inc=1, device_id=device, device_id_type=MESH)

    if lay.fast:
        r.share[...] = jnp.zeros(r.share.shape, BF16)
        for k in range(ranks):
            for j in range(dp_count):
                if k or j:
                    greet((other(k), lax.rem(dp + j, dp_count)))
        greetings = ranks * dp_count - 1
    else:
        across_dp(greet)
        for k in range(1, ranks):
            greet((other(k), dp))
        greetings = dp_count - 1 + ranks - 1

    def load_grids(m):
        slot = m % 2
        return (
            pltpu.make_async_copy(r.x_in.at[m], r.x_grid.at[slot], r.x_sem.at[0, slot]),
            pltpu.make_async_copy(r.x_in_2.at[m], r.x_grid_2.at[slot], r.x_sem.at[1, slot]),
        )

    for m in range(2):
        for copy in load_grids(m):
            copy.start()
    r.slide[...] = jnp.zeros(r.slide.shape, F32)
    r.fan[...] = jnp.zeros(r.fan.shape, F32)

    place = lax.rem(dp, 4)
    group = dp - place
    pair_place = lax.rem(place + 2, 4)
    pair = (section, group + pair_place)

    place_8 = lax.rem(dp, 8)
    group_8 = dp - place_8
    chip_8 = place_8 // 2
    EIGHTH, STEP = 9 * part // 8, 3 * part // 8

    def eighth(which, step):
        return r.b0.at[pl.ds(pl.multiple_of(EIGHTH * which + STEP * step, 16), STEP)]

    def eight_copy(way, step, src, dst, device):
        remote(src, dst, r.eight_send, r.eight_recv.at[way, step], device).start()

    def send_b0():
        for step in range(3):
            for k in range(1, ranks):
                row = READY * other(k) + 16 * place_8 + STEP * step
                src = ready.at[pl.ds(pl.multiple_of(row, 16), STEP)]
                eight_copy(0, step, src, eighth(place_8, step), (other(k), dp))

    def pass_on_b0(step):
        @pl.when(section != 0)
        def _():
            own = eighth(place_8, step)
            wait_bytes(own, r.eight_recv.at[0, step])
            for k in range(1, 4):
                target = lax.rem(chip_8 + k, 4)
                eight_copy(1, step, own, own, (section, group_8 + 2 * target + core))
            eight_copy(2, step, own, own, sibling)

    def pass_back_b0(step):
        @pl.when(section != 0)
        def _():
            wait_bytes(r.b0.at[pl.ds(0, 3 * STEP)], r.eight_recv.at[1, step])
            for k in range(1, 4):
                theirs = eighth(2 * lax.rem(chip_8 + k, 4) + core, step)
                eight_copy(3, step, theirs, theirs, sibling)

    def need_b0():
        @pl.when(section != 0)
        def _():
            for step in range(3):
                wait_bytes(r.b0.at[pl.ds(0, STEP)], r.eight_recv.at[2, step])
                wait_bytes(r.b0.at[pl.ds(0, 3 * STEP)], r.eight_recv.at[3, step])

    def b0_sent():
        @pl.when(section == 0)
        def _():
            wait_bytes(r.b0.at[pl.ds(0, 9 * STEP)], r.eight_send)

        @pl.when(section != 0)
        def _():
            wait_bytes(r.b0.at[pl.ds(0, 21 * STEP)], r.eight_send)

    ready = r.dw if lay.fast else r.ready

    def parts(number):
        return 2 if number in (A1, C1) else 4

    def place_in(number):
        return core if parts(number) == 2 else place

    def run_jobs(jobs):
        def load(number):
            start, count, _ = jobs[number]
            start = start if isinstance(start, int) else pl.multiple_of(start, 512)
            slot = number % SLOTS
            return pltpu.make_async_copy(
                r.w_in.at[pl.ds(start, count)], r.raw.at[slot, pl.ds(0, count)], r.raw_sem.at[slot]
            )

        for number in range(min(SLOTS, len(jobs))):
            load(number).start()
        for number, (_, count, use) in enumerate(jobs):
            load(number).wait()
            use(r.raw[number % SLOTS, pl.ds(0, count), :])
            if number + SLOTS < len(jobs):
                load(number + SLOTS).start()

    def by_rows(value):
        return value.reshape(value.shape[0] // 4, C_MID)

    def by_columns(value):
        return value.reshape(value.shape[0] // 16, C_OUT)

    def first_jobs(source):
        jobs = []

        def keep_a0(i):
            def use(value):
                r.a0_all[pl.ds(C_MID * i, C_MID), :] = by_rows(value)

            return (2048 * i, 2048, use)

        def keep_taps(base, row):
            def use(value):
                matrix = by_rows(value)
                for t in range(ranks):
                    if t != source:
                        ready[pl.ds(READY * t + row, part), :] = matrix[part * t : part * (t + 1)]

            return (2048 * base, 2048, use)

        def keep_wide(chunk, row):
            def use(value):
                matrix = by_columns(value)
                for t in range(ranks):
                    if t != source:
                        ready[pl.ds(READY * t + row, 128), :] = matrix[:, wide * t : wide * (t + 1)]

            return (2048 * chunk, 2048, use)

        def keep_tall(t):
            def use(value):
                ready[pl.ds(READY * t, 256), :] = by_rows(value)

            return (2048 * t + 1024 * core, 1024, use)

        if source == 0:
            jobs = [keep_a0(0), keep_a0(1)] + [keep_taps(2 + place_8 + j, part * j) for j in range(2)]
        elif source == 1:
            jobs = [keep_wide(place, 0)] + [keep_wide(4 + 2 * place + j, 128 + 128 * j) for j in range(2)]
        elif source == 2:
            jobs = [keep_tall(t) for t in range(ranks) if t != source]
            jobs += [keep_taps(4 + 2 * place + j, 256 + part * j) for j in range(3)]
        else:
            jobs = [keep_wide(2 * core + j, 128 * j) for j in range(2)]
        return jobs

    def own_jobs(source):
        def put(ref, row, count):
            def use(value):
                ref[pl.ds(row, count), :] = by_rows(value)

            return use

        def put_wide(ref, row):
            def use(value):
                ref[pl.ds(row, 128), :] = by_columns(value)[:, wide * source : wide * (source + 1)]

            return use

        if source == 0:
            return [(2048 * (2 + tap), 512, put(r.b0, part * tap, part)) for tap in range(9)]
        if source == 1:
            jobs = [(2048 * i, 2048, put_wide(r.c0, 128 * i)) for i in range(4)]
            return jobs + [(2048 * (4 + i), 2048, put_wide(r.p0, 128 * i)) for i in range(8)]
        if source == 2:
            jobs = [(2048 * source, 2048, put(r.a1, 0, wide))]
            start = 512 * source
            return jobs + [
                (2048 * (4 + tap) + start, 512, put(r.b1, part * tap, part)) for tap in range(9)
            ]
        return [(2048 * i, 2048, put_wide(r.c1, 128 * i)) for i in range(4)]

    def send_piece(number):
        count = pieces[number].shape[0] // parts(number)
        at = pl.ds(pl.multiple_of(place_in(number) * count, 32), count)
        for k in range(1, ranks):
            t = other(k)
            if number == A0:
                src = r.a0_all.at[at, pl.ds(pl.multiple_of(t * part, part), part)]
            else:
                row = {B1: 256 + 32 * place, P0: 128}.get(number, 0)
                src = ready.at[pl.ds(pl.multiple_of(READY * t + row, 32), count)]
            remote(
                src,
                pieces[number].at[at],
                r.piece_send.at[number],
                r.piece_recv.at[number],
                (t, dp),
            ).start()

    def quarter_of(number, which):
        ref = pieces[number]
        count = ref.shape[0] // parts(number)
        return ref.at[pl.ds(pl.multiple_of(which * count, 32), count)]

    def pass_quarter(number, way, which, device):
        quarter = quarter_of(number, which)
        remote(
            quarter, quarter, r.pass_send.at[number], r.pass_recv.at[number, way], device
        ).start()

    def pass_on(number):
        @pl.when(section != SOURCE[number])
        def _():
            own = place_in(number)
            wait_bytes(quarter_of(number, own), r.piece_recv.at[number])
            if parts(number) == 4:
                pass_quarter(number, 1, own, pair)
            pass_quarter(number, 0, own, sibling)

    def pass_back(number):
        @pl.when(section != SOURCE[number])
        def _():
            wait_bytes(quarter_of(number, pair_place), r.pass_recv.at[number, 1])
            pass_quarter(number, 2, pair_place, sibling)

    def need(number):
        @pl.when(section != SOURCE[number])
        def _():
            wait_bytes(quarter_of(number, 0), r.pass_recv.at[number, 0])
            if parts(number) == 4:
                wait_bytes(quarter_of(number, 0), r.pass_recv.at[number, 2])

    def at_source(source, action):
        @pl.when(section == source)
        def _():
            action()

    for source in range(ranks):
        at_source(source, lambda: run_jobs(first_jobs(source)))
    pl.semaphore_wait(barrier, greetings)
    scales = r.scales
    for k in range(1, ranks):
        for i, row in enumerate((r.gains_in, r.shifts_in)):
            remote(
                row, scales.at[i, section], r.scale_send.at[i], r.scale_recv.at[i], (other(k), dp)
            ).start()
    at_source(0, lambda: (send_piece(A0), send_b0()))
    at_source(2, lambda: (send_piece(A1), send_piece(B1)))
    at_source(3, lambda: send_piece(C1))
    scales[0, section] = r.gains_in[...]
    scales[1, section] = r.shifts_in[...]

    @pl.when(section == 0)
    def _():
        r.a0[...] = r.a0_all[:, :part]

    mine_columns = pl.ds(pl.multiple_of(section * wide, wide), wide)
    cot_copies = (
        pltpu.make_async_copy(r.cot_in.at[:, :, :, :, mine_columns], r.cot_grid, r.cot_sem.at[0]),
        pltpu.make_async_copy(
            r.cot_in_2.at[:, :, :, :, mine_columns], r.cot_grid_2, r.cot_sem.at[1]
        ),
    )
    for copy in cot_copies:
        copy.start()

    def clear_padding(ref):
        for used, (start, stop) in zip(lay.used, lay.spans):
            low = (start + used) // 16 * 16
            high = -(-stop // 16) * 16
            if start + used < stop:
                ref[pl.ds(low, high - low), :] = jnp.zeros((high - low, ref.shape[1]), BF16)

    def by_phase(grid, group, down, right):
        side, crops = lay.sides[group], lay.crops[group]
        split = grid.reshape(side, 2, side, 2, crops, C_IN)
        return split[:, down, :, right].reshape(side * side * crops, C_IN)

    for m in range(micro):
        for copy in load_grids(m):
            copy.wait()
        for phase in range(4):
            clear_padding(r.x.at[phase, m])
            for group, grid in enumerate((r.x_grid, r.x_grid_2)):
                at = pl.ds(lay.spans[group][0], lay.used[group])
                r.x[phase, m, at, :] = by_phase(grid[m % 2], group, phase // 2, phase % 2)
        if m + 2 < micro:
            for copy in load_grids(m + 2):
                copy.start()

    def affine(segment, start, width):
        at = pl.ds(pl.multiple_of(start + section * width, width), width)
        return scales[0, segment, :, at], scales[1, segment, :, at]

    def affine_n(norm):
        return affine(2 * (norm // 2), C_MID * (norm % 2), part)

    def affine_w(norm):
        return affine((1, 1, 3)[norm], (0, C_OUT, 0)[norm], wide)

    def per_group(function, *values):
        top = function(0, *[v[:first] for v in values])
        low = function(1, *[v[first:] for v in values])
        return jnp.concatenate([top, low], axis=0)

    def widened(flags, width):
        return flags if width == part else jnp.concatenate([flags] * (width // part), axis=1)

    def keep(values):
        flags = widened(masks[4], values.shape[1])
        return jnp.where(flags > 0, values, 0.0)

    def moments(values):
        return [
            jnp.sum(v, axis=0, keepdims=True)
            for v in (
                values[:first],
                values[first:],
                values[:first] * values[:first],
                values[first:] * values[first:],
            )
        ]

    f31, b31 = (F31, B31) if lay.fast else (F31_LATE, B31_LATE)
    narrow = (r.norm_n, r.norm_n_send, r.norm_n_recv)
    broad = (r.norm_w, r.norm_w_send, r.norm_w_recv)
    double = None if lay.fast else (r.norm_v, r.norm_v_send, r.norm_v_recv)

    def norm_sent(kind, first_event, last_event):
        buffer, send, _ = kind
        used = buffer.at[pl.ds(0, last_event - first_event), :, pl.ds(0, dp_count - 1)]
        wait_bytes(used, send.at[first_event // buffer.shape[0]])

    def norm_start(kind, event, m, sums):
        buffer, send, recv = kind
        turns = buffer.shape[0]
        slot = buffer.at[event % turns, m, dp]
        for i, value in enumerate(sums):
            slot[pl.ds(i, 1), :] = value
        for i in range(len(sums), buffer.shape[3]):
            slot[pl.ds(i, 1), :] = jnp.zeros((1, slot.shape[1]), F32)
        across_dp(
            lambda device: remote(
                slot, slot, send.at[event // turns], recv.at[event % turns, m], device
            ).start()
        )

    def norm_finish(kind, event, m):
        buffer, _, recv = kind
        turn = event % buffer.shape[0]
        wait_bytes(buffer.at[0, m, pl.ds(0, dp_count - 1)], recv.at[turn, m])
        return jnp.sum(buffer[event % buffer.shape[0], m], axis=0)

    half_lanes = wide // 2
    my_half = pl.ds(pl.multiple_of(core * half_lanes, half_lanes), half_lanes)
    sibling_half = pl.ds(pl.multiple_of((1 - core) * half_lanes, half_lanes), half_lanes)

    def joint_copy(event, way, m, src, dst, device):
        remote(
            src, dst, r.joint_send.at[way], r.joint_recv.at[event % 2, way, m], device
        ).start()

    def joint_start(event, m, sums):
        for i, value in enumerate(sums):
            r.joint[event, m, pl.ds(i, 1), :] = value
        for i in range(len(sums), 8):
            r.joint[event, m, pl.ds(i, 1), :] = jnp.zeros((1, wide), F32)
        joint_copy(
            event, 0, m, r.joint.at[event, m, :, sibling_half], r.joint_pair.at[event, m], sibling
        )

    def joint_line(event, m):
        wait_bytes(r.joint_pair.at[event, m], r.joint_recv.at[event % 2, 0, m])
        r.joint_line[event, m, dp // 2] = r.joint[event, m, :, my_half] + r.joint_pair[event, m]
        slot = r.joint_line.at[event, m, dp // 2]
        for k in range(1, dp_count // 2):
            target = lax.rem(dp // 2 + k, dp_count // 2)
            joint_copy(event, 1, m, slot, slot, (section, 2 * target + core))

    def joint_back(event, m):
        wait_bytes(
            r.joint_line.at[event, m, pl.ds(0, dp_count // 2 - 1)], r.joint_recv.at[event % 2, 1, m]
        )
        r.joint_all[event, m, :, my_half] = jnp.sum(r.joint_line[event, m], axis=0)
        slot = r.joint_all.at[event, m, :, my_half]
        joint_copy(event, 2, m, slot, slot, sibling)

    def joint_finish(event, m):
        wait_bytes(r.joint_pair.at[event, m], r.joint_recv.at[event % 2, 2, m])
        return r.joint_all[event, m]

    def each_joint(step, event):
        if lay.fast:
            each_micro(lambda m: step(event, m))

    def stage_joint(step, event):
        if lay.fast:
            stage(lambda m: step(event, m))

    def finish_moments(kind, event, m, store, fold):
        if kind is None:
            sums = joint_finish(event, m)
        else:
            sums = norm_finish(kind, event, m)
        ref, norm = store
        found = []
        for group in range(2):
            count = float(lay.totals[group] * fold)
            mean = sums[group : group + 1] / count
            square = sums[2 + group : 3 + group] / count
            found += [mean, lax.rsqrt(square - mean * mean + EPSILON)]
        for i, value in enumerate(found):
            ref[norm, m, pl.ds(i, 1), :] = value
        return found

    def moments_of(ref, norm, m):
        return [ref[norm, m, pl.ds(i, 1), :] for i in range(4)]

    def normalized(values, found):
        return per_group(lambda g, v: (v - found[2 * g]) * found[2 * g + 1], values)

    def norm_change(upstream, normed, found, gain, sums, fold):
        def one(group, u, n):
            count = float(lay.totals[group] * fold)
            plain = sums[0][group] * gain / count
            along = sums[1][group] * gain / count
            return found[2 * group + 1] * (u * gain - plain - n * along)

        return keep(per_group(one, upstream, normed)).astype(BF16)

    def add_gains(place, sums):
        at = pl.ds(place, sums[0][0].shape[1])
        own = r.gains.at[section]
        own[pl.ds(0, 1), at] += sums[1][0] + sums[1][1]
        own[pl.ds(1, 1), at] += sums[0][0] + sums[0][1]

    def rows_of(totals, at):
        return [totals[at : at + 1], totals[at + 1 : at + 2]]

    def upstream_sums(upstream, normeds):
        sums = []
        for v in [upstream] + [upstream * n for n in normeds]:
            sums += [
                jnp.sum(v[:first], axis=0, keepdims=True),
                jnp.sum(v[first:], axis=0, keepdims=True),
            ]
        return sums

    def slid(ref, cols, down, right):
        pieces = []
        for (start, stop), side, crops in zip(lay.spans, lay.sides, lay.crops):
            at = PAD + start + (down * side + right) * crops
            pieces.append(ref[pl.ds(at, stop - start), cols])
        values = jnp.concatenate(pieces, axis=0)
        flags = masks[(down + 1) * 3 + right + 1]
        return jnp.where(flags > 0, values, 0.0)

    def sum_start(event, m, values):
        send = r.sum_send
        send[event, m] = values.astype(BF16)
        for k in range(1, ranks):
            cols = pl.ds(pl.multiple_of(other(k) * part, part), part)
            remote(
                send.at[event, m, :, cols],
                r.sum_recv.at[event, m, k - 1],
                r.sum_send_sem,
                r.sum_recv_sem.at[event, m],
                (other(k), dp),
            ).start()

    def sum_finish(event, m):
        wait_bytes(r.sum_recv.at[event, m], r.sum_recv_sem.at[event, m])
        total = r.sum_send[event, m, :, mine].astype(F32)
        for k in range(ranks - 1):
            total = total + r.sum_recv[event, m, k].astype(F32)
        return total

    def get_start(event, m, values):
        get = r.get
        get[event, m, :, mine] = values
        for k in range(1, ranks):
            remote(
                get.at[event, m, :, mine],
                get.at[event, m, :, mine],
                r.get_send_sem,
                r.get_recv_sem.at[event, m],
                (other(k), dp),
            ).start()

    def get_wait(event, m):
        wait_bytes(
            r.get.at[event, m, :, pl.ds(0, C_MID - part)], r.get_recv_sem.at[event, m]
        )

    def get_finish(event, m):
        get_wait(event, m)
        return r.get[event, m]

    def own_start(number, m, src, dst):
        @pl.when(section != m)
        def _():
            remote(
                src, dst, r.own_send.at[number], r.own_recv.at[number], (m, dp)
            ).start()

        @pl.when(section == m)
        def _():
            pltpu.make_async_copy(src, dst, r.own_copy.at[number]).start()

    z1, zn, zw, y1 = r.z1, r.zn, r.zw, r.y1
    r.gains[section] = jnp.zeros(r.gains.shape[1:], F32)
    pass_on(A0)
    at_source(1, lambda: (send_piece(C0), send_piece(P0)))
    pass_on_b0(0)
    pass_back(A0)
    need(A0)
    pass_on_b0(1)

    def do_z1(m):
        sums = None
        for phase in range(4):
            value = dot(r.x[phase, m], r.a0[...])
            z1[phase, m] = value
            found = moments(value)
            sums = found if sums is None else [a + b for a, b in zip(sums, found)]
        norm_start(narrow, F01, m, sums)

    each_micro(do_z1)
    pass_on_b0(2)
    for source in range(ranks):
        at_source(source, lambda: run_jobs(own_jobs(source)))
    for group, grid in enumerate((r.cot_grid, r.cot_grid_2)):
        cot_copies[group].wait()
        for m in range(micro):
            if group == 0:
                clear_padding(r.cot.at[m])
            r.cot[m, pl.ds(lay.spans[group][0], lay.used[group]), :] = grid[m].reshape(
                lay.used[group], wide
            )
    for i in range(2):
        wait_bytes(scales.at[i, pl.ds(0, ranks - 1)], r.scale_recv.at[i])

    def do_a1(m):
        found = finish_moments(narrow, F01, m, (r.stat_n, N01), 4)
        gain, shift = affine_n(N01)
        taps = first_taps()
        for phase in range(4):
            value = silu(normalized(z1[phase, m], found) * gain + shift)
            r.slide[pl.ds(PAD, rows), :] = value
            for k, (at, down, right) in enumerate(taps):
                if at == phase:
                    r.patches[0, m, :, pl.ds(k * part, part)] = slid(
                        r.slide, slice(None), down, right
                    ).astype(BF16)

    each_micro(do_a1)
    for step in range(3):
        pass_back_b0(step)
    need_b0()

    def do_s2(m):
        sum_start(SUM_Z2, m, dot(r.patches[0, m], r.b0[...]))

    each_micro(do_s2)
    pass_on(A1)
    pass_on(C1)
    pass_on(C0)

    def do_z2(m):
        value = sum_finish(SUM_Z2, m)
        zn[0, m] = value
        norm_start(narrow, F02, m, moments(value))

    stage(do_z2)
    pass_on(P0)

    def do_zs(m):
        value = dot(r.x[0, m], r.p0[...])
        zw[N12, m] = value
        if lay.fast:
            joint_start(J12, m, moments(value))
        else:
            norm_start(broad, F12, m, moments(value))


    def do_h0(m):
        found = finish_moments(narrow, F02, m, (r.stat_n, N02), 1)
        gain, shift = affine_n(N02)
        get_start(GET_H0, m, keep(silu(normalized(zn[0, m], found) * gain + shift)).astype(BF16))

    stage(do_h0)
    flush()
    pass_back(C0)
    pass_back(P0)
    need(P0)
    each_micro(do_zs)
    each_joint(joint_line, J12)
    need(C0)

    def do_zc(m):
        value = dot(get_finish(GET_H0, m), r.c0[...])
        zw[N11, m] = value
        if lay.fast:
            joint_start(J11, m, moments(value))
        else:
            norm_start(broad, F11, m, moments(value))

    stage(do_zc)
    stage_joint(joint_line, J11)
    each_joint(joint_back, J12)
    stage_joint(joint_back, J11)
    need(A1)

    def before1(m):
        main = normalized(zw[N11, m], moments_of(r.stat_w, N11, m))
        short = normalized(zw[N12, m], moments_of(r.stat_w, N12, m))
        gain_main, shift_main = affine_w(N11)
        gain_short, shift_short = affine_w(N12)
        return main * gain_main + shift_main + short * gain_short + shift_short, main, short

    def do_y1(m):
        if lay.fast:
            finish_moments(None, J12, m, (r.stat_w, N12), 1)
            finish_moments(None, J11, m, (r.stat_w, N11), 1)
        else:
            finish_moments(broad, F12, m, (r.stat_w, N12), 1)
            finish_moments(broad, F11, m, (r.stat_w, N11), 1)
        value = keep(silu(before1(m)[0])).astype(BF16)
        y1[m] = value
        sum_start(SUM_ZA, m, dot(value, r.a1[...]))

    stage(do_y1)
    pass_on(B1)

    def do_za(m):
        value = sum_finish(SUM_ZA, m)
        zn[1, m] = value
        norm_start(narrow, F21, m, moments(value))

    stage(do_za)
    pass_back(B1)
    need(B1)

    def do_a2(m):
        found = finish_moments(narrow, F21, m, (r.stat_n, N21), 1)
        gain, shift = affine_n(N21)
        r.slide[pl.ds(PAD, rows), :] = silu(normalized(zn[1, m], found) * gain + shift)
        for k, (down, right) in enumerate(second_taps()):
            r.patches[1, m, :, pl.ds(k * part, part)] = slid(
                r.slide, slice(None), down, right
            ).astype(BF16)
        sum_start(SUM_ZB, m, dot(r.patches[1, m], r.b1[...]))

    stage(do_a2)

    def do_zb(m):
        value = sum_finish(SUM_ZB, m)
        zn[2, m] = value
        norm_start(narrow, F22, m, moments(value))

    stage(do_zb)

    def do_h2(m):
        found = finish_moments(narrow, F22, m, (r.stat_n, N22), 1)
        gain, shift = affine_n(N22)
        get_start(GET_H2, m, keep(silu(normalized(zn[2, m], found) * gain + shift)).astype(BF16))

    stage(do_h2)
    need(C1)

    def do_zd(m):
        value = dot(get_finish(GET_H2, m), r.c1[...])
        zw[N31, m] = value
        norm_start(broad, f31, m, moments(value))

    stage(do_zd)
    half_rows = pl.ds(pl.multiple_of(core * (C_IN // 2), 64), C_IN // 2)

    def lanes_of(which):
        return pl.ds(pl.multiple_of(which * part, part), part)

    for k in range(1, ranks):

        @pl.when(other(k) != 0)
        def _():
            remote(
                r.a0.at[half_rows],
                r.a0_all.at[half_rows, mine],
                r.all_send.at[0],
                r.all_recv.at[0],
                (other(k), dp),
            ).start()

    @pl.when(section != 0)
    def _():
        r.a0_all[:, mine] = r.a0[...]

    a0_others = r.a0_all.at[pl.ds(0, C_IN // 2), pl.ds(0, C_MID - part)]
    def do_output(m):
        found = finish_moments(broad, f31, m, (r.stat_w, N31), 1)
        gain, shift = affine_w(N31)
        normed = normalized(zw[N31, m], found)
        before = normed * gain + shift + y1[m].astype(F32)
        sigmoid = jax.nn.sigmoid(before)
        r.out_send[m] = (before * sigmoid).astype(BF16)
        upstream = r.cot[m].astype(F32) * (sigmoid * (1.0 + before * (1.0 - sigmoid)))
        r.skip[m] = upstream.astype(BF16)
        r.uw[m] = upstream
        norm_start(broad, b31, m, upstream_sums(upstream, [normed]))

    if not lay.fast:
        norm_sent(broad, 0, 3)
    stage(do_output)

    def do_ddzd(m):
        totals = norm_finish(broad, b31, m)
        sums = [rows_of(totals, 0), rows_of(totals, 2)]
        add_gains(C_MID + 2 * wide, sums)
        found = moments_of(r.stat_w, N31, m)
        normed = normalized(zw[N31, m], found)
        value = norm_change(r.uw[m], normed, found, affine_w(N31)[0], sums, 1)
        r.ddzd[m] = value
        sum_start(SUM_DH2, m, dot_back(value, r.c1[...]))

    stage(do_ddzd)

    def send_output(m):
        own_start(0, m, r.out_send.at[m], r.out_own.at[:, mine_wide])

    def narrow_upstream(norm, place, event, m, value):
        found = moments_of(r.stat_n, norm, m)
        gain, shift = affine_n(norm)
        normed = normalized(zn[place, m], found)
        upstream = value * silu_slope(normed * gain + shift)
        r.un[place, m] = upstream
        norm_start(narrow, event, m, upstream_sums(upstream, [normed]))

    def narrow_change(norm, place, event, m):
        totals = norm_finish(narrow, event, m)
        sums = [rows_of(totals, 0), rows_of(totals, 2)]
        add_gains(part * norm, sums)
        found = moments_of(r.stat_n, norm, m)
        normed = normalized(zn[place, m], found)
        return norm_change(r.un[place, m], normed, found, affine_n(norm)[0], sums, 1)

    def tall(ref, count):
        return ref.reshape(micro * rows, count)

    share_rows = ROWS // ranks
    slice_base = (0, 0, share_rows, share_rows + C_MID, 2 * share_rows, 2 * share_rows + wide, 3 * share_rows)
    chips = dp_count // 2
    chip = dp // 2
    base_rows = [sum(HEIGHTS[:number]) for number in range(7)]

    def own_piece(number, refs):
        whole, pair, near, total, relayed = refs
        base, height = base_rows[number], whole.shape[0] if number == A0 else HEIGHTS[number]
        each = height // dp_count
        return (
            whole.at[pl.ds(base, height)],
            pair.at[pl.ds(base // 2, height // 2)],
            near.at[:, pl.ds(base // dp_count, each)],
            total.at[pl.ds(base // dp_count, each)],
            relayed.at[pl.ds(base // dp_count, each)],
            height,
        )

    def gradient_refs(number):
        if number == A0:
            return own_piece(number, (r.da, r.da_pair, r.da_near, r.da_sum, r.da_relay))
        return own_piece(number, (r.dw, r.dw_pair, r.dw_near, r.dw_sum, r.dw_relay))

    def make(number, left, right, unit):
        height = HEIGHTS[number]
        right = right.reshape(micro * rows, C_MID)

        def step(i, carry):
            at = pl.multiple_of(i * unit, unit)
            value = dot_rows(left(pl.ds(at, unit)).reshape(micro * rows, unit), right)
            if lay.fast:
                r.dw[pl.ds(pl.multiple_of(base_rows[number] + at, 128), unit), :] = value.astype(BF16)
            else:
                r.stage[pl.ds(0, unit), :] = value.astype(BF16)
                copy = pltpu.make_async_copy(
                    r.stage.at[pl.ds(0, unit)],
                    r.dw.at[pl.ds(pl.multiple_of(slice_base[number] + at, 128), unit)],
                    r.stage_sem,
                )
                copy.start()
                copy.wait()
            return carry

        lax.fori_loop(0, height // unit, step, 0)
        to_sibling(number)

    def to_sibling(number):
        if not lay.fast:
            return
        whole, pair, _, _, _, height = gradient_refs(number)
        each = height // dp_count
        for i in range(chips):
            remote(
                whole.at[pl.ds(pl.multiple_of((2 * i + 1 - core) * each, 16), each)],
                pair.at[pl.ds(i * each, each)],
                r.pair_send.at[int(number == A0)],
                r.pair_recv.at[number],
                sibling,
            ).start()

    lined = chips == 4
    at_end = (chip == 0) | (chip == chips - 1)
    inner = jnp.where(chip < 2, 1, 2) if lined else chip
    across = 3 - inner

    def rows_for(number, target):
        each = gradient_refs(number)[-1] // dp_count
        return pl.ds(pl.multiple_of((2 * target + core) * each, 16), each)

    def send_near(number, target, k):
        whole, _, near, _, _, _ = gradient_refs(number)
        remote(
            whole.at[rows_for(number, target)],
            near.at[k - 1],
            r.near_send.at[int(number == A0)],
            r.near_recv.at[number],
            (section, 2 * target + core),
        ).start()

    def fold(number):
        if not lay.fast:
            return
        whole, pair, near, _, relayed, height = gradient_refs(number)
        each = height // dp_count
        wait_bytes(pair, r.pair_recv.at[number])
        for k in sorted(range(1, chips + 1), key=lambda k: k != 2):
            target = lax.rem(chip + k, chips)
            at = rows_for(number, target)
            theirs = pair[pl.ds(pl.multiple_of(target * each, 16), each), :]
            whole[at, :] = (whole[at, :].astype(F32) + theirs.astype(F32)).astype(BF16)
            if k == chips:
                continue
            if not lined or number == A0:
                send_near(number, target, k)
                continue

            @pl.when(jnp.logical_not(at_end) & (target != across))
            def _():
                send_near(number, target, k)

            @pl.when(at_end & (target != across))
            def _():
                send_near(number, target, k)

            @pl.when(at_end & (target == across))
            def _():
                remote(
                    whole.at[at],
                    relayed,
                    r.relay_send,
                    r.relay_recv.at[number],
                    (section, 2 * inner + core),
                ).start()

    def relay(number):
        if not (lay.fast and lined and number != A0):
            return
        whole, _, _, _, relayed, height = gradient_refs(number)

        @pl.when(jnp.logical_not(at_end))
        def _():
            wait_bytes(relayed, r.relay_recv.at[number])
            at = rows_for(number, across)
            whole[at, :] = (whole[at, :].astype(F32) + relayed[...].astype(F32)).astype(BF16)

            @pl.when(chip == 1)
            def _():
                send_near(number, across, 1)

            @pl.when(chip == 2)
            def _():
                send_near(number, across, 3)

    def units(number):
        height = C_IN if number == A0 else HEIGHTS[number]
        each = height // dp_count
        whole = ROWS // dp_count
        unit = 64 if number in (A0, A1) else 16
        found = []
        for i in range(each // unit):
            row = dp * each + i * unit
            if number == A0:
                owner, at, cols = row // whole, lax.rem(row, whole), mine
            elif number in (C0, P0, C1):
                row = row + (C_MID if number == P0 else 0)
                owner, cols = row // (whole // ranks), slice(None)
                at = section * (whole // ranks) + lax.rem(row, whole // ranks)
            else:
                if number == A1:
                    row = row + section * wide
                else:
                    base = C_IN if number == B0 else C_OUT
                    row = base + C_MID * (row // part) + part * section + lax.rem(row, part)
                owner, at, cols = row // whole, lax.rem(row, whole), slice(None)
            if number == C1:
                at = lax.rem(row, whole // ranks)
            keeper = {C1: r.hold_2, A1: r.hold, B1: r.hold}.get(number, r.share)
            place = keeper.at[pl.ds(pl.multiple_of(at, unit), unit), cols]
            found.append((owner, place))
        return unit, found

    def finish(number):
        if not lay.fast:
            return
        whole, pair, near, total, _, height = gradient_refs(number)
        each = height // dp_count
        value = whole[pl.ds(pl.multiple_of(dp * each, 16), each), :].astype(F32)
        if lined and number != A0:

            @pl.when(at_end)
            def _():
                wait_bytes(near, r.near_recv.at[number])

            @pl.when(jnp.logical_not(at_end))
            def _():
                wait_bytes(near.at[pl.ds(0, 2)], r.near_recv.at[number])

            second = jnp.where(at_end, near[1].astype(F32), 0.0)
            value = value + near[0].astype(F32) + second + near[2].astype(F32)
        else:
            wait_bytes(near, r.near_recv.at[number])
            for k in range(chips - 1):
                value = value + near[k].astype(F32)
        total[...] = value.astype(BF16)
        unit, found = units(number)
        held = number in HELD
        target = section if held else SOURCE[number]
        recv = r.hold_recv.at[HELD.index(number)] if held else r.share_recv
        send = r.share_send.at[int(number == A0)]
        for i, (owner, place) in enumerate(found):
            rows_here = pl.ds(i * unit, unit)
            src = total.at[rows_here]
            here = (owner == dp) & (section == target)

            @pl.when(here)
            def _():
                pltpu.make_async_copy(src, place, recv).start()
                pltpu.make_async_copy(src, pair.at[rows_here], send).start()

            @pl.when(jnp.logical_not(here))
            def _():
                remote(src, place, send, recv, (target, owner)).start()

    def held_blocks(number):
        if number == C1:
            found = []
            whole = ROWS // dp_count // ranks
            for device in range(dp_count):
                count = min(max(HEIGHTS[C1] - device * whole, 0), whole)
                if count:
                    at = pl.ds(pl.multiple_of(section * whole, 16), count)
                    found.append((dp == device, count, r.hold_2.at[pl.ds(0, count)], r.share.at[at]))
            return found
        blocks_64 = ROWS // dp_count // 64
        if number == A1:
            starts = [(wide // 64) * section + i for i in range(wide // 64)]
        else:
            starts = [
                C_OUT // 64 + (C_MID // 64) * (u // 2) + (part // 64) * section + u % 2
                for u in range(18)
            ]
        found = []
        for start in starts:
            at = pl.ds(pl.multiple_of(64 * lax.rem(start, blocks_64), 64), 64)
            found.append((start // blocks_64 == dp, 64, r.hold.at[at], r.share.at[at]))
        return found

    def held_rows(number, act):
        found = held_blocks(number)
        if number == C1:
            for here, count, _, _ in found:
                pl.when(here)(functools.partial(act, count))
            return
        total = sum(jnp.where(here, 1, 0) for here, _, _, _ in found)
        for count in range(1, 9 if number == A1 else 6):
            pl.when(total == count)(functools.partial(act, 64 * count))

    def ship(number):
        if not lay.fast:
            return
        which = HELD.index(number)
        held_rows(number, lambda count: wait_bytes(r.share.at[pl.ds(0, count)], r.hold_recv.at[which]))
        for here, _, src, dst in held_blocks(number):

            @pl.when(here & (section == SOURCE[number]))
            def _():
                pltpu.make_async_copy(src, dst, r.share_recv).start()

            @pl.when(here & (section != SOURCE[number]))
            def _():
                remote(
                    src, dst, r.ship_send.at[which], r.share_recv, (SOURCE[number], dp)
                ).start()

    def shipped(number):
        which = HELD.index(number)

        @pl.when(section != SOURCE[number])
        def _():
            held_rows(
                number, lambda count: wait_bytes(r.share.at[pl.ds(0, count)], r.ship_send.at[which])
            )

    def finish_shares():
        whole = ROWS // dp_count
        sizes = (C_IN + 9 * C_MID, ranks * (C_MID + C_IN), C_OUT + 9 * C_MID, ranks * C_MID)
        count = jnp.int32(0)
        for source, size in enumerate(sizes):
            count = jnp.where(section == source, size, count)
        count = jnp.clip(count - whole * dp, 0, whole)
        lengths = {min(max(size - whole * d, 0), whole) for size in sizes for d in range(dp_count)}
        for length in sorted(lengths):
            if length:

                @pl.when(count == length)
                def _():
                    wait_bytes(r.share.at[pl.ds(0, length)], r.share_recv)

    def store_norm_shares():
        shares = (r.gain_share, r.shift_share)
        count = GSEGMENT // dp_count
        for share in shares:
            share[...] = jnp.zeros(share.shape, F32)
        for source in range(ranks):
            for device in range(dp_count):
                start = device * count
                wide_norm = source % 2 == 1
                used = {1: 2 * C_OUT, 3: C_OUT}.get(source, 2 * C_MID)
                if start >= used:
                    continue

                @pl.when((section == source) & (dp == device))
                def _():
                    for i, share in enumerate(shares):
                        if wide_norm:
                            norm = start // C_OUT + (2 if source == 3 else 0)
                            place_in = start % C_OUT
                            at = C_MID + norm * wide + place_in % wide
                            share[...] = r.gains[place_in // wide, pl.ds(i, 1), pl.ds(at, count)]
                        else:
                            at = part * (source + start // C_MID)
                            for t in range(ranks):
                                share[:, pl.ds(part * t, part)] = r.gains[t, pl.ds(i, 1), pl.ds(at, part)]

    def gradients_sent():
        for group, (pair, near, total) in enumerate(
            ((r.dw_pair, r.dw_near, r.dw_sum), (r.da_pair, r.da_near, r.da_sum))
        ):
            wait_bytes(pair, r.pair_send.at[group])
            wait_bytes(total, r.share_send.at[group])
            if not lined or group == 1:
                wait_bytes(near, r.near_send.at[group])
                continue

            @pl.when(at_end)
            def _():
                wait_bytes(near.at[pl.ds(0, 2)], r.near_send.at[group])
                wait_bytes(r.dw_relay, r.relay_send)

            @pl.when(jnp.logical_not(at_end))
            def _():
                wait_bytes(near, r.near_send.at[group])

        for number in HELD:
            shipped(number)

    def do_dh2(m):
        value = sum_finish(SUM_DH2, m).astype(BF16).astype(F32)
        narrow_upstream(N22, 2, B22, m, value)

    norm_sent(narrow, 0, 4)
    stage(do_dh2)
    b0_sent()
    for number in (A0, C0, P0, A1, B1, C1):

        @pl.when(section != SOURCE[number])
        def _():
            count = pieces[number].shape[0] // parts(number)
            times = 3 if parts(number) == 4 else 1
            wait_bytes(pieces[number].at[pl.ds(0, times * count)], r.pass_send.at[number])

        @pl.when(section == SOURCE[number])
        def _():
            for _ in range(ranks - 1):
                wait_bytes(quarter_of(number, 0), r.piece_send.at[number])
    make(C1, lambda at: r.get[GET_H2, :, :, at], r.ddzd[...], 256)

    def do_ddzb(m):
        get_start(GET_DDZB, m, narrow_change(N22, 2, B22, m))

    stage(do_ddzb)
    fold(C1)

    def fan_out(m, event, weight):
        r.fan[pl.ds(PAD, rows), :] = dot_back(r.get[event, m], weight[...])

    def do_da2(m):
        get_finish(GET_DDZB, m)
        fan_out(m, GET_DDZB, r.b1)
        total = None
        for k, (down, right) in enumerate(second_taps()):
            term = slid(r.fan, pl.ds(k * part, part), -down, -right)
            total = term if total is None else total + term
        narrow_upstream(N21, 1, B21, m, total)

    stage(do_da2)

    @pl.when(section != 0)
    def _():
        wait_bytes(a0_others, r.all_recv.at[0])
        for k in range(1, ranks):
            block = r.a0_all.at[half_rows, lanes_of(other(k))]
            remote(block, block, r.all_send.at[1], r.all_recv.at[1], sibling).start()

    relay(C1)

    def do_ddza(m):
        get_start(GET_DDZA, m, narrow_change(N21, 1, B21, m))

    stage(do_ddza)
    make(B1, lambda at: r.patches[1, :, :, at], r.get[GET_DDZB], 128)
    finish(C1)

    def do_dy1(m):
        value = dot_back(get_finish(GET_DDZA, m), r.a1[...]) + r.skip[m].astype(F32)
        value = value.astype(BF16).astype(F32)
        before, main, short = before1(m)
        upstream = value * silu_slope(before)
        r.uw[m] = upstream
        sums = upstream_sums(upstream, [main, short])
        if lay.fast:
            joint_start(B11, m, sums)
        else:
            norm_start(double, B11, m, sums)

    stage(do_dy1)
    stage_joint(joint_line, B11)
    flush()
    each_micro(send_output)
    make(A1, lambda at: y1[:, :, at], r.get[GET_DDZA], 256)
    fold(B1)
    stage_joint(joint_back, B11)

    def do_ddzc(m):
        totals = joint_finish(B11, m) if lay.fast else norm_finish(double, B11, m)
        plain = rows_of(totals, 0)
        for norm, at, target in ((N11, 2, r.ddzd), (N12, 4, r.ddzs)):
            sums = [plain, rows_of(totals, at)]
            add_gains(C_MID + norm * wide, sums)
            found = moments_of(r.stat_w, norm, m)
            normed = normalized(zw[norm, m], found)
            target[m] = norm_change(r.uw[m], normed, found, affine_w(norm)[0], sums, 1)
        sum_start(SUM_DH0, m, dot_back(r.ddzd[m], r.c0[...]))

    stage(do_ddzc)
    flush()
    fold(A1)

    def do_dxs(m):
        r.dxs_send[m] = dot_back(r.ddzs[m], r.p0[...]).astype(BF16)

    each_micro(do_dxs)
    make(C0, lambda at: r.get[GET_H0, :, :, at], r.ddzd[...], 256)
    make(P0, lambda at: r.x[0, :, :, at], r.ddzs[...], 256)

    def do_dh0(m):
        value = sum_finish(SUM_DH0, m).astype(BF16).astype(F32)
        narrow_upstream(N02, 0, B02, m, value)

    def send_dxs(m):
        own_start(1, m, r.dxs_send.at[m], r.dxs_recv.at[section])

    stage(do_dh0)
    relay(B1)
    relay(A1)

    def do_ddz2(m):
        get_start(GET_DDZ2, m, narrow_change(N02, 0, B02, m))

    stage(do_ddz2)
    finish(A1)
    finish(B1)
    flush()
    fold(C0)

    def do_da1(m):
        get_wait(GET_DDZ2, m)

        @pl.when(m == micro - 2)
        def _():
            each_micro(send_dxs)

        fan_out(m, GET_DDZ2, r.b0)
        gain, shift = affine_n(N01)
        found = moments_of(r.stat_n, N01, m)
        sums = None
        for phase in range(4):
            total = None
            for k, (at, down, right) in enumerate(first_taps()):
                if at == phase:
                    term = slid(r.fan, pl.ds(k * part, part), -down, -right)
                    total = term if total is None else total + term
            normed = normalized(z1[phase, m], found)
            upstream = total * silu_slope(normed * gain + shift)
            r.u1[phase, m] = upstream
            terms = upstream_sums(upstream, [normed])
            sums = terms if sums is None else [a + b for a, b in zip(sums, terms)]
        norm_start(narrow, B01, m, sums)

    stage(do_da1)
    flush()
    fold(P0)
    relay(C0)
    make(B0, lambda at: r.patches[0, :, :, at], r.get[GET_DDZ2], 128)

    out_own = r.out_own
    wait_bytes(out_own.at[:, mine_wide], r.own_copy.at[0])
    wait_bytes(out_own.at[:, pl.ds(0, C_OUT - wide)], r.own_recv.at[0])
    def store_grid(refs, values, pick):
        for group, ref in enumerate(refs):
            start, used = lay.spans[group][0], lay.used[group]
            side, crops = lay.sides[group], lay.crops[group]
            grid = values[start : start + used].astype(BF16).reshape(side, side, crops, values.shape[1])
            pick(ref, grid)

    def store_output(ref, grid):
        ref[...] = grid

    store_grid((r.out_grid, r.out_grid_2), out_own[...].astype(F32), store_output)
    results = [
        pltpu.make_async_copy(src, dst, r.result_sem.at[i])
        for i, (src, dst) in enumerate(
            (
                (r.out_grid, r.out),
                (r.out_grid_2, r.out_2),
                (r.grad_grid, r.grad),
                (r.grad_grid_2, r.grad_2),
            )
        )
    ]
    results[0].start()
    results[1].start()

    def do_ddz1(m):
        totals = norm_finish(narrow, B01, m)
        sums = [rows_of(totals, 0), rows_of(totals, 2)]
        add_gains(0, sums)
        found = moments_of(r.stat_n, N01, m)
        gain = affine_n(N01)[0]
        for phase in range(4):
            normed = normalized(z1[phase, m], found)
            r.ddz1[phase, m] = norm_change(r.u1[phase, m], normed, found, gain, sums, 4)
        own_start(2, m, r.ddz1.at[:, m], r.ddz1_own.at[:, :, mine])

    each_micro(do_ddz1)
    fold(B0)
    relay(P0)
    ship(C1)
    ship(B1)
    ship(A1)
    for k in range(1, ranks):
        remote(
            r.gains.at[section],
            r.gains.at[section],
            r.gain_send,
            r.gain_recv,
            (other(k), dp),
        ).start()

    def da0_step(i, carry):
        at = pl.ds(pl.multiple_of(i * 128, 128), 128)
        total = None
        for phase in range(4):
            value = dot_rows(
                r.x[phase, :, :, at].reshape(micro * rows, 128),
                r.ddz1[phase].reshape(micro * rows, part),
            )
            total = value if total is None else total + value
        da0 = r.da if lay.fast else r.da0
        da0[pl.ds(pl.multiple_of(i * 128, 128), 128), :] = total.astype(BF16)
        return carry

    lax.fori_loop(0, C_IN // 128, da0_step, 0)
    to_sibling(A0)
    finish(C0)
    relay(B0)
    fold(A0)
    finish(P0)
    relay(A0)
    finish(B0)
    finish(A0)

    dxs, ddz1_own = r.dxs_recv, r.ddz1_own

    @pl.when(section != 0)
    def _():
        wait_bytes(a0_others, r.all_recv.at[1])

    wait_bytes(dxs.at[0], r.own_copy.at[1])
    wait_bytes(dxs.at[pl.ds(0, ranks - 1)], r.own_recv.at[1])
    wait_bytes(ddz1_own.at[:, :, mine], r.own_copy.at[2])
    wait_bytes(ddz1_own.at[:, :, pl.ds(0, C_MID - part)], r.own_recv.at[2])
    for phase in range(4):
        value = dot_back(ddz1_own[phase], r.a0_all[...])
        if phase == 0:
            extra = dxs[0].astype(F32)
            for k in range(1, ranks):
                extra = extra + dxs[k].astype(F32)
            value = value + extra.astype(BF16).astype(F32)

        def store_phase(ref, grid):
            ref[:, phase // 2, :, phase % 2] = grid

        store_grid((r.grad_grid, r.grad_grid_2), value, store_phase)
    wait_bytes(r.gains.at[pl.ds(0, ranks - 1)], r.gain_recv)
    if lay.fast:
        store_norm_shares()
    else:
        r.gains_out[...] = r.gains[...]

    results[2].start()
    results[3].start()
    if lay.fast:
        finish_shares()
        results.append(pltpu.make_async_copy(r.share, r.share_out, r.result_sem.at[4]))
        results[4].start()
        gradients_sent()

    wait_bytes(r.sum_recv, r.sum_send_sem)
    wait_bytes(r.get.at[:, :, :, pl.ds(0, C_MID - part)], r.get_send_sem)
    norm_sent(narrow, 4, 8)
    if lay.fast:
        norm_sent(broad, 0, 2)
        wait_bytes(r.joint_pair, r.joint_send.at[0])
        wait_bytes(r.joint_line.at[:, :, pl.ds(0, dp_count // 2 - 1)], r.joint_send.at[1])
        wait_bytes(r.joint_pair, r.joint_send.at[2])
    else:
        norm_sent(broad, 3, 4)
        norm_sent(double, 0, 1)
    for copy in results:
        copy.wait()
    wait_bytes(out_own.at[:, pl.ds(0, C_OUT - wide)], r.own_send.at[0])
    wait_bytes(dxs.at[pl.ds(0, ranks - 1)], r.own_send.at[1])
    wait_bytes(ddz1_own.at[:, :, pl.ds(0, C_MID - part)], r.own_send.at[2])

    @pl.when(section == 0)
    def _():
        wait_bytes(a0_others, r.all_send.at[0])

    @pl.when(section != 0)
    def _():
        wait_bytes(a0_others.at[:, pl.ds(0, (ranks - 2) * part)], r.all_send.at[0])
        wait_bytes(a0_others, r.all_send.at[1])

    wait_bytes(r.gains.at[pl.ds(0, ranks - 1)], r.gain_send)
    for i in range(2):
        wait_bytes(scales.at[i, pl.ds(0, ranks - 1)], r.scale_send.at[i])


def chain(lay, ranks, dp_count, operands):
    micro, rows = lay.micro, lay.rows
    part, wide = C_MID // ranks, C_OUT // ranks
    table = scratch_table(lay, ranks, dp_count)
    shapes = (
        *[jax.ShapeDtypeStruct(grid_shape(lay, group, 1, C_OUT), BF16) for group in range(2)],
        *[jax.ShapeDtypeStruct(phase_shape(lay, group), BF16) for group in range(2)],
    )
    if lay.fast:
        shapes += (jax.ShapeDtypeStruct((1, GSEGMENT // dp_count), F32),) * 2
        shapes += (jax.ShapeDtypeStruct((ROWS // dp_count, C_MID), BF16),)
    else:
        shapes += (
            jax.ShapeDtypeStruct((ranks, 2, C_MID + 3 * wide), F32),
            jax.ShapeDtypeStruct((ROWS, C_MID), BF16),
            jax.ShapeDtypeStruct((C_IN, part), BF16),
        )
    anywhere = pl.BlockSpec(memory_space=pl.ANY)
    inside = pl.BlockSpec(memory_space=pltpu.VMEM)
    return pl.pallas_call(
        functools.partial(chain_kernel, lay, ranks, dp_count, tuple(table)),
        out_shape=shapes,
        in_specs=[anywhere] * 5 + [inside] * 3,
        out_specs=[anywhere] * 4 + ([inside] * 2 + [anywhere] if lay.fast else [inside, anywhere, inside]),
        scratch_shapes=list(table.values()),
        compiler_params=pltpu.CompilerParams(
            collective_id=0, has_side_effects=True, vmem_limit_bytes=63 * 2**20
        ),
        name="chain",
    )(*operands)


def summed_gradient(slices, small, section, ranks):
    small = jnp.stack([small] + [jnp.zeros_like(small)] * (ranks - 1))
    slices = slices.reshape(ranks, ROWS // ranks, C_MID)
    arrived = lax.all_to_all(slices, "section", 0, 0, tiled=True).astype(F32)
    arrived_small = lax.all_to_all(small, "section", 0, 0, tiled=True).astype(F32)
    segment = segment_gradient(arrived, arrived_small, section, ranks)
    return lax.psum_scatter(segment.reshape(-1), "dp", scatter_dimension=0, tiled=True)


def norm_shares(gains, ranks, dp_count):
    part, wide = C_MID // ranks, C_OUT // ranks

    def joined(start, width):
        block = gains[:, :, start : start + width // ranks]
        return jnp.moveaxis(block, 0, 1).reshape(2, width)

    f01, f02, f21, f22 = [joined(part * i, C_MID) for i in range(4)]
    f11, f12, f31 = [joined(C_MID + wide * i, C_OUT) for i in range(3)]
    blank = jnp.zeros((2, GSEGMENT - 2 * C_MID), F32)
    segments = jnp.stack(
        [
            jnp.concatenate([f01, f02, blank], 1),
            jnp.concatenate([f11, f12], 1),
            jnp.concatenate([f21, f22, blank], 1),
            jnp.concatenate([f31, jnp.zeros((2, GSEGMENT - C_OUT), F32)], 1),
        ]
    )
    share = GSEGMENT // dp_count
    own_norms = lax.dynamic_index_in_dim(segments, lax.axis_index("section"), 0, keepdims=False)
    return lax.dynamic_slice_in_dim(own_norms, lax.axis_index("dp") * share, share, 1)


def deliver_kernel(ranks, *refs):
    plain, share_in, norms_in, refs = refs[:4], refs[4], refs[5:7], refs[7:]
    plain_out, share_out, norms_out, refs = refs[:4], refs[4], refs[5:7], refs[7:]
    held, share, order, load_sem, store_sem = refs[:4], refs[4], refs[5], refs[6], refs[7]
    loads = [
        pltpu.make_async_copy(src, dst, load_sem.at[i])
        for i, (src, dst) in enumerate(zip(plain + (share_in,), held + (share,)))
    ]
    stores = [
        pltpu.make_async_copy(src, dst, store_sem.at[i])
        for i, (src, dst) in enumerate(zip(held + (order,), plain_out + (share_out,)))
    ]
    turn = (4, 2, 0, 3, 1)
    for i in turn:
        loads[i].start()
    for src, dst in zip(norms_in, norms_out):
        dst[...] = src[...]
    whole, lanes = share.shape[0], 128
    for i in turn:
        loads[i].wait()
        if i == 4:
            odd = lax.rem(lax.axis_index("section"), 2)

            @pl.when(odd == 0)
            def _():
                for q in range(ranks):
                    order[pl.ds(q, whole, stride=ranks), :] = share[:, lanes * q : lanes * (q + 1)].astype(F32)

            @pl.when(odd == 1)
            def _():
                short = whole // ranks
                for t in range(ranks):
                    for q in range(ranks):
                        order[pl.ds(ranks * t + q, short, stride=ranks * ranks), :] = share[
                            t * short : (t + 1) * short, lanes * q : lanes * (q + 1)
                        ].astype(F32)

        stores[i].start()
    for i in turn:
        stores[i].wait()


def deliver(results, ranks):
    plain, norms, share = results[:4], results[4:6], results[6]
    order = jax.ShapeDtypeStruct((share.size // 128, 128), F32)
    anywhere = pl.BlockSpec(memory_space=pl.ANY)
    inside = pl.BlockSpec(memory_space=pltpu.VMEM)
    specs = [anywhere] * 5 + [inside] * 2
    like = [jax.ShapeDtypeStruct(v.shape, v.dtype) for v in plain]
    return pl.pallas_call(
        functools.partial(deliver_kernel, ranks),
        out_shape=like + [order] + [jax.ShapeDtypeStruct(v.shape, v.dtype) for v in norms],
        in_specs=specs,
        out_specs=specs,
        scratch_shapes=[pltpu.VMEM(v.shape, v.dtype) for v in list(plain) + [share, order]]
        + [pltpu.SemaphoreType.DMA((5,))] * 2,
        name="deliver",
    )(*plain, share, *norms)


def per_device(
    images_global, images_local, weights, norm_gains, norm_shifts, cotangent_global, cotangent_local
):
    section = lax.axis_index("section")
    ranks = lax.axis_size("section")
    dp_count = lax.axis_size("dp")
    lay = Layout(images_global.shape, images_local.shape, dp_count)
    micro, rows = lay.micro, lay.rows
    part = C_MID // ranks
    wide = C_OUT // ranks

    def cells_first(pictures):
        return jnp.moveaxis(pictures, 1, 3)

    masks = np.stack(
        [lay.valid(down, right) for down in (-1, 0, 1) for right in (-1, 0, 1)]
    ).astype(np.float32)
    masks = jnp.asarray(np.ascontiguousarray(np.broadcast_to(masks[:, :, None], (9, rows, part))))
    results = chain(
        lay,
        ranks,
        dp_count,
        (
            cells_first(images_global),
            cells_first(images_local),
            cells_first(cotangent_global),
            cells_first(cotangent_local),
            weights.reshape(-1, 128),
            norm_gains[None],
            norm_shifts[None],
            masks,
        ),
    )

    if lay.fast:
        results = deliver(results, ranks)
    out_global, out_local, grad_global, grad_local, *rest = results
    if lay.fast:
        share, gain_share, shift_share = rest
        own_norms, weight_gradient = (gain_share[0], shift_share[0]), share.reshape(-1)
    else:
        own_norms = norm_shares(rest[0], ranks, dp_count)
        weight_gradient = summed_gradient(*rest[1:], section, ranks)

    def crops_first(grid, side, crops):
        return jnp.moveaxis(grid.reshape(1, side, side, crops, -1), 3, 1)

    return (
        crops_first(out_global, lay.sides[0], lay.crops[0]),
        crops_first(out_local, lay.sides[1], lay.crops[1]),
        crops_first(grad_global, 2 * lay.sides[0], lay.crops[0]),
        crops_first(grad_local, 2 * lay.sides[1], lay.crops[1]),
        weight_gradient,
        own_norms[0],
        own_norms[1],
    )


def solution(mesh):
    images = P(None, "dp", None, None, None)
    made = P("section", "dp", None, None, None)
    return jax.shard_map(
        per_device,
        mesh=mesh,
        in_specs=(images, images, P("section"), P("section"), P("section"), images, images),
        out_specs=(made, made, made, made) + (P(("section", "dp")),) * 3,
        check_vma=False,
    )
```

```python
import functools
from types import SimpleNamespace

import jax
import jax.numpy as jnp
import numpy as np
from jax import lax
from jax.experimental import pallas as pl
from jax.experimental.pallas import tpu as pltpu
from jax.sharding import PartitionSpec as P

C_IN = 1024
C_MID = 512
C_OUT = 2048
WSEGMENT = 3407872
GSEGMENT = 4096
EPSILON = 1e-05
F32 = jnp.float32
BF16 = jnp.bfloat16


def round_up(value, unit):
    return -(-value // unit) * unit


class Layout:
    def __init__(self, shape_global, shape_local, dp_count):
        self.micro = shape_global[0]
        self.crops = (shape_global[1], shape_local[1])
        self.sides = (shape_global[2] // 2, shape_local[2] // 2)
        used = [crops * side * side for crops, side in zip(self.crops, self.sides)]
        self.used = used
        first = round_up(used[0], 8)
        self.rows = round_up(first + round_up(used[1], 8), 16)
        self.spans = ((0, first), (first, self.rows))
        self.totals = [count * dp_count for count in used]
        self.fast = dp_count == 8 and WSEGMENT // C_MID // dp_count % 64 == 0

    def valid(self, down, right):
        flags = np.zeros((self.rows,), bool)
        for (start, _), crops, side in zip(self.spans, self.crops, self.sides):
            for crop in range(crops):
                for i in range(side):
                    for j in range(side):
                        inside = 0 <= i + down < side and 0 <= j + right < side
                        flags[start + (i * side + j) * crops + crop] = inside
        return flags


def first_taps():
    return [
        (2 * (p != 1) + (q != 1), -(p == 0), -(q == 0)) for p in range(3) for q in range(3)
    ]


def second_taps():
    return [(p - 1, q - 1) for p in range(3) for q in range(3)]


def segment_gradient(pieces, small, section, ranks):
    part = C_MID // ranks
    total_rows = WSEGMENT // C_MID

    def finished(rows):
        return jnp.pad(rows, ((0, total_rows - rows.shape[0]), (0, 0)))

    def across(block):
        return block.transpose(1, 0, 2).reshape(-1, C_MID)

    def spatial(block):
        return block.reshape(ranks, 9, part, C_MID).transpose(1, 0, 2, 3).reshape(-1, C_MID)

    def first():
        return finished(
            jnp.concatenate(
                [small.transpose(1, 0, 2).reshape(-1, C_MID), spatial(pieces[:, : 9 * part])]
            )
        )

    def second():
        return finished(across(pieces[:, : C_MID + C_IN]))

    def third():
        tall = C_OUT // ranks
        return finished(
            jnp.concatenate(
                [pieces[:, :tall].reshape(-1, C_MID), spatial(pieces[:, tall : tall + 9 * part])]
            )
        )

    def fourth():
        return finished(across(pieces[:, :C_MID]))

    return lax.switch(section, [first, second, third, fourth])


MESH = pl.DeviceIdType.MESH
ROWS = WSEGMENT // C_MID
SUM_Z2, SUM_ZA, SUM_ZB, SUM_DH2, SUM_DH0 = range(5)
GET_H0, GET_H2, GET_DDZB, GET_DDZA, GET_DDZ2 = range(5)
F01, F02, F21, F22, B22, B21, B02, B01 = range(8)
F31, B31 = range(2)
F12, F11, F31_LATE, B31_LATE = range(4)
B11, J12, J11 = range(3)
N01, N02, N21, N22 = range(4)
N11, N12, N31 = range(3)
A0, B0, C0, P0, A1, B1, C1 = range(7)
SOURCE = (0, 0, 1, 1, 2, 2, 3, 0)
PAD = 16
SLOTS = 3
HELD = (4, 5, 6)
READY = 640
HEIGHTS = (0, C_MID, C_MID, C_IN, C_OUT // 4, 9 * C_MID // 4, C_MID, 5 * C_MID // 4)
B0_REST = 7


def dot(left, right):
    return lax.dot_general(left, right, (((1,), (0,)), ((), ())), preferred_element_type=F32)


def dot_back(left, right):
    return lax.dot_general(left, right, (((1,), (1,)), ((), ())), preferred_element_type=F32)


def dot_rows(left, right):
    return lax.dot_general(left, right, (((0,), (0,)), ((), ())), preferred_element_type=F32)


def silu(value):
    return value * jax.nn.sigmoid(value)


def silu_slope(before):
    sigmoid = jax.nn.sigmoid(before)
    return sigmoid * (1.0 + before * (1.0 - sigmoid))


def grid_shape(lay, group, fold, channels):
    side = fold * lay.sides[group]
    return (side, side, lay.crops[group], channels)


def phase_shape(lay, group):
    side = lay.sides[group]
    return (side, 2, side, 2, lay.crops[group], C_IN)


def scratch_table(lay, ranks, dp_count):
    micro, rows = lay.micro, lay.rows
    part, wide = C_MID // ranks, C_OUT // ranks
    others = ranks - 1
    vmem, dma = pltpu.VMEM, pltpu.SemaphoreType.DMA
    return dict(
        x=vmem((4, micro, rows, C_IN), BF16),
        cot=vmem((micro, rows, wide), BF16),
        x_grid=vmem((2,) + grid_shape(lay, 0, 2, C_IN), BF16),
        x_grid_2=vmem((2,) + grid_shape(lay, 1, 2, C_IN), BF16),
        cot_grid=vmem((micro,) + grid_shape(lay, 0, 1, wide), BF16),
        cot_grid_2=vmem((micro,) + grid_shape(lay, 1, 1, wide), BF16),
        a0=vmem((C_IN, part), BF16),
        b0=vmem((9 * part, C_MID), BF16),
        c0=vmem((C_MID, wide), BF16),
        p0=vmem((C_IN, wide), BF16),
        a1=vmem((wide, C_MID), BF16),
        b1=vmem((9 * part, C_MID), BF16),
        c1=vmem((C_MID, wide), BF16),
        a0_all=vmem((C_IN, C_MID), BF16),
        raw=vmem((SLOTS, 2048, 128), BF16),
        raw_sem=dma((SLOTS,)),
        scales=vmem((2, ranks, 1, GSEGMENT), F32),
        z1=vmem((4, micro, rows, part), F32),
        u1=vmem((4, micro, rows, part), F32),
        zn=vmem((3, micro, rows, part), F32),
        un=vmem((3, micro, rows, part), F32),
        zw=vmem((3, micro, rows, wide), F32),
        uw=vmem((micro, rows, wide), F32),
        y1=vmem((micro, rows, wide), BF16),
        skip=vmem((micro, rows, wide), BF16),
        ddzd=vmem((micro, rows, wide), BF16),
        ddzs=vmem((micro, rows, wide), BF16),
        patches=vmem((2, micro, rows, 9 * part), BF16),
        slide=vmem((PAD + rows + PAD, part), F32),
        fan=vmem((PAD + rows + PAD, 9 * part), F32),
        stat_n=vmem((4, micro, 8, part), F32),
        stat_w=vmem((3, micro, 8, wide), F32),
        sum_send=vmem((5, micro, rows, C_MID), BF16),
        sum_recv=vmem((5, micro, others, rows, part), BF16),
        get=vmem((5, micro, rows, C_MID), BF16),
        norm_n=vmem((4, micro, dp_count, 4, part), F32),
        norm_w=vmem((2 if lay.fast else 3, micro, dp_count, 4, wide), F32),
        **joint_scratch(lay, dp_count, wide),
        out_send=vmem((micro, rows, wide), BF16),
        out_own=vmem((rows, C_OUT), BF16),
        out_grid=vmem(grid_shape(lay, 0, 1, C_OUT), BF16),
        out_grid_2=vmem(grid_shape(lay, 1, 1, C_OUT), BF16),
        grad_grid=vmem(phase_shape(lay, 0), BF16),
        grad_grid_2=vmem(phase_shape(lay, 1), BF16),
        result_sem=dma((5,)),
        dxs_send=vmem((micro, rows, C_IN), BF16),
        dxs_recv=vmem((ranks, rows, C_IN), BF16),
        ddz1=vmem((4, micro, rows, part), BF16),
        ddz1_own=vmem((4, rows, C_MID), BF16),
        gains=vmem((ranks, 2, C_MID + 3 * wide), F32),
        x_sem=dma((2, 2)),
        cot_sem=dma((2,)),
        piece_send=dma((7,)),
        piece_recv=dma((7,)),
        pass_send=dma((7,)),
        pass_recv=dma((7, 3)),
        eight_send=dma,
        eight_recv=dma((4, 3)),
        scale_send=dma((2,)),
        scale_recv=dma((2,)),
        all_send=dma((2,)),
        all_recv=dma((2,)),
        sum_send_sem=dma,
        sum_recv_sem=dma((5, micro)),
        get_send_sem=dma,
        get_recv_sem=dma((5, micro)),
        norm_n_send=dma((2,)),
        norm_n_recv=dma((4, micro)),
        norm_w_send=dma((2,)),
        norm_w_recv=dma((2 if lay.fast else 3, micro)),
        own_send=dma((3,)),
        own_recv=dma((3,)),
        own_copy=dma((3,)),
        gain_send=dma,
        gain_recv=dma,
        **gradient_scratch(lay, ranks, dp_count),
    )


def joint_scratch(lay, dp_count, wide):
    vmem, dma, micro = pltpu.VMEM, pltpu.SemaphoreType.DMA, lay.micro
    if not lay.fast:
        return dict(
            norm_v=vmem((1, micro, dp_count, 8, wide), F32),
            norm_v_send=dma((1,)),
            norm_v_recv=dma((1, micro)),
        )
    return dict(
        joint=vmem((3, micro, 8, wide), F32),
        joint_all=vmem((3, micro, 8, wide), F32),
        joint_pair=vmem((3, micro, 8, wide // 2), F32),
        joint_line=vmem((3, micro, dp_count // 2, 8, wide // 2), F32),
        joint_send=dma((3,)),
        joint_recv=dma((2, 3, micro)),
    )


def gradient_scratch(lay, ranks, dp_count):
    vmem, dma = pltpu.VMEM, pltpu.SemaphoreType.DMA
    if not lay.fast:
        return dict(
            stage=vmem((256, C_MID), BF16),
            stage_sem=dma,
            ready=vmem((ranks * READY, C_MID), BF16),
        )
    part = C_MID // ranks
    height, chips = sum(HEIGHTS), dp_count // 2
    return dict(
        dw=vmem((height, C_MID), BF16),
        dw_pair=vmem((height // 2, C_MID), BF16),
        dw_near=vmem((chips - 1, height // dp_count, C_MID), BF16),
        dw_sum=vmem((height // dp_count, C_MID), BF16),
        da=vmem((C_IN, part), BF16),
        da_pair=vmem((C_IN // 2, part), BF16),
        da_near=vmem((chips - 1, C_IN // dp_count, part), BF16),
        dw_relay=vmem((height // dp_count, C_MID), BF16),
        da_relay=vmem((C_IN // dp_count, part), BF16),
        relay_send=dma,
        relay_recv=dma((8,)),
        da_sum=vmem((C_IN // dp_count, part), BF16),
        share=vmem((ROWS // dp_count, C_MID), BF16),
        pair_send=dma((2,)),
        pair_recv=dma((8,)),
        near_send=dma((2,)),
        near_recv=dma((8,)),
        share_send=dma((2,)),
        share_recv=dma,
        hold=vmem((ROWS // dp_count, C_MID), BF16),
        hold_2=vmem((ROWS // dp_count // ranks, C_MID), BF16),
        hold_recv=dma((3,)),
        ship_send=dma((3,)),
    )


def chain_kernel(lay, ranks, dp_count, names, *refs):
    inputs = ("x_in", "x_in_2", "cot_in", "cot_in_2", "w_in", "gains_in", "shifts_in", "masks")
    outputs = ("out", "out_2", "grad", "grad_2")
    outputs += ("gain_share", "shift_share", "share_out") if lay.fast else ("gains_out", "dw", "da0")
    r = SimpleNamespace(**dict(zip(inputs + outputs + names, refs)))
    pieces = (r.a0, r.b0, r.c0, r.p0, r.a1, r.b1, r.c1)
    micro, rows = lay.micro, lay.rows
    first = lay.spans[0][1]
    part, wide = C_MID // ranks, C_OUT // ranks
    section, dp = lax.axis_index("section"), lax.axis_index("dp")
    core = lax.rem(dp, 2)
    sibling = (section, dp + 1 - 2 * core)
    masks = r.masks
    mine = pl.ds(pl.multiple_of(section * part, part), part)
    mine_wide = pl.ds(pl.multiple_of(section * wide, wide), wide)

    def other(k):
        return lax.rem(section + k, ranks)

    def across_dp(act):
        if dp_count <= 8:
            for k in range(1, dp_count):
                act((section, lax.rem(dp + k, dp_count)))
        else:

            def step(k, carry):
                act((section, lax.rem(dp + k, dp_count)))
                return carry

            lax.fori_loop(1, dp_count, step, 0)

    def remote(src, dst, send, recv, device):
        return pltpu.make_async_remote_copy(
            src_ref=src,
            dst_ref=dst,
            send_sem=send,
            recv_sem=recv,
            device_id=device,
            device_id_type=MESH,
        )

    def wait_bytes(ref, sem):
        pltpu.make_async_copy(ref, ref, sem).wait()

    def some_micros(body, first_micro, last_micro):
        def step(m, carry):
            body(m)
            return carry

        lax.fori_loop(first_micro, last_micro, step, 0)

    def each_micro(body):
        some_micros(body, 0, micro)

    waiting = []

    def flush():
        while waiting:
            waiting.pop()(micro - 1)

    def stage(body):
        if not waiting:
            some_micros(body, 0, micro - 1)
        else:
            before = waiting.pop()

            def step(i, carry):
                @pl.when(i == 1)
                def _():
                    before(micro - 1)

                @pl.when(i != 1)
                def _():
                    body(jnp.maximum(i - 1, 0))

                return carry

            lax.fori_loop(0, micro, step, 0)
        waiting.append(body)

    barrier = pltpu.get_barrier_semaphore()

    def greet(device):
        pl.semaphore_signal(barrier, inc=1, device_id=device, device_id_type=MESH)

    if lay.fast:
        r.share[...] = jnp.zeros(r.share.shape, BF16)
        for k in range(ranks):
            for j in range(dp_count):
                if k or j:
                    greet((other(k), lax.rem(dp + j, dp_count)))
        greetings = ranks * dp_count - 1
    else:
        across_dp(greet)
        for k in range(1, ranks):
            greet((other(k), dp))
        greetings = dp_count - 1 + ranks - 1

    def load_grids(m):
        slot = m % 2
        return (
            pltpu.make_async_copy(r.x_in.at[m], r.x_grid.at[slot], r.x_sem.at[0, slot]),
            pltpu.make_async_copy(r.x_in_2.at[m], r.x_grid_2.at[slot], r.x_sem.at[1, slot]),
        )

    for m in range(2):
        for copy in load_grids(m):
            copy.start()
    r.slide[...] = jnp.zeros(r.slide.shape, F32)
    r.fan[...] = jnp.zeros(r.fan.shape, F32)

    place = lax.rem(dp, 4)
    group = dp - place
    pair_place = lax.rem(place + 2, 4)
    pair = (section, group + pair_place)

    place_8 = lax.rem(dp, 8)
    group_8 = dp - place_8
    chip_8 = place_8 // 2
    EIGHTH, STEP = 9 * part // 8, 3 * part // 8

    def eighth(which, step):
        return r.b0.at[pl.ds(pl.multiple_of(EIGHTH * which + STEP * step, 16), STEP)]

    def eight_copy(way, step, src, dst, device):
        remote(src, dst, r.eight_send, r.eight_recv.at[way, step], device).start()

    def send_b0():
        for step in range(3):
            for k in range(1, ranks):
                row = READY * other(k) + 16 * place_8 + STEP * step
                src = ready.at[pl.ds(pl.multiple_of(row, 16), STEP)]
                eight_copy(0, step, src, eighth(place_8, step), (other(k), dp))

    def pass_on_b0(step):
        @pl.when(section != 0)
        def _():
            own = eighth(place_8, step)
            wait_bytes(own, r.eight_recv.at[0, step])
            for k in range(1, 4):
                target = lax.rem(chip_8 + k, 4)
                eight_copy(1, step, own, own, (section, group_8 + 2 * target + core))
            eight_copy(2, step, own, own, sibling)

    def pass_back_b0(step):
        @pl.when(section != 0)
        def _():
            wait_bytes(r.b0.at[pl.ds(0, 3 * STEP)], r.eight_recv.at[1, step])
            for k in range(1, 4):
                theirs = eighth(2 * lax.rem(chip_8 + k, 4) + core, step)
                eight_copy(3, step, theirs, theirs, sibling)

    def need_b0():
        @pl.when(section != 0)
        def _():
            for step in range(3):
                wait_bytes(r.b0.at[pl.ds(0, STEP)], r.eight_recv.at[2, step])
                wait_bytes(r.b0.at[pl.ds(0, 3 * STEP)], r.eight_recv.at[3, step])

    def b0_sent():
        @pl.when(section == 0)
        def _():
            wait_bytes(r.b0.at[pl.ds(0, 9 * STEP)], r.eight_send)

        @pl.when(section != 0)
        def _():
            wait_bytes(r.b0.at[pl.ds(0, 21 * STEP)], r.eight_send)

    ready = r.dw if lay.fast else r.ready

    def parts(number):
        return 2 if number in (A1, C1) else 4

    def place_in(number):
        return core if parts(number) == 2 else place

    def run_jobs(jobs):
        def load(number):
            start, count, _ = jobs[number]
            start = start if isinstance(start, int) else pl.multiple_of(start, 512)
            slot = number % SLOTS
            return pltpu.make_async_copy(
                r.w_in.at[pl.ds(start, count)], r.raw.at[slot, pl.ds(0, count)], r.raw_sem.at[slot]
            )

        for number in range(min(SLOTS, len(jobs))):
            load(number).start()
        for number, (_, count, use) in enumerate(jobs):
            load(number).wait()
            use(r.raw[number % SLOTS, pl.ds(0, count), :])
            if number + SLOTS < len(jobs):
                load(number + SLOTS).start()

    def by_rows(value):
        return value.reshape(value.shape[0] // 4, C_MID)

    def by_columns(value):
        return value.reshape(value.shape[0] // 16, C_OUT)

    def first_jobs(source):
        jobs = []

        def keep_a0(i):
            def use(value):
                r.a0_all[pl.ds(C_MID * i, C_MID), :] = by_rows(value)

            return (2048 * i, 2048, use)

        def keep_taps(base, row):
            def use(value):
                matrix = by_rows(value)
                for t in range(ranks):
                    if t != source:
                        ready[pl.ds(READY * t + row, part), :] = matrix[part * t : part * (t + 1)]

            return (2048 * base, 2048, use)

        def keep_wide(chunk, row):
            def use(value):
                matrix = by_columns(value)
                for t in range(ranks):
                    if t != source:
                        ready[pl.ds(READY * t + row, 128), :] = matrix[:, wide * t : wide * (t + 1)]

            return (2048 * chunk, 2048, use)

        def keep_tall(t):
            def use(value):
                ready[pl.ds(READY * t, 256), :] = by_rows(value)

            return (2048 * t + 1024 * core, 1024, use)

        if source == 0:
            jobs = [keep_a0(0), keep_a0(1)] + [keep_taps(2 + place_8 + j, part * j) for j in range(2)]
        elif source == 1:
            jobs = [keep_wide(place, 0)] + [keep_wide(4 + 2 * place + j, 128 + 128 * j) for j in range(2)]
        elif source == 2:
            jobs = [keep_tall(t) for t in range(ranks) if t != source]
            jobs += [keep_taps(4 + 2 * place + j, 256 + part * j) for j in range(3)]
        else:
            jobs = [keep_wide(2 * core + j, 128 * j) for j in range(2)]
        return jobs

    def own_jobs(source):
        def put(ref, row, count):
            def use(value):
                ref[pl.ds(row, count), :] = by_rows(value)

            return use

        def put_wide(ref, row):
            def use(value):
                ref[pl.ds(row, 128), :] = by_columns(value)[:, wide * source : wide * (source + 1)]

            return use

        if source == 0:
            return [(2048 * (2 + tap), 512, put(r.b0, part * tap, part)) for tap in range(9)]
        if source == 1:
            jobs = [(2048 * i, 2048, put_wide(r.c0, 128 * i)) for i in range(4)]
            return jobs + [(2048 * (4 + i), 2048, put_wide(r.p0, 128 * i)) for i in range(8)]
        if source == 2:
            jobs = [(2048 * source, 2048, put(r.a1, 0, wide))]
            start = 512 * source
            return jobs + [
                (2048 * (4 + tap) + start, 512, put(r.b1, part * tap, part)) for tap in range(9)
            ]
        return [(2048 * i, 2048, put_wide(r.c1, 128 * i)) for i in range(4)]

    def send_piece(number):
        count = pieces[number].shape[0] // parts(number)
        at = pl.ds(pl.multiple_of(place_in(number) * count, 32), count)
        for k in range(1, ranks):
            t = other(k)
            if number == A0:
                src = r.a0_all.at[at, pl.ds(pl.multiple_of(t * part, part), part)]
            else:
                row = {B1: 256 + 32 * place, P0: 128}.get(number, 0)
                src = ready.at[pl.ds(pl.multiple_of(READY * t + row, 32), count)]
            remote(
                src,
                pieces[number].at[at],
                r.piece_send.at[number],
                r.piece_recv.at[number],
                (t, dp),
            ).start()

    def quarter_of(number, which):
        ref = pieces[number]
        count = ref.shape[0] // parts(number)
        return ref.at[pl.ds(pl.multiple_of(which * count, 32), count)]

    def pass_quarter(number, way, which, device):
        quarter = quarter_of(number, which)
        remote(
            quarter, quarter, r.pass_send.at[number], r.pass_recv.at[number, way], device
        ).start()

    def pass_on(number):
        @pl.when(section != SOURCE[number])
        def _():
            own = place_in(number)
            wait_bytes(quarter_of(number, own), r.piece_recv.at[number])
            if parts(number) == 4:
                pass_quarter(number, 1, own, pair)
            pass_quarter(number, 0, own, sibling)

    def pass_back(number):
        @pl.when(section != SOURCE[number])
        def _():
            wait_bytes(quarter_of(number, pair_place), r.pass_recv.at[number, 1])
            pass_quarter(number, 2, pair_place, sibling)

    def need(number):
        @pl.when(section != SOURCE[number])
        def _():
            wait_bytes(quarter_of(number, 0), r.pass_recv.at[number, 0])
            if parts(number) == 4:
                wait_bytes(quarter_of(number, 0), r.pass_recv.at[number, 2])

    def at_source(source, action):
        @pl.when(section == source)
        def _():
            action()

    for source in range(ranks):
        at_source(source, lambda: run_jobs(first_jobs(source)))
    pl.semaphore_wait(barrier, greetings)
    scales = r.scales
    for k in range(1, ranks):
        for i, row in enumerate((r.gains_in, r.shifts_in)):
            remote(
                row, scales.at[i, section], r.scale_send.at[i], r.scale_recv.at[i], (other(k), dp)
            ).start()
    at_source(0, lambda: (send_piece(A0), send_b0()))
    at_source(2, lambda: (send_piece(A1), send_piece(B1)))
    at_source(3, lambda: send_piece(C1))
    scales[0, section] = r.gains_in[...]
    scales[1, section] = r.shifts_in[...]

    @pl.when(section == 0)
    def _():
        r.a0[...] = r.a0_all[:, :part]

    mine_columns = pl.ds(pl.multiple_of(section * wide, wide), wide)
    cot_copies = (
        pltpu.make_async_copy(r.cot_in.at[:, :, :, :, mine_columns], r.cot_grid, r.cot_sem.at[0]),
        pltpu.make_async_copy(
            r.cot_in_2.at[:, :, :, :, mine_columns], r.cot_grid_2, r.cot_sem.at[1]
        ),
    )
    for copy in cot_copies:
        copy.start()

    def clear_padding(ref):
        for used, (start, stop) in zip(lay.used, lay.spans):
            low = (start + used) // 16 * 16
            high = -(-stop // 16) * 16
            if start + used < stop:
                ref[pl.ds(low, high - low), :] = jnp.zeros((high - low, ref.shape[1]), BF16)

    def by_phase(grid, group, down, right):
        side, crops = lay.sides[group], lay.crops[group]
        split = grid.reshape(side, 2, side, 2, crops, C_IN)
        return split[:, down, :, right].reshape(side * side * crops, C_IN)

    for m in range(micro):
        for copy in load_grids(m):
            copy.wait()
        for phase in range(4):
            clear_padding(r.x.at[phase, m])
            for group, grid in enumerate((r.x_grid, r.x_grid_2)):
                at = pl.ds(lay.spans[group][0], lay.used[group])
                r.x[phase, m, at, :] = by_phase(grid[m % 2], group, phase // 2, phase % 2)
        if m + 2 < micro:
            for copy in load_grids(m + 2):
                copy.start()

    def affine(segment, start, width):
        at = pl.ds(pl.multiple_of(start + section * width, width), width)
        return scales[0, segment, :, at], scales[1, segment, :, at]

    def affine_n(norm):
        return affine(2 * (norm // 2), C_MID * (norm % 2), part)

    def affine_w(norm):
        return affine((1, 1, 3)[norm], (0, C_OUT, 0)[norm], wide)

    def per_group(function, *values):
        top = function(0, *[v[:first] for v in values])
        low = function(1, *[v[first:] for v in values])
        return jnp.concatenate([top, low], axis=0)

    def widened(flags, width):
        return flags if width == part else jnp.concatenate([flags] * (width // part), axis=1)

    def keep(values):
        flags = widened(masks[4], values.shape[1])
        return jnp.where(flags > 0, values, 0.0)

    def moments(values):
        return [
            jnp.sum(v, axis=0, keepdims=True)
            for v in (
                values[:first],
                values[first:],
                values[:first] * values[:first],
                values[first:] * values[first:],
            )
        ]

    f31, b31 = (F31, B31) if lay.fast else (F31_LATE, B31_LATE)
    narrow = (r.norm_n, r.norm_n_send, r.norm_n_recv)
    broad = (r.norm_w, r.norm_w_send, r.norm_w_recv)
    double = None if lay.fast else (r.norm_v, r.norm_v_send, r.norm_v_recv)

    def norm_sent(kind, first_event, last_event):
        buffer, send, _ = kind
        used = buffer.at[pl.ds(0, last_event - first_event), :, pl.ds(0, dp_count - 1)]
        wait_bytes(used, send.at[first_event // buffer.shape[0]])

    def norm_start(kind, event, m, sums):
        buffer, send, recv = kind
        turns = buffer.shape[0]
        slot = buffer.at[event % turns, m, dp]
        for i, value in enumerate(sums):
            slot[pl.ds(i, 1), :] = value
        for i in range(len(sums), buffer.shape[3]):
            slot[pl.ds(i, 1), :] = jnp.zeros((1, slot.shape[1]), F32)
        across_dp(
            lambda device: remote(
                slot, slot, send.at[event // turns], recv.at[event % turns, m], device
            ).start()
        )

    def norm_finish(kind, event, m):
        buffer, _, recv = kind
        turn = event % buffer.shape[0]
        wait_bytes(buffer.at[0, m, pl.ds(0, dp_count - 1)], recv.at[turn, m])
        return jnp.sum(buffer[event % buffer.shape[0], m], axis=0)

    half_lanes = wide // 2
    my_half = pl.ds(pl.multiple_of(core * half_lanes, half_lanes), half_lanes)
    sibling_half = pl.ds(pl.multiple_of((1 - core) * half_lanes, half_lanes), half_lanes)

    def joint_copy(event, way, m, src, dst, device):
        remote(
            src, dst, r.joint_send.at[way], r.joint_recv.at[event % 2, way, m], device
        ).start()

    def joint_start(event, m, sums):
        for i, value in enumerate(sums):
            r.joint[event, m, pl.ds(i, 1), :] = value
        for i in range(len(sums), 8):
            r.joint[event, m, pl.ds(i, 1), :] = jnp.zeros((1, wide), F32)
        joint_copy(
            event, 0, m, r.joint.at[event, m, :, sibling_half], r.joint_pair.at[event, m], sibling
        )

    def joint_line(event, m):
        wait_bytes(r.joint_pair.at[event, m], r.joint_recv.at[event % 2, 0, m])
        r.joint_line[event, m, dp // 2] = r.joint[event, m, :, my_half] + r.joint_pair[event, m]
        slot = r.joint_line.at[event, m, dp // 2]
        for k in range(1, dp_count // 2):
            target = lax.rem(dp // 2 + k, dp_count // 2)
            joint_copy(event, 1, m, slot, slot, (section, 2 * target + core))

    def joint_back(event, m):
        wait_bytes(
            r.joint_line.at[event, m, pl.ds(0, dp_count // 2 - 1)], r.joint_recv.at[event % 2, 1, m]
        )
        r.joint_all[event, m, :, my_half] = jnp.sum(r.joint_line[event, m], axis=0)
        slot = r.joint_all.at[event, m, :, my_half]
        joint_copy(event, 2, m, slot, slot, sibling)

    def joint_finish(event, m):
        wait_bytes(r.joint_pair.at[event, m], r.joint_recv.at[event % 2, 2, m])
        return r.joint_all[event, m]

    def each_joint(step, event):
        if lay.fast:
            each_micro(lambda m: step(event, m))

    def stage_joint(step, event):
        if lay.fast:
            stage(lambda m: step(event, m))

    def finish_moments(kind, event, m, store, fold):
        if kind is None:
            sums = joint_finish(event, m)
        else:
            sums = norm_finish(kind, event, m)
        ref, norm = store
        found = []
        for group in range(2):
            count = float(lay.totals[group] * fold)
            mean = sums[group : group + 1] / count
            square = sums[2 + group : 3 + group] / count
            found += [mean, lax.rsqrt(square - mean * mean + EPSILON)]
        for i, value in enumerate(found):
            ref[norm, m, pl.ds(i, 1), :] = value
        return found

    def moments_of(ref, norm, m):
        return [ref[norm, m, pl.ds(i, 1), :] for i in range(4)]

    def normalized(values, found):
        return per_group(lambda g, v: (v - found[2 * g]) * found[2 * g + 1], values)

    def norm_change(upstream, normed, found, gain, sums, fold):
        def one(group, u, n):
            count = float(lay.totals[group] * fold)
            plain = sums[0][group] * gain / count
            along = sums[1][group] * gain / count
            return found[2 * group + 1] * (u * gain - plain - n * along)

        return keep(per_group(one, upstream, normed)).astype(BF16)

    def add_gains(place, sums):
        at = pl.ds(place, sums[0][0].shape[1])
        own = r.gains.at[section]
        own[pl.ds(0, 1), at] += sums[1][0] + sums[1][1]
        own[pl.ds(1, 1), at] += sums[0][0] + sums[0][1]

    def rows_of(totals, at):
        return [totals[at : at + 1], totals[at + 1 : at + 2]]

    def upstream_sums(upstream, normeds):
        sums = []
        for v in [upstream] + [upstream * n for n in normeds]:
            sums += [
                jnp.sum(v[:first], axis=0, keepdims=True),
                jnp.sum(v[first:], axis=0, keepdims=True),
            ]
        return sums

    def slid(ref, cols, down, right):
        pieces = []
        for (start, stop), side, crops in zip(lay.spans, lay.sides, lay.crops):
            at = PAD + start + (down * side + right) * crops
            pieces.append(ref[pl.ds(at, stop - start), cols])
        values = jnp.concatenate(pieces, axis=0)
        flags = masks[(down + 1) * 3 + right + 1]
        return jnp.where(flags > 0, values, 0.0)

    def sum_start(event, m, values):
        send = r.sum_send
        send[event, m] = values.astype(BF16)
        for k in range(1, ranks):
            cols = pl.ds(pl.multiple_of(other(k) * part, part), part)
            remote(
                send.at[event, m, :, cols],
                r.sum_recv.at[event, m, k - 1],
                r.sum_send_sem,
                r.sum_recv_sem.at[event, m],
                (other(k), dp),
            ).start()

    def sum_finish(event, m):
        wait_bytes(r.sum_recv.at[event, m], r.sum_recv_sem.at[event, m])
        total = r.sum_send[event, m, :, mine].astype(F32)
        for k in range(ranks - 1):
            total = total + r.sum_recv[event, m, k].astype(F32)
        return total

    def get_start(event, m, values):
        get = r.get
        get[event, m, :, mine] = values
        for k in range(1, ranks):
            remote(
                get.at[event, m, :, mine],
                get.at[event, m, :, mine],
                r.get_send_sem,
                r.get_recv_sem.at[event, m],
                (other(k), dp),
            ).start()

    def get_wait(event, m):
        wait_bytes(
            r.get.at[event, m, :, pl.ds(0, C_MID - part)], r.get_recv_sem.at[event, m]
        )

    def get_finish(event, m):
        get_wait(event, m)
        return r.get[event, m]

    def own_start(number, m, src, dst):
        @pl.when(section != m)
        def _():
            remote(
                src, dst, r.own_send.at[number], r.own_recv.at[number], (m, dp)
            ).start()

        @pl.when(section == m)
        def _():
            pltpu.make_async_copy(src, dst, r.own_copy.at[number]).start()

    z1, zn, zw, y1 = r.z1, r.zn, r.zw, r.y1
    r.gains[section] = jnp.zeros(r.gains.shape[1:], F32)
    pass_on(A0)
    at_source(1, lambda: (send_piece(C0), send_piece(P0)))
    pass_on_b0(0)
    pass_back(A0)
    need(A0)
    pass_on_b0(1)

    def do_z1(m):
        sums = None
        for phase in range(4):
            value = dot(r.x[phase, m], r.a0[...])
            z1[phase, m] = value
            found = moments(value)
            sums = found if sums is None else [a + b for a, b in zip(sums, found)]
        norm_start(narrow, F01, m, sums)

    each_micro(do_z1)
    pass_on_b0(2)
    for source in range(ranks):
        at_source(source, lambda: run_jobs(own_jobs(source)))
    for group, grid in enumerate((r.cot_grid, r.cot_grid_2)):
        cot_copies[group].wait()
        for m in range(micro):
            if group == 0:
                clear_padding(r.cot.at[m])
            r.cot[m, pl.ds(lay.spans[group][0], lay.used[group]), :] = grid[m].reshape(
                lay.used[group], wide
            )
    for i in range(2):
        wait_bytes(scales.at[i, pl.ds(0, ranks - 1)], r.scale_recv.at[i])

    def do_a1(m):
        found = finish_moments(narrow, F01, m, (r.stat_n, N01), 4)
        gain, shift = affine_n(N01)
        taps = first_taps()
        for phase in range(4):
            value = silu(normalized(z1[phase, m], found) * gain + shift)
            r.slide[pl.ds(PAD, rows), :] = value
            for k, (at, down, right) in enumerate(taps):
                if at == phase:
                    r.patches[0, m, :, pl.ds(k * part, part)] = slid(
                        r.slide, slice(None), down, right
                    ).astype(BF16)

    each_micro(do_a1)
    for step in range(3):
        pass_back_b0(step)
    need_b0()

    def do_s2(m):
        sum_start(SUM_Z2, m, dot(r.patches[0, m], r.b0[...]))

    each_micro(do_s2)
    pass_on(A1)
    pass_on(C1)
    pass_on(C0)

    def do_z2(m):
        value = sum_finish(SUM_Z2, m)
        zn[0, m] = value
        norm_start(narrow, F02, m, moments(value))

    stage(do_z2)
    pass_on(P0)

    def do_zs(m):
        value = dot(r.x[0, m], r.p0[...])
        zw[N12, m] = value
        if lay.fast:
            joint_start(J12, m, moments(value))
        else:
            norm_start(broad, F12, m, moments(value))


    def do_h0(m):
        found = finish_moments(narrow, F02, m, (r.stat_n, N02), 1)
        gain, shift = affine_n(N02)
        get_start(GET_H0, m, keep(silu(normalized(zn[0, m], found) * gain + shift)).astype(BF16))

    stage(do_h0)
    flush()
    pass_back(C0)
    pass_back(P0)
    need(P0)
    each_micro(do_zs)
    each_joint(joint_line, J12)
    need(C0)

    def do_zc(m):
        value = dot(get_finish(GET_H0, m), r.c0[...])
        zw[N11, m] = value
        if lay.fast:
            joint_start(J11, m, moments(value))
        else:
            norm_start(broad, F11, m, moments(value))

    stage(do_zc)
    stage_joint(joint_line, J11)
    each_joint(joint_back, J12)
    stage_joint(joint_back, J11)
    need(A1)

    def before1(m):
        main = normalized(zw[N11, m], moments_of(r.stat_w, N11, m))
        short = normalized(zw[N12, m], moments_of(r.stat_w, N12, m))
        gain_main, shift_main = affine_w(N11)
        gain_short, shift_short = affine_w(N12)
        return main * gain_main + shift_main + short * gain_short + shift_short, main, short

    def do_y1(m):
        if lay.fast:
            finish_moments(None, J12, m, (r.stat_w, N12), 1)
            finish_moments(None, J11, m, (r.stat_w, N11), 1)
        else:
            finish_moments(broad, F12, m, (r.stat_w, N12), 1)
            finish_moments(broad, F11, m, (r.stat_w, N11), 1)
        value = keep(silu(before1(m)[0])).astype(BF16)
        y1[m] = value
        sum_start(SUM_ZA, m, dot(value, r.a1[...]))

    stage(do_y1)
    pass_on(B1)

    def do_za(m):
        value = sum_finish(SUM_ZA, m)
        zn[1, m] = value
        norm_start(narrow, F21, m, moments(value))

    stage(do_za)
    pass_back(B1)
    need(B1)

    def do_a2(m):
        found = finish_moments(narrow, F21, m, (r.stat_n, N21), 1)
        gain, shift = affine_n(N21)
        r.slide[pl.ds(PAD, rows), :] = silu(normalized(zn[1, m], found) * gain + shift)
        for k, (down, right) in enumerate(second_taps()):
            r.patches[1, m, :, pl.ds(k * part, part)] = slid(
                r.slide, slice(None), down, right
            ).astype(BF16)
        sum_start(SUM_ZB, m, dot(r.patches[1, m], r.b1[...]))

    stage(do_a2)

    def do_zb(m):
        value = sum_finish(SUM_ZB, m)
        zn[2, m] = value
        norm_start(narrow, F22, m, moments(value))

    stage(do_zb)

    def do_h2(m):
        found = finish_moments(narrow, F22, m, (r.stat_n, N22), 1)
        gain, shift = affine_n(N22)
        get_start(GET_H2, m, keep(silu(normalized(zn[2, m], found) * gain + shift)).astype(BF16))

    stage(do_h2)
    need(C1)

    def do_zd(m):
        value = dot(get_finish(GET_H2, m), r.c1[...])
        zw[N31, m] = value
        norm_start(broad, f31, m, moments(value))

    stage(do_zd)
    half_rows = pl.ds(pl.multiple_of(core * (C_IN // 2), 64), C_IN // 2)

    def lanes_of(which):
        return pl.ds(pl.multiple_of(which * part, part), part)

    for k in range(1, ranks):

        @pl.when(other(k) != 0)
        def _():
            remote(
                r.a0.at[half_rows],
                r.a0_all.at[half_rows, mine],
                r.all_send.at[0],
                r.all_recv.at[0],
                (other(k), dp),
            ).start()

    @pl.when(section != 0)
    def _():
        r.a0_all[:, mine] = r.a0[...]

    a0_others = r.a0_all.at[pl.ds(0, C_IN // 2), pl.ds(0, C_MID - part)]
    def do_output(m):
        found = finish_moments(broad, f31, m, (r.stat_w, N31), 1)
        gain, shift = affine_w(N31)
        normed = normalized(zw[N31, m], found)
        before = normed * gain + shift + y1[m].astype(F32)
        sigmoid = jax.nn.sigmoid(before)
        r.out_send[m] = (before * sigmoid).astype(BF16)
        upstream = r.cot[m].astype(F32) * (sigmoid * (1.0 + before * (1.0 - sigmoid)))
        r.skip[m] = upstream.astype(BF16)
        r.uw[m] = upstream
        norm_start(broad, b31, m, upstream_sums(upstream, [normed]))

    if not lay.fast:
        norm_sent(broad, 0, 3)
    stage(do_output)

    def do_ddzd(m):
        totals = norm_finish(broad, b31, m)
        sums = [rows_of(totals, 0), rows_of(totals, 2)]
        add_gains(C_MID + 2 * wide, sums)
        found = moments_of(r.stat_w, N31, m)
        normed = normalized(zw[N31, m], found)
        value = norm_change(r.uw[m], normed, found, affine_w(N31)[0], sums, 1)
        r.ddzd[m] = value
        sum_start(SUM_DH2, m, dot_back(value, r.c1[...]))

    stage(do_ddzd)

    def send_output(m):
        own_start(0, m, r.out_send.at[m], r.out_own.at[:, mine_wide])

    def narrow_upstream(norm, place, event, m, value):
        found = moments_of(r.stat_n, norm, m)
        gain, shift = affine_n(norm)
        normed = normalized(zn[place, m], found)
        upstream = value * silu_slope(normed * gain + shift)
        r.un[place, m] = upstream
        norm_start(narrow, event, m, upstream_sums(upstream, [normed]))

    def narrow_change(norm, place, event, m):
        totals = norm_finish(narrow, event, m)
        sums = [rows_of(totals, 0), rows_of(totals, 2)]
        add_gains(part * norm, sums)
        found = moments_of(r.stat_n, norm, m)
        normed = normalized(zn[place, m], found)
        return norm_change(r.un[place, m], normed, found, affine_n(norm)[0], sums, 1)

    def tall(ref, count):
        return ref.reshape(micro * rows, count)

    share_rows = ROWS // ranks
    slice_base = (0, 0, share_rows, share_rows + C_MID, 2 * share_rows, 2 * share_rows + wide, 3 * share_rows, HEIGHTS[B0])
    chips = dp_count // 2
    chip = dp // 2
    base_rows = [sum(HEIGHTS[:number]) for number in range(8)]

    def own_piece(number, refs):
        whole, pair, near, total, relayed = refs
        base, height = base_rows[number], whole.shape[0] if number == A0 else HEIGHTS[number]
        each = height // dp_count
        return (
            whole.at[pl.ds(base, height)],
            pair.at[pl.ds(base // 2, height // 2)],
            near.at[:, pl.ds(base // dp_count, each)],
            total.at[pl.ds(base // dp_count, each)],
            relayed.at[pl.ds(base // dp_count, each)],
            height,
        )

    def gradient_refs(number):
        if number == A0:
            return own_piece(number, (r.da, r.da_pair, r.da_near, r.da_sum, r.da_relay))
        return own_piece(number, (r.dw, r.dw_pair, r.dw_near, r.dw_sum, r.dw_relay))

    def make(number, left, right, unit, skip=0):
        height = HEIGHTS[number]
        right = right.reshape(micro * rows, C_MID)

        def step(i, carry):
            at = pl.multiple_of(i * unit, unit)
            value = dot_rows(left(pl.ds(at + skip, unit)).reshape(micro * rows, unit), right)
            if lay.fast:
                r.dw[pl.ds(pl.multiple_of(base_rows[number] + at, 128), unit), :] = value.astype(BF16)
            else:
                r.stage[pl.ds(0, unit), :] = value.astype(BF16)
                copy = pltpu.make_async_copy(
                    r.stage.at[pl.ds(0, unit)],
                    r.dw.at[pl.ds(pl.multiple_of(slice_base[number] + at, 128), unit)],
                    r.stage_sem,
                )
                copy.start()
                copy.wait()
            return carry

        lax.fori_loop(0, height // unit, step, 0)
        to_sibling(number)

    def to_sibling(number):
        if not lay.fast:
            return
        whole, pair, _, _, _, height = gradient_refs(number)
        each = height // dp_count
        for i in range(chips):
            remote(
                whole.at[pl.ds(pl.multiple_of((2 * i + 1 - core) * each, 16), each)],
                pair.at[pl.ds(i * each, each)],
                r.pair_send.at[int(number == A0)],
                r.pair_recv.at[number],
                sibling,
            ).start()

    lined = chips == 4
    at_end = (chip == 0) | (chip == chips - 1)
    inner = jnp.where(chip < 2, 1, 2) if lined else chip
    across = 3 - inner

    def rows_for(number, target):
        each = gradient_refs(number)[-1] // dp_count
        return pl.ds(pl.multiple_of((2 * target + core) * each, 16), each)

    def send_near(number, target, k):
        whole, _, near, _, _, _ = gradient_refs(number)
        remote(
            whole.at[rows_for(number, target)],
            near.at[k - 1],
            r.near_send.at[int(number == A0)],
            r.near_recv.at[number],
            (section, 2 * target + core),
        ).start()

    def fold(number):
        if not lay.fast:
            return
        whole, pair, near, _, relayed, height = gradient_refs(number)
        each = height // dp_count
        wait_bytes(pair, r.pair_recv.at[number])
        for k in sorted(range(1, chips + 1), key=lambda k: k != 2):
            target = lax.rem(chip + k, chips)
            at = rows_for(number, target)
            theirs = pair[pl.ds(pl.multiple_of(target * each, 16), each), :]
            whole[at, :] = (whole[at, :].astype(F32) + theirs.astype(F32)).astype(BF16)
            if k == chips:
                continue
            if not lined or number == A0:
                send_near(number, target, k)
                continue

            @pl.when(jnp.logical_not(at_end) & (target != across))
            def _():
                send_near(number, target, k)

            @pl.when(at_end & (target != across))
            def _():
                send_near(number, target, k)

            @pl.when(at_end & (target == across))
            def _():
                remote(
                    whole.at[at],
                    relayed,
                    r.relay_send,
                    r.relay_recv.at[number],
                    (section, 2 * inner + core),
                ).start()

    def relay(number):
        if not (lay.fast and lined and number != A0):
            return
        whole, _, _, _, relayed, height = gradient_refs(number)

        @pl.when(jnp.logical_not(at_end))
        def _():
            wait_bytes(relayed, r.relay_recv.at[number])
            at = rows_for(number, across)
            whole[at, :] = (whole[at, :].astype(F32) + relayed[...].astype(F32)).astype(BF16)

            @pl.when(chip == 1)
            def _():
                send_near(number, across, 1)

            @pl.when(chip == 2)
            def _():
                send_near(number, across, 3)

    def units(number):
        height = C_IN if number == A0 else HEIGHTS[number]
        each = height // dp_count
        whole = ROWS // dp_count
        unit = 64 if number in (A0, A1) else 16
        found = []
        for i in range(each // unit):
            row = dp * each + i * unit
            if number == A0:
                owner, at, cols = row // whole, lax.rem(row, whole), mine
            elif number in (C0, P0, C1):
                row = row + (C_MID if number == P0 else 0)
                owner, cols = row // (whole // ranks), slice(None)
                at = section * (whole // ranks) + lax.rem(row, whole // ranks)
            else:
                if number == A1:
                    row = row + section * wide
                else:
                    base = C_OUT if number == B1 else C_IN
                    row = row + (HEIGHTS[B0] if number == B0_REST else 0)
                    row = base + C_MID * (row // part) + part * section + lax.rem(row, part)
                owner, at, cols = row // whole, lax.rem(row, whole), slice(None)
            if number == C1:
                at = lax.rem(row, whole // ranks)
            keeper = {C1: r.hold_2, A1: r.hold, B1: r.hold}.get(number, r.share)
            place = keeper.at[pl.ds(pl.multiple_of(at, unit), unit), cols]
            found.append((owner, place))
        return unit, found

    def finish(number):
        if not lay.fast:
            return
        whole, pair, near, total, _, height = gradient_refs(number)
        each = height // dp_count
        value = whole[pl.ds(pl.multiple_of(dp * each, 16), each), :].astype(F32)
        if lined and number != A0:

            @pl.when(at_end)
            def _():
                wait_bytes(near, r.near_recv.at[number])

            @pl.when(jnp.logical_not(at_end))
            def _():
                wait_bytes(near.at[pl.ds(0, 2)], r.near_recv.at[number])

            second = jnp.where(at_end, near[1].astype(F32), 0.0)
            value = value + near[0].astype(F32) + second + near[2].astype(F32)
        else:
            wait_bytes(near, r.near_recv.at[number])
            for k in range(chips - 1):
                value = value + near[k].astype(F32)
        total[...] = value.astype(BF16)
        unit, found = units(number)
        held = number in HELD
        target = section if held else SOURCE[number]
        recv = r.hold_recv.at[HELD.index(number)] if held else r.share_recv
        send = r.share_send.at[int(number == A0)]
        for i, (owner, place) in enumerate(found):
            rows_here = pl.ds(i * unit, unit)
            src = total.at[rows_here]
            here = (owner == dp) & (section == target)

            @pl.when(here)
            def _():
                pltpu.make_async_copy(src, place, recv).start()
                pltpu.make_async_copy(src, pair.at[rows_here], send).start()

            @pl.when(jnp.logical_not(here))
            def _():
                remote(src, place, send, recv, (target, owner)).start()

    def held_blocks(number):
        if number == C1:
            found = []
            whole = ROWS // dp_count // ranks
            for device in range(dp_count):
                count = min(max(HEIGHTS[C1] - device * whole, 0), whole)
                if count:
                    at = pl.ds(pl.multiple_of(section * whole, 16), count)
                    found.append((dp == device, count, r.hold_2.at[pl.ds(0, count)], r.share.at[at]))
            return found
        blocks_64 = ROWS // dp_count // 64
        if number == A1:
            starts = [(wide // 64) * section + i for i in range(wide // 64)]
        else:
            starts = [
                C_OUT // 64 + (C_MID // 64) * (u // 2) + (part // 64) * section + u % 2
                for u in range(18)
            ]
        found = []
        for start in starts:
            at = pl.ds(pl.multiple_of(64 * lax.rem(start, blocks_64), 64), 64)
            found.append((start // blocks_64 == dp, 64, r.hold.at[at], r.share.at[at]))
        return found

    def held_rows(number, act):
        found = held_blocks(number)
        if number == C1:
            for here, count, _, _ in found:
                pl.when(here)(functools.partial(act, count))
            return
        total = sum(jnp.where(here, 1, 0) for here, _, _, _ in found)
        for count in range(1, 9 if number == A1 else 6):
            pl.when(total == count)(functools.partial(act, 64 * count))

    def ship(number):
        if not lay.fast:
            return
        which = HELD.index(number)
        held_rows(number, lambda count: wait_bytes(r.share.at[pl.ds(0, count)], r.hold_recv.at[which]))
        for here, _, src, dst in held_blocks(number):

            @pl.when(here & (section == SOURCE[number]))
            def _():
                pltpu.make_async_copy(src, dst, r.share_recv).start()

            @pl.when(here & (section != SOURCE[number]))
            def _():
                remote(
                    src, dst, r.ship_send.at[which], r.share_recv, (SOURCE[number], dp)
                ).start()

    def shipped(number):
        which = HELD.index(number)

        @pl.when(section != SOURCE[number])
        def _():
            held_rows(
                number, lambda count: wait_bytes(r.share.at[pl.ds(0, count)], r.ship_send.at[which])
            )

    def finish_shares():
        whole = ROWS // dp_count
        sizes = (C_IN + 9 * C_MID, ranks * (C_MID + C_IN), C_OUT + 9 * C_MID, ranks * C_MID)
        count = jnp.int32(0)
        for source, size in enumerate(sizes):
            count = jnp.where(section == source, size, count)
        count = jnp.clip(count - whole * dp, 0, whole)
        lengths = {min(max(size - whole * d, 0), whole) for size in sizes for d in range(dp_count)}
        for length in sorted(lengths):
            if length:

                @pl.when(count == length)
                def _():
                    wait_bytes(r.share.at[pl.ds(0, length)], r.share_recv)

    def store_norm_shares():
        shares = (r.gain_share, r.shift_share)
        count = GSEGMENT // dp_count
        for share in shares:
            share[...] = jnp.zeros(share.shape, F32)
        for source in range(ranks):
            for device in range(dp_count):
                start = device * count
                wide_norm = source % 2 == 1
                used = {1: 2 * C_OUT, 3: C_OUT}.get(source, 2 * C_MID)
                if start >= used:
                    continue

                @pl.when((section == source) & (dp == device))
                def _():
                    for i, share in enumerate(shares):
                        if wide_norm:
                            norm = start // C_OUT + (2 if source == 3 else 0)
                            place_in = start % C_OUT
                            at = C_MID + norm * wide + place_in % wide
                            share[...] = r.gains[place_in // wide, pl.ds(i, 1), pl.ds(at, count)]
                        else:
                            at = part * (source + start // C_MID)
                            for t in range(ranks):
                                share[:, pl.ds(part * t, part)] = r.gains[t, pl.ds(i, 1), pl.ds(at, part)]

    def gradients_sent():
        for group, (pair, near, total) in enumerate(
            ((r.dw_pair, r.dw_near, r.dw_sum), (r.da_pair, r.da_near, r.da_sum))
        ):
            wait_bytes(pair, r.pair_send.at[group])
            wait_bytes(total, r.share_send.at[group])
            if not lined or group == 1:
                wait_bytes(near, r.near_send.at[group])
                continue

            @pl.when(at_end)
            def _():
                wait_bytes(near.at[pl.ds(0, 2)], r.near_send.at[group])
                wait_bytes(r.dw_relay, r.relay_send)

            @pl.when(jnp.logical_not(at_end))
            def _():
                wait_bytes(near, r.near_send.at[group])

        for number in HELD:
            shipped(number)

    def do_dh2(m):
        value = sum_finish(SUM_DH2, m).astype(BF16).astype(F32)
        narrow_upstream(N22, 2, B22, m, value)

    norm_sent(narrow, 0, 4)
    stage(do_dh2)
    b0_sent()
    for number in (A0, C0, P0, A1, B1, C1):

        @pl.when(section != SOURCE[number])
        def _():
            count = pieces[number].shape[0] // parts(number)
            times = 3 if parts(number) == 4 else 1
            wait_bytes(pieces[number].at[pl.ds(0, times * count)], r.pass_send.at[number])

        @pl.when(section == SOURCE[number])
        def _():
            for _ in range(ranks - 1):
                wait_bytes(quarter_of(number, 0), r.piece_send.at[number])
    make(C1, lambda at: r.get[GET_H2, :, :, at], r.ddzd[...], 256)

    def do_ddzb(m):
        get_start(GET_DDZB, m, narrow_change(N22, 2, B22, m))

    stage(do_ddzb)
    fold(C1)

    def fan_out(m, event, weight):
        r.fan[pl.ds(PAD, rows), :] = dot_back(r.get[event, m], weight[...])

    def do_da2(m):
        get_finish(GET_DDZB, m)
        fan_out(m, GET_DDZB, r.b1)
        total = None
        for k, (down, right) in enumerate(second_taps()):
            term = slid(r.fan, pl.ds(k * part, part), -down, -right)
            total = term if total is None else total + term
        narrow_upstream(N21, 1, B21, m, total)

    stage(do_da2)

    @pl.when(section != 0)
    def _():
        wait_bytes(a0_others, r.all_recv.at[0])
        for k in range(1, ranks):
            block = r.a0_all.at[half_rows, lanes_of(other(k))]
            remote(block, block, r.all_send.at[1], r.all_recv.at[1], sibling).start()

    relay(C1)

    def do_ddza(m):
        get_start(GET_DDZA, m, narrow_change(N21, 1, B21, m))

    stage(do_ddza)
    make(B1, lambda at: r.patches[1, :, :, at], r.get[GET_DDZB], 128)
    finish(C1)

    def do_dy1(m):
        value = dot_back(get_finish(GET_DDZA, m), r.a1[...]) + r.skip[m].astype(F32)
        value = value.astype(BF16).astype(F32)
        before, main, short = before1(m)
        upstream = value * silu_slope(before)
        r.uw[m] = upstream
        sums = upstream_sums(upstream, [main, short])
        if lay.fast:
            joint_start(B11, m, sums)
        else:
            norm_start(double, B11, m, sums)

    stage(do_dy1)
    stage_joint(joint_line, B11)
    flush()
    each_micro(send_output)
    make(A1, lambda at: y1[:, :, at], r.get[GET_DDZA], 256)
    fold(B1)
    stage_joint(joint_back, B11)

    def do_ddzc(m):
        totals = joint_finish(B11, m) if lay.fast else norm_finish(double, B11, m)
        plain = rows_of(totals, 0)
        for norm, at, target in ((N11, 2, r.ddzd), (N12, 4, r.ddzs)):
            sums = [plain, rows_of(totals, at)]
            add_gains(C_MID + norm * wide, sums)
            found = moments_of(r.stat_w, norm, m)
            normed = normalized(zw[norm, m], found)
            target[m] = norm_change(r.uw[m], normed, found, affine_w(norm)[0], sums, 1)
        sum_start(SUM_DH0, m, dot_back(r.ddzd[m], r.c0[...]))

    stage(do_ddzc)
    flush()
    fold(A1)

    def do_dxs(m):
        r.dxs_send[m] = dot_back(r.ddzs[m], r.p0[...]).astype(BF16)

    each_micro(do_dxs)
    make(C0, lambda at: r.get[GET_H0, :, :, at], r.ddzd[...], 256)
    make(P0, lambda at: r.x[0, :, :, at], r.ddzs[...], 256)

    def do_dh0(m):
        value = sum_finish(SUM_DH0, m).astype(BF16).astype(F32)
        narrow_upstream(N02, 0, B02, m, value)

    def send_dxs(m):
        own_start(1, m, r.dxs_send.at[m], r.dxs_recv.at[section])

    stage(do_dh0)
    relay(B1)
    relay(A1)

    def do_ddz2(m):
        get_start(GET_DDZ2, m, narrow_change(N02, 0, B02, m))

    stage(do_ddz2)
    fold(C0)
    fold(P0)
    finish(A1)
    finish(B1)
    flush()

    def do_da1(m):
        get_wait(GET_DDZ2, m)

        @pl.when(m == micro - 2)
        def _():
            each_micro(send_dxs)

        fan_out(m, GET_DDZ2, r.b0)
        gain, shift = affine_n(N01)
        found = moments_of(r.stat_n, N01, m)
        sums = None
        for phase in range(4):
            total = None
            for k, (at, down, right) in enumerate(first_taps()):
                if at == phase:
                    term = slid(r.fan, pl.ds(k * part, part), -down, -right)
                    total = term if total is None else total + term
            normed = normalized(z1[phase, m], found)
            upstream = total * silu_slope(normed * gain + shift)
            r.u1[phase, m] = upstream
            terms = upstream_sums(upstream, [normed])
            sums = terms if sums is None else [a + b for a, b in zip(sums, terms)]
        norm_start(narrow, B01, m, sums)

    stage(do_da1)
    flush()
    relay(C0)
    relay(P0)
    make(B0, lambda at: r.patches[0, :, :, at], r.get[GET_DDZ2], 128)
    make(B0_REST, lambda at: r.patches[0, :, :, at], r.get[GET_DDZ2], 128, HEIGHTS[B0])
    fold(B0)
    fold(B0_REST)
    relay(B0)

    out_own = r.out_own
    wait_bytes(out_own.at[:, mine_wide], r.own_copy.at[0])
    wait_bytes(out_own.at[:, pl.ds(0, C_OUT - wide)], r.own_recv.at[0])
    def store_grid(refs, values, pick):
        for group, ref in enumerate(refs):
            start, used = lay.spans[group][0], lay.used[group]
            side, crops = lay.sides[group], lay.crops[group]
            grid = values[start : start + used].astype(BF16).reshape(side, side, crops, values.shape[1])
            pick(ref, grid)

    def store_output(ref, grid):
        ref[...] = grid

    store_grid((r.out_grid, r.out_grid_2), out_own[...].astype(F32), store_output)
    results = [
        pltpu.make_async_copy(src, dst, r.result_sem.at[i])
        for i, (src, dst) in enumerate(
            (
                (r.out_grid, r.out),
                (r.out_grid_2, r.out_2),
                (r.grad_grid, r.grad),
                (r.grad_grid_2, r.grad_2),
            )
        )
    ]
    results[0].start()
    results[1].start()

    def do_ddz1(m):
        totals = norm_finish(narrow, B01, m)
        sums = [rows_of(totals, 0), rows_of(totals, 2)]
        add_gains(0, sums)
        found = moments_of(r.stat_n, N01, m)
        gain = affine_n(N01)[0]
        for phase in range(4):
            normed = normalized(z1[phase, m], found)
            r.ddz1[phase, m] = norm_change(r.u1[phase, m], normed, found, gain, sums, 4)
        own_start(2, m, r.ddz1.at[:, m], r.ddz1_own.at[:, :, mine])

    each_micro(do_ddz1)
    ship(C1)
    ship(B1)
    ship(A1)
    for k in range(1, ranks):
        remote(
            r.gains.at[section],
            r.gains.at[section],
            r.gain_send,
            r.gain_recv,
            (other(k), dp),
        ).start()

    def da0_step(i, carry):
        at = pl.ds(pl.multiple_of(i * 128, 128), 128)
        total = None
        for phase in range(4):
            value = dot_rows(
                r.x[phase, :, :, at].reshape(micro * rows, 128),
                r.ddz1[phase].reshape(micro * rows, part),
            )
            total = value if total is None else total + value
        da0 = r.da if lay.fast else r.da0
        da0[pl.ds(pl.multiple_of(i * 128, 128), 128), :] = total.astype(BF16)
        return carry

    lax.fori_loop(0, C_IN // 128, da0_step, 0)
    to_sibling(A0)
    finish(C0)
    relay(B0_REST)
    fold(A0)
    finish(P0)
    finish(B0)
    finish(B0_REST)
    finish(A0)

    dxs, ddz1_own = r.dxs_recv, r.ddz1_own

    @pl.when(section != 0)
    def _():
        wait_bytes(a0_others, r.all_recv.at[1])

    wait_bytes(dxs.at[0], r.own_copy.at[1])
    wait_bytes(dxs.at[pl.ds(0, ranks - 1)], r.own_recv.at[1])
    wait_bytes(ddz1_own.at[:, :, mine], r.own_copy.at[2])
    wait_bytes(ddz1_own.at[:, :, pl.ds(0, C_MID - part)], r.own_recv.at[2])
    for phase in range(4):
        value = dot_back(ddz1_own[phase], r.a0_all[...])
        if phase == 0:
            extra = dxs[0].astype(F32)
            for k in range(1, ranks):
                extra = extra + dxs[k].astype(F32)
            value = value + extra.astype(BF16).astype(F32)

        def store_phase(ref, grid):
            ref[:, phase // 2, :, phase % 2] = grid

        store_grid((r.grad_grid, r.grad_grid_2), value, store_phase)
    wait_bytes(r.gains.at[pl.ds(0, ranks - 1)], r.gain_recv)
    if lay.fast:
        store_norm_shares()
    else:
        r.gains_out[...] = r.gains[...]

    results[2].start()
    results[3].start()
    if lay.fast:
        finish_shares()
        results.append(pltpu.make_async_copy(r.share, r.share_out, r.result_sem.at[4]))
        results[4].start()
        gradients_sent()

    wait_bytes(r.sum_recv, r.sum_send_sem)
    wait_bytes(r.get.at[:, :, :, pl.ds(0, C_MID - part)], r.get_send_sem)
    norm_sent(narrow, 4, 8)
    if lay.fast:
        norm_sent(broad, 0, 2)
        wait_bytes(r.joint_pair, r.joint_send.at[0])
        wait_bytes(r.joint_line.at[:, :, pl.ds(0, dp_count // 2 - 1)], r.joint_send.at[1])
        wait_bytes(r.joint_pair, r.joint_send.at[2])
    else:
        norm_sent(broad, 3, 4)
        norm_sent(double, 0, 1)
    for copy in results:
        copy.wait()
    wait_bytes(out_own.at[:, pl.ds(0, C_OUT - wide)], r.own_send.at[0])
    wait_bytes(dxs.at[pl.ds(0, ranks - 1)], r.own_send.at[1])
    wait_bytes(ddz1_own.at[:, :, pl.ds(0, C_MID - part)], r.own_send.at[2])

    @pl.when(section == 0)
    def _():
        wait_bytes(a0_others, r.all_send.at[0])

    @pl.when(section != 0)
    def _():
        wait_bytes(a0_others.at[:, pl.ds(0, (ranks - 2) * part)], r.all_send.at[0])
        wait_bytes(a0_others, r.all_send.at[1])

    wait_bytes(r.gains.at[pl.ds(0, ranks - 1)], r.gain_send)
    for i in range(2):
        wait_bytes(scales.at[i, pl.ds(0, ranks - 1)], r.scale_send.at[i])


def chain(lay, ranks, dp_count, operands):
    micro, rows = lay.micro, lay.rows
    part, wide = C_MID // ranks, C_OUT // ranks
    table = scratch_table(lay, ranks, dp_count)
    shapes = (
        *[jax.ShapeDtypeStruct(grid_shape(lay, group, 1, C_OUT), BF16) for group in range(2)],
        *[jax.ShapeDtypeStruct(phase_shape(lay, group), BF16) for group in range(2)],
    )
    if lay.fast:
        shapes += (jax.ShapeDtypeStruct((1, GSEGMENT // dp_count), F32),) * 2
        shapes += (jax.ShapeDtypeStruct((ROWS // dp_count, C_MID), BF16),)
    else:
        shapes += (
            jax.ShapeDtypeStruct((ranks, 2, C_MID + 3 * wide), F32),
            jax.ShapeDtypeStruct((ROWS, C_MID), BF16),
            jax.ShapeDtypeStruct((C_IN, part), BF16),
        )
    anywhere = pl.BlockSpec(memory_space=pl.ANY)
    inside = pl.BlockSpec(memory_space=pltpu.VMEM)
    return pl.pallas_call(
        functools.partial(chain_kernel, lay, ranks, dp_count, tuple(table)),
        out_shape=shapes,
        in_specs=[anywhere] * 5 + [inside] * 3,
        out_specs=[anywhere] * 4 + ([inside] * 2 + [anywhere] if lay.fast else [inside, anywhere, inside]),
        scratch_shapes=list(table.values()),
        compiler_params=pltpu.CompilerParams(
            collective_id=0, has_side_effects=True, vmem_limit_bytes=63 * 2**20
        ),
        name="chain",
    )(*operands)


def summed_gradient(slices, small, section, ranks):
    small = jnp.stack([small] + [jnp.zeros_like(small)] * (ranks - 1))
    slices = slices.reshape(ranks, ROWS // ranks, C_MID)
    arrived = lax.all_to_all(slices, "section", 0, 0, tiled=True).astype(F32)
    arrived_small = lax.all_to_all(small, "section", 0, 0, tiled=True).astype(F32)
    segment = segment_gradient(arrived, arrived_small, section, ranks)
    return lax.psum_scatter(segment.reshape(-1), "dp", scatter_dimension=0, tiled=True)


def norm_shares(gains, ranks, dp_count):
    part, wide = C_MID // ranks, C_OUT // ranks

    def joined(start, width):
        block = gains[:, :, start : start + width // ranks]
        return jnp.moveaxis(block, 0, 1).reshape(2, width)

    f01, f02, f21, f22 = [joined(part * i, C_MID) for i in range(4)]
    f11, f12, f31 = [joined(C_MID + wide * i, C_OUT) for i in range(3)]
    blank = jnp.zeros((2, GSEGMENT - 2 * C_MID), F32)
    segments = jnp.stack(
        [
            jnp.concatenate([f01, f02, blank], 1),
            jnp.concatenate([f11, f12], 1),
            jnp.concatenate([f21, f22, blank], 1),
            jnp.concatenate([f31, jnp.zeros((2, GSEGMENT - C_OUT), F32)], 1),
        ]
    )
    share = GSEGMENT // dp_count
    own_norms = lax.dynamic_index_in_dim(segments, lax.axis_index("section"), 0, keepdims=False)
    return lax.dynamic_slice_in_dim(own_norms, lax.axis_index("dp") * share, share, 1)


def deliver_kernel(ranks, *refs):
    plain, share_in, norms_in, refs = refs[:4], refs[4], refs[5:7], refs[7:]
    plain_out, share_out, norms_out, refs = refs[:4], refs[4], refs[5:7], refs[7:]
    held, share, order, load_sem, store_sem = refs[:4], refs[4], refs[5], refs[6], refs[7]
    loads = [
        pltpu.make_async_copy(src, dst, load_sem.at[i])
        for i, (src, dst) in enumerate(zip(plain + (share_in,), held + (share,)))
    ]
    stores = [
        pltpu.make_async_copy(src, dst, store_sem.at[i])
        for i, (src, dst) in enumerate(zip(held + (order,), plain_out + (share_out,)))
    ]
    turn = (4, 2, 0, 3, 1)
    for i in turn:
        loads[i].start()
    for src, dst in zip(norms_in, norms_out):
        dst[...] = src[...]
    whole, lanes = share.shape[0], 128
    for i in turn:
        loads[i].wait()
        if i == 4:
            odd = lax.rem(lax.axis_index("section"), 2)

            @pl.when(odd == 0)
            def _():
                for q in range(ranks):
                    order[pl.ds(q, whole, stride=ranks), :] = share[:, lanes * q : lanes * (q + 1)].astype(F32)

            @pl.when(odd == 1)
            def _():
                short = whole // ranks
                for t in range(ranks):
                    for q in range(ranks):
                        order[pl.ds(ranks * t + q, short, stride=ranks * ranks), :] = share[
                            t * short : (t + 1) * short, lanes * q : lanes * (q + 1)
                        ].astype(F32)

        stores[i].start()
    for i in turn:
        stores[i].wait()


def deliver(results, ranks):
    plain, norms, share = results[:4], results[4:6], results[6]
    order = jax.ShapeDtypeStruct((share.size // 128, 128), F32)
    anywhere = pl.BlockSpec(memory_space=pl.ANY)
    inside = pl.BlockSpec(memory_space=pltpu.VMEM)
    specs = [anywhere] * 5 + [inside] * 2
    like = [jax.ShapeDtypeStruct(v.shape, v.dtype) for v in plain]
    return pl.pallas_call(
        functools.partial(deliver_kernel, ranks),
        out_shape=like + [order] + [jax.ShapeDtypeStruct(v.shape, v.dtype) for v in norms],
        in_specs=specs,
        out_specs=specs,
        scratch_shapes=[pltpu.VMEM(v.shape, v.dtype) for v in list(plain) + [share, order]]
        + [pltpu.SemaphoreType.DMA((5,))] * 2,
        name="deliver",
    )(*plain, share, *norms)


def per_device(
    images_global, images_local, weights, norm_gains, norm_shifts, cotangent_global, cotangent_local
):
    section = lax.axis_index("section")
    ranks = lax.axis_size("section")
    dp_count = lax.axis_size("dp")
    lay = Layout(images_global.shape, images_local.shape, dp_count)
    micro, rows = lay.micro, lay.rows
    part = C_MID // ranks
    wide = C_OUT // ranks

    def cells_first(pictures):
        return jnp.moveaxis(pictures, 1, 3)

    masks = np.stack(
        [lay.valid(down, right) for down in (-1, 0, 1) for right in (-1, 0, 1)]
    ).astype(np.float32)
    masks = jnp.asarray(np.ascontiguousarray(np.broadcast_to(masks[:, :, None], (9, rows, part))))
    results = chain(
        lay,
        ranks,
        dp_count,
        (
            cells_first(images_global),
            cells_first(images_local),
            cells_first(cotangent_global),
            cells_first(cotangent_local),
            weights.reshape(-1, 128),
            norm_gains[None],
            norm_shifts[None],
            masks,
        ),
    )

    if lay.fast:
        results = deliver(results, ranks)
    out_global, out_local, grad_global, grad_local, *rest = results
    if lay.fast:
        share, gain_share, shift_share = rest
        own_norms, weight_gradient = (gain_share[0], shift_share[0]), share.reshape(-1)
    else:
        own_norms = norm_shares(rest[0], ranks, dp_count)
        weight_gradient = summed_gradient(*rest[1:], section, ranks)

    def crops_first(grid, side, crops):
        return jnp.moveaxis(grid.reshape(1, side, side, crops, -1), 3, 1)

    return (
        crops_first(out_global, lay.sides[0], lay.crops[0]),
        crops_first(out_local, lay.sides[1], lay.crops[1]),
        crops_first(grad_global, 2 * lay.sides[0], lay.crops[0]),
        crops_first(grad_local, 2 * lay.sides[1], lay.crops[1]),
        weight_gradient,
        own_norms[0],
        own_norms[1],
    )


def solution(mesh):
    images = P(None, "dp", None, None, None)
    made = P("section", "dp", None, None, None)
    return jax.shard_map(
        per_device,
        mesh=mesh,
        in_specs=(images, images, P("section"), P("section"), P("section"), images, images),
        out_specs=(made, made, made, made) + (P(("section", "dp")),) * 3,
        check_vma=False,
    )
```

```python
import functools
from types import SimpleNamespace

import jax
import jax.numpy as jnp
import numpy as np
from jax import lax
from jax.experimental import pallas as pl
from jax.experimental.pallas import tpu as pltpu
from jax.sharding import PartitionSpec as P

C_IN = 1024
C_MID = 512
C_OUT = 2048
WSEGMENT = 3407872
GSEGMENT = 4096
EPSILON = 1e-05
F32 = jnp.float32
BF16 = jnp.bfloat16


def round_up(value, unit):
    return -(-value // unit) * unit


class Layout:
    def __init__(self, shape_global, shape_local, dp_count):
        self.micro = shape_global[0]
        self.crops = (shape_global[1], shape_local[1])
        self.sides = (shape_global[2] // 2, shape_local[2] // 2)
        used = [crops * side * side for crops, side in zip(self.crops, self.sides)]
        self.used = used
        first = round_up(used[0], 8)
        self.rows = round_up(first + round_up(used[1], 8), 16)
        self.spans = ((0, first), (first, self.rows))
        self.totals = [count * dp_count for count in used]
        self.fast = dp_count == 8 and WSEGMENT // C_MID // dp_count % 64 == 0

    def valid(self, down, right):
        flags = np.zeros((self.rows,), bool)
        for (start, _), crops, side in zip(self.spans, self.crops, self.sides):
            for crop in range(crops):
                for i in range(side):
                    for j in range(side):
                        inside = 0 <= i + down < side and 0 <= j + right < side
                        flags[start + (i * side + j) * crops + crop] = inside
        return flags


def first_taps():
    return [
        (2 * (p != 1) + (q != 1), -(p == 0), -(q == 0)) for p in range(3) for q in range(3)
    ]


def second_taps():
    return [(p - 1, q - 1) for p in range(3) for q in range(3)]


def segment_gradient(pieces, small, section, ranks):
    part = C_MID // ranks
    total_rows = WSEGMENT // C_MID

    def finished(rows):
        return jnp.pad(rows, ((0, total_rows - rows.shape[0]), (0, 0)))

    def across(block):
        return block.transpose(1, 0, 2).reshape(-1, C_MID)

    def spatial(block):
        return block.reshape(ranks, 9, part, C_MID).transpose(1, 0, 2, 3).reshape(-1, C_MID)

    def first():
        return finished(
            jnp.concatenate(
                [small.transpose(1, 0, 2).reshape(-1, C_MID), spatial(pieces[:, : 9 * part])]
            )
        )

    def second():
        return finished(across(pieces[:, : C_MID + C_IN]))

    def third():
        tall = C_OUT // ranks
        return finished(
            jnp.concatenate(
                [pieces[:, :tall].reshape(-1, C_MID), spatial(pieces[:, tall : tall + 9 * part])]
            )
        )

    def fourth():
        return finished(across(pieces[:, :C_MID]))

    return lax.switch(section, [first, second, third, fourth])


MESH = pl.DeviceIdType.MESH
ROWS = WSEGMENT // C_MID
SUM_Z2, SUM_ZA, SUM_ZB, SUM_DH2, SUM_DH0 = range(5)
GET_H0, GET_H2, GET_DDZB, GET_DDZA, GET_DDZ2 = range(5)
F01, F02, F21, F22, B22, B21, B02, B01 = range(8)
F31, B31 = range(2)
F12, F11, F31_LATE, B31_LATE = range(4)
B11, J12, J11 = range(3)
N01, N02, N21, N22 = range(4)
N11, N12, N31 = range(3)
A0, B0, C0, P0, A1, B1, C1 = range(7)
SOURCE = (0, 0, 1, 1, 2, 2, 3, 0)
PAD = 16
SLOTS = 3
HELD = (4, 5, 6)
READY = 640
HEIGHTS = (0, C_MID, C_MID, C_IN, C_OUT // 4, 9 * C_MID // 4, C_MID, 5 * C_MID // 4)
B0_REST = 7


def dot(left, right):
    return lax.dot_general(left, right, (((1,), (0,)), ((), ())), preferred_element_type=F32)


def dot_back(left, right):
    return lax.dot_general(left, right, (((1,), (1,)), ((), ())), preferred_element_type=F32)


def dot_rows(left, right):
    return lax.dot_general(left, right, (((0,), (0,)), ((), ())), preferred_element_type=F32)


def silu(value):
    return value * jax.nn.sigmoid(value)


def silu_slope(before):
    sigmoid = jax.nn.sigmoid(before)
    return sigmoid * (1.0 + before * (1.0 - sigmoid))


def grid_shape(lay, group, fold, channels):
    side = fold * lay.sides[group]
    return (side, side, lay.crops[group], channels)


def phase_shape(lay, group):
    side = lay.sides[group]
    return (side, 2, side, 2, lay.crops[group], C_IN)


def scratch_table(lay, ranks, dp_count):
    micro, rows = lay.micro, lay.rows
    part, wide = C_MID // ranks, C_OUT // ranks
    others = ranks - 1
    vmem, dma = pltpu.VMEM, pltpu.SemaphoreType.DMA
    return dict(
        x=vmem((4, micro, rows, C_IN), BF16),
        cot=vmem((micro, rows, wide), BF16),
        x_grid=vmem((2,) + grid_shape(lay, 0, 2, C_IN), BF16),
        x_grid_2=vmem((2,) + grid_shape(lay, 1, 2, C_IN), BF16),
        cot_grid=vmem((micro,) + grid_shape(lay, 0, 1, wide), BF16),
        cot_grid_2=vmem((micro,) + grid_shape(lay, 1, 1, wide), BF16),
        a0=vmem((C_IN, part), BF16),
        b0=vmem((9 * part, C_MID), BF16),
        c0=vmem((C_MID, wide), BF16),
        p0=vmem((C_IN, wide), BF16),
        a1=vmem((wide, C_MID), BF16),
        b1=vmem((9 * part, C_MID), BF16),
        c1=vmem((C_MID, wide), BF16),
        a0_all=vmem((C_IN, C_MID), BF16),
        raw=vmem((SLOTS, 2048, 128), BF16),
        raw_sem=dma((SLOTS,)),
        scales=vmem((2, ranks, 1, GSEGMENT), F32),
        z1=vmem((4, micro, rows, part), F32),
        u1=vmem((4, micro, rows, part), F32),
        zn=vmem((3, micro, rows, part), F32),
        un=vmem((3, micro, rows, part), F32),
        zw=vmem((3, micro, rows, wide), F32),
        uw=vmem((micro, rows, wide), F32),
        y1=vmem((micro, rows, wide), BF16),
        skip=vmem((micro, rows, wide), BF16),
        ddzd=vmem((micro, rows, wide), BF16),
        ddzs=vmem((micro, rows, wide), BF16),
        patches=vmem((2, micro, rows, 9 * part), BF16),
        slide=vmem((PAD + rows + PAD, part), F32),
        fan=vmem((PAD + rows + PAD, 9 * part), F32),
        stat_n=vmem((4, micro, 8, part), F32),
        stat_w=vmem((3, micro, 8, wide), F32),
        sum_send=vmem((5, micro, rows, C_MID), BF16),
        sum_recv=vmem((5, micro, others, rows, part), BF16),
        get=vmem((5, micro, rows, C_MID), BF16),
        norm_n=vmem((4, micro, dp_count, 4, part), F32),
        norm_w=vmem((2 if lay.fast else 3, micro, dp_count, 4, wide), F32),
        **joint_scratch(lay, dp_count, wide),
        out_send=vmem((micro, rows, wide), BF16),
        out_own=vmem((rows, C_OUT), BF16),
        out_grid=vmem(grid_shape(lay, 0, 1, C_OUT), BF16),
        out_grid_2=vmem(grid_shape(lay, 1, 1, C_OUT), BF16),
        grad_grid=vmem(phase_shape(lay, 0), BF16),
        grad_grid_2=vmem(phase_shape(lay, 1), BF16),
        result_sem=dma((5,)),
        dxs_send=vmem((micro, rows, C_IN), BF16),
        dxs_recv=vmem((ranks, rows, C_IN), BF16),
        ddz1=vmem((4, micro, rows, part), BF16),
        ddz1_own=vmem((4, rows, C_MID), BF16),
        gains=vmem((ranks, 2, C_MID + 3 * wide), F32),
        x_sem=dma((2, 2)),
        cot_sem=dma((2,)),
        piece_send=dma((7,)),
        piece_recv=dma((7,)),
        pass_send=dma((7,)),
        pass_recv=dma((7, 3)),
        eight_send=dma,
        eight_recv=dma((4, 3)),
        scale_send=dma((2,)),
        scale_recv=dma((2,)),
        all_send=dma((2,)),
        all_recv=dma((2,)),
        sum_send_sem=dma,
        sum_recv_sem=dma((5, micro)),
        get_send_sem=dma,
        get_recv_sem=dma((5, micro)),
        norm_n_send=dma((2,)),
        norm_n_recv=dma((4, micro)),
        norm_w_send=dma((2,)),
        norm_w_recv=dma((2 if lay.fast else 3, micro)),
        own_send=dma((3,)),
        own_recv=dma((3,)),
        own_copy=dma((3,)),
        gain_send=dma,
        gain_recv=dma,
        **gradient_scratch(lay, ranks, dp_count),
    )


def joint_scratch(lay, dp_count, wide):
    vmem, dma, micro = pltpu.VMEM, pltpu.SemaphoreType.DMA, lay.micro
    if not lay.fast:
        return dict(
            norm_v=vmem((1, micro, dp_count, 8, wide), F32),
            norm_v_send=dma((1,)),
            norm_v_recv=dma((1, micro)),
        )
    return dict(
        joint=vmem((3, micro, 8, wide), F32),
        joint_all=vmem((3, micro, 8, wide), F32),
        joint_pair=vmem((3, micro, 8, wide // 2), F32),
        joint_line=vmem((3, micro, dp_count // 2, 8, wide // 2), F32),
        joint_send=dma((3,)),
        joint_recv=dma((2, 3, micro)),
    )


def gradient_scratch(lay, ranks, dp_count):
    vmem, dma = pltpu.VMEM, pltpu.SemaphoreType.DMA
    if not lay.fast:
        return dict(
            stage=vmem((256, C_MID), BF16),
            stage_sem=dma,
            ready=vmem((ranks * READY, C_MID), BF16),
        )
    part = C_MID // ranks
    height, chips = sum(HEIGHTS), dp_count // 2
    return dict(
        dw=vmem((height, C_MID), BF16),
        dw_pair=vmem((height // 2, C_MID), BF16),
        dw_near=vmem((chips - 1, height // dp_count, C_MID), BF16),
        dw_sum=vmem((height // dp_count, C_MID), BF16),
        da=vmem((C_IN, part), BF16),
        da_pair=vmem((C_IN // 2, part), BF16),
        da_near=vmem((chips - 1, C_IN // dp_count, part), BF16),
        dw_relay=vmem((height // dp_count, C_MID), BF16),
        da_relay=vmem((C_IN // dp_count, part), BF16),
        relay_send=dma,
        relay_recv=dma((8,)),
        da_sum=vmem((C_IN // dp_count, part), BF16),
        share=vmem((ROWS // dp_count, C_MID), BF16),
        pair_send=dma((2,)),
        pair_recv=dma((8,)),
        near_send=dma((2,)),
        near_recv=dma((8,)),
        share_send=dma((2,)),
        share_recv=dma,
        hold=vmem((ROWS // dp_count, C_MID), BF16),
        hold_2=vmem((ROWS // dp_count // ranks, C_MID), BF16),
        hold_recv=dma((3,)),
        ship_send=dma((3,)),
    )


def chain_kernel(lay, ranks, dp_count, names, *refs):
    inputs = ("x_in", "x_in_2", "cot_in", "cot_in_2", "w_in", "gains_in", "shifts_in", "masks")
    outputs = ("out", "out_2", "grad", "grad_2")
    outputs += ("gain_share", "shift_share", "share_out") if lay.fast else ("gains_out", "dw", "da0")
    r = SimpleNamespace(**dict(zip(inputs + outputs + names, refs)))
    pieces = (r.a0, r.b0, r.c0, r.p0, r.a1, r.b1, r.c1)
    micro, rows = lay.micro, lay.rows
    first = lay.spans[0][1]
    part, wide = C_MID // ranks, C_OUT // ranks
    section, dp = lax.axis_index("section"), lax.axis_index("dp")
    core = lax.rem(dp, 2)
    sibling = (section, dp + 1 - 2 * core)
    masks = r.masks
    mine = pl.ds(pl.multiple_of(section * part, part), part)
    mine_wide = pl.ds(pl.multiple_of(section * wide, wide), wide)

    def other(k):
        return lax.rem(section + k, ranks)

    def across_dp(act):
        if dp_count <= 8:
            for k in range(1, dp_count):
                act((section, lax.rem(dp + k, dp_count)))
        else:

            def step(k, carry):
                act((section, lax.rem(dp + k, dp_count)))
                return carry

            lax.fori_loop(1, dp_count, step, 0)

    def remote(src, dst, send, recv, device):
        return pltpu.make_async_remote_copy(
            src_ref=src,
            dst_ref=dst,
            send_sem=send,
            recv_sem=recv,
            device_id=device,
            device_id_type=MESH,
        )

    def wait_bytes(ref, sem):
        pltpu.make_async_copy(ref, ref, sem).wait()

    def some_micros(body, first_micro, last_micro):
        def step(m, carry):
            body(m)
            return carry

        lax.fori_loop(first_micro, last_micro, step, 0)

    def each_micro(body):
        some_micros(body, 0, micro)

    waiting = []

    def flush():
        while waiting:
            waiting.pop()(micro - 1)

    def stage(body):
        if not waiting:
            some_micros(body, 0, micro - 1)
        else:
            before = waiting.pop()

            def step(i, carry):
                @pl.when(i == 1)
                def _():
                    before(micro - 1)

                @pl.when(i != 1)
                def _():
                    body(jnp.maximum(i - 1, 0))

                return carry

            lax.fori_loop(0, micro, step, 0)
        waiting.append(body)

    barrier = pltpu.get_barrier_semaphore()

    def greet(device):
        pl.semaphore_signal(barrier, inc=1, device_id=device, device_id_type=MESH)

    if lay.fast:
        r.share[...] = jnp.zeros(r.share.shape, BF16)
        for k in range(ranks):
            for j in range(dp_count):
                if k or j:
                    greet((other(k), lax.rem(dp + j, dp_count)))
        greetings = ranks * dp_count - 1
    else:
        across_dp(greet)
        for k in range(1, ranks):
            greet((other(k), dp))
        greetings = dp_count - 1 + ranks - 1

    def load_grids(m):
        slot = m % 2
        return (
            pltpu.make_async_copy(r.x_in.at[m], r.x_grid.at[slot], r.x_sem.at[0, slot]),
            pltpu.make_async_copy(r.x_in_2.at[m], r.x_grid_2.at[slot], r.x_sem.at[1, slot]),
        )

    for m in range(2):
        for copy in load_grids(m):
            copy.start()
    r.slide[...] = jnp.zeros(r.slide.shape, F32)
    r.fan[...] = jnp.zeros(r.fan.shape, F32)

    place = lax.rem(dp, 4)
    group = dp - place
    pair_place = lax.rem(place + 2, 4)
    pair = (section, group + pair_place)

    place_8 = lax.rem(dp, 8)
    group_8 = dp - place_8
    chip_8 = place_8 // 2
    EIGHTH, STEP = 9 * part // 8, 3 * part // 8

    def eighth(which, step):
        return r.b0.at[pl.ds(pl.multiple_of(EIGHTH * which + STEP * step, 16), STEP)]

    def eight_copy(way, step, src, dst, device):
        remote(src, dst, r.eight_send, r.eight_recv.at[way, step], device).start()

    def send_b0():
        for step in range(3):
            for k in range(1, ranks):
                row = READY * other(k) + 16 * place_8 + STEP * step
                src = ready.at[pl.ds(pl.multiple_of(row, 16), STEP)]
                eight_copy(0, step, src, eighth(place_8, step), (other(k), dp))

    def pass_on_b0(step):
        @pl.when(section != 0)
        def _():
            own = eighth(place_8, step)
            wait_bytes(own, r.eight_recv.at[0, step])
            for k in range(1, 4):
                target = lax.rem(chip_8 + k, 4)
                eight_copy(1, step, own, own, (section, group_8 + 2 * target + core))
            eight_copy(2, step, own, own, sibling)

    def pass_back_b0(step):
        @pl.when(section != 0)
        def _():
            wait_bytes(r.b0.at[pl.ds(0, 3 * STEP)], r.eight_recv.at[1, step])
            for k in range(1, 4):
                theirs = eighth(2 * lax.rem(chip_8 + k, 4) + core, step)
                eight_copy(3, step, theirs, theirs, sibling)

    def need_b0():
        @pl.when(section != 0)
        def _():
            for step in range(3):
                wait_bytes(r.b0.at[pl.ds(0, STEP)], r.eight_recv.at[2, step])
                wait_bytes(r.b0.at[pl.ds(0, 3 * STEP)], r.eight_recv.at[3, step])

    def b0_sent():
        @pl.when(section == 0)
        def _():
            wait_bytes(r.b0.at[pl.ds(0, 9 * STEP)], r.eight_send)

        @pl.when(section != 0)
        def _():
            wait_bytes(r.b0.at[pl.ds(0, 21 * STEP)], r.eight_send)

    ready = r.dw if lay.fast else r.ready

    def parts(number):
        return 2 if number in (A1, C1) else 4

    def place_in(number):
        return core if parts(number) == 2 else place

    def run_jobs(jobs):
        def load(number):
            start, count, _ = jobs[number]
            start = start if isinstance(start, int) else pl.multiple_of(start, 512)
            slot = number % SLOTS
            return pltpu.make_async_copy(
                r.w_in.at[pl.ds(start, count)], r.raw.at[slot, pl.ds(0, count)], r.raw_sem.at[slot]
            )

        for number in range(min(SLOTS, len(jobs))):
            load(number).start()
        for number, (_, count, use) in enumerate(jobs):
            load(number).wait()
            use(r.raw[number % SLOTS, pl.ds(0, count), :])
            if number + SLOTS < len(jobs):
                load(number + SLOTS).start()

    def by_rows(value):
        return value.reshape(value.shape[0] // 4, C_MID)

    def by_columns(value):
        return value.reshape(value.shape[0] // 16, C_OUT)

    def first_jobs(source):
        jobs = []

        def keep_a0(i):
            def use(value):
                r.a0_all[pl.ds(C_MID * i, C_MID), :] = by_rows(value)

            return (2048 * i, 2048, use)

        def keep_taps(base, row):
            def use(value):
                matrix = by_rows(value)
                for t in range(ranks):
                    if t != source:
                        ready[pl.ds(READY * t + row, part), :] = matrix[part * t : part * (t + 1)]

            return (2048 * base, 2048, use)

        def keep_wide(chunk, row):
            def use(value):
                matrix = by_columns(value)
                for t in range(ranks):
                    if t != source:
                        ready[pl.ds(READY * t + row, 128), :] = matrix[:, wide * t : wide * (t + 1)]

            return (2048 * chunk, 2048, use)

        def keep_tall(t):
            def use(value):
                ready[pl.ds(READY * t, 256), :] = by_rows(value)

            return (2048 * t + 1024 * core, 1024, use)

        if source == 0:
            jobs = [keep_a0(0), keep_a0(1)] + [keep_taps(2 + place_8 + j, part * j) for j in range(2)]
        elif source == 1:
            jobs = [keep_wide(place, 0)] + [keep_wide(4 + 2 * place + j, 128 + 128 * j) for j in range(2)]
        elif source == 2:
            jobs = [keep_tall(t) for t in range(ranks) if t != source]
            jobs += [keep_taps(4 + 2 * place + j, 256 + part * j) for j in range(3)]
        else:
            jobs = [keep_wide(2 * core + j, 128 * j) for j in range(2)]
        return jobs

    def own_jobs(source):
        def put(ref, row, count):
            def use(value):
                ref[pl.ds(row, count), :] = by_rows(value)

            return use

        def put_wide(ref, row):
            def use(value):
                ref[pl.ds(row, 128), :] = by_columns(value)[:, wide * source : wide * (source + 1)]

            return use

        if source == 0:
            return [(2048 * (2 + tap), 512, put(r.b0, part * tap, part)) for tap in range(9)]
        if source == 1:
            jobs = [(2048 * i, 2048, put_wide(r.c0, 128 * i)) for i in range(4)]
            return jobs + [(2048 * (4 + i), 2048, put_wide(r.p0, 128 * i)) for i in range(8)]
        if source == 2:
            jobs = [(2048 * source, 2048, put(r.a1, 0, wide))]
            start = 512 * source
            return jobs + [
                (2048 * (4 + tap) + start, 512, put(r.b1, part * tap, part)) for tap in range(9)
            ]
        return [(2048 * i, 2048, put_wide(r.c1, 128 * i)) for i in range(4)]

    def send_piece(number):
        count = pieces[number].shape[0] // parts(number)
        at = pl.ds(pl.multiple_of(place_in(number) * count, 32), count)
        for k in range(1, ranks):
            t = other(k)
            if number == A0:
                src = r.a0_all.at[at, pl.ds(pl.multiple_of(t * part, part), part)]
            else:
                row = {B1: 256 + 32 * place, P0: 128}.get(number, 0)
                src = ready.at[pl.ds(pl.multiple_of(READY * t + row, 32), count)]
            remote(
                src,
                pieces[number].at[at],
                r.piece_send.at[number],
                r.piece_recv.at[number],
                (t, dp),
            ).start()

    def quarter_of(number, which):
        ref = pieces[number]
        count = ref.shape[0] // parts(number)
        return ref.at[pl.ds(pl.multiple_of(which * count, 32), count)]

    def pass_quarter(number, way, which, device):
        quarter = quarter_of(number, which)
        remote(
            quarter, quarter, r.pass_send.at[number], r.pass_recv.at[number, way], device
        ).start()

    def pass_on(number):
        @pl.when(section != SOURCE[number])
        def _():
            own = place_in(number)
            wait_bytes(quarter_of(number, own), r.piece_recv.at[number])
            if parts(number) == 4:
                pass_quarter(number, 1, own, pair)
            pass_quarter(number, 0, own, sibling)

    def pass_back(number):
        @pl.when(section != SOURCE[number])
        def _():
            wait_bytes(quarter_of(number, pair_place), r.pass_recv.at[number, 1])
            pass_quarter(number, 2, pair_place, sibling)

    def need(number):
        @pl.when(section != SOURCE[number])
        def _():
            wait_bytes(quarter_of(number, 0), r.pass_recv.at[number, 0])
            if parts(number) == 4:
                wait_bytes(quarter_of(number, 0), r.pass_recv.at[number, 2])

    def at_source(source, action):
        @pl.when(section == source)
        def _():
            action()

    for source in range(ranks):
        at_source(source, lambda: run_jobs(first_jobs(source)))
    pl.semaphore_wait(barrier, greetings)
    scales = r.scales
    for k in range(1, ranks):
        for i, row in enumerate((r.gains_in, r.shifts_in)):
            remote(
                row, scales.at[i, section], r.scale_send.at[i], r.scale_recv.at[i], (other(k), dp)
            ).start()
    at_source(0, lambda: (send_piece(A0), send_b0()))
    at_source(2, lambda: (send_piece(A1), send_piece(B1)))
    at_source(3, lambda: send_piece(C1))
    scales[0, section] = r.gains_in[...]
    scales[1, section] = r.shifts_in[...]

    @pl.when(section == 0)
    def _():
        r.a0[...] = r.a0_all[:, :part]

    mine_columns = pl.ds(pl.multiple_of(section * wide, wide), wide)
    cot_copies = (
        pltpu.make_async_copy(r.cot_in.at[:, :, :, :, mine_columns], r.cot_grid, r.cot_sem.at[0]),
        pltpu.make_async_copy(
            r.cot_in_2.at[:, :, :, :, mine_columns], r.cot_grid_2, r.cot_sem.at[1]
        ),
    )
    for copy in cot_copies:
        copy.start()

    def clear_padding(ref):
        for used, (start, stop) in zip(lay.used, lay.spans):
            low = (start + used) // 16 * 16
            high = -(-stop // 16) * 16
            if start + used < stop:
                ref[pl.ds(low, high - low), :] = jnp.zeros((high - low, ref.shape[1]), BF16)

    def by_phase(grid, group, down, right):
        side, crops = lay.sides[group], lay.crops[group]
        split = grid.reshape(side, 2, side, 2, crops, C_IN)
        return split[:, down, :, right].reshape(side * side * crops, C_IN)

    for m in range(micro):
        for copy in load_grids(m):
            copy.wait()
        for phase in range(4):
            clear_padding(r.x.at[phase, m])
            for group, grid in enumerate((r.x_grid, r.x_grid_2)):
                at = pl.ds(lay.spans[group][0], lay.used[group])
                r.x[phase, m, at, :] = by_phase(grid[m % 2], group, phase // 2, phase % 2)
        if m + 2 < micro:
            for copy in load_grids(m + 2):
                copy.start()

    def affine(segment, start, width):
        at = pl.ds(pl.multiple_of(start + section * width, width), width)
        return scales[0, segment, :, at], scales[1, segment, :, at]

    def affine_n(norm):
        return affine(2 * (norm // 2), C_MID * (norm % 2), part)

    def affine_w(norm):
        return affine((1, 1, 3)[norm], (0, C_OUT, 0)[norm], wide)

    def per_group(function, *values):
        top = function(0, *[v[:first] for v in values])
        low = function(1, *[v[first:] for v in values])
        return jnp.concatenate([top, low], axis=0)

    def widened(flags, width):
        return flags if width == part else jnp.concatenate([flags] * (width // part), axis=1)

    def keep(values):
        flags = widened(masks[4], values.shape[1])
        return jnp.where(flags > 0, values, 0.0)

    def moments(values):
        return [
            jnp.sum(v, axis=0, keepdims=True)
            for v in (
                values[:first],
                values[first:],
                values[:first] * values[:first],
                values[first:] * values[first:],
            )
        ]

    f31, b31 = (F31, B31) if lay.fast else (F31_LATE, B31_LATE)
    narrow = (r.norm_n, r.norm_n_send, r.norm_n_recv)
    broad = (r.norm_w, r.norm_w_send, r.norm_w_recv)
    double = None if lay.fast else (r.norm_v, r.norm_v_send, r.norm_v_recv)

    def norm_sent(kind, first_event, last_event):
        buffer, send, _ = kind
        used = buffer.at[pl.ds(0, last_event - first_event), :, pl.ds(0, dp_count - 1)]
        wait_bytes(used, send.at[first_event // buffer.shape[0]])

    def norm_start(kind, event, m, sums):
        buffer, send, recv = kind
        turns = buffer.shape[0]
        slot = buffer.at[event % turns, m, dp]
        for i, value in enumerate(sums):
            slot[pl.ds(i, 1), :] = value
        for i in range(len(sums), buffer.shape[3]):
            slot[pl.ds(i, 1), :] = jnp.zeros((1, slot.shape[1]), F32)
        across_dp(
            lambda device: remote(
                slot, slot, send.at[event // turns], recv.at[event % turns, m], device
            ).start()
        )

    def norm_finish(kind, event, m):
        buffer, _, recv = kind
        turn = event % buffer.shape[0]
        wait_bytes(buffer.at[0, m, pl.ds(0, dp_count - 1)], recv.at[turn, m])
        return jnp.sum(buffer[event % buffer.shape[0], m], axis=0)

    half_lanes = wide // 2
    my_half = pl.ds(pl.multiple_of(core * half_lanes, half_lanes), half_lanes)
    sibling_half = pl.ds(pl.multiple_of((1 - core) * half_lanes, half_lanes), half_lanes)

    def joint_copy(event, way, m, src, dst, device):
        remote(
            src, dst, r.joint_send.at[way], r.joint_recv.at[event % 2, way, m], device
        ).start()

    def joint_start(event, m, sums):
        for i, value in enumerate(sums):
            r.joint[event, m, pl.ds(i, 1), :] = value
        for i in range(len(sums), 8):
            r.joint[event, m, pl.ds(i, 1), :] = jnp.zeros((1, wide), F32)
        joint_copy(
            event, 0, m, r.joint.at[event, m, :, sibling_half], r.joint_pair.at[event, m], sibling
        )

    def joint_line(event, m):
        wait_bytes(r.joint_pair.at[event, m], r.joint_recv.at[event % 2, 0, m])
        r.joint_line[event, m, dp // 2] = r.joint[event, m, :, my_half] + r.joint_pair[event, m]
        slot = r.joint_line.at[event, m, dp // 2]
        for k in range(1, dp_count // 2):
            target = lax.rem(dp // 2 + k, dp_count // 2)
            joint_copy(event, 1, m, slot, slot, (section, 2 * target + core))

    def joint_back(event, m):
        wait_bytes(
            r.joint_line.at[event, m, pl.ds(0, dp_count // 2 - 1)], r.joint_recv.at[event % 2, 1, m]
        )
        r.joint_all[event, m, :, my_half] = jnp.sum(r.joint_line[event, m], axis=0)
        slot = r.joint_all.at[event, m, :, my_half]
        joint_copy(event, 2, m, slot, slot, sibling)

    def joint_finish(event, m):
        wait_bytes(r.joint_pair.at[event, m], r.joint_recv.at[event % 2, 2, m])
        return r.joint_all[event, m]

    def each_joint(step, event):
        if lay.fast:
            each_micro(lambda m: step(event, m))

    def stage_joint(step, event):
        if lay.fast:
            stage(lambda m: step(event, m))

    def finish_moments(kind, event, m, store, fold):
        if kind is None:
            sums = joint_finish(event, m)
        else:
            sums = norm_finish(kind, event, m)
        ref, norm = store
        found = []
        for group in range(2):
            count = float(lay.totals[group] * fold)
            mean = sums[group : group + 1] / count
            square = sums[2 + group : 3 + group] / count
            found += [mean, lax.rsqrt(square - mean * mean + EPSILON)]
        for i, value in enumerate(found):
            ref[norm, m, pl.ds(i, 1), :] = value
        return found

    def moments_of(ref, norm, m):
        return [ref[norm, m, pl.ds(i, 1), :] for i in range(4)]

    def normalized(values, found):
        return per_group(lambda g, v: (v - found[2 * g]) * found[2 * g + 1], values)

    def norm_change(upstream, normed, found, gain, sums, fold):
        def one(group, u, n):
            count = float(lay.totals[group] * fold)
            plain = sums[0][group] * gain / count
            along = sums[1][group] * gain / count
            return found[2 * group + 1] * (u * gain - plain - n * along)

        return keep(per_group(one, upstream, normed)).astype(BF16)

    def add_gains(place, sums):
        at = pl.ds(place, sums[0][0].shape[1])
        own = r.gains.at[section]
        own[pl.ds(0, 1), at] += sums[1][0] + sums[1][1]
        own[pl.ds(1, 1), at] += sums[0][0] + sums[0][1]

    def rows_of(totals, at):
        return [totals[at : at + 1], totals[at + 1 : at + 2]]

    def upstream_sums(upstream, normeds):
        sums = []
        for v in [upstream] + [upstream * n for n in normeds]:
            sums += [
                jnp.sum(v[:first], axis=0, keepdims=True),
                jnp.sum(v[first:], axis=0, keepdims=True),
            ]
        return sums

    def slid(ref, cols, down, right):
        pieces = []
        for (start, stop), side, crops in zip(lay.spans, lay.sides, lay.crops):
            at = PAD + start + (down * side + right) * crops
            pieces.append(ref[pl.ds(at, stop - start), cols])
        values = jnp.concatenate(pieces, axis=0)
        flags = masks[(down + 1) * 3 + right + 1]
        return jnp.where(flags > 0, values, 0.0)

    def tile_rows(used):
        low = used // 8 * 8
        assert used + 3 <= low + 8
        return low

    def center(values):
        pieces_of = []
        for used, (start, stop) in zip(lay.used, lay.spans):
            block = values[start:stop]
            low = tile_rows(used)
            mean = jnp.sum(block, axis=0, keepdims=True) / float(used)
            high = mean.astype(BF16).astype(F32)
            middle = (mean - high).astype(BF16).astype(F32)
            tile = block[low : low + 8]
            row = lax.broadcasted_iota(jnp.int32, tile.shape, 0) + low
            ends = jnp.where(row == used, high, jnp.where(row == used + 1, middle, mean - high - middle))
            ends = jnp.where(row < used + 3, ends, 0.0)
            pieces_of += [block[:low] - mean, jnp.where(row < used, tile - mean, ends)]
            if stop - start > low + 8:
                pieces_of.append(jnp.zeros((stop - start - low - 8, values.shape[1]), F32))
        return jnp.concatenate(pieces_of, axis=0)

    def uncenter(values):
        pieces_of = []
        for used, (start, stop) in zip(lay.used, lay.spans):
            block = values[start:stop]
            mean = block[used : used + 1] + block[used + 1 : used + 2] + block[used + 2 : used + 3]
            pieces_of.append(block + mean)
        return keep(jnp.concatenate(pieces_of, axis=0))

    def sum_start(event, m, values):
        send = r.sum_send
        send[event, m] = values.astype(BF16)
        for k in range(1, ranks):
            cols = pl.ds(pl.multiple_of(other(k) * part, part), part)
            remote(
                send.at[event, m, :, cols],
                r.sum_recv.at[event, m, k - 1],
                r.sum_send_sem,
                r.sum_recv_sem.at[event, m],
                (other(k), dp),
            ).start()

    def sum_finish(event, m):
        wait_bytes(r.sum_recv.at[event, m], r.sum_recv_sem.at[event, m])
        total = r.sum_send[event, m, :, mine].astype(F32)
        for k in range(ranks - 1):
            total = total + r.sum_recv[event, m, k].astype(F32)
        return total

    def get_start(event, m, values):
        get = r.get
        get[event, m, :, mine] = values
        for k in range(1, ranks):
            remote(
                get.at[event, m, :, mine],
                get.at[event, m, :, mine],
                r.get_send_sem,
                r.get_recv_sem.at[event, m],
                (other(k), dp),
            ).start()

    def get_wait(event, m):
        wait_bytes(
            r.get.at[event, m, :, pl.ds(0, C_MID - part)], r.get_recv_sem.at[event, m]
        )

    def get_finish(event, m):
        get_wait(event, m)
        return r.get[event, m]

    def own_start(number, m, src, dst):
        @pl.when(section != m)
        def _():
            remote(
                src, dst, r.own_send.at[number], r.own_recv.at[number], (m, dp)
            ).start()

        @pl.when(section == m)
        def _():
            pltpu.make_async_copy(src, dst, r.own_copy.at[number]).start()

    z1, zn, zw, y1 = r.z1, r.zn, r.zw, r.y1
    r.gains[section] = jnp.zeros(r.gains.shape[1:], F32)
    pass_on(A0)
    at_source(1, lambda: (send_piece(C0), send_piece(P0)))
    pass_on_b0(0)
    pass_back(A0)
    need(A0)
    pass_on_b0(1)

    def do_z1(m):
        sums = None
        for phase in range(4):
            value = dot(r.x[phase, m], r.a0[...])
            z1[phase, m] = value
            found = moments(value)
            sums = found if sums is None else [a + b for a, b in zip(sums, found)]
        norm_start(narrow, F01, m, sums)

    each_micro(do_z1)
    pass_on_b0(2)
    for source in range(ranks):
        at_source(source, lambda: run_jobs(own_jobs(source)))
    for group, grid in enumerate((r.cot_grid, r.cot_grid_2)):
        cot_copies[group].wait()
        for m in range(micro):
            if group == 0:
                clear_padding(r.cot.at[m])
            r.cot[m, pl.ds(lay.spans[group][0], lay.used[group]), :] = grid[m].reshape(
                lay.used[group], wide
            )
    for i in range(2):
        wait_bytes(scales.at[i, pl.ds(0, ranks - 1)], r.scale_recv.at[i])

    def do_a1(m):
        found = finish_moments(narrow, F01, m, (r.stat_n, N01), 4)
        gain, shift = affine_n(N01)
        taps = first_taps()
        for phase in range(4):
            value = silu(normalized(z1[phase, m], found) * gain + shift)
            r.slide[pl.ds(PAD, rows), :] = value
            for k, (at, down, right) in enumerate(taps):
                if at == phase:
                    r.patches[0, m, :, pl.ds(k * part, part)] = slid(
                        r.slide, slice(None), down, right
                    ).astype(BF16)

    each_micro(do_a1)
    for step in range(3):
        pass_back_b0(step)
    need_b0()

    def do_s2(m):
        sum_start(SUM_Z2, m, center(dot(r.patches[0, m], r.b0[...])))

    each_micro(do_s2)
    pass_on(A1)
    pass_on(C1)
    pass_on(C0)

    def do_z2(m):
        value = uncenter(sum_finish(SUM_Z2, m))
        zn[0, m] = value
        norm_start(narrow, F02, m, moments(value))

    stage(do_z2)
    pass_on(P0)

    def do_zs(m):
        value = dot(r.x[0, m], r.p0[...])
        zw[N12, m] = value
        if lay.fast:
            joint_start(J12, m, moments(value))
        else:
            norm_start(broad, F12, m, moments(value))


    def do_h0(m):
        found = finish_moments(narrow, F02, m, (r.stat_n, N02), 1)
        gain, shift = affine_n(N02)
        get_start(GET_H0, m, keep(silu(normalized(zn[0, m], found) * gain + shift)).astype(BF16))

    stage(do_h0)
    flush()
    pass_back(C0)
    pass_back(P0)
    need(P0)
    each_micro(do_zs)
    each_joint(joint_line, J12)
    need(C0)

    def do_zc(m):
        value = dot(get_finish(GET_H0, m), r.c0[...])
        zw[N11, m] = value
        if lay.fast:
            joint_start(J11, m, moments(value))
        else:
            norm_start(broad, F11, m, moments(value))

    stage(do_zc)
    stage_joint(joint_line, J11)
    each_joint(joint_back, J12)
    stage_joint(joint_back, J11)
    need(A1)

    def before1(m):
        main = normalized(zw[N11, m], moments_of(r.stat_w, N11, m))
        short = normalized(zw[N12, m], moments_of(r.stat_w, N12, m))
        gain_main, shift_main = affine_w(N11)
        gain_short, shift_short = affine_w(N12)
        return main * gain_main + shift_main + short * gain_short + shift_short, main, short

    def do_y1(m):
        if lay.fast:
            finish_moments(None, J12, m, (r.stat_w, N12), 1)
            finish_moments(None, J11, m, (r.stat_w, N11), 1)
        else:
            finish_moments(broad, F12, m, (r.stat_w, N12), 1)
            finish_moments(broad, F11, m, (r.stat_w, N11), 1)
        value = keep(silu(before1(m)[0])).astype(BF16)
        y1[m] = value
        sum_start(SUM_ZA, m, center(dot(value, r.a1[...])))

    stage(do_y1)
    pass_on(B1)

    def do_za(m):
        value = uncenter(sum_finish(SUM_ZA, m))
        zn[1, m] = value
        norm_start(narrow, F21, m, moments(value))

    stage(do_za)
    pass_back(B1)
    need(B1)

    def do_a2(m):
        found = finish_moments(narrow, F21, m, (r.stat_n, N21), 1)
        gain, shift = affine_n(N21)
        r.slide[pl.ds(PAD, rows), :] = silu(normalized(zn[1, m], found) * gain + shift)
        for k, (down, right) in enumerate(second_taps()):
            r.patches[1, m, :, pl.ds(k * part, part)] = slid(
                r.slide, slice(None), down, right
            ).astype(BF16)
        sum_start(SUM_ZB, m, center(dot(r.patches[1, m], r.b1[...])))

    stage(do_a2)

    def do_zb(m):
        value = uncenter(sum_finish(SUM_ZB, m))
        zn[2, m] = value
        norm_start(narrow, F22, m, moments(value))

    stage(do_zb)

    def do_h2(m):
        found = finish_moments(narrow, F22, m, (r.stat_n, N22), 1)
        gain, shift = affine_n(N22)
        get_start(GET_H2, m, keep(silu(normalized(zn[2, m], found) * gain + shift)).astype(BF16))

    stage(do_h2)
    need(C1)

    def do_zd(m):
        value = dot(get_finish(GET_H2, m), r.c1[...])
        zw[N31, m] = value
        norm_start(broad, f31, m, moments(value))

    stage(do_zd)
    half_rows = pl.ds(pl.multiple_of(core * (C_IN // 2), 64), C_IN // 2)

    def lanes_of(which):
        return pl.ds(pl.multiple_of(which * part, part), part)

    for k in range(1, ranks):

        @pl.when(other(k) != 0)
        def _():
            remote(
                r.a0.at[half_rows],
                r.a0_all.at[half_rows, mine],
                r.all_send.at[0],
                r.all_recv.at[0],
                (other(k), dp),
            ).start()

    @pl.when(section != 0)
    def _():
        r.a0_all[:, mine] = r.a0[...]

    a0_others = r.a0_all.at[pl.ds(0, C_IN // 2), pl.ds(0, C_MID - part)]
    def do_output(m):
        found = finish_moments(broad, f31, m, (r.stat_w, N31), 1)
        gain, shift = affine_w(N31)
        normed = normalized(zw[N31, m], found)
        before = normed * gain + shift + y1[m].astype(F32)
        sigmoid = jax.nn.sigmoid(before)
        r.out_send[m] = (before * sigmoid).astype(BF16)
        upstream = r.cot[m].astype(F32) * (sigmoid * (1.0 + before * (1.0 - sigmoid)))
        r.skip[m] = upstream.astype(BF16)
        r.uw[m] = upstream
        norm_start(broad, b31, m, upstream_sums(upstream, [normed]))

    if not lay.fast:
        norm_sent(broad, 0, 3)
    stage(do_output)

    def do_ddzd(m):
        totals = norm_finish(broad, b31, m)
        sums = [rows_of(totals, 0), rows_of(totals, 2)]
        add_gains(C_MID + 2 * wide, sums)
        found = moments_of(r.stat_w, N31, m)
        normed = normalized(zw[N31, m], found)
        value = norm_change(r.uw[m], normed, found, affine_w(N31)[0], sums, 1)
        r.ddzd[m] = value
        sum_start(SUM_DH2, m, dot_back(value, r.c1[...]))

    stage(do_ddzd)

    def send_output(m):
        own_start(0, m, r.out_send.at[m], r.out_own.at[:, mine_wide])

    def narrow_upstream(norm, place, event, m, value):
        found = moments_of(r.stat_n, norm, m)
        gain, shift = affine_n(norm)
        normed = normalized(zn[place, m], found)
        upstream = value * silu_slope(normed * gain + shift)
        r.un[place, m] = upstream
        norm_start(narrow, event, m, upstream_sums(upstream, [normed]))

    def narrow_change(norm, place, event, m):
        totals = norm_finish(narrow, event, m)
        sums = [rows_of(totals, 0), rows_of(totals, 2)]
        add_gains(part * norm, sums)
        found = moments_of(r.stat_n, norm, m)
        normed = normalized(zn[place, m], found)
        return norm_change(r.un[place, m], normed, found, affine_n(norm)[0], sums, 1)

    def tall(ref, count):
        return ref.reshape(micro * rows, count)

    share_rows = ROWS // ranks
    slice_base = (0, 0, share_rows, share_rows + C_MID, 2 * share_rows, 2 * share_rows + wide, 3 * share_rows, HEIGHTS[B0])
    chips = dp_count // 2
    chip = dp // 2
    base_rows = [sum(HEIGHTS[:number]) for number in range(8)]

    def own_piece(number, refs):
        whole, pair, near, total, relayed = refs
        base, height = base_rows[number], whole.shape[0] if number == A0 else HEIGHTS[number]
        each = height // dp_count
        return (
            whole.at[pl.ds(base, height)],
            pair.at[pl.ds(base // 2, height // 2)],
            near.at[:, pl.ds(base // dp_count, each)],
            total.at[pl.ds(base // dp_count, each)],
            relayed.at[pl.ds(base // dp_count, each)],
            height,
        )

    def gradient_refs(number):
        if number == A0:
            return own_piece(number, (r.da, r.da_pair, r.da_near, r.da_sum, r.da_relay))
        return own_piece(number, (r.dw, r.dw_pair, r.dw_near, r.dw_sum, r.dw_relay))

    def make(number, left, right, unit, skip=0):
        height = HEIGHTS[number]
        right = right.reshape(micro * rows, C_MID)

        def step(i, carry):
            at = pl.multiple_of(i * unit, unit)
            value = dot_rows(left(pl.ds(at + skip, unit)).reshape(micro * rows, unit), right)
            if lay.fast:
                r.dw[pl.ds(pl.multiple_of(base_rows[number] + at, 128), unit), :] = value.astype(BF16)
            else:
                r.stage[pl.ds(0, unit), :] = value.astype(BF16)
                copy = pltpu.make_async_copy(
                    r.stage.at[pl.ds(0, unit)],
                    r.dw.at[pl.ds(pl.multiple_of(slice_base[number] + at, 128), unit)],
                    r.stage_sem,
                )
                copy.start()
                copy.wait()
            return carry

        lax.fori_loop(0, height // unit, step, 0)
        to_sibling(number)

    def to_sibling(number):
        if not lay.fast:
            return
        whole, pair, _, _, _, height = gradient_refs(number)
        each = height // dp_count
        for i in range(chips):
            remote(
                whole.at[pl.ds(pl.multiple_of((2 * i + 1 - core) * each, 16), each)],
                pair.at[pl.ds(i * each, each)],
                r.pair_send.at[int(number == A0)],
                r.pair_recv.at[number],
                sibling,
            ).start()

    lined = chips == 4
    at_end = (chip == 0) | (chip == chips - 1)
    inner = jnp.where(chip < 2, 1, 2) if lined else chip
    across = 3 - inner

    def rows_for(number, target):
        each = gradient_refs(number)[-1] // dp_count
        return pl.ds(pl.multiple_of((2 * target + core) * each, 16), each)

    def send_near(number, target, k):
        whole, _, near, _, _, _ = gradient_refs(number)
        remote(
            whole.at[rows_for(number, target)],
            near.at[k - 1],
            r.near_send.at[int(number == A0)],
            r.near_recv.at[number],
            (section, 2 * target + core),
        ).start()

    def fold(number):
        if not lay.fast:
            return
        whole, pair, near, _, relayed, height = gradient_refs(number)
        each = height // dp_count
        wait_bytes(pair, r.pair_recv.at[number])
        for k in sorted(range(1, chips + 1), key=lambda k: k != 2):
            target = lax.rem(chip + k, chips)
            at = rows_for(number, target)
            theirs = pair[pl.ds(pl.multiple_of(target * each, 16), each), :]
            whole[at, :] = (whole[at, :].astype(F32) + theirs.astype(F32)).astype(BF16)
            if k == chips:
                continue
            if not lined or number == A0:
                send_near(number, target, k)
                continue

            @pl.when(jnp.logical_not(at_end) & (target != across))
            def _():
                send_near(number, target, k)

            @pl.when(at_end & (target != across))
            def _():
                send_near(number, target, k)

            @pl.when(at_end & (target == across))
            def _():
                remote(
                    whole.at[at],
                    relayed,
                    r.relay_send,
                    r.relay_recv.at[number],
                    (section, 2 * inner + core),
                ).start()

    def relay(number):
        if not (lay.fast and lined and number != A0):
            return
        whole, _, _, _, relayed, height = gradient_refs(number)

        @pl.when(jnp.logical_not(at_end))
        def _():
            wait_bytes(relayed, r.relay_recv.at[number])
            at = rows_for(number, across)
            whole[at, :] = (whole[at, :].astype(F32) + relayed[...].astype(F32)).astype(BF16)

            @pl.when(chip == 1)
            def _():
                send_near(number, across, 1)

            @pl.when(chip == 2)
            def _():
                send_near(number, across, 3)

    def units(number):
        height = C_IN if number == A0 else HEIGHTS[number]
        each = height // dp_count
        whole = ROWS // dp_count
        unit = 64 if number in (A0, A1) else 16
        found = []
        for i in range(each // unit):
            row = dp * each + i * unit
            if number == A0:
                owner, at, cols = row // whole, lax.rem(row, whole), mine
            elif number in (C0, P0, C1):
                row = row + (C_MID if number == P0 else 0)
                owner, cols = row // (whole // ranks), slice(None)
                at = section * (whole // ranks) + lax.rem(row, whole // ranks)
            else:
                if number == A1:
                    row = row + section * wide
                else:
                    base = C_OUT if number == B1 else C_IN
                    row = row + (HEIGHTS[B0] if number == B0_REST else 0)
                    row = base + C_MID * (row // part) + part * section + lax.rem(row, part)
                owner, at, cols = row // whole, lax.rem(row, whole), slice(None)
            if number == C1:
                at = lax.rem(row, whole // ranks)
            keeper = {C1: r.hold_2, A1: r.hold, B1: r.hold}.get(number, r.share)
            place = keeper.at[pl.ds(pl.multiple_of(at, unit), unit), cols]
            found.append((owner, place))
        return unit, found

    def finish(number):
        if not lay.fast:
            return
        whole, pair, near, total, _, height = gradient_refs(number)
        each = height // dp_count
        value = whole[pl.ds(pl.multiple_of(dp * each, 16), each), :].astype(F32)
        if lined and number != A0:

            @pl.when(at_end)
            def _():
                wait_bytes(near, r.near_recv.at[number])

            @pl.when(jnp.logical_not(at_end))
            def _():
                wait_bytes(near.at[pl.ds(0, 2)], r.near_recv.at[number])

            second = jnp.where(at_end, near[1].astype(F32), 0.0)
            value = value + near[0].astype(F32) + second + near[2].astype(F32)
        else:
            wait_bytes(near, r.near_recv.at[number])
            for k in range(chips - 1):
                value = value + near[k].astype(F32)
        total[...] = value.astype(BF16)
        unit, found = units(number)
        held = number in HELD
        target = section if held else SOURCE[number]
        recv = r.hold_recv.at[HELD.index(number)] if held else r.share_recv
        send = r.share_send.at[int(number == A0)]
        for i, (owner, place) in enumerate(found):
            rows_here = pl.ds(i * unit, unit)
            src = total.at[rows_here]
            here = (owner == dp) & (section == target)

            @pl.when(here)
            def _():
                pltpu.make_async_copy(src, place, recv).start()
                pltpu.make_async_copy(src, pair.at[rows_here], send).start()

            @pl.when(jnp.logical_not(here))
            def _():
                remote(src, place, send, recv, (target, owner)).start()

    def held_blocks(number):
        if number == C1:
            found = []
            whole = ROWS // dp_count // ranks
            for device in range(dp_count):
                count = min(max(HEIGHTS[C1] - device * whole, 0), whole)
                if count:
                    at = pl.ds(pl.multiple_of(section * whole, 16), count)
                    found.append((dp == device, count, r.hold_2.at[pl.ds(0, count)], r.share.at[at]))
            return found
        blocks_64 = ROWS // dp_count // 64
        if number == A1:
            starts = [(wide // 64) * section + i for i in range(wide // 64)]
        else:
            starts = [
                C_OUT // 64 + (C_MID // 64) * (u // 2) + (part // 64) * section + u % 2
                for u in range(18)
            ]
        found = []
        for start in starts:
            at = pl.ds(pl.multiple_of(64 * lax.rem(start, blocks_64), 64), 64)
            found.append((start // blocks_64 == dp, 64, r.hold.at[at], r.share.at[at]))
        return found

    def held_rows(number, act):
        found = held_blocks(number)
        if number == C1:
            for here, count, _, _ in found:
                pl.when(here)(functools.partial(act, count))
            return
        total = sum(jnp.where(here, 1, 0) for here, _, _, _ in found)
        for count in range(1, 9 if number == A1 else 6):
            pl.when(total == count)(functools.partial(act, 64 * count))

    def ship(number):
        if not lay.fast:
            return
        which = HELD.index(number)
        held_rows(number, lambda count: wait_bytes(r.share.at[pl.ds(0, count)], r.hold_recv.at[which]))
        for here, _, src, dst in held_blocks(number):

            @pl.when(here & (section == SOURCE[number]))
            def _():
                pltpu.make_async_copy(src, dst, r.share_recv).start()

            @pl.when(here & (section != SOURCE[number]))
            def _():
                remote(
                    src, dst, r.ship_send.at[which], r.share_recv, (SOURCE[number], dp)
                ).start()

    def shipped(number):
        which = HELD.index(number)

        @pl.when(section != SOURCE[number])
        def _():
            held_rows(
                number, lambda count: wait_bytes(r.share.at[pl.ds(0, count)], r.ship_send.at[which])
            )

    def finish_shares():
        whole = ROWS // dp_count
        sizes = (C_IN + 9 * C_MID, ranks * (C_MID + C_IN), C_OUT + 9 * C_MID, ranks * C_MID)
        count = jnp.int32(0)
        for source, size in enumerate(sizes):
            count = jnp.where(section == source, size, count)
        count = jnp.clip(count - whole * dp, 0, whole)
        lengths = {min(max(size - whole * d, 0), whole) for size in sizes for d in range(dp_count)}
        for length in sorted(lengths):
            if length:

                @pl.when(count == length)
                def _():
                    wait_bytes(r.share.at[pl.ds(0, length)], r.share_recv)

    def store_norm_shares():
        shares = (r.gain_share, r.shift_share)
        count = GSEGMENT // dp_count
        for share in shares:
            share[...] = jnp.zeros(share.shape, F32)
        for source in range(ranks):
            for device in range(dp_count):
                start = device * count
                wide_norm = source % 2 == 1
                used = {1: 2 * C_OUT, 3: C_OUT}.get(source, 2 * C_MID)
                if start >= used:
                    continue

                @pl.when((section == source) & (dp == device))
                def _():
                    for i, share in enumerate(shares):
                        if wide_norm:
                            norm = start // C_OUT + (2 if source == 3 else 0)
                            place_in = start % C_OUT
                            at = C_MID + norm * wide + place_in % wide
                            share[...] = r.gains[place_in // wide, pl.ds(i, 1), pl.ds(at, count)]
                        else:
                            at = part * (source + start // C_MID)
                            for t in range(ranks):
                                share[:, pl.ds(part * t, part)] = r.gains[t, pl.ds(i, 1), pl.ds(at, part)]

    def gradients_sent():
        for group, (pair, near, total) in enumerate(
            ((r.dw_pair, r.dw_near, r.dw_sum), (r.da_pair, r.da_near, r.da_sum))
        ):
            wait_bytes(pair, r.pair_send.at[group])
            wait_bytes(total, r.share_send.at[group])
            if not lined or group == 1:
                wait_bytes(near, r.near_send.at[group])
                continue

            @pl.when(at_end)
            def _():
                wait_bytes(near.at[pl.ds(0, 2)], r.near_send.at[group])
                wait_bytes(r.dw_relay, r.relay_send)

            @pl.when(jnp.logical_not(at_end))
            def _():
                wait_bytes(near, r.near_send.at[group])

        for number in HELD:
            shipped(number)

    def do_dh2(m):
        value = sum_finish(SUM_DH2, m).astype(BF16).astype(F32)
        narrow_upstream(N22, 2, B22, m, value)

    norm_sent(narrow, 0, 4)
    stage(do_dh2)
    b0_sent()
    for number in (A0, C0, P0, A1, B1, C1):

        @pl.when(section != SOURCE[number])
        def _():
            count = pieces[number].shape[0] // parts(number)
            times = 3 if parts(number) == 4 else 1
            wait_bytes(pieces[number].at[pl.ds(0, times * count)], r.pass_send.at[number])

        @pl.when(section == SOURCE[number])
        def _():
            for _ in range(ranks - 1):
                wait_bytes(quarter_of(number, 0), r.piece_send.at[number])
    make(C1, lambda at: r.get[GET_H2, :, :, at], r.ddzd[...], 256)

    def do_ddzb(m):
        get_start(GET_DDZB, m, narrow_change(N22, 2, B22, m))

    stage(do_ddzb)
    fold(C1)

    def fan_out(m, event, weight):
        r.fan[pl.ds(PAD, rows), :] = dot_back(r.get[event, m], weight[...])

    def do_da2(m):
        get_finish(GET_DDZB, m)
        fan_out(m, GET_DDZB, r.b1)
        total = None
        for k, (down, right) in enumerate(second_taps()):
            term = slid(r.fan, pl.ds(k * part, part), -down, -right)
            total = term if total is None else total + term
        narrow_upstream(N21, 1, B21, m, total)

    stage(do_da2)

    @pl.when(section != 0)
    def _():
        wait_bytes(a0_others, r.all_recv.at[0])
        for k in range(1, ranks):
            block = r.a0_all.at[half_rows, lanes_of(other(k))]
            remote(block, block, r.all_send.at[1], r.all_recv.at[1], sibling).start()

    relay(C1)

    def do_ddza(m):
        get_start(GET_DDZA, m, narrow_change(N21, 1, B21, m))

    stage(do_ddza)
    make(B1, lambda at: r.patches[1, :, :, at], r.get[GET_DDZB], 128)
    finish(C1)

    def do_dy1(m):
        value = dot_back(get_finish(GET_DDZA, m), r.a1[...]) + r.skip[m].astype(F32)
        value = value.astype(BF16).astype(F32)
        before, main, short = before1(m)
        upstream = value * silu_slope(before)
        r.uw[m] = upstream
        sums = upstream_sums(upstream, [main, short])
        if lay.fast:
            joint_start(B11, m, sums)
        else:
            norm_start(double, B11, m, sums)

    stage(do_dy1)
    stage_joint(joint_line, B11)
    flush()
    each_micro(send_output)
    make(A1, lambda at: y1[:, :, at], r.get[GET_DDZA], 256)
    fold(B1)
    stage_joint(joint_back, B11)

    def do_ddzc(m):
        totals = joint_finish(B11, m) if lay.fast else norm_finish(double, B11, m)
        plain = rows_of(totals, 0)
        for norm, at, target in ((N11, 2, r.ddzd), (N12, 4, r.ddzs)):
            sums = [plain, rows_of(totals, at)]
            add_gains(C_MID + norm * wide, sums)
            found = moments_of(r.stat_w, norm, m)
            normed = normalized(zw[norm, m], found)
            target[m] = norm_change(r.uw[m], normed, found, affine_w(norm)[0], sums, 1)
        sum_start(SUM_DH0, m, dot_back(r.ddzd[m], r.c0[...]))

    stage(do_ddzc)
    flush()
    fold(A1)

    def do_dxs(m):
        r.dxs_send[m] = dot_back(r.ddzs[m], r.p0[...]).astype(BF16)

    each_micro(do_dxs)
    make(C0, lambda at: r.get[GET_H0, :, :, at], r.ddzd[...], 256)
    make(P0, lambda at: r.x[0, :, :, at], r.ddzs[...], 256)

    def do_dh0(m):
        value = sum_finish(SUM_DH0, m).astype(BF16).astype(F32)
        narrow_upstream(N02, 0, B02, m, value)

    def send_dxs(m):
        own_start(1, m, r.dxs_send.at[m], r.dxs_recv.at[section])

    stage(do_dh0)
    relay(B1)
    relay(A1)

    def do_ddz2(m):
        get_start(GET_DDZ2, m, narrow_change(N02, 0, B02, m))

    stage(do_ddz2)
    fold(C0)
    fold(P0)
    finish(A1)
    finish(B1)
    flush()

    def do_da1(m):
        get_wait(GET_DDZ2, m)

        @pl.when(m == micro - 2)
        def _():
            each_micro(send_dxs)

        fan_out(m, GET_DDZ2, r.b0)
        gain, shift = affine_n(N01)
        found = moments_of(r.stat_n, N01, m)
        sums = None
        for phase in range(4):
            total = None
            for k, (at, down, right) in enumerate(first_taps()):
                if at == phase:
                    term = slid(r.fan, pl.ds(k * part, part), -down, -right)
                    total = term if total is None else total + term
            normed = normalized(z1[phase, m], found)
            upstream = total * silu_slope(normed * gain + shift)
            r.u1[phase, m] = upstream
            terms = upstream_sums(upstream, [normed])
            sums = terms if sums is None else [a + b for a, b in zip(sums, terms)]
        norm_start(narrow, B01, m, sums)

    stage(do_da1)
    flush()
    relay(C0)
    relay(P0)
    make(B0, lambda at: r.patches[0, :, :, at], r.get[GET_DDZ2], 128)
    make(B0_REST, lambda at: r.patches[0, :, :, at], r.get[GET_DDZ2], 128, HEIGHTS[B0])
    fold(B0)
    fold(B0_REST)
    relay(B0)

    out_own = r.out_own
    wait_bytes(out_own.at[:, mine_wide], r.own_copy.at[0])
    wait_bytes(out_own.at[:, pl.ds(0, C_OUT - wide)], r.own_recv.at[0])
    def store_grid(refs, values, pick):
        for group, ref in enumerate(refs):
            start, used = lay.spans[group][0], lay.used[group]
            side, crops = lay.sides[group], lay.crops[group]
            grid = values[start : start + used].astype(BF16).reshape(side, side, crops, values.shape[1])
            pick(ref, grid)

    def store_output(ref, grid):
        ref[...] = grid

    store_grid((r.out_grid, r.out_grid_2), out_own[...].astype(F32), store_output)
    results = [
        pltpu.make_async_copy(src, dst, r.result_sem.at[i])
        for i, (src, dst) in enumerate(
            (
                (r.out_grid, r.out),
                (r.out_grid_2, r.out_2),
                (r.grad_grid, r.grad),
                (r.grad_grid_2, r.grad_2),
            )
        )
    ]
    results[0].start()
    results[1].start()

    def do_ddz1(m):
        totals = norm_finish(narrow, B01, m)
        sums = [rows_of(totals, 0), rows_of(totals, 2)]
        add_gains(0, sums)
        found = moments_of(r.stat_n, N01, m)
        gain = affine_n(N01)[0]
        for phase in range(4):
            normed = normalized(z1[phase, m], found)
            r.ddz1[phase, m] = norm_change(r.u1[phase, m], normed, found, gain, sums, 4)
        own_start(2, m, r.ddz1.at[:, m], r.ddz1_own.at[:, :, mine])

    each_micro(do_ddz1)
    ship(C1)
    ship(B1)
    ship(A1)
    for k in range(1, ranks):
        remote(
            r.gains.at[section],
            r.gains.at[section],
            r.gain_send,
            r.gain_recv,
            (other(k), dp),
        ).start()

    def da0_step(i, carry):
        at = pl.ds(pl.multiple_of(i * 128, 128), 128)
        total = None
        for phase in range(4):
            value = dot_rows(
                r.x[phase, :, :, at].reshape(micro * rows, 128),
                r.ddz1[phase].reshape(micro * rows, part),
            )
            total = value if total is None else total + value
        da0 = r.da if lay.fast else r.da0
        da0[pl.ds(pl.multiple_of(i * 128, 128), 128), :] = total.astype(BF16)
        return carry

    lax.fori_loop(0, C_IN // 128, da0_step, 0)
    to_sibling(A0)
    finish(C0)
    relay(B0_REST)
    fold(A0)
    finish(P0)
    finish(B0)
    finish(B0_REST)
    finish(A0)

    dxs, ddz1_own = r.dxs_recv, r.ddz1_own

    @pl.when(section != 0)
    def _():
        wait_bytes(a0_others, r.all_recv.at[1])

    wait_bytes(dxs.at[0], r.own_copy.at[1])
    wait_bytes(dxs.at[pl.ds(0, ranks - 1)], r.own_recv.at[1])
    wait_bytes(ddz1_own.at[:, :, mine], r.own_copy.at[2])
    wait_bytes(ddz1_own.at[:, :, pl.ds(0, C_MID - part)], r.own_recv.at[2])
    for phase in range(4):
        value = dot_back(ddz1_own[phase], r.a0_all[...])
        if phase == 0:
            extra = dxs[0].astype(F32)
            for k in range(1, ranks):
                extra = extra + dxs[k].astype(F32)
            value = value + extra.astype(BF16).astype(F32)

        def store_phase(ref, grid):
            ref[:, phase // 2, :, phase % 2] = grid

        store_grid((r.grad_grid, r.grad_grid_2), value, store_phase)
    wait_bytes(r.gains.at[pl.ds(0, ranks - 1)], r.gain_recv)
    if lay.fast:
        store_norm_shares()
    else:
        r.gains_out[...] = r.gains[...]

    results[2].start()
    results[3].start()
    if lay.fast:
        finish_shares()
        results.append(pltpu.make_async_copy(r.share, r.share_out, r.result_sem.at[4]))
        results[4].start()
        gradients_sent()

    wait_bytes(r.sum_recv, r.sum_send_sem)
    wait_bytes(r.get.at[:, :, :, pl.ds(0, C_MID - part)], r.get_send_sem)
    norm_sent(narrow, 4, 8)
    if lay.fast:
        norm_sent(broad, 0, 2)
        wait_bytes(r.joint_pair, r.joint_send.at[0])
        wait_bytes(r.joint_line.at[:, :, pl.ds(0, dp_count // 2 - 1)], r.joint_send.at[1])
        wait_bytes(r.joint_pair, r.joint_send.at[2])
    else:
        norm_sent(broad, 3, 4)
        norm_sent(double, 0, 1)
    for copy in results:
        copy.wait()
    wait_bytes(out_own.at[:, pl.ds(0, C_OUT - wide)], r.own_send.at[0])
    wait_bytes(dxs.at[pl.ds(0, ranks - 1)], r.own_send.at[1])
    wait_bytes(ddz1_own.at[:, :, pl.ds(0, C_MID - part)], r.own_send.at[2])

    @pl.when(section == 0)
    def _():
        wait_bytes(a0_others, r.all_send.at[0])

    @pl.when(section != 0)
    def _():
        wait_bytes(a0_others.at[:, pl.ds(0, (ranks - 2) * part)], r.all_send.at[0])
        wait_bytes(a0_others, r.all_send.at[1])

    wait_bytes(r.gains.at[pl.ds(0, ranks - 1)], r.gain_send)
    for i in range(2):
        wait_bytes(scales.at[i, pl.ds(0, ranks - 1)], r.scale_send.at[i])


def chain(lay, ranks, dp_count, operands):
    micro, rows = lay.micro, lay.rows
    part, wide = C_MID // ranks, C_OUT // ranks
    table = scratch_table(lay, ranks, dp_count)
    shapes = (
        *[jax.ShapeDtypeStruct(grid_shape(lay, group, 1, C_OUT), BF16) for group in range(2)],
        *[jax.ShapeDtypeStruct(phase_shape(lay, group), BF16) for group in range(2)],
    )
    if lay.fast:
        shapes += (jax.ShapeDtypeStruct((1, GSEGMENT // dp_count), F32),) * 2
        shapes += (jax.ShapeDtypeStruct((ROWS // dp_count, C_MID), BF16),)
    else:
        shapes += (
            jax.ShapeDtypeStruct((ranks, 2, C_MID + 3 * wide), F32),
            jax.ShapeDtypeStruct((ROWS, C_MID), BF16),
            jax.ShapeDtypeStruct((C_IN, part), BF16),
        )
    anywhere = pl.BlockSpec(memory_space=pl.ANY)
    inside = pl.BlockSpec(memory_space=pltpu.VMEM)
    return pl.pallas_call(
        functools.partial(chain_kernel, lay, ranks, dp_count, tuple(table)),
        out_shape=shapes,
        in_specs=[anywhere] * 5 + [inside] * 3,
        out_specs=[anywhere] * 4 + ([inside] * 2 + [anywhere] if lay.fast else [inside, anywhere, inside]),
        scratch_shapes=list(table.values()),
        compiler_params=pltpu.CompilerParams(
            collective_id=0, has_side_effects=True, vmem_limit_bytes=63 * 2**20
        ),
        name="chain",
    )(*operands)


def summed_gradient(slices, small, section, ranks):
    small = jnp.stack([small] + [jnp.zeros_like(small)] * (ranks - 1))
    slices = slices.reshape(ranks, ROWS // ranks, C_MID)
    arrived = lax.all_to_all(slices, "section", 0, 0, tiled=True).astype(F32)
    arrived_small = lax.all_to_all(small, "section", 0, 0, tiled=True).astype(F32)
    segment = segment_gradient(arrived, arrived_small, section, ranks)
    return lax.psum_scatter(segment.reshape(-1), "dp", scatter_dimension=0, tiled=True)


def norm_shares(gains, ranks, dp_count):
    part, wide = C_MID // ranks, C_OUT // ranks

    def joined(start, width):
        block = gains[:, :, start : start + width // ranks]
        return jnp.moveaxis(block, 0, 1).reshape(2, width)

    f01, f02, f21, f22 = [joined(part * i, C_MID) for i in range(4)]
    f11, f12, f31 = [joined(C_MID + wide * i, C_OUT) for i in range(3)]
    blank = jnp.zeros((2, GSEGMENT - 2 * C_MID), F32)
    segments = jnp.stack(
        [
            jnp.concatenate([f01, f02, blank], 1),
            jnp.concatenate([f11, f12], 1),
            jnp.concatenate([f21, f22, blank], 1),
            jnp.concatenate([f31, jnp.zeros((2, GSEGMENT - C_OUT), F32)], 1),
        ]
    )
    share = GSEGMENT // dp_count
    own_norms = lax.dynamic_index_in_dim(segments, lax.axis_index("section"), 0, keepdims=False)
    return lax.dynamic_slice_in_dim(own_norms, lax.axis_index("dp") * share, share, 1)


def deliver_kernel(ranks, *refs):
    plain, share_in, norms_in, refs = refs[:4], refs[4], refs[5:7], refs[7:]
    plain_out, share_out, norms_out, refs = refs[:4], refs[4], refs[5:7], refs[7:]
    held, share, order, load_sem, store_sem = refs[:4], refs[4], refs[5], refs[6], refs[7]
    loads = [
        pltpu.make_async_copy(src, dst, load_sem.at[i])
        for i, (src, dst) in enumerate(zip(plain + (share_in,), held + (share,)))
    ]
    stores = [
        pltpu.make_async_copy(src, dst, store_sem.at[i])
        for i, (src, dst) in enumerate(zip(held + (order,), plain_out + (share_out,)))
    ]
    turn = (4, 2, 0, 3, 1)
    for i in turn:
        loads[i].start()
    for src, dst in zip(norms_in, norms_out):
        dst[...] = src[...]
    whole, lanes = share.shape[0], 128
    for i in turn:
        loads[i].wait()
        if i == 4:
            odd = lax.rem(lax.axis_index("section"), 2)

            @pl.when(odd == 0)
            def _():
                for q in range(ranks):
                    order[pl.ds(q, whole, stride=ranks), :] = share[:, lanes * q : lanes * (q + 1)].astype(F32)

            @pl.when(odd == 1)
            def _():
                short = whole // ranks
                for t in range(ranks):
                    for q in range(ranks):
                        order[pl.ds(ranks * t + q, short, stride=ranks * ranks), :] = share[
                            t * short : (t + 1) * short, lanes * q : lanes * (q + 1)
                        ].astype(F32)

        stores[i].start()
    for i in turn:
        stores[i].wait()


def deliver(results, ranks):
    plain, norms, share = results[:4], results[4:6], results[6]
    order = jax.ShapeDtypeStruct((share.size // 128, 128), F32)
    anywhere = pl.BlockSpec(memory_space=pl.ANY)
    inside = pl.BlockSpec(memory_space=pltpu.VMEM)
    specs = [anywhere] * 5 + [inside] * 2
    like = [jax.ShapeDtypeStruct(v.shape, v.dtype) for v in plain]
    return pl.pallas_call(
        functools.partial(deliver_kernel, ranks),
        out_shape=like + [order] + [jax.ShapeDtypeStruct(v.shape, v.dtype) for v in norms],
        in_specs=specs,
        out_specs=specs,
        scratch_shapes=[pltpu.VMEM(v.shape, v.dtype) for v in list(plain) + [share, order]]
        + [pltpu.SemaphoreType.DMA((5,))] * 2,
        name="deliver",
    )(*plain, share, *norms)


def per_device(
    images_global, images_local, weights, norm_gains, norm_shifts, cotangent_global, cotangent_local
):
    section = lax.axis_index("section")
    ranks = lax.axis_size("section")
    dp_count = lax.axis_size("dp")
    lay = Layout(images_global.shape, images_local.shape, dp_count)
    micro, rows = lay.micro, lay.rows
    part = C_MID // ranks
    wide = C_OUT // ranks

    def cells_first(pictures):
        return jnp.moveaxis(pictures, 1, 3)

    masks = np.stack(
        [lay.valid(down, right) for down in (-1, 0, 1) for right in (-1, 0, 1)]
    ).astype(np.float32)
    masks = jnp.asarray(np.ascontiguousarray(np.broadcast_to(masks[:, :, None], (9, rows, part))))
    results = chain(
        lay,
        ranks,
        dp_count,
        (
            cells_first(images_global),
            cells_first(images_local),
            cells_first(cotangent_global),
            cells_first(cotangent_local),
            weights.reshape(-1, 128),
            norm_gains[None],
            norm_shifts[None],
            masks,
        ),
    )

    if lay.fast:
        results = deliver(results, ranks)
    out_global, out_local, grad_global, grad_local, *rest = results
    if lay.fast:
        share, gain_share, shift_share = rest
        own_norms, weight_gradient = (gain_share[0], shift_share[0]), share.reshape(-1)
    else:
        own_norms = norm_shares(rest[0], ranks, dp_count)
        weight_gradient = summed_gradient(*rest[1:], section, ranks)

    def crops_first(grid, side, crops):
        return jnp.moveaxis(grid.reshape(1, side, side, crops, -1), 3, 1)

    return (
        crops_first(out_global, lay.sides[0], lay.crops[0]),
        crops_first(out_local, lay.sides[1], lay.crops[1]),
        crops_first(grad_global, 2 * lay.sides[0], lay.crops[0]),
        crops_first(grad_local, 2 * lay.sides[1], lay.crops[1]),
        weight_gradient,
        own_norms[0],
        own_norms[1],
    )


def solution(mesh):
    images = P(None, "dp", None, None, None)
    made = P("section", "dp", None, None, None)
    return jax.shard_map(
        per_device,
        mesh=mesh,
        in_specs=(images, images, P("section"), P("section"), P("section"), images, images),
        out_specs=(made, made, made, made) + (P(("section", "dp")),) * 3,
        check_vma=False,
    )
```

```python
import functools
from types import SimpleNamespace

import jax
import jax.numpy as jnp
import numpy as np
from jax import lax
from jax.experimental import pallas as pl
from jax.experimental.pallas import tpu as pltpu
from jax.sharding import PartitionSpec as P

C_IN = 1024
C_MID = 512
C_OUT = 2048
WSEGMENT = 3407872
GSEGMENT = 4096
EPSILON = 1e-05
F32 = jnp.float32
BF16 = jnp.bfloat16


def round_up(value, unit):
    return -(-value // unit) * unit


class Layout:
    def __init__(self, shape_global, shape_local, dp_count):
        self.micro = shape_global[0]
        self.crops = (shape_global[1], shape_local[1])
        self.sides = (shape_global[2] // 2, shape_local[2] // 2)
        used = [crops * side * side for crops, side in zip(self.crops, self.sides)]
        self.used = used
        first = round_up(used[0], 8)
        self.rows = round_up(first + round_up(used[1], 8), 16)
        self.spans = ((0, first), (first, self.rows))
        self.totals = [count * dp_count for count in used]
        self.fast = dp_count == 8 and WSEGMENT // C_MID // dp_count % 64 == 0

    def valid(self, down, right):
        flags = np.zeros((self.rows,), bool)
        for (start, _), crops, side in zip(self.spans, self.crops, self.sides):
            for crop in range(crops):
                for i in range(side):
                    for j in range(side):
                        inside = 0 <= i + down < side and 0 <= j + right < side
                        flags[start + (i * side + j) * crops + crop] = inside
        return flags


def first_taps():
    return [
        (2 * (p != 1) + (q != 1), -(p == 0), -(q == 0)) for p in range(3) for q in range(3)
    ]


def second_taps():
    return [(p - 1, q - 1) for p in range(3) for q in range(3)]


def segment_gradient(pieces, small, section, ranks):
    part = C_MID // ranks
    total_rows = WSEGMENT // C_MID

    def finished(rows):
        return jnp.pad(rows, ((0, total_rows - rows.shape[0]), (0, 0)))

    def across(block):
        return block.transpose(1, 0, 2).reshape(-1, C_MID)

    def spatial(block):
        return block.reshape(ranks, 9, part, C_MID).transpose(1, 0, 2, 3).reshape(-1, C_MID)

    def first():
        return finished(
            jnp.concatenate(
                [small.transpose(1, 0, 2).reshape(-1, C_MID), spatial(pieces[:, : 9 * part])]
            )
        )

    def second():
        return finished(across(pieces[:, : C_MID + C_IN]))

    def third():
        tall = C_OUT // ranks
        return finished(
            jnp.concatenate(
                [pieces[:, :tall].reshape(-1, C_MID), spatial(pieces[:, tall : tall + 9 * part])]
            )
        )

    def fourth():
        return finished(across(pieces[:, :C_MID]))

    return lax.switch(section, [first, second, third, fourth])


MESH = pl.DeviceIdType.MESH
ROWS = WSEGMENT // C_MID
SUM_Z2, SUM_ZA, SUM_ZB, SUM_DH2, SUM_DH0 = range(5)
GET_H0, GET_H2, GET_DDZB, GET_DDZA, GET_DDZ2 = range(5)
F01, F02, F21, F22, B22, B21, B02, B01 = range(8)
F31, B31 = range(2)
F12, F11, F31_LATE, B31_LATE = range(4)
B11, J12, J11 = range(3)
N01, N02, N21, N22 = range(4)
N11, N12, N31 = range(3)
A0, B0, C0, P0, A1, B1, C1 = range(7)
SOURCE = (0, 0, 1, 1, 2, 2, 3, 0)
PAD = 16
SLOTS = 3
HELD = (4, 5, 6)
READY = 640
HEIGHTS = (0, C_MID, C_MID, C_IN, C_OUT // 4, 9 * C_MID // 4, C_MID, 5 * C_MID // 4)
B0_REST = 7


def dot(left, right):
    return lax.dot_general(left, right, (((1,), (0,)), ((), ())), preferred_element_type=F32)


def dot_back(left, right):
    return lax.dot_general(left, right, (((1,), (1,)), ((), ())), preferred_element_type=F32)


def dot_rows(left, right):
    return lax.dot_general(left, right, (((0,), (0,)), ((), ())), preferred_element_type=F32)


def silu(value):
    return value * jax.nn.sigmoid(value)


def silu_slope(before):
    sigmoid = jax.nn.sigmoid(before)
    return sigmoid * (1.0 + before * (1.0 - sigmoid))


def grid_shape(lay, group, fold, channels):
    side = fold * lay.sides[group]
    return (side, side, lay.crops[group], channels)


def phase_shape(lay, group):
    side = lay.sides[group]
    return (side, 2, side, 2, lay.crops[group], C_IN)


def scratch_table(lay, ranks, dp_count):
    micro, rows = lay.micro, lay.rows
    part, wide = C_MID // ranks, C_OUT // ranks
    others = ranks - 1
    vmem, dma = pltpu.VMEM, pltpu.SemaphoreType.DMA
    return dict(
        x=vmem((4, micro, rows, C_IN), BF16),
        cot=vmem((micro, rows, wide), BF16),
        x_grid=vmem((2,) + grid_shape(lay, 0, 2, C_IN), BF16),
        x_grid_2=vmem((2,) + grid_shape(lay, 1, 2, C_IN), BF16),
        cot_grid=vmem((micro,) + grid_shape(lay, 0, 1, wide), BF16),
        cot_grid_2=vmem((micro,) + grid_shape(lay, 1, 1, wide), BF16),
        a0=vmem((C_IN, part), BF16),
        b0=vmem((9 * part, C_MID), BF16),
        c0=vmem((C_MID, wide), BF16),
        p0=vmem((C_IN, wide), BF16),
        a1=vmem((wide, C_MID), BF16),
        b1=vmem((9 * part, C_MID), BF16),
        c1=vmem((C_MID, wide), BF16),
        a0_all=vmem((C_IN, C_MID), BF16),
        raw=vmem((SLOTS, 2048, 128), BF16),
        raw_sem=dma((SLOTS,)),
        scales=vmem((2, ranks, 1, GSEGMENT), F32),
        z1=vmem((4, micro, rows, part), F32),
        u1=vmem((4, micro, rows, part), F32),
        zn=vmem((3, micro, rows, part), F32),
        un=vmem((3, micro, rows, part), F32),
        zw=vmem((3, micro, rows, wide), F32),
        uw=vmem((micro, rows, wide), F32),
        y1=vmem((micro, rows, wide), BF16),
        skip=vmem((micro, rows, wide), BF16),
        ddzd=vmem((micro, rows, wide), BF16),
        ddzs=vmem((micro, rows, wide), BF16),
        patches=vmem((2, micro, rows, 9 * part), BF16),
        slide=vmem((PAD + rows + PAD, part), F32),
        fan=vmem((PAD + rows + PAD, 9 * part), F32),
        stat_n=vmem((4, micro, 8, part), F32),
        stat_w=vmem((3, micro, 8, wide), F32),
        sum_send=vmem((5, micro, rows, C_MID), BF16),
        sum_recv=vmem((5, micro, others, rows, part), BF16),
        get=vmem((5, micro, rows, C_MID), BF16),
        norm_n=vmem((4, micro, dp_count, 4, part), F32),
        norm_w=vmem((2 if lay.fast else 3, micro, dp_count, 4, wide), F32),
        **joint_scratch(lay, dp_count, wide),
        out_send=vmem((micro, rows, wide), BF16),
        out_own=vmem((rows, C_OUT), BF16),
        out_grid=vmem(grid_shape(lay, 0, 1, C_OUT), BF16),
        out_grid_2=vmem(grid_shape(lay, 1, 1, C_OUT), BF16),
        grad_grid=vmem(phase_shape(lay, 0), BF16),
        grad_grid_2=vmem(phase_shape(lay, 1), BF16),
        result_sem=dma((5,)),
        dxs_send=vmem((micro, rows, C_IN), BF16),
        dxs_recv=vmem((ranks, rows, C_IN), BF16),
        ddz1=vmem((4, micro, rows, part), BF16),
        ddz1_own=vmem((4, rows, C_MID), BF16),
        gains=vmem((ranks, 2, C_MID + 3 * wide), F32),
        x_sem=dma((2, 2)),
        cot_sem=dma((2,)),
        piece_send=dma((7,)),
        piece_recv=dma((7,)),
        pass_send=dma((7,)),
        pass_recv=dma((7, 3)),
        eight_send=dma,
        eight_recv=dma((4, 3)),
        scale_send=dma((2,)),
        scale_recv=dma((2,)),
        all_send=dma((2,)),
        all_recv=dma((2,)),
        sum_send_sem=dma,
        sum_recv_sem=dma((5, micro)),
        get_send_sem=dma,
        get_recv_sem=dma((5, micro)),
        norm_n_send=dma((2,)),
        norm_n_recv=dma((4, micro)),
        norm_w_send=dma((2,)),
        norm_w_recv=dma((2 if lay.fast else 3, micro)),
        own_send=dma((3,)),
        own_recv=dma((3,)),
        own_copy=dma((3,)),
        gain_send=dma,
        gain_recv=dma,
        **gradient_scratch(lay, ranks, dp_count),
    )


def joint_scratch(lay, dp_count, wide):
    vmem, dma, micro = pltpu.VMEM, pltpu.SemaphoreType.DMA, lay.micro
    if not lay.fast:
        return dict(
            norm_v=vmem((1, micro, dp_count, 8, wide), F32),
            norm_v_send=dma((1,)),
            norm_v_recv=dma((1, micro)),
        )
    return dict(
        joint=vmem((3, micro, 8, wide), F32),
        joint_all=vmem((3, micro, 8, wide), F32),
        joint_pair=vmem((3, micro, 8, wide // 2), F32),
        joint_line=vmem((3, micro, dp_count // 2, 8, wide // 2), F32),
        joint_send=dma((3,)),
        joint_recv=dma((2, 3, micro)),
    )


def gradient_scratch(lay, ranks, dp_count):
    vmem, dma = pltpu.VMEM, pltpu.SemaphoreType.DMA
    if not lay.fast:
        return dict(
            stage=vmem((256, C_MID), BF16),
            stage_sem=dma,
            ready=vmem((ranks * READY, C_MID), BF16),
        )
    part = C_MID // ranks
    height, chips = sum(HEIGHTS), dp_count // 2
    return dict(
        dw=vmem((height, C_MID), BF16),
        dw_pair=vmem((height // 2, C_MID), BF16),
        dw_near=vmem((chips - 1, height // dp_count, C_MID), BF16),
        dw_sum=vmem((height // dp_count, C_MID), BF16),
        da=vmem((C_IN, part), BF16),
        da_pair=vmem((C_IN // 2, part), BF16),
        da_near=vmem((chips - 1, C_IN // dp_count, part), BF16),
        dw_relay=vmem((height // dp_count, C_MID), BF16),
        da_relay=vmem((C_IN // dp_count, part), BF16),
        relay_send=dma,
        relay_recv=dma((8,)),
        da_sum=vmem((C_IN // dp_count, part), BF16),
        share=vmem((ROWS // dp_count, C_MID), BF16),
        pair_send=dma((2,)),
        pair_recv=dma((8,)),
        near_send=dma((2,)),
        near_recv=dma((8,)),
        share_send=dma((2,)),
        share_recv=dma,
        hold=vmem((ROWS // dp_count, C_MID), BF16),
        hold_2=vmem((ROWS // dp_count // ranks, C_MID), BF16),
        hold_recv=dma((3,)),
        ship_send=dma((3,)),
    )


def chain_kernel(lay, ranks, dp_count, names, *refs):
    inputs = ("x_in", "x_in_2", "cot_in", "cot_in_2", "w_in", "gains_in", "shifts_in", "masks")
    outputs = ("out", "out_2", "grad", "grad_2")
    outputs += ("gain_share", "shift_share", "share_out") if lay.fast else ("gains_out", "dw", "da0")
    r = SimpleNamespace(**dict(zip(inputs + outputs + names, refs)))
    pieces = (r.a0, r.b0, r.c0, r.p0, r.a1, r.b1, r.c1)
    micro, rows = lay.micro, lay.rows
    first = lay.spans[0][1]
    part, wide = C_MID // ranks, C_OUT // ranks
    section, dp = lax.axis_index("section"), lax.axis_index("dp")
    core = lax.rem(dp, 2)
    sibling = (section, dp + 1 - 2 * core)
    masks = r.masks
    mine = pl.ds(pl.multiple_of(section * part, part), part)
    mine_wide = pl.ds(pl.multiple_of(section * wide, wide), wide)

    def other(k):
        return lax.rem(section + k, ranks)

    def across_dp(act):
        if dp_count <= 8:
            for k in (6, 2, 7, 3, 4, 5, 1) if dp_count == 8 else range(1, dp_count):
                act((section, lax.rem(dp + k, dp_count)))
        else:

            def step(k, carry):
                act((section, lax.rem(dp + k, dp_count)))
                return carry

            lax.fori_loop(1, dp_count, step, 0)

    def remote(src, dst, send, recv, device):
        return pltpu.make_async_remote_copy(
            src_ref=src,
            dst_ref=dst,
            send_sem=send,
            recv_sem=recv,
            device_id=device,
            device_id_type=MESH,
        )

    def wait_bytes(ref, sem):
        pltpu.make_async_copy(ref, ref, sem).wait()

    def some_micros(body, first_micro, last_micro):
        def step(m, carry):
            body(m)
            return carry

        lax.fori_loop(first_micro, last_micro, step, 0)

    def each_micro(body):
        some_micros(body, 0, micro)

    waiting = []

    def flush():
        while waiting:
            waiting.pop()(micro - 1)

    def stage(body):
        if not waiting:
            some_micros(body, 0, micro - 1)
        else:
            before = waiting.pop()

            def step(i, carry):
                @pl.when(i == 1)
                def _():
                    before(micro - 1)

                @pl.when(i != 1)
                def _():
                    body(jnp.maximum(i - 1, 0))

                return carry

            lax.fori_loop(0, micro, step, 0)
        waiting.append(body)

    barrier = pltpu.get_barrier_semaphore()

    def greet(device):
        pl.semaphore_signal(barrier, inc=1, device_id=device, device_id_type=MESH)

    if lay.fast:
        r.share[...] = jnp.zeros(r.share.shape, BF16)
        for k in range(ranks):
            for j in range(dp_count):
                if k or j:
                    greet((other(k), lax.rem(dp + j, dp_count)))
        greetings = ranks * dp_count - 1
    else:
        across_dp(greet)
        for k in range(1, ranks):
            greet((other(k), dp))
        greetings = dp_count - 1 + ranks - 1

    def load_grids(m):
        slot = m % 2
        return (
            pltpu.make_async_copy(r.x_in.at[m], r.x_grid.at[slot], r.x_sem.at[0, slot]),
            pltpu.make_async_copy(r.x_in_2.at[m], r.x_grid_2.at[slot], r.x_sem.at[1, slot]),
        )

    for m in range(2):
        for copy in load_grids(m):
            copy.start()
    r.slide[...] = jnp.zeros(r.slide.shape, F32)
    r.fan[...] = jnp.zeros(r.fan.shape, F32)

    place = lax.rem(dp, 4)
    group = dp - place
    pair_place = lax.rem(place + 2, 4)
    pair = (section, group + pair_place)

    place_8 = lax.rem(dp, 8)
    group_8 = dp - place_8
    chip_8 = place_8 // 2
    EIGHTH, STEP = 9 * part // 8, 3 * part // 8

    def eighth(which, step):
        return r.b0.at[pl.ds(pl.multiple_of(EIGHTH * which + STEP * step, 16), STEP)]

    def eight_copy(way, step, src, dst, device):
        remote(src, dst, r.eight_send, r.eight_recv.at[way, step], device).start()

    def send_b0():
        for step in range(3):
            for k in range(1, ranks):
                row = READY * other(k) + 16 * place_8 + STEP * step
                src = ready.at[pl.ds(pl.multiple_of(row, 16), STEP)]
                eight_copy(0, step, src, eighth(place_8, step), (other(k), dp))

    def pass_on_b0(step):
        @pl.when(section != 0)
        def _():
            own = eighth(place_8, step)
            wait_bytes(own, r.eight_recv.at[0, step])
            for k in range(1, 4):
                target = lax.rem(chip_8 + k, 4)
                eight_copy(1, step, own, own, (section, group_8 + 2 * target + core))
            eight_copy(2, step, own, own, sibling)

    def pass_back_b0(step):
        @pl.when(section != 0)
        def _():
            wait_bytes(r.b0.at[pl.ds(0, 3 * STEP)], r.eight_recv.at[1, step])
            for k in range(1, 4):
                theirs = eighth(2 * lax.rem(chip_8 + k, 4) + core, step)
                eight_copy(3, step, theirs, theirs, sibling)

    def need_b0():
        @pl.when(section != 0)
        def _():
            for step in range(3):
                wait_bytes(r.b0.at[pl.ds(0, STEP)], r.eight_recv.at[2, step])
                wait_bytes(r.b0.at[pl.ds(0, 3 * STEP)], r.eight_recv.at[3, step])

    def b0_sent():
        @pl.when(section == 0)
        def _():
            wait_bytes(r.b0.at[pl.ds(0, 9 * STEP)], r.eight_send)

        @pl.when(section != 0)
        def _():
            wait_bytes(r.b0.at[pl.ds(0, 21 * STEP)], r.eight_send)

    ready = r.dw if lay.fast else r.ready

    def parts(number):
        return 2 if number in (A1, C1) else 4

    def place_in(number):
        return core if parts(number) == 2 else place

    def run_jobs(jobs):
        def load(number):
            start, count, _ = jobs[number]
            start = start if isinstance(start, int) else pl.multiple_of(start, 512)
            slot = number % SLOTS
            return pltpu.make_async_copy(
                r.w_in.at[pl.ds(start, count)], r.raw.at[slot, pl.ds(0, count)], r.raw_sem.at[slot]
            )

        for number in range(min(SLOTS, len(jobs))):
            load(number).start()
        for number, (_, count, use) in enumerate(jobs):
            load(number).wait()
            use(r.raw[number % SLOTS, pl.ds(0, count), :])
            if number + SLOTS < len(jobs):
                load(number + SLOTS).start()

    def by_rows(value):
        return value.reshape(value.shape[0] // 4, C_MID)

    def by_columns(value):
        return value.reshape(value.shape[0] // 16, C_OUT)

    def first_jobs(source):
        jobs = []

        def keep_a0(i):
            def use(value):
                r.a0_all[pl.ds(C_MID * i, C_MID), :] = by_rows(value)

            return (2048 * i, 2048, use)

        def keep_taps(base, row):
            def use(value):
                matrix = by_rows(value)
                for t in range(ranks):
                    if t != source:
                        ready[pl.ds(READY * t + row, part), :] = matrix[part * t : part * (t + 1)]

            return (2048 * base, 2048, use)

        def keep_wide(chunk, row):
            def use(value):
                matrix = by_columns(value)
                for t in range(ranks):
                    if t != source:
                        ready[pl.ds(READY * t + row, 128), :] = matrix[:, wide * t : wide * (t + 1)]

            return (2048 * chunk, 2048, use)

        def keep_tall(t):
            def use(value):
                ready[pl.ds(READY * t, 256), :] = by_rows(value)

            return (2048 * t + 1024 * core, 1024, use)

        if source == 0:
            jobs = [keep_a0(0), keep_a0(1)] + [keep_taps(2 + place_8 + j, part * j) for j in range(2)]
        elif source == 1:
            jobs = [keep_wide(place, 0)] + [keep_wide(4 + 2 * place + j, 128 + 128 * j) for j in range(2)]
        elif source == 2:
            jobs = [keep_tall(t) for t in range(ranks) if t != source]
            jobs += [keep_taps(4 + 2 * place + j, 256 + part * j) for j in range(3)]
        else:
            jobs = [keep_wide(2 * core + j, 128 * j) for j in range(2)]
        return jobs

    def own_jobs(source):
        def put(ref, row, count):
            def use(value):
                ref[pl.ds(row, count), :] = by_rows(value)

            return use

        def put_wide(ref, row):
            def use(value):
                ref[pl.ds(row, 128), :] = by_columns(value)[:, wide * source : wide * (source + 1)]

            return use

        if source == 0:
            return [(2048 * (2 + tap), 512, put(r.b0, part * tap, part)) for tap in range(9)]
        if source == 1:
            jobs = [(2048 * i, 2048, put_wide(r.c0, 128 * i)) for i in range(4)]
            return jobs + [(2048 * (4 + i), 2048, put_wide(r.p0, 128 * i)) for i in range(8)]
        if source == 2:
            jobs = [(2048 * source, 2048, put(r.a1, 0, wide))]
            start = 512 * source
            return jobs + [
                (2048 * (4 + tap) + start, 512, put(r.b1, part * tap, part)) for tap in range(9)
            ]
        return [(2048 * i, 2048, put_wide(r.c1, 128 * i)) for i in range(4)]

    def send_piece(number):
        count = pieces[number].shape[0] // parts(number)
        at = pl.ds(pl.multiple_of(place_in(number) * count, 32), count)
        for k in range(1, ranks):
            t = other(k)
            if number == A0:
                src = r.a0_all.at[at, pl.ds(pl.multiple_of(t * part, part), part)]
            else:
                row = {B1: 256 + 32 * place, P0: 128}.get(number, 0)
                src = ready.at[pl.ds(pl.multiple_of(READY * t + row, 32), count)]
            remote(
                src,
                pieces[number].at[at],
                r.piece_send.at[number],
                r.piece_recv.at[number],
                (t, dp),
            ).start()

    def quarter_of(number, which):
        ref = pieces[number]
        count = ref.shape[0] // parts(number)
        return ref.at[pl.ds(pl.multiple_of(which * count, 32), count)]

    def pass_quarter(number, way, which, device):
        quarter = quarter_of(number, which)
        remote(
            quarter, quarter, r.pass_send.at[number], r.pass_recv.at[number, way], device
        ).start()

    def pass_on(number):
        @pl.when(section != SOURCE[number])
        def _():
            own = place_in(number)
            wait_bytes(quarter_of(number, own), r.piece_recv.at[number])
            if parts(number) == 4:
                pass_quarter(number, 1, own, pair)
            pass_quarter(number, 0, own, sibling)

    def pass_back(number):
        @pl.when(section != SOURCE[number])
        def _():
            wait_bytes(quarter_of(number, pair_place), r.pass_recv.at[number, 1])
            pass_quarter(number, 2, pair_place, sibling)

    def need(number):
        @pl.when(section != SOURCE[number])
        def _():
            wait_bytes(quarter_of(number, 0), r.pass_recv.at[number, 0])
            if parts(number) == 4:
                wait_bytes(quarter_of(number, 0), r.pass_recv.at[number, 2])

    def at_source(source, action):
        @pl.when(section == source)
        def _():
            action()

    for source in range(ranks):
        at_source(source, lambda: run_jobs(first_jobs(source)))
    pl.semaphore_wait(barrier, greetings)
    scales = r.scales
    for k in range(1, ranks):
        for i, row in enumerate((r.gains_in, r.shifts_in)):
            remote(
                row, scales.at[i, section], r.scale_send.at[i], r.scale_recv.at[i], (other(k), dp)
            ).start()
    at_source(0, lambda: (send_piece(A0), send_b0()))
    at_source(2, lambda: (send_piece(A1), send_piece(B1)))
    at_source(3, lambda: send_piece(C1))
    scales[0, section] = r.gains_in[...]
    scales[1, section] = r.shifts_in[...]

    @pl.when(section == 0)
    def _():
        r.a0[...] = r.a0_all[:, :part]

    mine_columns = pl.ds(pl.multiple_of(section * wide, wide), wide)
    cot_copies = (
        pltpu.make_async_copy(r.cot_in.at[:, :, :, :, mine_columns], r.cot_grid, r.cot_sem.at[0]),
        pltpu.make_async_copy(
            r.cot_in_2.at[:, :, :, :, mine_columns], r.cot_grid_2, r.cot_sem.at[1]
        ),
    )
    for copy in cot_copies:
        copy.start()

    def clear_padding(ref):
        for used, (start, stop) in zip(lay.used, lay.spans):
            low = (start + used) // 16 * 16
            high = -(-stop // 16) * 16
            if start + used < stop:
                ref[pl.ds(low, high - low), :] = jnp.zeros((high - low, ref.shape[1]), BF16)

    def by_phase(grid, group, down, right):
        side, crops = lay.sides[group], lay.crops[group]
        split = grid.reshape(side, 2, side, 2, crops, C_IN)
        return split[:, down, :, right].reshape(side * side * crops, C_IN)

    for m in range(micro):
        for copy in load_grids(m):
            copy.wait()
        for phase in range(4):
            clear_padding(r.x.at[phase, m])
            for group, grid in enumerate((r.x_grid, r.x_grid_2)):
                at = pl.ds(lay.spans[group][0], lay.used[group])
                r.x[phase, m, at, :] = by_phase(grid[m % 2], group, phase // 2, phase % 2)
        if m + 2 < micro:
            for copy in load_grids(m + 2):
                copy.start()

    def affine(segment, start, width):
        at = pl.ds(pl.multiple_of(start + section * width, width), width)
        return scales[0, segment, :, at], scales[1, segment, :, at]

    def affine_n(norm):
        return affine(2 * (norm // 2), C_MID * (norm % 2), part)

    def affine_w(norm):
        return affine((1, 1, 3)[norm], (0, C_OUT, 0)[norm], wide)

    def per_group(function, *values):
        top = function(0, *[v[:first] for v in values])
        low = function(1, *[v[first:] for v in values])
        return jnp.concatenate([top, low], axis=0)

    def widened(flags, width):
        return flags if width == part else jnp.concatenate([flags] * (width // part), axis=1)

    def keep(values):
        flags = widened(masks[4], values.shape[1])
        return jnp.where(flags > 0, values, 0.0)

    def moments(values):
        return [
            jnp.sum(v, axis=0, keepdims=True)
            for v in (
                values[:first],
                values[first:],
                values[:first] * values[:first],
                values[first:] * values[first:],
            )
        ]

    f31, b31 = (F31, B31) if lay.fast else (F31_LATE, B31_LATE)
    narrow = (r.norm_n, r.norm_n_send, r.norm_n_recv)
    broad = (r.norm_w, r.norm_w_send, r.norm_w_recv)
    double = None if lay.fast else (r.norm_v, r.norm_v_send, r.norm_v_recv)

    def norm_sent(kind, first_event, last_event):
        buffer, send, _ = kind
        used = buffer.at[pl.ds(0, last_event - first_event), :, pl.ds(0, dp_count - 1)]
        wait_bytes(used, send.at[first_event // buffer.shape[0]])

    def norm_start(kind, event, m, sums):
        buffer, send, recv = kind
        turns = buffer.shape[0]
        slot = buffer.at[event % turns, m, dp]
        for i, value in enumerate(sums):
            slot[pl.ds(i, 1), :] = value
        for i in range(len(sums), buffer.shape[3]):
            slot[pl.ds(i, 1), :] = jnp.zeros((1, slot.shape[1]), F32)
        across_dp(
            lambda device: remote(
                slot, slot, send.at[event // turns], recv.at[event % turns, m], device
            ).start()
        )

    def norm_finish(kind, event, m):
        buffer, _, recv = kind
        turn = event % buffer.shape[0]
        wait_bytes(buffer.at[0, m, pl.ds(0, dp_count - 1)], recv.at[turn, m])
        return jnp.sum(buffer[event % buffer.shape[0], m], axis=0)

    half_lanes = wide // 2
    my_half = pl.ds(pl.multiple_of(core * half_lanes, half_lanes), half_lanes)
    sibling_half = pl.ds(pl.multiple_of((1 - core) * half_lanes, half_lanes), half_lanes)

    def joint_copy(event, way, m, src, dst, device):
        remote(
            src, dst, r.joint_send.at[way], r.joint_recv.at[event % 2, way, m], device
        ).start()

    def joint_start(event, m, sums):
        for i, value in enumerate(sums):
            r.joint[event, m, pl.ds(i, 1), :] = value
        for i in range(len(sums), 8):
            r.joint[event, m, pl.ds(i, 1), :] = jnp.zeros((1, wide), F32)
        joint_copy(
            event, 0, m, r.joint.at[event, m, :, sibling_half], r.joint_pair.at[event, m], sibling
        )

    def joint_line(event, m):
        wait_bytes(r.joint_pair.at[event, m], r.joint_recv.at[event % 2, 0, m])
        r.joint_line[event, m, dp // 2] = r.joint[event, m, :, my_half] + r.joint_pair[event, m]
        slot = r.joint_line.at[event, m, dp // 2]
        for k in range(1, dp_count // 2):
            target = lax.rem(dp // 2 + k, dp_count // 2)
            joint_copy(event, 1, m, slot, slot, (section, 2 * target + core))

    def joint_back(event, m):
        wait_bytes(
            r.joint_line.at[event, m, pl.ds(0, dp_count // 2 - 1)], r.joint_recv.at[event % 2, 1, m]
        )
        r.joint_all[event, m, :, my_half] = jnp.sum(r.joint_line[event, m], axis=0)
        slot = r.joint_all.at[event, m, :, my_half]
        joint_copy(event, 2, m, slot, slot, sibling)

    def joint_finish(event, m):
        wait_bytes(r.joint_pair.at[event, m], r.joint_recv.at[event % 2, 2, m])
        return r.joint_all[event, m]

    def each_joint(step, event):
        if lay.fast:
            each_micro(lambda m: step(event, m))

    def stage_joint(step, event):
        if lay.fast:
            stage(lambda m: step(event, m))

    def finish_moments(kind, event, m, store, fold):
        if kind is None:
            sums = joint_finish(event, m)
        else:
            sums = norm_finish(kind, event, m)
        ref, norm = store
        found = []
        for group in range(2):
            count = float(lay.totals[group] * fold)
            mean = sums[group : group + 1] / count
            square = sums[2 + group : 3 + group] / count
            found += [mean, lax.rsqrt(square - mean * mean + EPSILON)]
        for i, value in enumerate(found):
            ref[norm, m, pl.ds(i, 1), :] = value
        return found

    def moments_of(ref, norm, m):
        return [ref[norm, m, pl.ds(i, 1), :] for i in range(4)]

    def normalized(values, found):
        return per_group(lambda g, v: (v - found[2 * g]) * found[2 * g + 1], values)

    def norm_change(upstream, normed, found, gain, sums, fold):
        def one(group, u, n):
            count = float(lay.totals[group] * fold)
            plain = sums[0][group] * gain / count
            along = sums[1][group] * gain / count
            return found[2 * group + 1] * (u * gain - plain - n * along)

        return keep(per_group(one, upstream, normed)).astype(BF16)

    def add_gains(place, sums):
        at = pl.ds(place, sums[0][0].shape[1])
        own = r.gains.at[section]
        own[pl.ds(0, 1), at] += sums[1][0] + sums[1][1]
        own[pl.ds(1, 1), at] += sums[0][0] + sums[0][1]

    def rows_of(totals, at):
        return [totals[at : at + 1], totals[at + 1 : at + 2]]

    def upstream_sums(upstream, normeds):
        sums = []
        for v in [upstream] + [upstream * n for n in normeds]:
            sums += [
                jnp.sum(v[:first], axis=0, keepdims=True),
                jnp.sum(v[first:], axis=0, keepdims=True),
            ]
        return sums

    def slid(ref, cols, down, right):
        pieces = []
        for (start, stop), side, crops in zip(lay.spans, lay.sides, lay.crops):
            at = PAD + start + (down * side + right) * crops
            pieces.append(ref[pl.ds(at, stop - start), cols])
        values = jnp.concatenate(pieces, axis=0)
        flags = masks[(down + 1) * 3 + right + 1]
        return jnp.where(flags > 0, values, 0.0)

    def tile_rows(used):
        low = used // 8 * 8
        assert used + 3 <= low + 8
        return low

    def center(values):
        pieces_of = []
        for used, (start, stop) in zip(lay.used, lay.spans):
            block = values[start:stop]
            low = tile_rows(used)
            mean = jnp.sum(block, axis=0, keepdims=True) / float(used)
            high = mean.astype(BF16).astype(F32)
            middle = (mean - high).astype(BF16).astype(F32)
            tile = block[low : low + 8]
            row = lax.broadcasted_iota(jnp.int32, tile.shape, 0) + low
            ends = jnp.where(row == used, high, jnp.where(row == used + 1, middle, mean - high - middle))
            ends = jnp.where(row < used + 3, ends, 0.0)
            pieces_of += [block[:low] - mean, jnp.where(row < used, tile - mean, ends)]
            if stop - start > low + 8:
                pieces_of.append(jnp.zeros((stop - start - low - 8, values.shape[1]), F32))
        return jnp.concatenate(pieces_of, axis=0)

    def uncenter(values):
        pieces_of = []
        for used, (start, stop) in zip(lay.used, lay.spans):
            block = values[start:stop]
            mean = block[used : used + 1] + block[used + 1 : used + 2] + block[used + 2 : used + 3]
            pieces_of.append(block + mean)
        return keep(jnp.concatenate(pieces_of, axis=0))

    def sum_start(event, m, values):
        send = r.sum_send
        send[event, m] = values.astype(BF16)
        for k in (1, 3, 2) if ranks == 4 else range(1, ranks):
            cols = pl.ds(pl.multiple_of(other(k) * part, part), part)
            remote(
                send.at[event, m, :, cols],
                r.sum_recv.at[event, m, k - 1],
                r.sum_send_sem,
                r.sum_recv_sem.at[event, m],
                (other(k), dp),
            ).start()

    def sum_finish(event, m):
        wait_bytes(r.sum_recv.at[event, m], r.sum_recv_sem.at[event, m])
        total = r.sum_send[event, m, :, mine].astype(F32)
        for k in range(ranks - 1):
            total = total + r.sum_recv[event, m, k].astype(F32)
        return total

    def get_start(event, m, values):
        get = r.get
        get[event, m, :, mine] = values
        for k in (1, 3, 2) if ranks == 4 else range(1, ranks):
            remote(
                get.at[event, m, :, mine],
                get.at[event, m, :, mine],
                r.get_send_sem,
                r.get_recv_sem.at[event, m],
                (other(k), dp),
            ).start()

    def get_wait(event, m):
        wait_bytes(
            r.get.at[event, m, :, pl.ds(0, C_MID - part)], r.get_recv_sem.at[event, m]
        )

    def get_finish(event, m):
        get_wait(event, m)
        return r.get[event, m]

    def own_start(number, m, src, dst):
        @pl.when(section != m)
        def _():
            remote(
                src, dst, r.own_send.at[number], r.own_recv.at[number], (m, dp)
            ).start()

        @pl.when(section == m)
        def _():
            pltpu.make_async_copy(src, dst, r.own_copy.at[number]).start()

    z1, zn, zw, y1 = r.z1, r.zn, r.zw, r.y1
    r.gains[section] = jnp.zeros(r.gains.shape[1:], F32)
    pass_on(A0)
    at_source(1, lambda: (send_piece(C0), send_piece(P0)))
    pass_on_b0(0)
    pass_back(A0)
    need(A0)
    pass_on_b0(1)

    def do_z1(m):
        sums = None
        for phase in range(4):
            value = dot(r.x[phase, m], r.a0[...])
            z1[phase, m] = value
            found = moments(value)
            sums = found if sums is None else [a + b for a, b in zip(sums, found)]
        norm_start(narrow, F01, m, sums)

    each_micro(do_z1)
    pass_on_b0(2)
    for source in range(ranks):
        at_source(source, lambda: run_jobs(own_jobs(source)))
    for group, grid in enumerate((r.cot_grid, r.cot_grid_2)):
        cot_copies[group].wait()
        for m in range(micro):
            if group == 0:
                clear_padding(r.cot.at[m])
            r.cot[m, pl.ds(lay.spans[group][0], lay.used[group]), :] = grid[m].reshape(
                lay.used[group], wide
            )
    for i in range(2):
        wait_bytes(scales.at[i, pl.ds(0, ranks - 1)], r.scale_recv.at[i])

    def do_a1(m):
        found = finish_moments(narrow, F01, m, (r.stat_n, N01), 4)
        gain, shift = affine_n(N01)
        taps = first_taps()
        for phase in range(4):
            value = silu(normalized(z1[phase, m], found) * gain + shift)
            r.slide[pl.ds(PAD, rows), :] = value
            for k, (at, down, right) in enumerate(taps):
                if at == phase:
                    r.patches[0, m, :, pl.ds(k * part, part)] = slid(
                        r.slide, slice(None), down, right
                    ).astype(BF16)

    each_micro(do_a1)
    for step in range(3):
        pass_back_b0(step)
    need_b0()

    def do_s2(m):
        sum_start(SUM_Z2, m, center(dot(r.patches[0, m], r.b0[...])))

    each_micro(do_s2)
    pass_on(A1)
    pass_on(C1)
    pass_on(C0)

    def do_z2(m):
        value = uncenter(sum_finish(SUM_Z2, m))
        zn[0, m] = value
        norm_start(narrow, F02, m, moments(value))

    stage(do_z2)
    pass_on(P0)

    def do_zs(m):
        value = dot(r.x[0, m], r.p0[...])
        zw[N12, m] = value
        if lay.fast:
            joint_start(J12, m, moments(value))
        else:
            norm_start(broad, F12, m, moments(value))


    def do_h0(m):
        found = finish_moments(narrow, F02, m, (r.stat_n, N02), 1)
        gain, shift = affine_n(N02)
        get_start(GET_H0, m, keep(silu(normalized(zn[0, m], found) * gain + shift)).astype(BF16))

    stage(do_h0)
    flush()
    pass_back(C0)
    pass_back(P0)
    need(P0)
    each_micro(do_zs)
    each_joint(joint_line, J12)
    need(C0)

    def do_zc(m):
        value = dot(get_finish(GET_H0, m), r.c0[...])
        zw[N11, m] = value
        if lay.fast:
            joint_start(J11, m, moments(value))
        else:
            norm_start(broad, F11, m, moments(value))

    stage(do_zc)
    stage_joint(joint_line, J11)
    each_joint(joint_back, J12)
    stage_joint(joint_back, J11)
    need(A1)

    def before1(m):
        main = normalized(zw[N11, m], moments_of(r.stat_w, N11, m))
        short = normalized(zw[N12, m], moments_of(r.stat_w, N12, m))
        gain_main, shift_main = affine_w(N11)
        gain_short, shift_short = affine_w(N12)
        return main * gain_main + shift_main + short * gain_short + shift_short, main, short

    def do_y1(m):
        if lay.fast:
            finish_moments(None, J12, m, (r.stat_w, N12), 1)
            finish_moments(None, J11, m, (r.stat_w, N11), 1)
        else:
            finish_moments(broad, F12, m, (r.stat_w, N12), 1)
            finish_moments(broad, F11, m, (r.stat_w, N11), 1)
        value = keep(silu(before1(m)[0])).astype(BF16)
        y1[m] = value
        sum_start(SUM_ZA, m, center(dot(value, r.a1[...])))

    stage(do_y1)
    pass_on(B1)

    def do_za(m):
        value = uncenter(sum_finish(SUM_ZA, m))
        zn[1, m] = value
        norm_start(narrow, F21, m, moments(value))

    stage(do_za)
    pass_back(B1)
    need(B1)

    def do_a2(m):
        found = finish_moments(narrow, F21, m, (r.stat_n, N21), 1)
        gain, shift = affine_n(N21)
        r.slide[pl.ds(PAD, rows), :] = silu(normalized(zn[1, m], found) * gain + shift)
        for k, (down, right) in enumerate(second_taps()):
            r.patches[1, m, :, pl.ds(k * part, part)] = slid(
                r.slide, slice(None), down, right
            ).astype(BF16)
        sum_start(SUM_ZB, m, center(dot(r.patches[1, m], r.b1[...])))

    stage(do_a2)

    def do_zb(m):
        value = uncenter(sum_finish(SUM_ZB, m))
        zn[2, m] = value
        norm_start(narrow, F22, m, moments(value))

    stage(do_zb)

    def do_h2(m):
        found = finish_moments(narrow, F22, m, (r.stat_n, N22), 1)
        gain, shift = affine_n(N22)
        get_start(GET_H2, m, keep(silu(normalized(zn[2, m], found) * gain + shift)).astype(BF16))

    stage(do_h2)
    need(C1)

    def do_zd(m):
        value = dot(get_finish(GET_H2, m), r.c1[...])
        zw[N31, m] = value
        norm_start(broad, f31, m, moments(value))

    stage(do_zd)
    half_rows = pl.ds(pl.multiple_of(core * (C_IN // 2), 64), C_IN // 2)

    def lanes_of(which):
        return pl.ds(pl.multiple_of(which * part, part), part)

    for k in range(1, ranks):

        @pl.when(other(k) != 0)
        def _():
            remote(
                r.a0.at[half_rows],
                r.a0_all.at[half_rows, mine],
                r.all_send.at[0],
                r.all_recv.at[0],
                (other(k), dp),
            ).start()

    @pl.when(section != 0)
    def _():
        r.a0_all[:, mine] = r.a0[...]

    a0_others = r.a0_all.at[pl.ds(0, C_IN // 2), pl.ds(0, C_MID - part)]
    def do_output(m):
        found = finish_moments(broad, f31, m, (r.stat_w, N31), 1)
        gain, shift = affine_w(N31)
        normed = normalized(zw[N31, m], found)
        before = normed * gain + shift + y1[m].astype(F32)
        sigmoid = jax.nn.sigmoid(before)
        r.out_send[m] = (before * sigmoid).astype(BF16)
        upstream = r.cot[m].astype(F32) * (sigmoid * (1.0 + before * (1.0 - sigmoid)))
        r.skip[m] = upstream.astype(BF16)
        r.uw[m] = upstream
        norm_start(broad, b31, m, upstream_sums(upstream, [normed]))

    if not lay.fast:
        norm_sent(broad, 0, 3)
    stage(do_output)

    def do_ddzd(m):
        totals = norm_finish(broad, b31, m)
        sums = [rows_of(totals, 0), rows_of(totals, 2)]
        add_gains(C_MID + 2 * wide, sums)
        found = moments_of(r.stat_w, N31, m)
        normed = normalized(zw[N31, m], found)
        value = norm_change(r.uw[m], normed, found, affine_w(N31)[0], sums, 1)
        r.ddzd[m] = value
        sum_start(SUM_DH2, m, dot_back(value, r.c1[...]))

    stage(do_ddzd)

    def send_output(m):
        own_start(0, m, r.out_send.at[m], r.out_own.at[:, mine_wide])

    def narrow_upstream(norm, place, event, m, value):
        found = moments_of(r.stat_n, norm, m)
        gain, shift = affine_n(norm)
        normed = normalized(zn[place, m], found)
        upstream = value * silu_slope(normed * gain + shift)
        r.un[place, m] = upstream
        norm_start(narrow, event, m, upstream_sums(upstream, [normed]))

    def narrow_change(norm, place, event, m):
        totals = norm_finish(narrow, event, m)
        sums = [rows_of(totals, 0), rows_of(totals, 2)]
        add_gains(part * norm, sums)
        found = moments_of(r.stat_n, norm, m)
        normed = normalized(zn[place, m], found)
        return norm_change(r.un[place, m], normed, found, affine_n(norm)[0], sums, 1)

    def tall(ref, count):
        return ref.reshape(micro * rows, count)

    share_rows = ROWS // ranks
    slice_base = (0, 0, share_rows, share_rows + C_MID, 2 * share_rows, 2 * share_rows + wide, 3 * share_rows, HEIGHTS[B0])
    chips = dp_count // 2
    chip = dp // 2
    base_rows = [sum(HEIGHTS[:number]) for number in range(8)]

    def own_piece(number, refs):
        whole, pair, near, total, relayed = refs
        base, height = base_rows[number], whole.shape[0] if number == A0 else HEIGHTS[number]
        each = height // dp_count
        return (
            whole.at[pl.ds(base, height)],
            pair.at[pl.ds(base // 2, height // 2)],
            near.at[:, pl.ds(base // dp_count, each)],
            total.at[pl.ds(base // dp_count, each)],
            relayed.at[pl.ds(base // dp_count, each)],
            height,
        )

    def gradient_refs(number):
        if number == A0:
            return own_piece(number, (r.da, r.da_pair, r.da_near, r.da_sum, r.da_relay))
        return own_piece(number, (r.dw, r.dw_pair, r.dw_near, r.dw_sum, r.dw_relay))

    def make(number, left, right, unit, skip=0):
        height = HEIGHTS[number]
        right = right.reshape(micro * rows, C_MID)

        def step(i, carry):
            at = pl.multiple_of(i * unit, unit)
            value = dot_rows(left(pl.ds(at + skip, unit)).reshape(micro * rows, unit), right)
            if lay.fast:
                r.dw[pl.ds(pl.multiple_of(base_rows[number] + at, 128), unit), :] = value.astype(BF16)
            else:
                r.stage[pl.ds(0, unit), :] = value.astype(BF16)
                copy = pltpu.make_async_copy(
                    r.stage.at[pl.ds(0, unit)],
                    r.dw.at[pl.ds(pl.multiple_of(slice_base[number] + at, 128), unit)],
                    r.stage_sem,
                )
                copy.start()
                copy.wait()
            return carry

        lax.fori_loop(0, height // unit, step, 0)
        to_sibling(number)

    def to_sibling(number):
        if not lay.fast:
            return
        whole, pair, _, _, _, height = gradient_refs(number)
        each = height // dp_count
        for i in range(chips):
            remote(
                whole.at[pl.ds(pl.multiple_of((2 * i + 1 - core) * each, 16), each)],
                pair.at[pl.ds(i * each, each)],
                r.pair_send.at[int(number == A0)],
                r.pair_recv.at[number],
                sibling,
            ).start()

    lined = chips == 4
    at_end = (chip == 0) | (chip == chips - 1)
    inner = jnp.where(chip < 2, 1, 2) if lined else chip
    across = 3 - inner

    def rows_for(number, target):
        each = gradient_refs(number)[-1] // dp_count
        return pl.ds(pl.multiple_of((2 * target + core) * each, 16), each)

    def send_near(number, target, k):
        whole, _, near, _, _, _ = gradient_refs(number)
        remote(
            whole.at[rows_for(number, target)],
            near.at[k - 1],
            r.near_send.at[int(number == A0)],
            r.near_recv.at[number],
            (section, 2 * target + core),
        ).start()

    def fold(number):
        if not lay.fast:
            return
        whole, pair, near, _, relayed, height = gradient_refs(number)
        each = height // dp_count
        wait_bytes(pair, r.pair_recv.at[number])
        for k in sorted(range(1, chips + 1), key=lambda k: k != 2):
            target = lax.rem(chip + k, chips)
            at = rows_for(number, target)
            theirs = pair[pl.ds(pl.multiple_of(target * each, 16), each), :]
            whole[at, :] = (whole[at, :].astype(F32) + theirs.astype(F32)).astype(BF16)
            if k == chips:
                continue
            if not lined or number == A0:
                send_near(number, target, k)
                continue

            @pl.when(jnp.logical_not(at_end) & (target != across))
            def _():
                send_near(number, target, k)

            @pl.when(at_end & (target != across))
            def _():
                send_near(number, target, k)

            @pl.when(at_end & (target == across))
            def _():
                remote(
                    whole.at[at],
                    relayed,
                    r.relay_send,
                    r.relay_recv.at[number],
                    (section, 2 * inner + core),
                ).start()

    def relay(number):
        if not (lay.fast and lined and number != A0):
            return
        whole, _, _, _, relayed, height = gradient_refs(number)

        @pl.when(jnp.logical_not(at_end))
        def _():
            wait_bytes(relayed, r.relay_recv.at[number])
            at = rows_for(number, across)
            whole[at, :] = (whole[at, :].astype(F32) + relayed[...].astype(F32)).astype(BF16)

            @pl.when(chip == 1)
            def _():
                send_near(number, across, 1)

            @pl.when(chip == 2)
            def _():
                send_near(number, across, 3)

    def units(number):
        height = C_IN if number == A0 else HEIGHTS[number]
        each = height // dp_count
        whole = ROWS // dp_count
        unit = 64 if number in (A0, A1) else 16
        found = []
        for i in range(each // unit):
            row = dp * each + i * unit
            if number == A0:
                owner, at, cols = row // whole, lax.rem(row, whole), mine
            elif number in (C0, P0, C1):
                row = row + (C_MID if number == P0 else 0)
                owner, cols = row // (whole // ranks), slice(None)
                at = section * (whole // ranks) + lax.rem(row, whole // ranks)
            else:
                if number == A1:
                    row = row + section * wide
                else:
                    base = C_OUT if number == B1 else C_IN
                    row = row + (HEIGHTS[B0] if number == B0_REST else 0)
                    row = base + C_MID * (row // part) + part * section + lax.rem(row, part)
                owner, at, cols = row // whole, lax.rem(row, whole), slice(None)
            if number == C1:
                at = lax.rem(row, whole // ranks)
            keeper = {C1: r.hold_2, A1: r.hold, B1: r.hold}.get(number, r.share)
            place = keeper.at[pl.ds(pl.multiple_of(at, unit), unit), cols]
            found.append((owner, place))
        return unit, found

    def finish(number):
        if not lay.fast:
            return
        whole, pair, near, total, _, height = gradient_refs(number)
        each = height // dp_count
        value = whole[pl.ds(pl.multiple_of(dp * each, 16), each), :].astype(F32)
        if lined and number != A0:

            @pl.when(at_end)
            def _():
                wait_bytes(near, r.near_recv.at[number])

            @pl.when(jnp.logical_not(at_end))
            def _():
                wait_bytes(near.at[pl.ds(0, 2)], r.near_recv.at[number])

            second = jnp.where(at_end, near[1].astype(F32), 0.0)
            value = value + near[0].astype(F32) + second + near[2].astype(F32)
        else:
            wait_bytes(near, r.near_recv.at[number])
            for k in range(chips - 1):
                value = value + near[k].astype(F32)
        total[...] = value.astype(BF16)
        unit, found = units(number)
        held = number in HELD
        target = section if held else SOURCE[number]
        recv = r.hold_recv.at[HELD.index(number)] if held else r.share_recv
        send = r.share_send.at[int(number == A0)]
        for i, (owner, place) in enumerate(found):
            rows_here = pl.ds(i * unit, unit)
            src = total.at[rows_here]
            here = (owner == dp) & (section == target)

            @pl.when(here)
            def _():
                pltpu.make_async_copy(src, place, recv).start()
                pltpu.make_async_copy(src, pair.at[rows_here], send).start()

            @pl.when(jnp.logical_not(here))
            def _():
                remote(src, place, send, recv, (target, owner)).start()

    def held_blocks(number):
        if number == C1:
            found = []
            whole = ROWS // dp_count // ranks
            for device in range(dp_count):
                count = min(max(HEIGHTS[C1] - device * whole, 0), whole)
                if count:
                    at = pl.ds(pl.multiple_of(section * whole, 16), count)
                    found.append((dp == device, count, r.hold_2.at[pl.ds(0, count)], r.share.at[at]))
            return found
        blocks_64 = ROWS // dp_count // 64
        if number == A1:
            starts = [(wide // 64) * section + i for i in range(wide // 64)]
        else:
            starts = [
                C_OUT // 64 + (C_MID // 64) * (u // 2) + (part // 64) * section + u % 2
                for u in range(18)
            ]
        found = []
        for start in starts:
            at = pl.ds(pl.multiple_of(64 * lax.rem(start, blocks_64), 64), 64)
            found.append((start // blocks_64 == dp, 64, r.hold.at[at], r.share.at[at]))
        return found

    def held_rows(number, act):
        found = held_blocks(number)
        if number == C1:
            for here, count, _, _ in found:
                pl.when(here)(functools.partial(act, count))
            return
        total = sum(jnp.where(here, 1, 0) for here, _, _, _ in found)
        for count in range(1, 9 if number == A1 else 6):
            pl.when(total == count)(functools.partial(act, 64 * count))

    def ship(number):
        if not lay.fast:
            return
        which = HELD.index(number)
        held_rows(number, lambda count: wait_bytes(r.share.at[pl.ds(0, count)], r.hold_recv.at[which]))
        for here, _, src, dst in held_blocks(number):

            @pl.when(here & (section == SOURCE[number]))
            def _():
                pltpu.make_async_copy(src, dst, r.share_recv).start()

            @pl.when(here & (section != SOURCE[number]))
            def _():
                remote(
                    src, dst, r.ship_send.at[which], r.share_recv, (SOURCE[number], dp)
                ).start()

    def shipped(number):
        which = HELD.index(number)

        @pl.when(section != SOURCE[number])
        def _():
            held_rows(
                number, lambda count: wait_bytes(r.share.at[pl.ds(0, count)], r.ship_send.at[which])
            )

    def finish_shares():
        whole = ROWS // dp_count
        sizes = (C_IN + 9 * C_MID, ranks * (C_MID + C_IN), C_OUT + 9 * C_MID, ranks * C_MID)
        count = jnp.int32(0)
        for source, size in enumerate(sizes):
            count = jnp.where(section == source, size, count)
        count = jnp.clip(count - whole * dp, 0, whole)
        lengths = {min(max(size - whole * d, 0), whole) for size in sizes for d in range(dp_count)}
        for length in sorted(lengths):
            if length:

                @pl.when(count == length)
                def _():
                    wait_bytes(r.share.at[pl.ds(0, length)], r.share_recv)

    def store_norm_shares():
        shares = (r.gain_share, r.shift_share)
        count = GSEGMENT // dp_count
        for share in shares:
            share[...] = jnp.zeros(share.shape, F32)
        for source in range(ranks):
            for device in range(dp_count):
                start = device * count
                wide_norm = source % 2 == 1
                used = {1: 2 * C_OUT, 3: C_OUT}.get(source, 2 * C_MID)
                if start >= used:
                    continue

                @pl.when((section == source) & (dp == device))
                def _():
                    for i, share in enumerate(shares):
                        if wide_norm:
                            norm = start // C_OUT + (2 if source == 3 else 0)
                            place_in = start % C_OUT
                            at = C_MID + norm * wide + place_in % wide
                            share[...] = r.gains[place_in // wide, pl.ds(i, 1), pl.ds(at, count)]
                        else:
                            at = part * (source + start // C_MID)
                            for t in range(ranks):
                                share[:, pl.ds(part * t, part)] = r.gains[t, pl.ds(i, 1), pl.ds(at, part)]

    def gradients_sent():
        for group, (pair, near, total) in enumerate(
            ((r.dw_pair, r.dw_near, r.dw_sum), (r.da_pair, r.da_near, r.da_sum))
        ):
            wait_bytes(pair, r.pair_send.at[group])
            wait_bytes(total, r.share_send.at[group])
            if not lined or group == 1:
                wait_bytes(near, r.near_send.at[group])
                continue

            @pl.when(at_end)
            def _():
                wait_bytes(near.at[pl.ds(0, 2)], r.near_send.at[group])
                wait_bytes(r.dw_relay, r.relay_send)

            @pl.when(jnp.logical_not(at_end))
            def _():
                wait_bytes(near, r.near_send.at[group])

        for number in HELD:
            shipped(number)

    def do_dh2(m):
        value = sum_finish(SUM_DH2, m).astype(BF16).astype(F32)
        narrow_upstream(N22, 2, B22, m, value)

    norm_sent(narrow, 0, 4)
    stage(do_dh2)
    b0_sent()
    for number in (A0, C0, P0, A1, B1, C1):

        @pl.when(section != SOURCE[number])
        def _():
            count = pieces[number].shape[0] // parts(number)
            times = 3 if parts(number) == 4 else 1
            wait_bytes(pieces[number].at[pl.ds(0, times * count)], r.pass_send.at[number])

        @pl.when(section == SOURCE[number])
        def _():
            for _ in range(ranks - 1):
                wait_bytes(quarter_of(number, 0), r.piece_send.at[number])
    make(C1, lambda at: r.get[GET_H2, :, :, at], r.ddzd[...], 256)

    def do_ddzb(m):
        get_start(GET_DDZB, m, narrow_change(N22, 2, B22, m))

    stage(do_ddzb)
    fold(C1)

    def fan_out(m, event, weight):
        r.fan[pl.ds(PAD, rows), :] = dot_back(r.get[event, m], weight[...])

    def do_da2(m):
        get_finish(GET_DDZB, m)
        fan_out(m, GET_DDZB, r.b1)
        total = None
        for k, (down, right) in enumerate(second_taps()):
            term = slid(r.fan, pl.ds(k * part, part), -down, -right)
            total = term if total is None else total + term
        narrow_upstream(N21, 1, B21, m, total)

    stage(do_da2)

    @pl.when(section != 0)
    def _():
        wait_bytes(a0_others, r.all_recv.at[0])
        for k in range(1, ranks):
            block = r.a0_all.at[half_rows, lanes_of(other(k))]
            remote(block, block, r.all_send.at[1], r.all_recv.at[1], sibling).start()

    relay(C1)

    def do_ddza(m):
        get_start(GET_DDZA, m, narrow_change(N21, 1, B21, m))

    stage(do_ddza)
    make(B1, lambda at: r.patches[1, :, :, at], r.get[GET_DDZB], 128)
    finish(C1)

    def do_dy1(m):
        value = dot_back(get_finish(GET_DDZA, m), r.a1[...]) + r.skip[m].astype(F32)
        value = value.astype(BF16).astype(F32)
        before, main, short = before1(m)
        upstream = value * silu_slope(before)
        r.uw[m] = upstream
        sums = upstream_sums(upstream, [main, short])
        if lay.fast:
            joint_start(B11, m, sums)
        else:
            norm_start(double, B11, m, sums)

    stage(do_dy1)
    stage_joint(joint_line, B11)
    flush()
    each_micro(send_output)
    make(A1, lambda at: y1[:, :, at], r.get[GET_DDZA], 256)
    fold(B1)
    stage_joint(joint_back, B11)

    def do_ddzc(m):
        totals = joint_finish(B11, m) if lay.fast else norm_finish(double, B11, m)
        plain = rows_of(totals, 0)
        for norm, at, target in ((N11, 2, r.ddzd), (N12, 4, r.ddzs)):
            sums = [plain, rows_of(totals, at)]
            add_gains(C_MID + norm * wide, sums)
            found = moments_of(r.stat_w, norm, m)
            normed = normalized(zw[norm, m], found)
            target[m] = norm_change(r.uw[m], normed, found, affine_w(norm)[0], sums, 1)
        sum_start(SUM_DH0, m, dot_back(r.ddzd[m], r.c0[...]))

    stage(do_ddzc)
    flush()
    fold(A1)

    def do_dxs(m):
        r.dxs_send[m] = dot_back(r.ddzs[m], r.p0[...]).astype(BF16)

    each_micro(do_dxs)
    make(C0, lambda at: r.get[GET_H0, :, :, at], r.ddzd[...], 256)
    make(P0, lambda at: r.x[0, :, :, at], r.ddzs[...], 256)

    def do_dh0(m):
        value = sum_finish(SUM_DH0, m).astype(BF16).astype(F32)
        narrow_upstream(N02, 0, B02, m, value)

    def send_dxs(m):
        own_start(1, m, r.dxs_send.at[m], r.dxs_recv.at[section])

    stage(do_dh0)
    relay(B1)
    relay(A1)

    def do_ddz2(m):
        get_start(GET_DDZ2, m, narrow_change(N02, 0, B02, m))

    stage(do_ddz2)
    fold(C0)
    fold(P0)
    finish(A1)
    finish(B1)
    flush()

    def do_da1(m):
        get_wait(GET_DDZ2, m)

        @pl.when(m == micro - 2)
        def _():
            each_micro(send_dxs)

        fan_out(m, GET_DDZ2, r.b0)
        gain, shift = affine_n(N01)
        found = moments_of(r.stat_n, N01, m)
        sums = None
        for phase in range(4):
            total = None
            for k, (at, down, right) in enumerate(first_taps()):
                if at == phase:
                    term = slid(r.fan, pl.ds(k * part, part), -down, -right)
                    total = term if total is None else total + term
            normed = normalized(z1[phase, m], found)
            upstream = total * silu_slope(normed * gain + shift)
            r.u1[phase, m] = upstream
            terms = upstream_sums(upstream, [normed])
            sums = terms if sums is None else [a + b for a, b in zip(sums, terms)]
        norm_start(narrow, B01, m, sums)

    stage(do_da1)
    flush()
    relay(C0)
    relay(P0)
    make(B0, lambda at: r.patches[0, :, :, at], r.get[GET_DDZ2], 128)
    make(B0_REST, lambda at: r.patches[0, :, :, at], r.get[GET_DDZ2], 128, HEIGHTS[B0])
    fold(B0)
    fold(B0_REST)
    relay(B0)

    out_own = r.out_own
    wait_bytes(out_own.at[:, mine_wide], r.own_copy.at[0])
    wait_bytes(out_own.at[:, pl.ds(0, C_OUT - wide)], r.own_recv.at[0])
    def store_grid(refs, values, pick):
        for group, ref in enumerate(refs):
            start, used = lay.spans[group][0], lay.used[group]
            side, crops = lay.sides[group], lay.crops[group]
            grid = values[start : start + used].astype(BF16).reshape(side, side, crops, values.shape[1])
            pick(ref, grid)

    def store_output(ref, grid):
        ref[...] = grid

    store_grid((r.out_grid, r.out_grid_2), out_own[...].astype(F32), store_output)
    results = [
        pltpu.make_async_copy(src, dst, r.result_sem.at[i])
        for i, (src, dst) in enumerate(
            (
                (r.out_grid, r.out),
                (r.out_grid_2, r.out_2),
                (r.grad_grid, r.grad),
                (r.grad_grid_2, r.grad_2),
            )
        )
    ]
    results[0].start()
    results[1].start()

    def do_ddz1(m):
        totals = norm_finish(narrow, B01, m)
        sums = [rows_of(totals, 0), rows_of(totals, 2)]
        add_gains(0, sums)
        found = moments_of(r.stat_n, N01, m)
        gain = affine_n(N01)[0]
        for phase in range(4):
            normed = normalized(z1[phase, m], found)
            r.ddz1[phase, m] = norm_change(r.u1[phase, m], normed, found, gain, sums, 4)
        own_start(2, m, r.ddz1.at[:, m], r.ddz1_own.at[:, :, mine])

    each_micro(do_ddz1)
    ship(C1)
    ship(B1)
    ship(A1)
    for k in range(1, ranks):
        remote(
            r.gains.at[section],
            r.gains.at[section],
            r.gain_send,
            r.gain_recv,
            (other(k), dp),
        ).start()

    def da0_step(i, carry):
        at = pl.ds(pl.multiple_of(i * 128, 128), 128)
        total = None
        for phase in range(4):
            value = dot_rows(
                r.x[phase, :, :, at].reshape(micro * rows, 128),
                r.ddz1[phase].reshape(micro * rows, part),
            )
            total = value if total is None else total + value
        da0 = r.da if lay.fast else r.da0
        da0[pl.ds(pl.multiple_of(i * 128, 128), 128), :] = total.astype(BF16)
        return carry

    lax.fori_loop(0, C_IN // 128, da0_step, 0)
    to_sibling(A0)
    finish(C0)
    relay(B0_REST)
    fold(A0)
    finish(P0)
    finish(B0)
    finish(B0_REST)
    finish(A0)

    dxs, ddz1_own = r.dxs_recv, r.ddz1_own

    @pl.when(section != 0)
    def _():
        wait_bytes(a0_others, r.all_recv.at[1])

    wait_bytes(dxs.at[0], r.own_copy.at[1])
    wait_bytes(dxs.at[pl.ds(0, ranks - 1)], r.own_recv.at[1])
    wait_bytes(ddz1_own.at[:, :, mine], r.own_copy.at[2])
    wait_bytes(ddz1_own.at[:, :, pl.ds(0, C_MID - part)], r.own_recv.at[2])
    for phase in range(4):
        value = dot_back(ddz1_own[phase], r.a0_all[...])
        if phase == 0:
            extra = dxs[0].astype(F32)
            for k in range(1, ranks):
                extra = extra + dxs[k].astype(F32)
            value = value + extra.astype(BF16).astype(F32)

        def store_phase(ref, grid):
            ref[:, phase // 2, :, phase % 2] = grid

        store_grid((r.grad_grid, r.grad_grid_2), value, store_phase)
    wait_bytes(r.gains.at[pl.ds(0, ranks - 1)], r.gain_recv)
    if lay.fast:
        store_norm_shares()
    else:
        r.gains_out[...] = r.gains[...]

    results[2].start()
    results[3].start()
    if lay.fast:
        finish_shares()
        results.append(pltpu.make_async_copy(r.share, r.share_out, r.result_sem.at[4]))
        results[4].start()
        gradients_sent()

    wait_bytes(r.sum_recv, r.sum_send_sem)
    wait_bytes(r.get.at[:, :, :, pl.ds(0, C_MID - part)], r.get_send_sem)
    norm_sent(narrow, 4, 8)
    if lay.fast:
        norm_sent(broad, 0, 2)
        wait_bytes(r.joint_pair, r.joint_send.at[0])
        wait_bytes(r.joint_line.at[:, :, pl.ds(0, dp_count // 2 - 1)], r.joint_send.at[1])
        wait_bytes(r.joint_pair, r.joint_send.at[2])
    else:
        norm_sent(broad, 3, 4)
        norm_sent(double, 0, 1)
    for copy in results:
        copy.wait()
    wait_bytes(out_own.at[:, pl.ds(0, C_OUT - wide)], r.own_send.at[0])
    wait_bytes(dxs.at[pl.ds(0, ranks - 1)], r.own_send.at[1])
    wait_bytes(ddz1_own.at[:, :, pl.ds(0, C_MID - part)], r.own_send.at[2])

    @pl.when(section == 0)
    def _():
        wait_bytes(a0_others, r.all_send.at[0])

    @pl.when(section != 0)
    def _():
        wait_bytes(a0_others.at[:, pl.ds(0, (ranks - 2) * part)], r.all_send.at[0])
        wait_bytes(a0_others, r.all_send.at[1])

    wait_bytes(r.gains.at[pl.ds(0, ranks - 1)], r.gain_send)
    for i in range(2):
        wait_bytes(scales.at[i, pl.ds(0, ranks - 1)], r.scale_send.at[i])


def chain(lay, ranks, dp_count, operands):
    micro, rows = lay.micro, lay.rows
    part, wide = C_MID // ranks, C_OUT // ranks
    table = scratch_table(lay, ranks, dp_count)
    shapes = (
        *[jax.ShapeDtypeStruct(grid_shape(lay, group, 1, C_OUT), BF16) for group in range(2)],
        *[jax.ShapeDtypeStruct(phase_shape(lay, group), BF16) for group in range(2)],
    )
    if lay.fast:
        shapes += (jax.ShapeDtypeStruct((1, GSEGMENT // dp_count), F32),) * 2
        shapes += (jax.ShapeDtypeStruct((ROWS // dp_count, C_MID), BF16),)
    else:
        shapes += (
            jax.ShapeDtypeStruct((ranks, 2, C_MID + 3 * wide), F32),
            jax.ShapeDtypeStruct((ROWS, C_MID), BF16),
            jax.ShapeDtypeStruct((C_IN, part), BF16),
        )
    anywhere = pl.BlockSpec(memory_space=pl.ANY)
    inside = pl.BlockSpec(memory_space=pltpu.VMEM)
    return pl.pallas_call(
        functools.partial(chain_kernel, lay, ranks, dp_count, tuple(table)),
        out_shape=shapes,
        in_specs=[anywhere] * 5 + [inside] * 3,
        out_specs=[anywhere] * 4 + ([inside] * 2 + [anywhere] if lay.fast else [inside, anywhere, inside]),
        scratch_shapes=list(table.values()),
        compiler_params=pltpu.CompilerParams(
            collective_id=0, has_side_effects=True, vmem_limit_bytes=63 * 2**20
        ),
        name="chain",
    )(*operands)


def summed_gradient(slices, small, section, ranks):
    small = jnp.stack([small] + [jnp.zeros_like(small)] * (ranks - 1))
    slices = slices.reshape(ranks, ROWS // ranks, C_MID)
    arrived = lax.all_to_all(slices, "section", 0, 0, tiled=True).astype(F32)
    arrived_small = lax.all_to_all(small, "section", 0, 0, tiled=True).astype(F32)
    segment = segment_gradient(arrived, arrived_small, section, ranks)
    return lax.psum_scatter(segment.reshape(-1), "dp", scatter_dimension=0, tiled=True)


def norm_shares(gains, ranks, dp_count):
    part, wide = C_MID // ranks, C_OUT // ranks

    def joined(start, width):
        block = gains[:, :, start : start + width // ranks]
        return jnp.moveaxis(block, 0, 1).reshape(2, width)

    f01, f02, f21, f22 = [joined(part * i, C_MID) for i in range(4)]
    f11, f12, f31 = [joined(C_MID + wide * i, C_OUT) for i in range(3)]
    blank = jnp.zeros((2, GSEGMENT - 2 * C_MID), F32)
    segments = jnp.stack(
        [
            jnp.concatenate([f01, f02, blank], 1),
            jnp.concatenate([f11, f12], 1),
            jnp.concatenate([f21, f22, blank], 1),
            jnp.concatenate([f31, jnp.zeros((2, GSEGMENT - C_OUT), F32)], 1),
        ]
    )
    share = GSEGMENT // dp_count
    own_norms = lax.dynamic_index_in_dim(segments, lax.axis_index("section"), 0, keepdims=False)
    return lax.dynamic_slice_in_dim(own_norms, lax.axis_index("dp") * share, share, 1)


def deliver_kernel(ranks, *refs):
    plain, share_in, norms_in, refs = refs[:4], refs[4], refs[5:7], refs[7:]
    plain_out, share_out, norms_out, refs = refs[:4], refs[4], refs[5:7], refs[7:]
    held, share, order, load_sem, store_sem = refs[:4], refs[4], refs[5], refs[6], refs[7]
    loads = [
        pltpu.make_async_copy(src, dst, load_sem.at[i])
        for i, (src, dst) in enumerate(zip(plain + (share_in,), held + (share,)))
    ]
    stores = [
        pltpu.make_async_copy(src, dst, store_sem.at[i])
        for i, (src, dst) in enumerate(zip(held + (order,), plain_out + (share_out,)))
    ]
    turn = (4, 2, 0, 3, 1)
    for i in turn:
        loads[i].start()
    for src, dst in zip(norms_in, norms_out):
        dst[...] = src[...]
    whole, lanes = share.shape[0], 128
    for i in turn:
        loads[i].wait()
        if i == 4:
            odd = lax.rem(lax.axis_index("section"), 2)

            @pl.when(odd == 0)
            def _():
                for q in range(ranks):
                    order[pl.ds(q, whole, stride=ranks), :] = share[:, lanes * q : lanes * (q + 1)].astype(F32)

            @pl.when(odd == 1)
            def _():
                short = whole // ranks
                for t in range(ranks):
                    for q in range(ranks):
                        order[pl.ds(ranks * t + q, short, stride=ranks * ranks), :] = share[
                            t * short : (t + 1) * short, lanes * q : lanes * (q + 1)
                        ].astype(F32)

        stores[i].start()
    for i in turn:
        stores[i].wait()


def deliver(results, ranks):
    plain, norms, share = results[:4], results[4:6], results[6]
    order = jax.ShapeDtypeStruct((share.size // 128, 128), F32)
    anywhere = pl.BlockSpec(memory_space=pl.ANY)
    inside = pl.BlockSpec(memory_space=pltpu.VMEM)
    specs = [anywhere] * 5 + [inside] * 2
    like = [jax.ShapeDtypeStruct(v.shape, v.dtype) for v in plain]
    return pl.pallas_call(
        functools.partial(deliver_kernel, ranks),
        out_shape=like + [order] + [jax.ShapeDtypeStruct(v.shape, v.dtype) for v in norms],
        in_specs=specs,
        out_specs=specs,
        scratch_shapes=[pltpu.VMEM(v.shape, v.dtype) for v in list(plain) + [share, order]]
        + [pltpu.SemaphoreType.DMA((5,))] * 2,
        name="deliver",
    )(*plain, share, *norms)


def per_device(
    images_global, images_local, weights, norm_gains, norm_shifts, cotangent_global, cotangent_local
):
    section = lax.axis_index("section")
    ranks = lax.axis_size("section")
    dp_count = lax.axis_size("dp")
    lay = Layout(images_global.shape, images_local.shape, dp_count)
    micro, rows = lay.micro, lay.rows
    part = C_MID // ranks
    wide = C_OUT // ranks

    def cells_first(pictures):
        return jnp.moveaxis(pictures, 1, 3)

    masks = np.stack(
        [lay.valid(down, right) for down in (-1, 0, 1) for right in (-1, 0, 1)]
    ).astype(np.float32)
    masks = jnp.asarray(np.ascontiguousarray(np.broadcast_to(masks[:, :, None], (9, rows, part))))
    results = chain(
        lay,
        ranks,
        dp_count,
        (
            cells_first(images_global),
            cells_first(images_local),
            cells_first(cotangent_global),
            cells_first(cotangent_local),
            weights.reshape(-1, 128),
            norm_gains[None],
            norm_shifts[None],
            masks,
        ),
    )

    if lay.fast:
        results = deliver(results, ranks)
    out_global, out_local, grad_global, grad_local, *rest = results
    if lay.fast:
        share, gain_share, shift_share = rest
        own_norms, weight_gradient = (gain_share[0], shift_share[0]), share.reshape(-1)
    else:
        own_norms = norm_shares(rest[0], ranks, dp_count)
        weight_gradient = summed_gradient(*rest[1:], section, ranks)

    def crops_first(grid, side, crops):
        return jnp.moveaxis(grid.reshape(1, side, side, crops, -1), 3, 1)

    return (
        crops_first(out_global, lay.sides[0], lay.crops[0]),
        crops_first(out_local, lay.sides[1], lay.crops[1]),
        crops_first(grad_global, 2 * lay.sides[0], lay.crops[0]),
        crops_first(grad_local, 2 * lay.sides[1], lay.crops[1]),
        weight_gradient,
        own_norms[0],
        own_norms[1],
    )


def solution(mesh):
    images = P(None, "dp", None, None, None)
    made = P("section", "dp", None, None, None)
    return jax.shard_map(
        per_device,
        mesh=mesh,
        in_specs=(images, images, P("section"), P("section"), P("section"), images, images),
        out_specs=(made, made, made, made) + (P(("section", "dp")),) * 3,
        check_vma=False,
    )
```
